32 devices in a mesh: lon: 8 (over y, x, core), lat: 4 (over z).
Axes of the slice: x: 2, y: 2, z: 4, core: 2. Of those that a mesh axis runs over, the one named last changes fastest.
Arguments:
- noise: bfloat16 [4, 4, 256, 1024], P(None, None, 'lon', 'lat'), may hold values from -6 to 6
- velocity_u: float32 [4, 2, 256, 1024], P(None, None, 'lon', 'lat'), may hold values from -3 to 3
- velocity_v: float32 [4, 2, 256, 1024], P(None, None, 'lon', 'lat'), may hold values from -3 to 3
- thickness: float32 [4, 2, 256, 1024], P(None, None, 'lon', 'lat'), may hold values from 0.5 to 1.5
- land_sea: int32 [256, 1024], P('lon', 'lat'), may hold values 0 or 1
- conv_first: bfloat16 [32, 10, 3, 3], replicated, may hold values from -0.625 to 0.625
- bias_first: float32 [32], replicated, may hold values from -4 to 4
- conv_second: bfloat16 [32, 32, 3, 3], replicated, may hold values from -0.375 to 0.375
- bias_second: float32 [32], replicated, may hold values from -4 to 4
- conv_third: bfloat16 [32, 32, 3, 3], replicated, may hold values from -0.375 to 0.375
- bias_third: float32 [32], replicated, may hold values from -4 to 4
- conv_last: bfloat16 [4, 32, 3, 3], replicated, may hold values from -0.375 to 0.375
- bias_last: float32 [4], replicated, may hold values from -4 to 4
Outputs:
- new_u: float32 [4, 2, 256, 1024], P(None, None, 'lon', 'lat')
- new_v: float32 [4, 2, 256, 1024], P(None, None, 'lon', 'lat')
- new_h: float32 [4, 2, 256, 1024], P(None, None, 'lon', 'lat')
The draws below stay inside these ranges and needn't reach their ends.
All inputs are finite; a program needn't handle non-finite values. No bound on the sum of `land_sea` on one device may be relied on, other than what follows from the above.
Results may differ from the reference program's by a relative error of at most 0.0014.
Values may be sent and summed in bfloat16 or wider, within the bound.
No kernel may reach another device: no remote copies, remote signals or barrier semaphores. Data moves between devices by JAX's collectives and lax.ppermute only.
A program may use at most 128 MiB of HBM per device.

```python
import jax
import jax.numpy as jnp
from jax import lax

MEMBERS = 4
CH = 32
NOISE = 4
LEVELS = 2
NX = 256
NY = 1024


def place_ends(array, key, least, top_value):
    spot = [jax.random.randint(jax.random.fold_in(key, axis), (), 0, length) for axis, length in enumerate(array.shape)]
    main_axis = array.shape.index(max(array.shape))
    neighbour = spot[:main_axis] + [(spot[main_axis] + 1) % array.shape[main_axis]] + spot[main_axis + 1:]
    return array.at[tuple(spot)].set(least).at[tuple(neighbour)].set(top_value)


def block_scale(own_key, dims, pieces, low, top_value):
    factor_of, own = 1.0, jax.random.fold_in(own_key, 6)
    for position, parts in pieces:
        steps = jnp.exp(jax.random.uniform(jax.random.fold_in(own, position), (parts,), jnp.float32, low / len(pieces), top_value / len(pieces)))
        factor_of = factor_of * jnp.repeat(steps, dims[position] // parts).reshape([-1 if axis == position else 1 for axis in range(len(dims))])
    return factor_of


def bell_draw(key, extent, scale, limit, shards=(), held_as=jnp.bfloat16):
    gain = block_scale(key, extent, shards, -0.22, 0.18) if shards else 1.0
    values = jax.random.normal(key, extent, jnp.float32) * scale * gain
    return jnp.minimum(jnp.maximum(values, -limit), limit).astype(held_as)


def setup_inputs(seed: int = 0) -> dict:
    splits = jax.random.split(jax.random.key(seed), 14)
    noise = bell_draw(splits[0], (MEMBERS, NOISE, NX, NY), 1.0, 6.0, ((2, 8), (3, 4)))
    velocity_u = bell_draw(splits[1], (MEMBERS, LEVELS, NX, NY), 0.5, 3.0, ((2, 8), (3, 4)), jnp.float32)
    velocity_v = bell_draw(splits[2], (MEMBERS, LEVELS, NX, NY), 0.5, 3.0, ((2, 8), (3, 4)), jnp.float32)
    thickness = jnp.clip(0.5 + 1.0 * jax.random.uniform(splits[3], (MEMBERS, LEVELS, NX, NY), jnp.float32) ** block_scale(splits[3], (MEMBERS, LEVELS, NX, NY), ((2, 8), (3, 4)), -0.2, 0.2), 0.5, 1.5)
    land_sea = place_ends((jax.random.randint(splits[4], (NX, NY), 0, 8) < 7).astype(jnp.int32), jax.random.fold_in(splits[4], 1), 0, 1)
    conv_first = bell_draw(splits[5], (CH, NOISE + 3 * LEVELS, 3, 3), (9 * (NOISE + 3 * LEVELS)) ** -0.5, 0.625)
    bias_first = bell_draw(splits[6], (CH,), 1.0, 4.0, (), jnp.float32)
    conv_second = bell_draw(splits[7], (CH, CH, 3, 3), (9 * CH) ** -0.5, 0.375)
    bias_second = bell_draw(splits[8], (CH,), 1.0, 4.0, (), jnp.float32)
    conv_third = bell_draw(splits[9], (CH, CH, 3, 3), (9 * CH) ** -0.5, 0.375)
    bias_third = bell_draw(splits[10], (CH,), 1.0, 4.0, (), jnp.float32)
    conv_last = bell_draw(splits[11], (2 * LEVELS, CH, 3, 3), (9 * CH) ** -0.5, 0.375)
    bias_last = bell_draw(splits[12], (2 * LEVELS,), 1.0, 4.0, (), jnp.float32)
    return dict(noise=noise, velocity_u=velocity_u, velocity_v=velocity_v, thickness=thickness, land_sea=land_sea, conv_first=conv_first, bias_first=bias_first, conv_second=conv_second, bias_second=bias_second, conv_third=conv_third, bias_third=bias_third, conv_last=conv_last, bias_last=bias_last)


GRAVITY = 1.0
REDUCED = 0.5
TIME_STEP = 0.2
VISCOSITY = 0.05
CORIOLIS = 0.4


def extend(field, parity):
    wrapped = jnp.concatenate([field[..., -1:, :], field, field[..., :1, :]], axis=-2)
    top_row = wrapped[..., :, -1]
    north_rim = parity.astype(field.dtype)[:, None] * jnp.flip(top_row, axis=-1)
    south_rim = jnp.zeros_like(top_row)
    return jnp.concatenate([south_rim[..., None], wrapped, north_rim[..., None]], axis=-1)


def convolve(padded, weight, bias):
    result = lax.conv_general_dilated(padded.astype(jnp.float32)[None], weight.astype(jnp.float32), (1, 1), "VALID", dimension_numbers=("NCHW", "OIHW", "NCHW"), precision=lax.Precision.HIGHEST)[0]
    return result + bias[:, None, None]


def centre(quantity):
    return quantity[..., 1:-1, 1:-1]


def diff_lon(quantity):
    return 0.5 * (quantity[..., 2:, 1:-1] - quantity[..., :-2, 1:-1])


def diff_lat(quantity):
    return 0.5 * (quantity[..., 1:-1, 2:] - quantity[..., 1:-1, :-2])


def laplace(quantity):
    return quantity[..., 2:, 1:-1] + quantity[..., :-2, 1:-1] + quantity[..., 1:-1, 2:] + quantity[..., 1:-1, :-2] - 4.0 * centre(quantity)


def advance(pad_u, pad_v, pad_h, forcing, ocean, coriolis, levels):
    upper = GRAVITY * (pad_h[..., 0:1, :, :] + pad_h[..., 1:2, :, :])
    pressure = jnp.concatenate([upper, upper + REDUCED * pad_h[..., 1:2, :, :]], axis=-3)
    cell_u = centre(pad_u)
    cell_v = centre(pad_v)
    cell_h = centre(pad_h)
    new_u = ocean * (cell_u + TIME_STEP * (coriolis * cell_v - diff_lon(pressure) + forcing[..., :levels, :, :] + VISCOSITY * laplace(pad_u)))
    new_v = ocean * (cell_v + TIME_STEP * (-coriolis * cell_u - diff_lat(pressure) + forcing[..., levels:, :, :] + VISCOSITY * laplace(pad_v)))
    new_h = cell_h - TIME_STEP * (diff_lon(pad_h * pad_u) + diff_lat(pad_h * pad_v))
    return new_u, new_v, new_h


def reference(noise, velocity_u, velocity_v, thickness, land_sea, conv_first, bias_first, conv_second, bias_second, conv_third, bias_third, conv_last, bias_last):
    ocean = land_sea.astype(jnp.float32)
    lat_rows = jnp.arange(NY).astype(jnp.float32)
    coriolis = CORIOLIS * (2.0 * (lat_rows + 0.5) / NY - 1.0)
    hidden_layers = ((conv_first, bias_first), (conv_second, bias_second), (conv_third, bias_third))
    parity_first = jnp.concatenate([jnp.ones((NOISE,), jnp.float32), -jnp.ones((2 * LEVELS,), jnp.float32), jnp.ones((LEVELS,), jnp.float32)])
    parity_hidden = jnp.ones((CH,), jnp.float32)
    parity_state = jnp.concatenate([-jnp.ones((2 * LEVELS,), jnp.float32), jnp.ones((LEVELS,), jnp.float32)])

    def member(items):
        noise_one, u_one, v_one, h_one = items
        features = jnp.concatenate([noise_one.astype(jnp.float32), u_one, v_one, h_one], axis=0).astype(jnp.bfloat16)
        parity = parity_first
        for weight, bias in hidden_layers:
            pre = convolve(extend(features, parity), weight, bias)
            features = (jax.nn.silu(pre) * ocean).astype(jnp.bfloat16)
            parity = parity_hidden
        forcing = convolve(extend(features, parity), conv_last, bias_last) * ocean
        state = jnp.concatenate([u_one, v_one, h_one], axis=0)
        padded = extend(state, parity_state)
        return advance(padded[:LEVELS], padded[LEVELS:2 * LEVELS], padded[2 * LEVELS:], forcing, ocean, coriolis, LEVELS)

    new_u, new_v, new_h = lax.map(member, (noise, velocity_u, velocity_v, thickness))
    return (new_u, new_v, new_h)
```

```python
import functools

import jax
import jax.numpy as jnp
from jax import lax
from jax.experimental import pallas as pl
from jax.experimental.pallas import tpu as pltpu
from jax.sharding import PartitionSpec as P

REDUCED = 0.5
TIME_STEP = 0.2
VISCOSITY = 0.05
CORIOLIS = 0.4

RIM = 4
GAP = 32
NORTH, STRIP, GHOST, SOUTH = 0, 12, 16, 28
SUB = 16
LANES = 128
GROUP = 8
LAND = 2.0**100

f32 = jnp.float32
bf16 = jnp.bfloat16


def iota(shape, dim):
    return lax.broadcasted_iota(jnp.int32, shape, dim)


def dot(a, b):
    return jnp.dot(a, b, preferred_element_type=f32)


def exact_dot(a, b):
    return jnp.dot(a, b, preferred_element_type=f32, precision=lax.Precision.HIGHEST)


def pack_lon_kernel(sizes, n_lo, u_lo, v_lo, h_lo, s_lo, n_hi, u_hi, v_hi, h_hi, s_hi, head, tail):
    members, noises, levels = sizes
    fields = noises + 3 * levels
    lats = head.shape[1]
    upper = iota((GROUP, lats), 0) < RIM

    def field(m, c, refs):
        noise, u, v, h = refs
        if c < noises:
            full = noise[m, c].astype(f32)
            return full[:GROUP] if noise is n_lo else full[-GROUP:]
        c -= noises
        return (u, v, h)[c // levels][m, c % levels]

    lo = (n_lo, u_lo, v_lo, h_lo)
    hi = (n_hi, u_hi, v_hi, h_hi)
    for m in range(members):
        for c in range(0, fields, 2):
            rows = pl.ds((m * fields + c) * RIM, GROUP)
            head[rows] = jnp.where(upper, field(m, c, lo), pltpu.roll(field(m, c + 1, lo), RIM, 0))
            tail[rows] = jnp.where(upper, pltpu.roll(field(m, c, hi), RIM, 0), field(m, c + 1, hi))
    rows = pl.ds(members * fields * RIM, GROUP)
    head[rows] = s_lo[...].astype(f32)
    tail[rows] = pltpu.roll(s_hi[...].astype(f32), RIM, 0)


def group_tile(sizes, m, c, g, refs, groups):
    noise, u, v, h, sea, left, right = refs
    members, noises, levels = sizes
    fields = noises + 3 * levels
    if c == fields + 1:
        if g == groups - 1:
            return None
        c, g = fields, g + 1
    if g == 0 or g == groups - 1:
        src = left if g == 0 else right
        row = (m * fields + c) * RIM if c < fields else members * fields * RIM
        odd = (row // RIM) % 2
        tile = src[pl.ds(row // GROUP * GROUP, GROUP)]
        if odd == (1 if g == 0 else 0):
            return tile
        return pltpu.roll(tile, RIM, 0)
    rows = slice((g - 1) * GROUP, g * GROUP)
    if c < noises:
        return noise[m, c].astype(f32)[rows]
    if c == fields:
        return sea[rows].astype(f32)
    c -= noises
    return (u, v, h)[c // levels][m, c % levels, rows]


def pack_lat_kernel(
    sizes, n_lo, u_lo, v_lo, h_lo, s_lo, n_hi, u_hi, v_hi, h_hi, s_hi, left, right, head, tail
):
    members, noises, levels = sizes
    channels = noises + 3 * levels + 2
    groups = s_lo.shape[0] // GROUP + 2
    lane = iota((GROUP, LANES), 1)
    for out, refs, lanes in (
        (head, (n_lo, u_lo, v_lo, h_lo, s_lo), slice(0, LANES)),
        (tail, (n_hi, u_hi, v_hi, h_hi, s_hi), slice(left.shape[1] - LANES, left.shape[1])),
    ):
        refs = refs + (left.at[:, lanes], right.at[:, lanes])
        first = 0 if out is head else LANES - RIM
        for c in range(channels):
            total = jnp.zeros((GROUP, LANES), f32)
            for g in range(groups):
                for m in range(members):
                    tile = group_tile(sizes, m, c, g, refs, groups)
                    if tile is None:
                        continue
                    place = (g * members + m) * RIM
                    moved = pltpu.roll(tile, (place - first) % LANES, 1)
                    total = jnp.where((lane >= place) & (lane < place + RIM), moved, total)
            out[pl.ds(c * GROUP, GROUP)] = total


def weights_kernel(w1, w2, w3, w4, biases, t1, t2, t3, t4):
    hidden = w2.shape[2]
    per = LANES // hidden
    lane = iota((hidden, LANES), 1)
    fields = w1.shape[1] // GROUP
    rows = fields * GROUP
    out_lon = iota((rows, LANES), 1) // hidden
    in_lon = iota((rows, LANES), 0) % GROUP
    bias_row = iota((GROUP, LANES), 0)

    def bias_rows(layer, tile):
        part = 0.5 * biases[pl.ds(layer, 1), :]
        b1 = part.astype(bf16).astype(f32)
        b2 = (part - b1).astype(bf16).astype(f32)
        b3 = part - b1 - b2
        zero = jnp.zeros((GROUP, LANES), f32)
        return jnp.where(
            bias_row == 0,
            b1,
            jnp.where(bias_row == 1, b2, jnp.where(bias_row == 2, b3, zero)),
        )

    def sea_rows(shift, tile):
        lon = iota((2 * GROUP, LANES), 0)
        out = iota((2 * GROUP, LANES), 1) // hidden + per * tile
        return jnp.where(lon == out + shift, LAND, 0.0)

    pad = jnp.zeros((LANES - rows - 3 * GROUP, LANES), f32)
    empty = jnp.zeros((3 * GROUP, LANES), f32)
    for dj in range(3):
        for half in range(2):
            for tile in range(2):
                total = jnp.zeros((rows, LANES), f32)
                for di in range(3):
                    hit = in_lon + GROUP * half == out_lon + per * tile + di + RIM
                    total = jnp.where(hit, 0.5 * w1[dj * 3 + di].astype(f32), total)
                extra = empty
                if dj == 1 and half == 0:
                    extra = jnp.concatenate([sea_rows(5, tile), bias_rows(0, tile)], axis=0)
                block = jnp.concatenate([total, extra, pad], axis=0)
                t1[pl.ds((dj * 2 + half) * LANES, LANES), pl.ds(tile * LANES, LANES)] = block.astype(bf16)

    for layer, (w, t) in enumerate(((w2, t2), (w3, t3))):
        for dj in range(3):
            taps = []
            for di in range(3):
                cell = 0.5 * w[di, dj].astype(f32)
                wide = jnp.concatenate([cell, jnp.zeros((hidden, LANES - hidden), f32)], axis=1)
                square = jnp.concatenate([wide] * per, axis=0)
                taps.append(jnp.transpose(square)[:hidden])
            for lon in range(GROUP + 2):
                for tile in range(2):
                    total = jnp.zeros((hidden, LANES), f32)
                    for di in range(3):
                        total = jnp.where(lane // hidden + per * tile == lon - di, taps[di], total)
                    if lon < GROUP:
                        row = dj * GROUP * hidden + lon * hidden
                    else:
                        row = 3 * GROUP * hidden + dj * 2 * hidden + (lon - GROUP) * hidden
                    t[pl.ds(row, hidden), pl.ds(tile * LANES, LANES)] = total.astype(bf16)
        for tile in range(2):
            block = jnp.concatenate(
                [
                    jnp.zeros((2 * GROUP, LANES), f32),
                    sea_rows(6 + layer, tile),
                    bias_rows(1 + layer, tile),
                    jnp.zeros((3 * GROUP, LANES), f32),
                ],
                axis=0,
            )
            row = 3 * GROUP * hidden + 6 * hidden
            t[pl.ds(row, 2 * hidden), pl.ds(tile * LANES, LANES)] = block.astype(bf16)

    outs = w4.shape[2]
    lons = LANES // outs
    depth = t4.shape[0] // 3
    for dj in range(3):
        taps = []
        for di in range(3):
            cell = w4[di, dj].astype(f32)
            wide = jnp.concatenate([cell, jnp.zeros((outs, LANES - hidden), f32)], axis=1)
            square = jnp.concatenate(
                [jnp.broadcast_to(wide[c : c + 1], (lons, LANES)) for c in range(outs)], axis=0
            )
            taps.append(jnp.transpose(square)[:hidden])
        for lon in range(depth // hidden):
            total = jnp.zeros((hidden, LANES), f32)
            for di in range(3):
                total = jnp.where(lane % lons == lon - di, taps[di], total)
            t4[pl.ds(dj * depth + lon * hidden, hidden), :] = total.astype(bf16)


def main_kernel(
    sizes,
    place,
    bias_last,
    noise,
    u,
    v,
    h,
    sea,
    coriolis,
    left,
    right,
    south,
    north,
    strip,
    own_tail,
    t1,
    t2,
    t3,
    t4,
    new_u,
    new_v,
    new_h,
    cells,
    first,
    odd,
    even,
    force,
    turned,
):
    members, noises, levels = sizes
    fields = noises + 3 * levels
    lons, lats = sea.shape
    groups = lons // GROUP + 2
    chunks = SUB // members
    blocks = (lats + GAP) // chunks
    rows = blocks * SUB
    gap_k = lats - (chunks - 1) * blocks
    top = place[0] == 1
    refs = (noise, u, v, h, sea, left, right)

    wide = fields * GROUP + 2 * GROUP
    lane = iota((wide, LANES), 1)
    row_to = iota((wide, wide), 0)
    row_from = iota((wide, wide), 1)
    channel = row_to // GROUP
    same = channel == row_from // GROUP
    mirrored = same & (row_from % GROUP == GROUP - 1 - row_to % GROUP)
    odd_parity = (channel >= noises) & (channel < noises + 2 * levels)
    flip_rows = jnp.where(mirrored, jnp.where(odd_parity, -1.0, 1.0), 0.0)
    lane_from = iota((LANES, LANES), 0)
    lane_to = iota((LANES, LANES), 1)
    span = members * RIM
    source = (groups - 1 - lane_to // span) * span + lane_to % span + RIM - 1
    flip_lanes = jnp.where((lane_to % RIM == 0) & (lane_to < groups * span) & (lane_from == source), 1.0, 0.0)
    pair = exact_dot(flip_rows, jnp.concatenate([strip[...], own_tail[...]], axis=1))
    folded = exact_dot(pair[:, :LANES], flip_lanes)
    ghost = exact_dot(pair[:, LANES:], flip_lanes)
    north_rim = jnp.where((lane % RIM == 0) & top, folded, north[...])

    ones = jnp.ones((GROUP, LANES), f32)
    blank = jnp.zeros((LANES - wide - GROUP, LANES), f32)
    for g in range(groups):
        for m in range(members):
            cells[g, pl.ds(gap_k * SUB + m * chunks + chunks - 1, GAP, stride=SUB), :] = jnp.zeros(
                (GAP, LANES), f32
            )
    for n, (message, offset) in enumerate(
        ((south[...], SOUTH), (north_rim, NORTH), (strip[...], STRIP), (ghost, GHOST))
    ):
        body_rows = fields * GROUP
        tall = jnp.concatenate([message[:body_rows], message[body_rows:] - 1.0, ones, blank], axis=0)
        turned[n] = jnp.transpose(tall)
        for g in range(groups):
            for m in range(members):
                gap = (m - 1) % members if offset == SOUTH else m
                start = (gap_k + offset) * SUB + gap * chunks + chunks - 1
                cells[g, pl.ds(start, RIM, stride=SUB), :] = turned[n, pl.ds((g * members + m) * RIM, RIM), :]

    for t in range(lats // LANES):
        lanes = slice(t * LANES, (t + 1) * LANES)
        views = (
            noise.at[:, :, :, lanes],
            u.at[:, :, :, lanes],
            v.at[:, :, :, lanes],
            h.at[:, :, :, lanes],
            sea.at[:, lanes],
            left.at[:, lanes],
            right.at[:, lanes],
        )
        for g in range(groups):
            for m in range(members):
                tiles = [group_tile(sizes, m, c, g, views, groups) for c in range(fields)]
                own = group_tile(sizes, m, fields, g, views, groups) - 1.0
                following = group_tile(sizes, m, fields + 1, g, views, groups)
                following = jnp.zeros_like(own) if following is None else following - 1.0
                block = jnp.transpose(jnp.concatenate(tiles + [own, following, ones, blank], axis=0))
                for q in range(chunks):
                    lo = max(q * blocks, t * LANES)
                    hi = min((q + 1) * blocks, (t + 1) * LANES, lats)
                    if lo < hi:
                        start = (lo - q * blocks) * SUB + m * chunks + q
                        cells[g, pl.ds(start, hi - lo, stride=SUB), :] = block[lo - t * LANES : hi - t * LANES]

    for g in range(groups):
        first[g, pl.ds(SUB, rows), :] = cells[g].astype(bf16)
        first[g, pl.ds(0, SUB), :] = pltpu.roll(cells[g, pl.ds(rows - SUB, SUB), :], 1, 0).astype(bf16)
        first[g, pl.ds(SUB + rows, SUB), :] = pltpu.roll(cells[g, pl.ds(0, SUB), :], SUB - 1, 0).astype(bf16)

    hidden = LANES // 4
    per = LANES // hidden
    tiles = odd.shape[0]
    step = rows // 3
    lower = iota((step, LANES), 1) < 2 * hidden

    def activate(pre):
        return (pre * jnp.tanh(pre) + pre).astype(bf16)

    def finish(x, valid):
        @pl.when(top)
        def _():
            strip_top = SUB * (1 + gap_k + STRIP + RIM - 1)
            own_top = SUB * gap_k
            strip_ghost = SUB * (1 + gap_k + GHOST)
            own_ghost = SUB * (1 + gap_k + NORTH)
            last_chunk = iota((SUB, LANES), 0) % chunks == chunks - 1
            spot = iota((SUB, LANES), 1) // hidden
            used = (valid + per - 1) // per
            for src, dst in ((strip_top, own_ghost), (own_top, strip_ghost)):
                found = [x[t, pl.ds(src, SUB), :].astype(f32) for t in range(used)]
                for t in range(used):
                    total = x[t, pl.ds(dst, SUB), :].astype(f32)
                    for i in range(per):
                        lon = valid - 1 - (per * t + i)
                        if lon < 0:
                            continue
                        moved = pltpu.roll(found[lon // per], (hidden * (i - lon % per)) % LANES, 1)
                        total = jnp.where(last_chunk & (spot == i), moved, total)
                    x[t, pl.ds(dst, SUB), :] = total.astype(bf16)

        for t in range(tiles):
            end = x[t, pl.ds(rows, SUB), :].astype(f32)
            x[t, pl.ds(0, SUB), :] = pltpu.roll(end, 1, 0).astype(bf16)
            begin = x[t, pl.ds(SUB, SUB), :].astype(f32)
            x[t, pl.ds(SUB + rows, SUB), :] = pltpu.roll(begin, SUB - 1, 0).astype(bf16)

    for x in (odd, even):
        x[tiles - 1] = jnp.zeros(x.shape[1:], bf16)

    spread = groups - 1

    def layer_first(b, carry):
        for n in range(rows // step):
            r = n * step
            parts = [first[b + e, pl.ds(r + SUB * d, step), :] for d in range(3) for e in range(2)]
            out = activate(dot(jnp.concatenate(parts, axis=1), t1[...]))
            odd[2 * b, pl.ds(SUB + r, step), :] = out[:, :LANES]
            odd[2 * b + 1, pl.ds(SUB + r, step), :] = out[:, LANES:]
        return carry

    lax.fori_loop(0, spread, layer_first, 0)
    finish(odd, lons + 6)

    def layer(x, y, t, b, carry):
        for n in range(rows // step):
            r = n * step
            parts = [x[2 * b + e, pl.ds(r + SUB * d, step), :] for d in range(3) for e in range(2)]
            rest = [x[2 * b + 2, pl.ds(r + SUB * d, step), :] for d in range(3)]
            parts.append(jnp.where(lower, rest[0], pltpu.roll(rest[1], 2 * hidden, 1)))
            parts.append(jnp.where(lower, rest[2], first[b, pl.ds(r + SUB, step), :]))
            out = activate(dot(jnp.concatenate(parts, axis=1), t[...]))
            y[2 * b, pl.ds(SUB + r, step), :] = out[:, :LANES]
            y[2 * b + 1, pl.ds(SUB + r, step), :] = out[:, LANES:]
        return carry

    lax.fori_loop(0, spread, functools.partial(layer, odd, even, t2), 0)
    finish(even, lons + 4)
    lax.fori_loop(0, spread, functools.partial(layer, even, odd, t3), 0)
    finish(odd, lons + 2)

    depth = t4.shape[0] // 3 // LANES
    for n in range(rows // step):
        r = n * step
        parts = [odd[t, pl.ds(r + SUB * d, step), :] for d in range(3) for t in range(depth)]
        force[pl.ds(r, step), :] = dot(jnp.concatenate(parts, axis=1), t4[...])

    ocean = sea[...].astype(f32)
    turn = coriolis[...]
    at_first = iota((lons, lats), 0) == 0
    at_last = iota((lons, lats), 0) == lons - 1
    at_south = iota((lons, lats), 1) == 0
    at_north = iota((lons, lats), 1) == lats - 1
    for m in range(members):
        pieces = []
        for q in range(chunks):
            size = min(blocks, lats - q * blocks)
            pieces.append(force[pl.ds(m * chunks + q, size, stride=SUB), :])
        forcing = jnp.transpose(jnp.concatenate(pieces, axis=0))

        def rims(c):
            row = (m * fields + c) * RIM
            west = left[pl.ds(row + RIM - 1, 1)]
            east = right[pl.ds(row, 1)]
            low, high = [], []
            for g in range(1, groups - 1):
                spot = (g * members + m) * RIM
                low.append(south[c * GROUP : (c + 1) * GROUP, spot + RIM - 1 : spot + RIM])
                high.append(north_rim[c * GROUP : (c + 1) * GROUP, spot : spot + 1])
            return west, east, jnp.concatenate(low, axis=0), jnp.concatenate(high, axis=0)

        def around(x, rim):
            west, east, low, high = rim
            return (
                jnp.where(at_first, west, pltpu.roll(x, 1, 0)),
                jnp.where(at_last, east, pltpu.roll(x, lons - 1, 0)),
                jnp.where(at_south, low, pltpu.roll(x, 1, 1)),
                jnp.where(at_north, high, pltpu.roll(x, lats - 1, 1)),
            )

        sets = []
        for level in range(levels):
            sets.append(
                [
                    (x[m, level], around(x[m, level], rims(noises + n * levels + level)))
                    for n, x in enumerate((u, v, h))
                ]
            )
        for level in range(levels):
            (cu, au), (cv, av), (ch, ah) = sets[level]
            upper, lower_h = sets[0][2][1], sets[1][2][1]
            pressure = [upper[i] + lower_h[i] for i in range(4)]
            if level == 1:
                pressure = [pressure[i] + REDUCED * lower_h[i] for i in range(4)]
            push_u = (forcing[level * lons : (level + 1) * lons] + bias_last[level]) * ocean
            wide_v = levels + level
            push_v = (forcing[wide_v * lons : (wide_v + 1) * lons] + bias_last[wide_v]) * ocean
            lap_u = au[1] + au[0] + au[3] + au[2] - 4.0 * cu
            lap_v = av[1] + av[0] + av[3] + av[2] - 4.0 * cv
            dx = 0.5 * (pressure[1] - pressure[0])
            dy = 0.5 * (pressure[3] - pressure[2])
            new_u[m, level] = ocean * (cu + TIME_STEP * (turn * cv - dx + push_u + VISCOSITY * lap_u))
            new_v[m, level] = ocean * (cv + TIME_STEP * (-turn * cu - dy + push_v + VISCOSITY * lap_v))
            flow = 0.5 * (ah[1] * au[1] - ah[0] * au[0]) + 0.5 * (ah[3] * av[3] - ah[2] * av[2])
            new_h[m, level] = ch - TIME_STEP * flow


def body(
    noise,
    velocity_u,
    velocity_v,
    thickness,
    land_sea,
    conv_first,
    bias_first,
    conv_second,
    bias_second,
    conv_third,
    bias_third,
    conv_last,
    bias_last,
):
    members, noises, lons, lats = noise.shape
    levels = velocity_u.shape[1]
    fields = noises + 3 * levels
    sizes = (members, noises, levels)
    hidden = conv_first.shape[0]
    outs = conv_last.shape[0]
    groups = lons // GROUP + 2
    rows = members * (lats + GAP)
    assert hidden * 4 == LANES and outs * lons == LANES and members * RIM * groups <= LANES
    assert lats % LANES == 0 and SUB % members == 0 and (lats + GAP) % (SUB // members) == 0
    lon_count, lat_count = lax.axis_size("lon"), lax.axis_size("lat")
    lat_index = lax.axis_index("lat")
    state = (noise, velocity_u, velocity_v, thickness, land_sea)
    whole = pl.BlockSpec(memory_space=pltpu.VMEM)

    def edge(index, dim, size):
        specs = []
        for x in state:
            shape, at = list(x.shape), [0] * x.ndim
            if not (dim == -2 and x.dtype == bf16):
                at[dim] = (shape[dim] // size - 1) * index
                shape[dim] = size
            specs.append(pl.BlockSpec(tuple(shape), functools.partial(lambda at, *_: tuple(at), at)))
        return specs

    tall = members * fields * RIM + GROUP
    head, tail = pl.pallas_call(
        functools.partial(pack_lon_kernel, sizes),
        grid=(1,),
        out_shape=[jax.ShapeDtypeStruct((tall, lats), f32)] * 2,
        in_specs=edge(0, -2, GROUP) + edge(1, -2, GROUP),
        out_specs=[pl.BlockSpec((tall, lats), lambda i: (0, 0))] * 2,
        name="pack_lon",
    )(*state, *state)
    ring = [(i, (i + 1) % lon_count) for i in range(lon_count)]
    left = lax.ppermute(tail, "lon", ring)
    right = lax.ppermute(head, "lon", [(b, a) for a, b in ring])

    wide = (fields + 2) * GROUP
    south_edge, north_edge = pl.pallas_call(
        functools.partial(pack_lat_kernel, sizes),
        grid=(1,),
        out_shape=[jax.ShapeDtypeStruct((wide, LANES), f32)] * 2,
        in_specs=edge(0, -1, LANES) + edge(1, -1, LANES) + [pl.BlockSpec((tall, lats), lambda i: (0, 0))] * 2,
        out_specs=[pl.BlockSpec((wide, LANES), lambda i: (0, 0))] * 2,
        name="pack_lat",
    )(*state, *state, left, right)
    south = lax.ppermute(north_edge, "lat", [(i, i + 1) for i in range(lat_count - 1)])
    north = lax.ppermute(south_edge, "lat", [(i + 1, i) for i in range(lat_count - 1)])
    last = lat_count - 1
    strip = lax.ppermute(
        north_edge,
        ("lon", "lat"),
        [(i * lat_count + last, (lon_count - 1 - i) * lat_count + last) for i in range(lon_count)],
    )

    taps = conv_first.transpose(3, 2, 1, 0)[:, :, :, None, None, :]
    taps = jnp.broadcast_to(taps, (3, 3, fields, GROUP, LANES // hidden, hidden)).reshape(9, -1, LANES)
    biases = jnp.tile(jnp.stack([bias_first, bias_second, bias_third]), (1, LANES // hidden))
    deep = -(-(lons + 2) * hidden // LANES) * LANES
    t1, t2, t3, t4 = pl.pallas_call(
        weights_kernel,
        out_shape=[
            jax.ShapeDtypeStruct((6 * LANES, 2 * LANES), bf16),
            jax.ShapeDtypeStruct((8 * LANES, 2 * LANES), bf16),
            jax.ShapeDtypeStruct((8 * LANES, 2 * LANES), bf16),
            jax.ShapeDtypeStruct((3 * deep, LANES), bf16),
        ],
        cost_estimate=pl.CostEstimate(flops=10**7, bytes_accessed=3 * 10**6, transcendentals=0),
        name="banded_matrices",
    )(
        taps,
        conv_second.transpose(2, 3, 0, 1),
        conv_third.transpose(2, 3, 0, 1),
        conv_last.transpose(2, 3, 0, 1),
        biases,
    )

    lat_rows = (lat_index * lats + jnp.arange(lats)).astype(f32)
    coriolis = CORIOLIS * (2.0 * (lat_rows + 0.5) / (lats * lat_count) - 1.0)
    place = (lat_index == last).astype(jnp.int32)[None]
    smem = pl.BlockSpec(memory_space=pltpu.SMEM)
    padded = rows + 2 * SUB
    tiles = 2 * (groups - 1) + 1
    out = jax.ShapeDtypeStruct(velocity_u.shape, f32)
    return pl.pallas_call(
        functools.partial(main_kernel, sizes),
        out_shape=[out] * 3,
        in_specs=[smem, smem] + [whole] * 16,
        out_specs=[whole] * 3,
        scratch_shapes=[
            pltpu.VMEM((groups, rows, LANES), f32),
            pltpu.VMEM((groups, padded, LANES), bf16),
            pltpu.VMEM((tiles, padded, LANES), bf16),
            pltpu.VMEM((tiles, padded, LANES), bf16),
            pltpu.VMEM((rows, LANES), f32),
            pltpu.VMEM((4, LANES, LANES), f32),
        ],
        compiler_params=pltpu.CompilerParams(vmem_limit_bytes=48 * 2**20),
        cost_estimate=pl.CostEstimate(flops=2 * 10**10, bytes_accessed=10**7, transcendentals=4 * 10**6),
        name="network_and_step",
    )(
        place,
        bias_last,
        *state,
        coriolis[None],
        left,
        right,
        south,
        north,
        strip,
        north_edge,
        t1,
        t2,
        t3,
        t4,
    )


def solution(mesh):
    tiles = P(None, None, "lon", "lat")
    return jax.shard_map(
        body,
        mesh=mesh,
        in_specs=(tiles,) * 4 + (P("lon", "lat"),) + (P(),) * 8,
        out_specs=(tiles,) * 3,
        check_vma=False,
    )
```

```python
import functools

import jax
import jax.numpy as jnp
from jax import lax
from jax.experimental import pallas as pl
from jax.experimental.pallas import tpu as pltpu
from jax.sharding import PartitionSpec as P

REDUCED = 0.5
TIME_STEP = 0.2
VISCOSITY = 0.05
CORIOLIS = 0.4

RIM = 4
GAP = 32
NORTH, STRIP, GHOST, SOUTH = 0, 12, 16, 28
SUB = 16
LANES = 128
GROUP = 8
LAND = 2.0**100

f32 = jnp.float32
bf16 = jnp.bfloat16


def iota(shape, dim):
    return lax.broadcasted_iota(jnp.int32, shape, dim)


def dot(a, b):
    return jnp.dot(a, b, preferred_element_type=f32)


def exact_dot(a, b):
    return jnp.dot(a, b, preferred_element_type=f32, precision=lax.Precision.HIGHEST)


def pack_lon_kernel(sizes, noise, u, v, h, sea, head, tail, noises_in, states, seas, done):
    members, noises, levels = sizes
    fields = noises + 3 * levels
    lons, lats = sea.shape
    copies = [pltpu.make_async_copy(noise, noises_in, done.at[0])]
    for side in range(2):
        at = pl.ds(side * (lons - GROUP), GROUP)
        copies.append(pltpu.make_async_copy(sea.at[at], seas.at[side], done.at[1 + 4 * side]))
        for n, x in enumerate((u, v, h)):
            copies.append(
                pltpu.make_async_copy(x.at[:, :, at], states.at[side, n], done.at[2 + 4 * side + n])
            )
    for copy in copies:
        copy.start()
    for copy in copies:
        copy.wait()
    upper = iota((GROUP, lats), 0) < RIM

    def field(m, c, side):
        if c < noises:
            full = noises_in[m, c].astype(f32)
            return full[-GROUP:] if side else full[:GROUP]
        c -= noises
        return states[side, c // levels, m, c % levels]

    for m in range(members):
        for c in range(0, fields, 2):
            rows = pl.ds((m * fields + c) * RIM, GROUP)
            head[rows] = jnp.where(upper, field(m, c, 0), pltpu.roll(field(m, c + 1, 0), RIM, 0))
            tail[rows] = jnp.where(upper, pltpu.roll(field(m, c, 1), RIM, 0), field(m, c + 1, 1))
    rows = pl.ds(members * fields * RIM, GROUP)
    head[rows] = seas[0].astype(f32)
    tail[rows] = pltpu.roll(seas[1].astype(f32), RIM, 0)


def group_tile(sizes, m, c, g, refs, groups):
    noise, u, v, h, sea, left, right = refs
    members, noises, levels = sizes
    fields = noises + 3 * levels
    if c == fields + 1:
        if g == groups - 1:
            return None
        c, g = fields, g + 1
    if g == 0 or g == groups - 1:
        src = left if g == 0 else right
        if src is None:
            return None
        row = (m * fields + c) * RIM if c < fields else members * fields * RIM
        odd = (row // RIM) % 2
        tile = src[pl.ds(row // GROUP * GROUP, GROUP)]
        if odd == (1 if g == 0 else 0):
            return tile
        return pltpu.roll(tile, RIM, 0)
    rows = slice((g - 1) * GROUP, g * GROUP)
    if c == fields:
        return None if sea is None else sea[rows].astype(f32)
    if noise is None:
        return None
    if c < noises:
        return noise[m, c].astype(f32)[rows]
    c -= noises
    return (u, v, h)[c // levels][m, c % levels, rows]


def edge_message(sizes, refs, groups, first, part):
    members, noises, levels = sizes
    lane = iota((GROUP, LANES), 1)
    rows = []
    for c in range(noises + 3 * levels + 2):
        total = jnp.zeros((GROUP, LANES), f32) if part is None else part[pl.ds(c * GROUP, GROUP)]
        for g in range(groups):
            for m in range(members):
                tile = group_tile(sizes, m, c, g, refs, groups)
                if tile is None:
                    continue
                place = (g * members + m) * RIM
                moved = pltpu.roll(tile, (place - first) % LANES, 1)
                total = jnp.where((lane >= place) & (lane < place + RIM), moved, total)
        rows.append(total)
    return rows


def store_lats(block, t, dst, lats, chunks, m):
    tile, m = m
    blocks = (lats + GAP) // chunks
    for q in range(chunks):
        lo = max(q * blocks, t * LANES)
        hi = min((q + 1) * blocks, (t + 1) * LANES, lats)
        if lo < hi:
            start = (lo - q * blocks) * SUB + m * chunks + q
            dst[tile, pl.ds(start, hi - lo, stride=SUB), :] = block[lo - t * LANES : hi - t * LANES]


def own_kernel(sizes, noise, u, v, h, sea, own, head, tail, cells):
    members, noises, levels = sizes
    fields = noises + 3 * levels
    lons, lats = sea.shape
    groups = lons // GROUP + 2
    chunks = SUB // members
    gap_k = lats - (chunks - 1) * ((lats + GAP) // chunks)
    for g in range(groups - 2):
        for m in range(members):
            empty = pl.ds(gap_k * SUB + (m + 1) * chunks - 1, GAP, stride=SUB)
            cells[g, empty, :] = jnp.zeros((GAP, LANES), f32)
    for t in range(lats // LANES):
        lanes = slice(t * LANES, (t + 1) * LANES)
        refs = tuple(x.at[:, :, :, lanes] for x in (noise, u, v, h)) + (sea.at[:, lanes], None, None)
        if t == 0:
            for c, row in enumerate(edge_message(sizes, refs, groups, 0, None)):
                head[pl.ds(c * GROUP, GROUP)] = row
        if t == lats // LANES - 1:
            for c, row in enumerate(edge_message(sizes, refs, groups, LANES - RIM, None)):
                tail[pl.ds(c * GROUP, GROUP)] = row
        ones = jnp.ones((GROUP, LANES), f32)
        blank = jnp.zeros((LANES - (fields + 3) * GROUP, LANES), f32)
        for g in range(1, groups - 1):
            for m in range(members):
                tiles = [group_tile(sizes, m, c, g, refs, groups) for c in range(fields)]
                mask = group_tile(sizes, m, fields, g, refs, groups) - 1.0
                following = group_tile(sizes, m, fields + 1, g, refs, groups)
                following = jnp.zeros_like(mask) if following is None else following - 1.0
                block = jnp.transpose(jnp.concatenate(tiles + [mask, following, ones, blank], axis=0))
                store_lats(block, t, cells, lats, chunks, (g - 1, m))
    for g in range(groups - 2):
        own[g] = cells[g].astype(bf16)


def join_kernel(sizes, place, sea, left, right, head, tail, even, odd):
    groups = sea.shape[0] // GROUP + 2
    lats = left.shape[1]
    blank = (None,) * 5
    low = edge_message(sizes, blank + (left.at[:, :LANES], right.at[:, :LANES]), groups, 0, head)
    high = edge_message(
        sizes, blank + (left.at[:, lats - LANES :], right.at[:, lats - LANES :]), groups, LANES - RIM, tail
    )
    to_south = place[1] == 1
    for c, (a, b) in enumerate(zip(low, high)):
        even[pl.ds(c * GROUP, GROUP)] = jnp.where(to_south, a, b)
        odd[pl.ds(c * GROUP, GROUP)] = jnp.where(to_south, b, a)


def weights_kernel(w1, w2, w3, w4, biases, t1, t2, t3, t4):
    hidden = w2.shape[2]
    per = LANES // hidden
    lane = iota((hidden, LANES), 1)
    fields = w1.shape[1] // GROUP
    rows = fields * GROUP
    out_lon = iota((rows, LANES), 1) // hidden
    in_lon = iota((rows, LANES), 0) % GROUP
    bias_row = iota((GROUP, LANES), 0)

    def bias_rows(layer, tile):
        part = 0.5 * biases[pl.ds(layer, 1), :]
        b1 = part.astype(bf16).astype(f32)
        b2 = (part - b1).astype(bf16).astype(f32)
        b3 = part - b1 - b2
        zero = jnp.zeros((GROUP, LANES), f32)
        return jnp.where(
            bias_row == 0,
            b1,
            jnp.where(bias_row == 1, b2, jnp.where(bias_row == 2, b3, zero)),
        )

    def sea_rows(shift, tile):
        lon = iota((2 * GROUP, LANES), 0)
        out = iota((2 * GROUP, LANES), 1) // hidden + per * tile
        return jnp.where(lon == out + shift, LAND, 0.0)

    pad = jnp.zeros((LANES - rows - 3 * GROUP, LANES), f32)
    empty = jnp.zeros((3 * GROUP, LANES), f32)
    for dj in range(3):
        for half in range(2):
            for tile in range(2):
                total = jnp.zeros((rows, LANES), f32)
                for di in range(3):
                    hit = in_lon + GROUP * half == out_lon + per * tile + di + RIM
                    total = jnp.where(hit, 0.5 * w1[dj * 3 + di].astype(f32), total)
                extra = empty
                if dj == 1 and half == 0:
                    extra = jnp.concatenate([sea_rows(5, tile), bias_rows(0, tile)], axis=0)
                block = jnp.concatenate([total, extra, pad], axis=0)
                t1[pl.ds((dj * 2 + half) * LANES, LANES), pl.ds(tile * LANES, LANES)] = block.astype(bf16)

    for layer, (w, t) in enumerate(((w2, t2), (w3, t3))):
        for dj in range(3):
            taps = []
            for di in range(3):
                cell = 0.5 * w[di, dj].astype(f32)
                wide = jnp.concatenate([cell, jnp.zeros((hidden, LANES - hidden), f32)], axis=1)
                square = jnp.concatenate([wide] * per, axis=0)
                taps.append(jnp.transpose(square)[:hidden])
            for lon in range(GROUP + 2):
                for tile in range(2):
                    total = jnp.zeros((hidden, LANES), f32)
                    for di in range(3):
                        total = jnp.where(lane // hidden + per * tile == lon - di, taps[di], total)
                    if lon < GROUP:
                        row = dj * GROUP * hidden + lon * hidden
                    else:
                        row = 3 * GROUP * hidden + dj * 2 * hidden + (lon - GROUP) * hidden
                    t[pl.ds(row, hidden), pl.ds(tile * LANES, LANES)] = total.astype(bf16)
        for tile in range(2):
            block = jnp.concatenate(
                [
                    jnp.zeros((2 * GROUP, LANES), f32),
                    sea_rows(6 + layer, tile),
                    bias_rows(1 + layer, tile),
                    jnp.zeros((3 * GROUP, LANES), f32),
                ],
                axis=0,
            )
            row = 3 * GROUP * hidden + 6 * hidden
            t[pl.ds(row, 2 * hidden), pl.ds(tile * LANES, LANES)] = block.astype(bf16)

    outs = w4.shape[2]
    lons = LANES // outs
    depth = t4.shape[0] // 3
    for dj in range(3):
        taps = []
        for di in range(3):
            cell = w4[di, dj].astype(f32)
            wide = jnp.concatenate([cell, jnp.zeros((outs, LANES - hidden), f32)], axis=1)
            square = jnp.concatenate(
                [jnp.broadcast_to(wide[c : c + 1], (lons, LANES)) for c in range(outs)], axis=0
            )
            taps.append(jnp.transpose(square)[:hidden])
        for lon in range(depth // hidden):
            total = jnp.zeros((hidden, LANES), f32)
            for di in range(3):
                total = jnp.where(lane % lons == lon - di, taps[di], total)
            t4[pl.ds(dj * depth + lon * hidden, hidden), :] = total.astype(bf16)


def main_kernel(
    sizes,
    place,
    bias_last,
    own,
    u,
    v,
    h,
    sea,
    coriolis,
    left,
    right,
    even_rim,
    odd_rim,
    own_tail,
    t1,
    t2,
    t3,
    t4,
    new_u,
    new_v,
    new_h,
    cells,
    first,
    odd,
    even,
    force,
    turned,
    gaps,
):
    members, noises, levels = sizes
    fields = noises + 3 * levels
    lons, lats = sea.shape
    groups = lons // GROUP + 2
    chunks = SUB // members
    blocks = (lats + GAP) // chunks
    rows = blocks * SUB
    gap_k = lats - (chunks - 1) * blocks
    top = place[0] == 1
    is_odd = place[1] == 1
    bottom = place[2] == 1
    strip = odd_rim[...]
    south = jnp.where(is_odd, even_rim[...], jnp.where(bottom, 0.0, strip))

    wide = fields * GROUP + 2 * GROUP
    lane = iota((wide, LANES), 1)
    row_to = iota((wide, wide), 0)
    row_from = iota((wide, wide), 1)
    channel = row_to // GROUP
    same = channel == row_from // GROUP
    mirrored = same & (row_from % GROUP == GROUP - 1 - row_to % GROUP)
    odd_parity = (channel >= noises) & (channel < noises + 2 * levels)
    flip_rows = jnp.where(mirrored, jnp.where(odd_parity, -1.0, 1.0), 0.0)
    lane_from = iota((LANES, LANES), 0)
    lane_to = iota((LANES, LANES), 1)
    span = members * RIM
    source = (groups - 1 - lane_to // span) * span + lane_to % span + RIM - 1
    flip_lanes = jnp.where((lane_to % RIM == 0) & (lane_to < groups * span) & (lane_from == source), 1.0, 0.0)
    pair = exact_dot(flip_rows, jnp.concatenate([strip, own_tail[...]], axis=1))
    folded = exact_dot(pair[:, :LANES], flip_lanes)
    ghost = exact_dot(pair[:, LANES:], flip_lanes)
    north = jnp.where(is_odd, strip, even_rim[...])
    north_rim = jnp.where((lane % RIM == 0) & top, folded, north)

    ones = jnp.ones((GROUP, LANES), f32)
    blank = jnp.zeros((LANES - wide - GROUP, LANES), f32)
    body_rows = fields * GROUP
    offsets = (NORTH, STRIP, GHOST, SOUTH)
    for n, message in enumerate((north_rim, strip, ghost, south)):
        tall = jnp.concatenate([message[:body_rows], message[body_rows:] - 1.0, ones, blank], axis=0)
        turned[n] = jnp.transpose(tall)
        for g in range(groups):
            for m in range(members):
                gap = (m - 1) % members if offsets[n] == SOUTH else m
                start = n * RIM * SUB + gap * chunks + chunks - 1
                gaps[g, pl.ds(start, RIM, stride=SUB), :] = turned[n, pl.ds((g * members + m) * RIM, RIM), :]

    for side in range(2):
        for m in range(members):
            empty = pl.ds(gap_k * SUB + (m + 1) * chunks - 1, GAP, stride=SUB)
            cells[side, empty, :] = jnp.zeros((GAP, LANES), f32)
    for t in range(lats // LANES):
        lanes = slice(t * LANES, (t + 1) * LANES)
        refs = (None,) * 4 + (sea.at[:, lanes], left.at[:, lanes], right.at[:, lanes])
        for side, g in enumerate((0, groups - 1)):
            for m in range(members):
                tiles = [group_tile(sizes, m, c, g, refs, groups) for c in range(fields)]
                mask = group_tile(sizes, m, fields, g, refs, groups) - 1.0
                following = group_tile(sizes, m, fields + 1, g, refs, groups)
                following = jnp.zeros_like(mask) if following is None else following - 1.0
                block = jnp.transpose(jnp.concatenate(tiles + [mask, following, ones, blank], axis=0))
                store_lats(block, t, cells, lats, chunks, (side, m))

    in_gap = iota((RIM * SUB, LANES), 0) % chunks == chunks - 1
    next_mask = iota((rows, LANES), 1) // GROUP == fields + 1
    for g in range(groups):
        if g == 0:
            first[g, pl.ds(SUB, rows), :] = cells[0].astype(bf16)
        elif g == groups - 1:
            first[g, pl.ds(SUB, rows), :] = cells[1].astype(bf16)
        elif g == groups - 2:
            moved = pltpu.roll(cells[1], GROUP, 1)
            first[g, pl.ds(SUB, rows), :] = jnp.where(next_mask, moved, own[g - 1].astype(f32)).astype(bf16)
        else:
            first[g, pl.ds(SUB, rows), :] = own[g - 1]
        for n, offset in enumerate(offsets):
            spot = pl.ds((1 + gap_k + offset) * SUB, RIM * SUB)
            kept = first[g, spot, :].astype(f32)
            first[g, spot, :] = jnp.where(in_gap, gaps[g, pl.ds(n * RIM * SUB, RIM * SUB), :], kept).astype(bf16)
        end = first[g, pl.ds(rows, SUB), :].astype(f32)
        first[g, pl.ds(0, SUB), :] = pltpu.roll(end, 1, 0).astype(bf16)
        begin = first[g, pl.ds(SUB, SUB), :].astype(f32)
        first[g, pl.ds(SUB + rows, SUB), :] = pltpu.roll(begin, SUB - 1, 0).astype(bf16)

    hidden = LANES // 4
    per = LANES // hidden
    tiles = odd.shape[0]
    step = rows // 3
    lower = iota((step, LANES), 1) < 2 * hidden

    def activate(pre):
        return (pre * jnp.tanh(pre) + pre).astype(bf16)

    def finish(x, valid):
        @pl.when(top)
        def _():
            strip_top = SUB * (1 + gap_k + STRIP + RIM - 1)
            own_top = SUB * gap_k
            strip_ghost = SUB * (1 + gap_k + GHOST)
            own_ghost = SUB * (1 + gap_k + NORTH)
            last_chunk = iota((SUB, LANES), 0) % chunks == chunks - 1
            spot = iota((SUB, LANES), 1) // hidden
            used = (valid + per - 1) // per
            for src, dst in ((strip_top, own_ghost), (own_top, strip_ghost)):
                found = [x[t, pl.ds(src, SUB), :].astype(f32) for t in range(used)]
                for t in range(used):
                    total = x[t, pl.ds(dst, SUB), :].astype(f32)
                    for i in range(per):
                        lon = valid - 1 - (per * t + i)
                        if lon < 0:
                            continue
                        moved = pltpu.roll(found[lon // per], (hidden * (i - lon % per)) % LANES, 1)
                        total = jnp.where(last_chunk & (spot == i), moved, total)
                    x[t, pl.ds(dst, SUB), :] = total.astype(bf16)

        for t in range(tiles):
            end = x[t, pl.ds(rows, SUB), :].astype(f32)
            x[t, pl.ds(0, SUB), :] = pltpu.roll(end, 1, 0).astype(bf16)
            begin = x[t, pl.ds(SUB, SUB), :].astype(f32)
            x[t, pl.ds(SUB + rows, SUB), :] = pltpu.roll(begin, SUB - 1, 0).astype(bf16)

    for x in (odd, even):
        x[tiles - 1] = jnp.zeros(x.shape[1:], bf16)

    spread = groups - 1

    def layer_first(b, carry):
        for n in range(rows // step):
            r = n * step
            parts = [first[b + e, pl.ds(r + SUB * d, step), :] for d in range(3) for e in range(2)]
            out = activate(dot(jnp.concatenate(parts, axis=1), t1[...]))
            odd[2 * b, pl.ds(SUB + r, step), :] = out[:, :LANES]
            odd[2 * b + 1, pl.ds(SUB + r, step), :] = out[:, LANES:]
        return carry

    lax.fori_loop(0, spread, layer_first, 0)
    finish(odd, lons + 6)

    def layer(x, y, t, b, carry):
        for n in range(rows // step):
            r = n * step
            parts = [x[2 * b + e, pl.ds(r + SUB * d, step), :] for d in range(3) for e in range(2)]
            rest = [x[2 * b + 2, pl.ds(r + SUB * d, step), :] for d in range(3)]
            parts.append(jnp.where(lower, rest[0], pltpu.roll(rest[1], 2 * hidden, 1)))
            parts.append(jnp.where(lower, rest[2], first[b, pl.ds(r + SUB, step), :]))
            out = activate(dot(jnp.concatenate(parts, axis=1), t[...]))
            y[2 * b, pl.ds(SUB + r, step), :] = out[:, :LANES]
            y[2 * b + 1, pl.ds(SUB + r, step), :] = out[:, LANES:]
        return carry

    lax.fori_loop(0, spread, functools.partial(layer, odd, even, t2), 0)
    finish(even, lons + 4)
    lax.fori_loop(0, spread, functools.partial(layer, even, odd, t3), 0)
    finish(odd, lons + 2)

    depth = t4.shape[0] // 3 // LANES
    for n in range(rows // step):
        r = n * step
        parts = [odd[t, pl.ds(r + SUB * d, step), :] for d in range(3) for t in range(depth)]
        force[pl.ds(r, step), :] = dot(jnp.concatenate(parts, axis=1), t4[...])

    ocean = sea[...].astype(f32)
    turn = coriolis[...]
    at_first = iota((lons, lats), 0) == 0
    at_last = iota((lons, lats), 0) == lons - 1
    at_south = iota((lons, lats), 1) == 0
    at_north = iota((lons, lats), 1) == lats - 1
    for m in range(members):
        pieces = []
        for q in range(chunks):
            size = min(blocks, lats - q * blocks)
            pieces.append(force[pl.ds(m * chunks + q, size, stride=SUB), :])
        forcing = jnp.transpose(jnp.concatenate(pieces, axis=0))

        def rims(c):
            row = (m * fields + c) * RIM
            west = left[pl.ds(row + RIM - 1, 1)]
            east = right[pl.ds(row, 1)]
            low, high = [], []
            for g in range(1, groups - 1):
                spot = (g * members + m) * RIM
                low.append(south[c * GROUP : (c + 1) * GROUP, spot + RIM - 1 : spot + RIM])
                high.append(north_rim[c * GROUP : (c + 1) * GROUP, spot : spot + 1])
            return west, east, jnp.concatenate(low, axis=0), jnp.concatenate(high, axis=0)

        def around(x, rim):
            west, east, low, high = rim
            return (
                jnp.where(at_first, west, pltpu.roll(x, 1, 0)),
                jnp.where(at_last, east, pltpu.roll(x, lons - 1, 0)),
                jnp.where(at_south, low, pltpu.roll(x, 1, 1)),
                jnp.where(at_north, high, pltpu.roll(x, lats - 1, 1)),
            )

        sets = []
        for level in range(levels):
            sets.append(
                [
                    (x[m, level], around(x[m, level], rims(noises + n * levels + level)))
                    for n, x in enumerate((u, v, h))
                ]
            )
        for level in range(levels):
            (cu, au), (cv, av), (ch, ah) = sets[level]
            upper, lower_h = sets[0][2][1], sets[1][2][1]
            pressure = [upper[i] + lower_h[i] for i in range(4)]
            if level == 1:
                pressure = [pressure[i] + REDUCED * lower_h[i] for i in range(4)]
            push_u = (forcing[level * lons : (level + 1) * lons] + bias_last[level]) * ocean
            wide_v = levels + level
            push_v = (forcing[wide_v * lons : (wide_v + 1) * lons] + bias_last[wide_v]) * ocean
            lap_u = au[1] + au[0] + au[3] + au[2] - 4.0 * cu
            lap_v = av[1] + av[0] + av[3] + av[2] - 4.0 * cv
            dx = 0.5 * (pressure[1] - pressure[0])
            dy = 0.5 * (pressure[3] - pressure[2])
            new_u[m, level] = ocean * (cu + TIME_STEP * (turn * cv - dx + push_u + VISCOSITY * lap_u))
            new_v[m, level] = ocean * (cv + TIME_STEP * (-turn * cu - dy + push_v + VISCOSITY * lap_v))
            flow = 0.5 * (ah[1] * au[1] - ah[0] * au[0]) + 0.5 * (ah[3] * av[3] - ah[2] * av[2])
            new_h[m, level] = ch - TIME_STEP * flow


def body(
    noise,
    velocity_u,
    velocity_v,
    thickness,
    land_sea,
    conv_first,
    bias_first,
    conv_second,
    bias_second,
    conv_third,
    bias_third,
    conv_last,
    bias_last,
):
    members, noises, lons, lats = noise.shape
    levels = velocity_u.shape[1]
    fields = noises + 3 * levels
    sizes = (members, noises, levels)
    hidden = conv_first.shape[0]
    outs = conv_last.shape[0]
    groups = lons // GROUP + 2
    rows = members * (lats + GAP)
    assert hidden * 4 == LANES and outs * lons == LANES and members * RIM * groups <= LANES
    assert lats % LANES == 0 and SUB % members == 0 and (lats + GAP) % (SUB // members) == 0
    lon_count, lat_count = lax.axis_size("lon"), lax.axis_size("lat")
    assert lon_count % 2 == 0 and lat_count % 2 == 0
    lat_index = lax.axis_index("lat")
    state = (noise, velocity_u, velocity_v, thickness, land_sea)
    whole = pl.BlockSpec(memory_space=pltpu.VMEM)

    tall = members * fields * RIM + GROUP
    head, tail = pl.pallas_call(
        functools.partial(pack_lon_kernel, sizes),
        out_shape=[pltpu.VMEM((tall, lats), f32)] * 2,
        in_specs=[pl.BlockSpec(memory_space=pltpu.HBM)] * 5,
        out_specs=[whole] * 2,
        scratch_shapes=[
            pltpu.VMEM(noise.shape, noise.dtype),
            pltpu.VMEM((2, 3, members, levels, GROUP, lats), f32),
            pltpu.VMEM((2, GROUP, lats), land_sea.dtype),
            pltpu.SemaphoreType.DMA((9,)),
        ],
        name="pack_lon",
    )(*state)
    ring = [(i, (i + 1) % lon_count) for i in range(lon_count)]
    left = lax.ppermute(tail, "lon", ring)
    right = lax.ppermute(head, "lon", [(b, a) for a, b in ring])

    wide = (fields + 2) * GROUP
    message = pltpu.VMEM((wide, LANES), f32)
    own, own_head, own_tail = pl.pallas_call(
        functools.partial(own_kernel, sizes),
        out_shape=[pltpu.VMEM((groups - 2, rows, LANES), bf16), message, message],
        in_specs=[whole] * 5,
        out_specs=[whole] * 3,
        scratch_shapes=[pltpu.VMEM((groups - 2, rows, LANES), f32)],
        cost_estimate=pl.CostEstimate(flops=10**7, bytes_accessed=10**7, transcendentals=0),
        name="own_cells",
    )(*state)
    last = lat_count - 1
    place = jnp.stack([lat_index == last, lat_index % 2 == 1, lat_index == 0]).astype(jnp.int32)
    smem = pl.BlockSpec(memory_space=pltpu.SMEM)
    to_even, to_odd = pl.pallas_call(
        functools.partial(join_kernel, sizes),
        out_shape=[message] * 2,
        in_specs=[smem] + [whole] * 5,
        out_specs=[whole] * 2,
        name="join_rims",
    )(place, land_sea, left, right, own_head, own_tail)
    even_rim = lax.ppermute(to_even, "lat", [(i, i ^ 1) for i in range(lat_count)])
    pairs = []
    for t in range(lon_count):
        at = t * lat_count
        pairs += [(at + k, at + k - 1 + 2 * (k % 2)) for k in range(1, last)]
        pairs += [(at, (t ^ 1) * lat_count), (at + last, (lon_count - 1 - t) * lat_count + last)]
    odd_rim = lax.ppermute(to_odd, ("lon", "lat"), pairs)

    taps = conv_first.transpose(3, 2, 1, 0)[:, :, :, None, None, :]
    taps = jnp.broadcast_to(taps, (3, 3, fields, GROUP, LANES // hidden, hidden)).reshape(9, -1, LANES)
    biases = jnp.tile(jnp.stack([bias_first, bias_second, bias_third]), (1, LANES // hidden))
    deep = -(-(lons + 2) * hidden // LANES) * LANES
    t1, t2, t3, t4 = pl.pallas_call(
        weights_kernel,
        out_shape=[
            pltpu.VMEM((6 * LANES, 2 * LANES), bf16),
            pltpu.VMEM((8 * LANES, 2 * LANES), bf16),
            pltpu.VMEM((8 * LANES, 2 * LANES), bf16),
            pltpu.VMEM((3 * deep, LANES), bf16),
        ],
        in_specs=[whole] * 5,
        out_specs=[whole] * 4,
        cost_estimate=pl.CostEstimate(flops=10**7, bytes_accessed=3 * 10**6, transcendentals=0),
        name="banded_matrices",
    )(
        taps,
        conv_second.transpose(2, 3, 0, 1),
        conv_third.transpose(2, 3, 0, 1),
        conv_last.transpose(2, 3, 0, 1),
        biases,
    )

    lat_rows = (lat_index * lats + jnp.arange(lats)).astype(f32)
    coriolis = CORIOLIS * (2.0 * (lat_rows + 0.5) / (lats * lat_count) - 1.0)
    padded = rows + 2 * SUB
    tiles = 2 * (groups - 1) + 1
    out = jax.ShapeDtypeStruct(velocity_u.shape, f32)
    return pl.pallas_call(
        functools.partial(main_kernel, sizes),
        out_shape=[out] * 3,
        in_specs=[smem, smem] + [whole] * 15,
        out_specs=[whole] * 3,
        scratch_shapes=[
            pltpu.VMEM((2, rows, LANES), f32),
            pltpu.VMEM((groups, padded, LANES), bf16),
            pltpu.VMEM((tiles, padded, LANES), bf16),
            pltpu.VMEM((tiles, padded, LANES), bf16),
            pltpu.VMEM((rows, LANES), f32),
            pltpu.VMEM((4, LANES, LANES), f32),
            pltpu.VMEM((groups, 4 * RIM * SUB, LANES), f32),
        ],
        compiler_params=pltpu.CompilerParams(vmem_limit_bytes=32 * 2**20),
        cost_estimate=pl.CostEstimate(flops=2 * 10**10, bytes_accessed=10**7, transcendentals=4 * 10**6),
        name="network_and_step",
    )(
        place,
        bias_last,
        own,
        *state[1:],
        coriolis[None],
        left,
        right,
        even_rim,
        odd_rim,
        to_odd,
        t1,
        t2,
        t3,
        t4,
    )


def solution(mesh):
    tiles = P(None, None, "lon", "lat")
    return jax.shard_map(
        body,
        mesh=mesh,
        in_specs=(tiles,) * 4 + (P("lon", "lat"),) + (P(),) * 8,
        out_specs=(tiles,) * 3,
        check_vma=False,
    )
```

```python
import functools

import jax
import jax.numpy as jnp
from jax import lax
from jax.experimental import pallas as pl
from jax.experimental.pallas import tpu as pltpu
from jax.sharding import PartitionSpec as P

REDUCED = 0.5
TIME_STEP = 0.2
VISCOSITY = 0.05
CORIOLIS = 0.4

RIM = 4
GAP = 32
NORTH, STRIP, GHOST, SOUTH = 0, 12, 16, 28
SUB = 16
LANES = 128
GROUP = 8
LAND = 2.0**100

f32 = jnp.float32
bf16 = jnp.bfloat16


def iota(shape, dim):
    return lax.broadcasted_iota(jnp.int32, shape, dim)


def dot(a, b):
    return jnp.dot(a, b, preferred_element_type=f32)


def exact_dot(a, b):
    return jnp.dot(a, b, preferred_element_type=f32, precision=lax.Precision.HIGHEST)


def pack_lon_kernel(sizes, noise, u, v, h, sea, head, tail, noises_in, states, seas, done):
    members, noises, levels = sizes
    fields = noises + 3 * levels
    lons, lats = sea.shape
    copies = [pltpu.make_async_copy(noise, noises_in, done.at[0])]
    for side in range(2):
        at = pl.ds(side * (lons - GROUP), GROUP)
        copies.append(pltpu.make_async_copy(sea.at[at], seas.at[side], done.at[1 + 4 * side]))
        for n, x in enumerate((u, v, h)):
            copies.append(
                pltpu.make_async_copy(x.at[:, :, at], states.at[side, n], done.at[2 + 4 * side + n])
            )
    for copy in copies:
        copy.start()
    for copy in copies:
        copy.wait()
    upper = iota((GROUP, lats), 0) < RIM

    def field(m, c, side):
        if c < noises:
            full = noises_in[m, c].astype(f32)
            return full[-GROUP:] if side else full[:GROUP]
        c -= noises
        return states[side, c // levels, m, c % levels]

    for m in range(members):
        for c in range(0, fields, 2):
            rows = pl.ds((m * fields + c) * RIM, GROUP)
            head[rows] = jnp.where(upper, field(m, c, 0), pltpu.roll(field(m, c + 1, 0), RIM, 0))
            tail[rows] = jnp.where(upper, pltpu.roll(field(m, c, 1), RIM, 0), field(m, c + 1, 1))
    rows = pl.ds(members * fields * RIM, GROUP)
    head[rows] = seas[0].astype(f32)
    tail[rows] = pltpu.roll(seas[1].astype(f32), RIM, 0)


def group_tile(sizes, m, c, g, refs, groups):
    noise, u, v, h, sea, left, right = refs
    members, noises, levels = sizes
    fields = noises + 3 * levels
    if c == fields + 1:
        if g == groups - 1:
            return None
        c, g = fields, g + 1
    if g == 0 or g == groups - 1:
        src = left if g == 0 else right
        if src is None:
            return None
        row = (m * fields + c) * RIM if c < fields else members * fields * RIM
        odd = (row // RIM) % 2
        tile = src[pl.ds(row // GROUP * GROUP, GROUP)]
        if odd == (1 if g == 0 else 0):
            return tile
        return pltpu.roll(tile, RIM, 0)
    rows = slice((g - 1) * GROUP, g * GROUP)
    if c == fields:
        return None if sea is None else sea[rows].astype(f32)
    if noise is None:
        return None
    if c < noises:
        return noise[m, c].astype(f32)[rows]
    c -= noises
    return (u, v, h)[c // levels][m, c % levels, rows]


def edge_message(sizes, refs, groups, first, part):
    members, noises, levels = sizes
    lane = iota((GROUP, LANES), 1)
    rows = []
    for c in range(noises + 3 * levels + 2):
        total = jnp.zeros((GROUP, LANES), f32) if part is None else part[pl.ds(c * GROUP, GROUP)]
        for g in range(groups):
            for m in range(members):
                tile = group_tile(sizes, m, c, g, refs, groups)
                if tile is None:
                    continue
                place = (g * members + m) * RIM
                moved = pltpu.roll(tile, (place - first) % LANES, 1)
                total = jnp.where((lane >= place) & (lane < place + RIM), moved, total)
        rows.append(total)
    return rows


def store_lats(block, t, dst, lats, chunks, m):
    tile, m = m
    blocks = (lats + GAP) // chunks
    for q in range(chunks):
        lo = max(q * blocks, t * LANES)
        hi = min((q + 1) * blocks, (t + 1) * LANES, lats)
        if lo < hi:
            start = (lo - q * blocks) * SUB + m * chunks + q
            dst[tile, pl.ds(start, hi - lo, stride=SUB), :] = block[lo - t * LANES : hi - t * LANES]


def own_kernel(sizes, noise, u, v, h, sea, own, head, tail, cells):
    members, noises, levels = sizes
    fields = noises + 3 * levels
    lons, lats = sea.shape
    groups = lons // GROUP + 2
    chunks = SUB // members
    gap_k = lats - (chunks - 1) * ((lats + GAP) // chunks)
    for g in range(groups - 2):
        for m in range(members):
            empty = pl.ds(gap_k * SUB + (m + 1) * chunks - 1, GAP, stride=SUB)
            cells[g, empty, :] = jnp.zeros((GAP, LANES), f32)
    for t in range(lats // LANES):
        lanes = slice(t * LANES, (t + 1) * LANES)
        refs = tuple(x.at[:, :, :, lanes] for x in (noise, u, v, h)) + (sea.at[:, lanes], None, None)
        if t == 0:
            for c, row in enumerate(edge_message(sizes, refs, groups, 0, None)):
                head[pl.ds(c * GROUP, GROUP)] = row
        if t == lats // LANES - 1:
            for c, row in enumerate(edge_message(sizes, refs, groups, LANES - RIM, None)):
                tail[pl.ds(c * GROUP, GROUP)] = row
        ones = jnp.ones((GROUP, LANES), f32)
        blank = jnp.zeros((LANES - (fields + 3) * GROUP, LANES), f32)
        for g in range(1, groups - 1):
            for m in range(members):
                tiles = [group_tile(sizes, m, c, g, refs, groups) for c in range(fields)]
                mask = group_tile(sizes, m, fields, g, refs, groups) - 1.0
                following = group_tile(sizes, m, fields + 1, g, refs, groups)
                following = jnp.zeros_like(mask) if following is None else following - 1.0
                block = jnp.transpose(jnp.concatenate(tiles + [mask, following, ones, blank], axis=0))
                store_lats(block, t, cells, lats, chunks, (g - 1, m))
    for g in range(groups - 2):
        own[g] = cells[g].astype(bf16)


def join_kernel(sizes, sea, left, right, head, tail, even, odd):
    groups = sea.shape[0] // GROUP + 2
    lats = left.shape[1]
    blank = (None,) * 5
    low = edge_message(sizes, blank + (left.at[:, :LANES], right.at[:, :LANES]), groups, 0, head)
    high = edge_message(
        sizes, blank + (left.at[:, lats - LANES :], right.at[:, lats - LANES :]), groups, LANES - RIM, tail
    )
    to_south = lax.axis_index("lat") % 2 == 1
    for c, (a, b) in enumerate(zip(low, high)):
        even[pl.ds(c * GROUP, GROUP)] = jnp.where(to_south, a, b)
        odd[pl.ds(c * GROUP, GROUP)] = jnp.where(to_south, b, a)


def weights_kernel(w1, w2, w3, w4, bias1, bias2, bias3, t1, t2, t3, t4):
    hidden = w2.shape[2]
    per = LANES // hidden
    lane = iota((hidden, LANES), 1)
    fields = w1.shape[2]
    rows = fields * GROUP
    out_lon = iota((rows, LANES), 1) // hidden
    in_lon = iota((rows, LANES), 0) % GROUP
    bias_row = iota((GROUP, LANES), 0)

    def bias_rows(layer):
        part = 0.5 * jnp.concatenate([(bias1, bias2, bias3)[layer][...]] * per, axis=1)
        b1 = part.astype(bf16).astype(f32)
        b2 = (part - b1).astype(bf16).astype(f32)
        b3 = part - b1 - b2
        zero = jnp.zeros((GROUP, LANES), f32)
        return jnp.where(
            bias_row == 0,
            b1,
            jnp.where(bias_row == 1, b2, jnp.where(bias_row == 2, b3, zero)),
        )

    def sea_rows(shift, tile):
        lon = iota((2 * GROUP, LANES), 0)
        out = iota((2 * GROUP, LANES), 1) // hidden + per * tile
        return jnp.where(lon == out + shift, LAND, 0.0)

    pad = jnp.zeros((LANES - rows - 3 * GROUP, LANES), f32)
    empty = jnp.zeros((3 * GROUP, LANES), f32)
    for dj in range(3):
        taps = []
        for di in range(3):
            cell = 0.5 * jnp.concatenate([w1[dj, di].astype(f32)] * per, axis=1)
            taps.append(
                jnp.concatenate(
                    [jnp.broadcast_to(cell[c : c + 1], (GROUP, LANES)) for c in range(fields)], axis=0
                )
            )
        for half in range(2):
            for tile in range(2):
                total = jnp.zeros((rows, LANES), f32)
                for di in range(3):
                    hit = in_lon + GROUP * half == out_lon + per * tile + di + RIM
                    total = jnp.where(hit, taps[di], total)
                extra = empty
                if dj == 1 and half == 0:
                    extra = jnp.concatenate([sea_rows(5, tile), bias_rows(0)], axis=0)
                block = jnp.concatenate([total, extra, pad], axis=0)
                t1[pl.ds((dj * 2 + half) * LANES, LANES), pl.ds(tile * LANES, LANES)] = block.astype(bf16)

    for layer, (w, t) in enumerate(((w2, t2), (w3, t3))):
        for dj in range(3):
            taps = []
            for di in range(3):
                cell = 0.5 * w[di, dj].astype(f32)
                wide = jnp.concatenate([cell, jnp.zeros((hidden, LANES - hidden), f32)], axis=1)
                square = jnp.concatenate([wide] * per, axis=0)
                taps.append(jnp.transpose(square)[:hidden])
            for lon in range(GROUP + 2):
                for tile in range(2):
                    total = jnp.zeros((hidden, LANES), f32)
                    for di in range(3):
                        total = jnp.where(lane // hidden + per * tile == lon - di, taps[di], total)
                    if lon < GROUP:
                        row = dj * GROUP * hidden + lon * hidden
                    else:
                        row = 3 * GROUP * hidden + dj * 2 * hidden + (lon - GROUP) * hidden
                    t[pl.ds(row, hidden), pl.ds(tile * LANES, LANES)] = total.astype(bf16)
        for tile in range(2):
            block = jnp.concatenate(
                [
                    jnp.zeros((2 * GROUP, LANES), f32),
                    sea_rows(6 + layer, tile),
                    bias_rows(1 + layer),
                    jnp.zeros((3 * GROUP, LANES), f32),
                ],
                axis=0,
            )
            row = 3 * GROUP * hidden + 6 * hidden
            t[pl.ds(row, 2 * hidden), pl.ds(tile * LANES, LANES)] = block.astype(bf16)

    outs = w4.shape[2]
    lons = LANES // outs
    depth = t4.shape[0] // 3
    for dj in range(3):
        taps = []
        for di in range(3):
            cell = w4[di, dj].astype(f32)
            wide = jnp.concatenate([cell, jnp.zeros((outs, LANES - hidden), f32)], axis=1)
            square = jnp.concatenate(
                [jnp.broadcast_to(wide[c : c + 1], (lons, LANES)) for c in range(outs)], axis=0
            )
            taps.append(jnp.transpose(square)[:hidden])
        for lon in range(depth // hidden):
            total = jnp.zeros((hidden, LANES), f32)
            for di in range(3):
                total = jnp.where(lane % lons == lon - di, taps[di], total)
            t4[pl.ds(dj * depth + lon * hidden, hidden), :] = total.astype(bf16)


def main_kernel(
    sizes,
    bias_last,
    own,
    u,
    v,
    h,
    sea,
    left,
    right,
    even_rim,
    odd_rim,
    own_tail,
    t1,
    t2,
    t3,
    t4,
    new_u,
    new_v,
    new_h,
    cells,
    first,
    odd,
    even,
    force,
    turned,
    gaps,
    results,
    done,
):
    members, noises, levels = sizes
    fields = noises + 3 * levels
    lons, lats = sea.shape
    groups = lons // GROUP + 2
    chunks = SUB // members
    blocks = (lats + GAP) // chunks
    rows = blocks * SUB
    gap_k = lats - (chunks - 1) * blocks
    lat_index, lat_count = lax.axis_index("lat"), lax.axis_size("lat")
    top = lat_index == lat_count - 1
    is_odd = lat_index % 2 == 1
    bottom = lat_index == 0
    strip = odd_rim[...]
    south = jnp.where(is_odd, even_rim[...], jnp.where(bottom, 0.0, strip))

    wide = fields * GROUP + 2 * GROUP
    lane = iota((wide, LANES), 1)
    row_to = iota((wide, wide), 0)
    row_from = iota((wide, wide), 1)
    channel = row_to // GROUP
    same = channel == row_from // GROUP
    mirrored = same & (row_from % GROUP == GROUP - 1 - row_to % GROUP)
    odd_parity = (channel >= noises) & (channel < noises + 2 * levels)
    flip_rows = jnp.where(mirrored, jnp.where(odd_parity, -1.0, 1.0), 0.0)
    lane_from = iota((LANES, LANES), 0)
    lane_to = iota((LANES, LANES), 1)
    span = members * RIM
    source = (groups - 1 - lane_to // span) * span + lane_to % span + RIM - 1
    flip_lanes = jnp.where((lane_to % RIM == 0) & (lane_to < groups * span) & (lane_from == source), 1.0, 0.0)
    pair = exact_dot(flip_rows, jnp.concatenate([strip, own_tail[...]], axis=1))
    folded = exact_dot(pair[:, :LANES], flip_lanes)
    ghost = exact_dot(pair[:, LANES:], flip_lanes)
    north = jnp.where(is_odd, strip, even_rim[...])
    north_rim = jnp.where((lane % RIM == 0) & top, folded, north)

    ones = jnp.ones((GROUP, LANES), f32)
    blank = jnp.zeros((LANES - wide - GROUP, LANES), f32)
    body_rows = fields * GROUP
    offsets = (NORTH, STRIP, GHOST, SOUTH)
    for n, message in enumerate((north_rim, strip, ghost, south)):
        tall = jnp.concatenate([message[:body_rows], message[body_rows:] - 1.0, ones, blank], axis=0)
        turned[n] = jnp.transpose(tall)
        for g in range(groups):
            for m in range(members):
                gap = (m - 1) % members if offsets[n] == SOUTH else m
                start = n * RIM * SUB + gap * chunks + chunks - 1
                gaps[g, pl.ds(start, RIM, stride=SUB), :] = turned[n, pl.ds((g * members + m) * RIM, RIM), :]

    for side in range(2):
        for m in range(members):
            empty = pl.ds(gap_k * SUB + (m + 1) * chunks - 1, GAP, stride=SUB)
            cells[side, empty, :] = jnp.zeros((GAP, LANES), f32)
    for t in range(lats // LANES):
        lanes = slice(t * LANES, (t + 1) * LANES)
        refs = (None,) * 4 + (sea.at[:, lanes], left.at[:, lanes], right.at[:, lanes])
        for side, g in enumerate((0, groups - 1)):
            for m in range(members):
                tiles = [group_tile(sizes, m, c, g, refs, groups) for c in range(fields)]
                mask = group_tile(sizes, m, fields, g, refs, groups) - 1.0
                following = group_tile(sizes, m, fields + 1, g, refs, groups)
                following = jnp.zeros_like(mask) if following is None else following - 1.0
                block = jnp.transpose(jnp.concatenate(tiles + [mask, following, ones, blank], axis=0))
                store_lats(block, t, cells, lats, chunks, (side, m))

    in_gap = iota((RIM * SUB, LANES), 0) % chunks == chunks - 1
    next_mask = iota((rows, LANES), 1) // GROUP == fields + 1
    for g in range(groups):
        if g == 0:
            first[g, pl.ds(SUB, rows), :] = cells[0].astype(bf16)
        elif g == groups - 1:
            first[g, pl.ds(SUB, rows), :] = cells[1].astype(bf16)
        elif g == groups - 2:
            moved = pltpu.roll(cells[1], GROUP, 1)
            first[g, pl.ds(SUB, rows), :] = jnp.where(next_mask, moved, own[g - 1].astype(f32)).astype(bf16)
        else:
            first[g, pl.ds(SUB, rows), :] = own[g - 1]
        for n, offset in enumerate(offsets):
            spot = pl.ds((1 + gap_k + offset) * SUB, RIM * SUB)
            kept = first[g, spot, :].astype(f32)
            first[g, spot, :] = jnp.where(in_gap, gaps[g, pl.ds(n * RIM * SUB, RIM * SUB), :], kept).astype(bf16)
        end = first[g, pl.ds(rows, SUB), :].astype(f32)
        first[g, pl.ds(0, SUB), :] = pltpu.roll(end, 1, 0).astype(bf16)
        begin = first[g, pl.ds(SUB, SUB), :].astype(f32)
        first[g, pl.ds(SUB + rows, SUB), :] = pltpu.roll(begin, SUB - 1, 0).astype(bf16)

    hidden = LANES // 4
    per = LANES // hidden
    tiles = odd.shape[0]
    step = rows // 3
    lower = iota((step, LANES), 1) < 2 * hidden

    def activate(pre):
        return (pre * jnp.tanh(pre) + pre).astype(bf16)

    def finish(x, valid):
        @pl.when(top)
        def _():
            strip_top = SUB * (1 + gap_k + STRIP + RIM - 1)
            own_top = SUB * gap_k
            strip_ghost = SUB * (1 + gap_k + GHOST)
            own_ghost = SUB * (1 + gap_k + NORTH)
            last_chunk = iota((SUB, LANES), 0) % chunks == chunks - 1
            spot = iota((SUB, LANES), 1) // hidden
            used = (valid + per - 1) // per
            for src, dst in ((strip_top, own_ghost), (own_top, strip_ghost)):
                found = [x[t, pl.ds(src, SUB), :].astype(f32) for t in range(used)]
                for t in range(used):
                    total = x[t, pl.ds(dst, SUB), :].astype(f32)
                    for i in range(per):
                        lon = valid - 1 - (per * t + i)
                        if lon < 0:
                            continue
                        moved = pltpu.roll(found[lon // per], (hidden * (i - lon % per)) % LANES, 1)
                        total = jnp.where(last_chunk & (spot == i), moved, total)
                    x[t, pl.ds(dst, SUB), :] = total.astype(bf16)

        for t in range(tiles):
            end = x[t, pl.ds(rows, SUB), :].astype(f32)
            x[t, pl.ds(0, SUB), :] = pltpu.roll(end, 1, 0).astype(bf16)
            begin = x[t, pl.ds(SUB, SUB), :].astype(f32)
            x[t, pl.ds(SUB + rows, SUB), :] = pltpu.roll(begin, SUB - 1, 0).astype(bf16)

    for x in (odd, even):
        x[tiles - 1] = jnp.zeros(x.shape[1:], bf16)

    spread = groups - 1

    def layer_first(b, carry):
        for n in range(rows // step):
            r = n * step
            parts = [first[b + e, pl.ds(r + SUB * d, step), :] for d in range(3) for e in range(2)]
            out = activate(dot(jnp.concatenate(parts, axis=1), t1[...]))
            odd[2 * b, pl.ds(SUB + r, step), :] = out[:, :LANES]
            odd[2 * b + 1, pl.ds(SUB + r, step), :] = out[:, LANES:]
        return carry

    lax.fori_loop(0, spread, layer_first, 0)
    finish(odd, lons + 6)

    def layer(x, y, t, b, carry):
        for n in range(rows // step):
            r = n * step
            parts = [x[2 * b + e, pl.ds(r + SUB * d, step), :] for d in range(3) for e in range(2)]
            rest = [x[2 * b + 2, pl.ds(r + SUB * d, step), :] for d in range(3)]
            parts.append(jnp.where(lower, rest[0], pltpu.roll(rest[1], 2 * hidden, 1)))
            parts.append(jnp.where(lower, rest[2], first[b, pl.ds(r + SUB, step), :]))
            out = activate(dot(jnp.concatenate(parts, axis=1), t[...]))
            y[2 * b, pl.ds(SUB + r, step), :] = out[:, :LANES]
            y[2 * b + 1, pl.ds(SUB + r, step), :] = out[:, LANES:]
        return carry

    lax.fori_loop(0, spread, functools.partial(layer, odd, even, t2), 0)
    finish(even, lons + 4)
    lax.fori_loop(0, spread, functools.partial(layer, even, odd, t3), 0)
    finish(odd, lons + 2)

    depth = t4.shape[0] // 3 // LANES
    for n in range(rows // step):
        r = n * step
        parts = [odd[t, pl.ds(r + SUB * d, step), :] for d in range(3) for t in range(depth)]
        force[pl.ds(r, step), :] = dot(jnp.concatenate(parts, axis=1), t4[...])

    ocean = sea[...].astype(f32)
    at_lat = iota((lons, lats), 1).astype(f32)
    lat_rows = (lat_index * lats).astype(f32) + at_lat
    turn = CORIOLIS * (2.0 * (lat_rows + 0.5) / (lats * lat_count) - 1.0)
    at_first = iota((lons, lats), 0) == 0
    at_last = iota((lons, lats), 0) == lons - 1
    at_south = iota((lons, lats), 1) == 0
    at_north = iota((lons, lats), 1) == lats - 1
    for m in range(members):
        pieces = []
        for q in range(chunks):
            size = min(blocks, lats - q * blocks)
            pieces.append(force[pl.ds(m * chunks + q, size, stride=SUB), :])
        forcing = jnp.transpose(jnp.concatenate(pieces, axis=0))

        def rims(c):
            row = (m * fields + c) * RIM
            west = left[pl.ds(row + RIM - 1, 1)]
            east = right[pl.ds(row, 1)]
            low, high = [], []
            for g in range(1, groups - 1):
                spot = (g * members + m) * RIM
                low.append(south[c * GROUP : (c + 1) * GROUP, spot + RIM - 1 : spot + RIM])
                high.append(north_rim[c * GROUP : (c + 1) * GROUP, spot : spot + 1])
            return west, east, jnp.concatenate(low, axis=0), jnp.concatenate(high, axis=0)

        def around(x, rim):
            west, east, low, high = rim
            return (
                jnp.where(at_first, west, pltpu.roll(x, 1, 0)),
                jnp.where(at_last, east, pltpu.roll(x, lons - 1, 0)),
                jnp.where(at_south, low, pltpu.roll(x, 1, 1)),
                jnp.where(at_north, high, pltpu.roll(x, lats - 1, 1)),
            )

        sets = []
        for level in range(levels):
            sets.append(
                [
                    (x[m, level], around(x[m, level], rims(noises + n * levels + level)))
                    for n, x in enumerate((u, v, h))
                ]
            )
        for level in range(levels):
            (cu, au), (cv, av), (ch, ah) = sets[level]
            upper, lower_h = sets[0][2][1], sets[1][2][1]
            pressure = [upper[i] + lower_h[i] for i in range(4)]
            if level == 1:
                pressure = [pressure[i] + REDUCED * lower_h[i] for i in range(4)]
            push_u = (forcing[level * lons : (level + 1) * lons] + bias_last[level]) * ocean
            wide_v = levels + level
            push_v = (forcing[wide_v * lons : (wide_v + 1) * lons] + bias_last[wide_v]) * ocean
            lap_u = au[1] + au[0] + au[3] + au[2] - 4.0 * cu
            lap_v = av[1] + av[0] + av[3] + av[2] - 4.0 * cv
            dx = 0.5 * (pressure[1] - pressure[0])
            dy = 0.5 * (pressure[3] - pressure[2])
            results[0, m, level] = ocean * (cu + TIME_STEP * (turn * cv - dx + push_u + VISCOSITY * lap_u))
            results[1, m, level] = ocean * (cv + TIME_STEP * (-turn * cu - dy + push_v + VISCOSITY * lap_v))
            flow = 0.5 * (ah[1] * au[1] - ah[0] * au[0]) + 0.5 * (ah[3] * av[3] - ah[2] * av[2])
            results[2, m, level] = ch - TIME_STEP * flow
        for n, out in enumerate((new_u, new_v, new_h)):
            pltpu.make_async_copy(results.at[n, m], out.at[m], done.at[n, m]).start()
    for m in range(members):
        for n, out in enumerate((new_u, new_v, new_h)):
            pltpu.make_async_copy(results.at[n, m], out.at[m], done.at[n, m]).wait()


def body(
    noise,
    velocity_u,
    velocity_v,
    thickness,
    land_sea,
    conv_first,
    bias_first,
    conv_second,
    bias_second,
    conv_third,
    bias_third,
    conv_last,
    bias_last,
):
    members, noises, lons, lats = noise.shape
    levels = velocity_u.shape[1]
    fields = noises + 3 * levels
    sizes = (members, noises, levels)
    hidden = conv_first.shape[0]
    outs = conv_last.shape[0]
    groups = lons // GROUP + 2
    rows = members * (lats + GAP)
    assert hidden * 4 == LANES and outs * lons == LANES and members * RIM * groups <= LANES
    assert lats % LANES == 0 and SUB % members == 0 and (lats + GAP) % (SUB // members) == 0
    lon_count, lat_count = lax.axis_size("lon"), lax.axis_size("lat")
    assert lon_count % 2 == 0 and lat_count % 2 == 0
    state = (noise, velocity_u, velocity_v, thickness, land_sea)
    whole = pl.BlockSpec(memory_space=pltpu.VMEM)

    tall = members * fields * RIM + GROUP
    head, tail = pl.pallas_call(
        functools.partial(pack_lon_kernel, sizes),
        out_shape=[pltpu.VMEM((tall, lats), f32)] * 2,
        in_specs=[pl.BlockSpec(memory_space=pltpu.HBM)] * 5,
        out_specs=[whole] * 2,
        scratch_shapes=[
            pltpu.VMEM(noise.shape, noise.dtype),
            pltpu.VMEM((2, 3, members, levels, GROUP, lats), f32),
            pltpu.VMEM((2, GROUP, lats), land_sea.dtype),
            pltpu.SemaphoreType.DMA((9,)),
        ],
        name="pack_lon",
    )(*state)
    ring = [(i, (i + 1) % lon_count) for i in range(lon_count)]
    left = lax.ppermute(tail, "lon", ring)
    right = lax.ppermute(head, "lon", [(b, a) for a, b in ring])

    wide = (fields + 2) * GROUP
    message = pltpu.VMEM((wide, LANES), f32)
    own, own_head, own_tail = pl.pallas_call(
        functools.partial(own_kernel, sizes),
        out_shape=[pltpu.VMEM((groups - 2, rows, LANES), bf16), message, message],
        in_specs=[whole] * 5,
        out_specs=[whole] * 3,
        scratch_shapes=[pltpu.VMEM((groups - 2, rows, LANES), f32)],
        compiler_params=pltpu.CompilerParams(vmem_limit_bytes=8 * 2**20),
        cost_estimate=pl.CostEstimate(flops=10**7, bytes_accessed=10**7, transcendentals=0),
        name="own_cells",
    )(*state)
    last = lat_count - 1
    smem = pl.BlockSpec(memory_space=pltpu.SMEM)
    to_even, to_odd = pl.pallas_call(
        functools.partial(join_kernel, sizes),
        out_shape=[message] * 2,
        in_specs=[whole] * 5,
        out_specs=[whole] * 2,
        compiler_params=pltpu.CompilerParams(vmem_limit_bytes=4 * 2**20),
        name="join_rims",
    )(land_sea, left, right, own_head, own_tail)
    even_rim = lax.ppermute(to_even, "lat", [(i, i ^ 1) for i in range(lat_count)])
    pairs = []
    for t in range(lon_count):
        at = t * lat_count
        pairs += [(at + k, at + k - 1 + 2 * (k % 2)) for k in range(1, last)]
        pairs += [(at, (t ^ 1) * lat_count), (at + last, (lon_count - 1 - t) * lat_count + last)]
    odd_rim = lax.ppermute(to_odd, ("lon", "lat"), pairs)

    deep = -(-(lons + 2) * hidden // LANES) * LANES
    t1, t2, t3, t4 = pl.pallas_call(
        weights_kernel,
        out_shape=[
            pltpu.VMEM((6 * LANES, 2 * LANES), bf16),
            pltpu.VMEM((8 * LANES, 2 * LANES), bf16),
            pltpu.VMEM((8 * LANES, 2 * LANES), bf16),
            pltpu.VMEM((3 * deep, LANES), bf16),
        ],
        in_specs=[whole] * 7,
        out_specs=[whole] * 4,
        compiler_params=pltpu.CompilerParams(vmem_limit_bytes=8 * 2**20),
        cost_estimate=pl.CostEstimate(flops=10**7, bytes_accessed=3 * 10**6, transcendentals=0),
        name="banded_matrices",
    )(
        conv_first.transpose(3, 2, 1, 0),
        conv_second.transpose(2, 3, 0, 1),
        conv_third.transpose(2, 3, 0, 1),
        conv_last.transpose(2, 3, 0, 1),
        bias_first[None],
        bias_second[None],
        bias_third[None],
    )

    padded = rows + 2 * SUB
    tiles = 2 * (groups - 1) + 1
    out = jax.ShapeDtypeStruct(velocity_u.shape, f32)
    return pl.pallas_call(
        functools.partial(main_kernel, sizes),
        out_shape=[out] * 3,
        in_specs=[smem] + [whole] * 14,
        out_specs=[pl.BlockSpec(memory_space=pltpu.HBM)] * 3,
        scratch_shapes=[
            pltpu.VMEM((2, rows, LANES), f32),
            pltpu.VMEM((groups, padded, LANES), bf16),
            pltpu.VMEM((tiles, padded, LANES), bf16),
            pltpu.VMEM((tiles, padded, LANES), bf16),
            pltpu.VMEM((rows, LANES), f32),
            pltpu.VMEM((4, LANES, LANES), f32),
            pltpu.VMEM((groups, 4 * RIM * SUB, LANES), f32),
            pltpu.VMEM((3, *velocity_u.shape), f32),
            pltpu.SemaphoreType.DMA((3, members)),
        ],
        compiler_params=pltpu.CompilerParams(vmem_limit_bytes=32 * 2**20),
        cost_estimate=pl.CostEstimate(flops=2 * 10**10, bytes_accessed=10**7, transcendentals=4 * 10**6),
        name="network_and_step",
    )(
        bias_last,
        own,
        *state[1:],
        left,
        right,
        even_rim,
        odd_rim,
        to_odd,
        t1,
        t2,
        t3,
        t4,
    )


def solution(mesh):
    tiles = P(None, None, "lon", "lat")
    return jax.shard_map(
        body,
        mesh=mesh,
        in_specs=(tiles,) * 4 + (P("lon", "lat"),) + (P(),) * 8,
        out_specs=(tiles,) * 3,
        check_vma=False,
    )
```

```python
import functools

import jax
import jax.numpy as jnp
from jax import lax
from jax.experimental import pallas as pl
from jax.experimental.pallas import tpu as pltpu
from jax.sharding import PartitionSpec as P

REDUCED = 0.5
TIME_STEP = 0.2
VISCOSITY = 0.05
CORIOLIS = 0.4

RIM = 4
GAP = 32
NORTH, STRIP, GHOST, SOUTH = 0, 12, 16, 28
SUB = 16
LANES = 128
GROUP = 8
LAND = 2.0**100

f32 = jnp.float32
bf16 = jnp.bfloat16


def iota(shape, dim):
    return lax.broadcasted_iota(jnp.int32, shape, dim)


def dot(a, b):
    return jnp.dot(a, b, preferred_element_type=f32)


def exact_dot(a, b):
    return jnp.dot(a, b, preferred_element_type=f32, precision=lax.Precision.HIGHEST)


def pack_lon_kernel(sizes, noise, u, v, h, sea, head, tail, noises_in, states, seas, done):
    members, noises, levels = sizes
    fields = noises + 3 * levels
    lons, lats = sea.shape
    copies = [pltpu.make_async_copy(noise, noises_in, done.at[0])]
    for side in range(2):
        at = pl.ds(side * (lons - GROUP), GROUP)
        copies.append(pltpu.make_async_copy(sea.at[at], seas.at[side], done.at[1 + 4 * side]))
        for n, x in enumerate((u, v, h)):
            copies.append(
                pltpu.make_async_copy(x.at[:, :, at], states.at[side, n], done.at[2 + 4 * side + n])
            )
    for copy in copies:
        copy.start()
    for copy in copies:
        copy.wait()
    upper = iota((GROUP, lats), 0) < RIM

    def field(m, c, side):
        if c < noises:
            full = noises_in[m, c].astype(f32)
            return full[-GROUP:] if side else full[:GROUP]
        c -= noises
        return states[side, c // levels, m, c % levels]

    for m in range(members):
        for c in range(0, fields, 2):
            rows = pl.ds((m * fields + c) * RIM, GROUP)
            head[rows] = jnp.where(upper, field(m, c, 0), pltpu.roll(field(m, c + 1, 0), RIM, 0))
            tail[rows] = jnp.where(upper, pltpu.roll(field(m, c, 1), RIM, 0), field(m, c + 1, 1))
    rows = pl.ds(members * fields * RIM, GROUP)
    head[rows] = seas[0].astype(f32)
    tail[rows] = pltpu.roll(seas[1].astype(f32), RIM, 0)


def group_tile(sizes, m, c, g, refs, groups):
    noise, u, v, h, sea, left, right = refs
    members, noises, levels = sizes
    fields = noises + 3 * levels
    if c == fields + 1:
        if g == groups - 1:
            return None
        c, g = fields, g + 1
    if g == 0 or g == groups - 1:
        src = left if g == 0 else right
        if src is None:
            return None
        row = (m * fields + c) * RIM if c < fields else members * fields * RIM
        odd = (row // RIM) % 2
        tile = src[pl.ds(row // GROUP * GROUP, GROUP)]
        if odd == (1 if g == 0 else 0):
            return tile
        return pltpu.roll(tile, RIM, 0)
    rows = slice((g - 1) * GROUP, g * GROUP)
    if c == fields:
        return None if sea is None else sea[rows].astype(f32)
    if noise is None:
        return None
    if c < noises:
        return noise[m, c].astype(f32)[rows]
    c -= noises
    return (u, v, h)[c // levels][m, c % levels, rows]


def edge_message(sizes, refs, groups, first, part):
    members, noises, levels = sizes
    lane = iota((GROUP, LANES), 1)
    rows = []
    for c in range(noises + 3 * levels + 2):
        total = jnp.zeros((GROUP, LANES), f32) if part is None else part[pl.ds(c * GROUP, GROUP)]
        for g in range(groups):
            for m in range(members):
                tile = group_tile(sizes, m, c, g, refs, groups)
                if tile is None:
                    continue
                place = (g * members + m) * RIM
                moved = pltpu.roll(tile, (place - first) % LANES, 1)
                total = jnp.where((lane >= place) & (lane < place + RIM), moved, total)
        rows.append(total)
    return rows


def store_lats(block, t, dst, lats, chunks, m):
    tile, m = m
    blocks = (lats + GAP) // chunks
    for q in range(chunks):
        lo = max(q * blocks, t * LANES)
        hi = min((q + 1) * blocks, (t + 1) * LANES, lats)
        if lo < hi:
            start = (lo - q * blocks) * SUB + m * chunks + q
            dst[tile, pl.ds(start, hi - lo, stride=SUB), :] = block[lo - t * LANES : hi - t * LANES]


def own_kernel(sizes, noise, u, v, h, sea, own, head, tail, cells):
    members, noises, levels = sizes
    fields = noises + 3 * levels
    lons, lats = sea.shape
    groups = lons // GROUP + 2
    chunks = SUB // members
    gap_k = lats - (chunks - 1) * ((lats + GAP) // chunks)
    for g in range(groups - 2):
        for m in range(members):
            empty = pl.ds(gap_k * SUB + (m + 1) * chunks - 1, GAP, stride=SUB)
            cells[g, empty, :] = jnp.zeros((GAP, LANES), f32)
    for t in range(lats // LANES):
        lanes = slice(t * LANES, (t + 1) * LANES)
        refs = tuple(x.at[:, :, :, lanes] for x in (noise, u, v, h)) + (sea.at[:, lanes], None, None)
        if t == 0:
            for c, row in enumerate(edge_message(sizes, refs, groups, 0, None)):
                head[pl.ds(c * GROUP, GROUP)] = row
        if t == lats // LANES - 1:
            for c, row in enumerate(edge_message(sizes, refs, groups, LANES - RIM, None)):
                tail[pl.ds(c * GROUP, GROUP)] = row
        ones = jnp.ones((GROUP, LANES), f32)
        blank = jnp.zeros((LANES - (fields + 3) * GROUP, LANES), f32)
        for g in range(1, groups - 1):
            for m in range(members):
                tiles = [group_tile(sizes, m, c, g, refs, groups) for c in range(fields)]
                mask = group_tile(sizes, m, fields, g, refs, groups) - 1.0
                following = group_tile(sizes, m, fields + 1, g, refs, groups)
                following = jnp.zeros_like(mask) if following is None else following - 1.0
                block = jnp.transpose(jnp.concatenate(tiles + [mask, following, ones, blank], axis=0))
                store_lats(block, t, cells, lats, chunks, (g - 1, m))
    for g in range(groups - 2):
        own[g] = cells[g].astype(bf16)


def join_kernel(sizes, sea, left, right, head, tail, even, odd):
    groups = sea.shape[0] // GROUP + 2
    lats = left.shape[1]
    blank = (None,) * 5
    low = edge_message(sizes, blank + (left.at[:, :LANES], right.at[:, :LANES]), groups, 0, head)
    high = edge_message(
        sizes, blank + (left.at[:, lats - LANES :], right.at[:, lats - LANES :]), groups, LANES - RIM, tail
    )
    to_south = lax.axis_index("lat") % 2 == 1
    for c, (a, b) in enumerate(zip(low, high)):
        even[pl.ds(c * GROUP, GROUP)] = jnp.where(to_south, a, b)
        odd[pl.ds(c * GROUP, GROUP)] = jnp.where(to_south, b, a)


def weights_kernel(w1, w2, w3, w4, bias1, bias2, bias3, t1, t2, t3, t4):
    hidden = w2.shape[2]
    per = LANES // hidden
    lane = iota((hidden, LANES), 1)
    fields = w1.shape[2]
    rows = fields * GROUP
    out_lon = iota((rows, LANES), 1) // hidden
    in_lon = iota((rows, LANES), 0) % GROUP
    bias_row = iota((GROUP, LANES), 0)

    def bias_rows(layer):
        part = 0.5 * jnp.concatenate([(bias1, bias2, bias3)[layer][...]] * per, axis=1)
        b1 = part.astype(bf16).astype(f32)
        b2 = (part - b1).astype(bf16).astype(f32)
        b3 = part - b1 - b2
        zero = jnp.zeros((GROUP, LANES), f32)
        return jnp.where(
            bias_row == 0,
            b1,
            jnp.where(bias_row == 1, b2, jnp.where(bias_row == 2, b3, zero)),
        )

    def sea_rows(shift, tile):
        lon = iota((2 * GROUP, LANES), 0)
        out = iota((2 * GROUP, LANES), 1) // hidden + per * tile
        return jnp.where(lon == out + shift, LAND, 0.0)

    pad = jnp.zeros((LANES - rows - 3 * GROUP, LANES), f32)
    empty = jnp.zeros((3 * GROUP, LANES), f32)
    for dj in range(3):
        taps = []
        for di in range(3):
            cell = 0.5 * jnp.concatenate([w1[dj, di].astype(f32)] * per, axis=1)
            taps.append(
                jnp.concatenate(
                    [jnp.broadcast_to(cell[c : c + 1], (GROUP, LANES)) for c in range(fields)], axis=0
                )
            )
        for half in range(2):
            for tile in range(2):
                total = jnp.zeros((rows, LANES), f32)
                for di in range(3):
                    hit = in_lon + GROUP * half == out_lon + per * tile + di + RIM
                    total = jnp.where(hit, taps[di], total)
                extra = empty
                if dj == 1 and half == 0:
                    extra = jnp.concatenate([sea_rows(5, tile), bias_rows(0)], axis=0)
                block = jnp.concatenate([total, extra, pad], axis=0)
                t1[pl.ds((dj * 2 + half) * LANES, LANES), pl.ds(tile * LANES, LANES)] = block.astype(bf16)

    for layer, (w, t) in enumerate(((w2, t2), (w3, t3))):
        for dj in range(3):
            taps = []
            for di in range(3):
                cell = 0.5 * w[di, dj].astype(f32)
                wide = jnp.concatenate([cell, jnp.zeros((hidden, LANES - hidden), f32)], axis=1)
                square = jnp.concatenate([wide] * per, axis=0)
                taps.append(jnp.transpose(square)[:hidden])
            for lon in range(GROUP + 2):
                for tile in range(2):
                    total = jnp.zeros((hidden, LANES), f32)
                    for di in range(3):
                        total = jnp.where(lane // hidden + per * tile == lon - di, taps[di], total)
                    if lon < GROUP:
                        row = dj * GROUP * hidden + lon * hidden
                    else:
                        row = 3 * GROUP * hidden + dj * 2 * hidden + (lon - GROUP) * hidden
                    t[pl.ds(row, hidden), pl.ds(tile * LANES, LANES)] = total.astype(bf16)
        for tile in range(2):
            block = jnp.concatenate(
                [
                    jnp.zeros((2 * GROUP, LANES), f32),
                    sea_rows(6 + layer, tile),
                    bias_rows(1 + layer),
                    jnp.zeros((3 * GROUP, LANES), f32),
                ],
                axis=0,
            )
            row = 3 * GROUP * hidden + 6 * hidden
            t[pl.ds(row, 2 * hidden), pl.ds(tile * LANES, LANES)] = block.astype(bf16)

    outs = w4.shape[2]
    lons = LANES // outs
    depth = t4.shape[0] // 3
    for dj in range(3):
        taps = []
        for di in range(3):
            cell = w4[di, dj].astype(f32)
            wide = jnp.concatenate([cell, jnp.zeros((outs, LANES - hidden), f32)], axis=1)
            square = jnp.concatenate(
                [jnp.broadcast_to(wide[c : c + 1], (lons, LANES)) for c in range(outs)], axis=0
            )
            taps.append(jnp.transpose(square)[:hidden])
        for lon in range(depth // hidden):
            total = jnp.zeros((hidden, LANES), f32)
            for di in range(3):
                total = jnp.where(lane % lons == lon - di, taps[di], total)
            t4[pl.ds(dj * depth + lon * hidden, hidden), :] = total.astype(bf16)


def main_kernel(
    sizes,
    bias_last,
    own,
    u,
    v,
    h,
    sea,
    left,
    right,
    even_rim,
    odd_rim,
    own_tail,
    t1,
    t2,
    t3,
    t4,
    new_u,
    new_v,
    new_h,
    cells,
    first,
    odd,
    even,
    force,
    turned,
    gaps,
    results,
    done,
):
    members, noises, levels = sizes
    fields = noises + 3 * levels
    lons, lats = sea.shape
    groups = lons // GROUP + 2
    chunks = SUB // members
    blocks = (lats + GAP) // chunks
    rows = blocks * SUB
    gap_k = lats - (chunks - 1) * blocks
    lat_index, lat_count = lax.axis_index("lat"), lax.axis_size("lat")
    top = lat_index == lat_count - 1
    is_odd = lat_index % 2 == 1
    bottom = lat_index == 0
    strip = odd_rim[...]
    south = jnp.where(is_odd, even_rim[...], jnp.where(bottom, 0.0, strip))

    wide = fields * GROUP + 2 * GROUP
    lane = iota((wide, LANES), 1)
    row_to = iota((wide, wide), 0)
    row_from = iota((wide, wide), 1)
    channel = row_to // GROUP
    same = channel == row_from // GROUP
    mirrored = same & (row_from % GROUP == GROUP - 1 - row_to % GROUP)
    odd_parity = (channel >= noises) & (channel < noises + 2 * levels)
    flip_rows = jnp.where(mirrored, jnp.where(odd_parity, -1.0, 1.0), 0.0)
    lane_from = iota((LANES, LANES), 0)
    lane_to = iota((LANES, LANES), 1)
    span = members * RIM
    source = (groups - 1 - lane_to // span) * span + lane_to % span + RIM - 1
    flip_lanes = jnp.where((lane_to % RIM == 0) & (lane_to < groups * span) & (lane_from == source), 1.0, 0.0)
    pair = exact_dot(flip_rows, jnp.concatenate([strip, own_tail[...]], axis=1))
    folded = exact_dot(pair[:, :LANES], flip_lanes)
    ghost = exact_dot(pair[:, LANES:], flip_lanes)
    north = jnp.where(is_odd, strip, even_rim[...])
    north_rim = jnp.where((lane % RIM == 0) & top, folded, north)

    ones = jnp.ones((GROUP, LANES), f32)
    blank = jnp.zeros((LANES - wide - GROUP, LANES), f32)
    body_rows = fields * GROUP
    offsets = (NORTH, STRIP, GHOST, SOUTH)
    for n, message in enumerate((north_rim, strip, ghost, south)):
        tall = jnp.concatenate([message[:body_rows], message[body_rows:] - 1.0, ones, blank], axis=0)
        turned[n] = jnp.transpose(tall)
        for g in range(groups):
            for m in range(members):
                gap = (m - 1) % members if offsets[n] == SOUTH else m
                start = n * RIM * SUB + gap * chunks + chunks - 1
                gaps[g, pl.ds(start, RIM, stride=SUB), :] = turned[n, pl.ds((g * members + m) * RIM, RIM), :]

    for side in range(2):
        for m in range(members):
            empty = pl.ds(gap_k * SUB + (m + 1) * chunks - 1, GAP, stride=SUB)
            cells[side, empty, :] = jnp.zeros((GAP, LANES), f32)
    for t in range(lats // LANES):
        lanes = slice(t * LANES, (t + 1) * LANES)
        refs = (None,) * 4 + (sea.at[:, lanes], left.at[:, lanes], right.at[:, lanes])
        for side, g in enumerate((0, groups - 1)):
            for m in range(members):
                tiles = [group_tile(sizes, m, c, g, refs, groups) for c in range(fields)]
                mask = group_tile(sizes, m, fields, g, refs, groups) - 1.0
                following = group_tile(sizes, m, fields + 1, g, refs, groups)
                following = jnp.zeros_like(mask) if following is None else following - 1.0
                block = jnp.transpose(jnp.concatenate(tiles + [mask, following, ones, blank], axis=0))
                store_lats(block, t, cells, lats, chunks, (side, m))

    in_gap = iota((RIM * SUB, LANES), 0) % chunks == chunks - 1
    next_mask = iota((rows, LANES), 1) // GROUP == fields + 1
    for g in range(groups):
        if g == 0:
            first[g, pl.ds(SUB, rows), :] = cells[0].astype(bf16)
        elif g == groups - 1:
            first[g, pl.ds(SUB, rows), :] = cells[1].astype(bf16)
        elif g == groups - 2:
            moved = pltpu.roll(cells[1], GROUP, 1)
            first[g, pl.ds(SUB, rows), :] = jnp.where(next_mask, moved, own[g - 1].astype(f32)).astype(bf16)
        else:
            first[g, pl.ds(SUB, rows), :] = own[g - 1]
        for n, offset in enumerate(offsets):
            spot = pl.ds((1 + gap_k + offset) * SUB, RIM * SUB)
            kept = first[g, spot, :].astype(f32)
            first[g, spot, :] = jnp.where(in_gap, gaps[g, pl.ds(n * RIM * SUB, RIM * SUB), :], kept).astype(bf16)
        end = first[g, pl.ds(rows, SUB), :].astype(f32)
        first[g, pl.ds(0, SUB), :] = pltpu.roll(end, 1, 0).astype(bf16)
        begin = first[g, pl.ds(SUB, SUB), :].astype(f32)
        first[g, pl.ds(SUB + rows, SUB), :] = pltpu.roll(begin, SUB - 1, 0).astype(bf16)

    hidden = LANES // 4
    per = LANES // hidden
    tiles = odd.shape[0]
    step = rows // 3
    lower = iota((step, LANES), 1) < 2 * hidden

    def activate(pre):
        return (pre * jnp.tanh(pre) + pre).astype(bf16)

    def finish(x, valid):
        @pl.when(top)
        def _():
            strip_top = SUB * (1 + gap_k + STRIP + RIM - 1)
            own_top = SUB * gap_k
            strip_ghost = SUB * (1 + gap_k + GHOST)
            own_ghost = SUB * (1 + gap_k + NORTH)
            last_chunk = iota((SUB, LANES), 0) % chunks == chunks - 1
            spot = iota((SUB, LANES), 1) // hidden
            used = (valid + per - 1) // per
            for src, dst in ((strip_top, own_ghost), (own_top, strip_ghost)):
                found = [x[t, pl.ds(src, SUB), :].astype(f32) for t in range(used)]
                for t in range(used):
                    total = x[t, pl.ds(dst, SUB), :].astype(f32)
                    for i in range(per):
                        lon = valid - 1 - (per * t + i)
                        if lon < 0:
                            continue
                        moved = pltpu.roll(found[lon // per], (hidden * (i - lon % per)) % LANES, 1)
                        total = jnp.where(last_chunk & (spot == i), moved, total)
                    x[t, pl.ds(dst, SUB), :] = total.astype(bf16)

        for t in range(tiles):
            end = x[t, pl.ds(rows, SUB), :].astype(f32)
            x[t, pl.ds(0, SUB), :] = pltpu.roll(end, 1, 0).astype(bf16)
            begin = x[t, pl.ds(SUB, SUB), :].astype(f32)
            x[t, pl.ds(SUB + rows, SUB), :] = pltpu.roll(begin, SUB - 1, 0).astype(bf16)

    for x in (odd, even):
        x[tiles - 1] = jnp.zeros(x.shape[1:], bf16)

    spread = groups - 1

    def layer_first(b):
        for n in range(rows // step):
            r = n * step
            parts = [first[b + e, pl.ds(r + SUB * d, step), :] for d in range(3) for e in range(2)]
            out = activate(dot(jnp.concatenate(parts, axis=1), t1[...]))
            odd[2 * b, pl.ds(SUB + r, step), :] = out[:, :LANES]
            odd[2 * b + 1, pl.ds(SUB + r, step), :] = out[:, LANES:]

    for b in range(spread):
        layer_first(b)
    finish(odd, lons + 6)

    def layer(x, y, t, b):
        for n in range(rows // step):
            r = n * step
            parts = [x[2 * b + e, pl.ds(r + SUB * d, step), :] for d in range(3) for e in range(2)]
            rest = [x[2 * b + 2, pl.ds(r + SUB * d, step), :] for d in range(3)]
            parts.append(jnp.where(lower, rest[0], pltpu.roll(rest[1], 2 * hidden, 1)))
            parts.append(jnp.where(lower, rest[2], first[b, pl.ds(r + SUB, step), :]))
            out = activate(dot(jnp.concatenate(parts, axis=1), t[...]))
            y[2 * b, pl.ds(SUB + r, step), :] = out[:, :LANES]
            y[2 * b + 1, pl.ds(SUB + r, step), :] = out[:, LANES:]

    for b in range(spread):
        layer(odd, even, t2, b)
    finish(even, lons + 4)
    for b in range(spread):
        layer(even, odd, t3, b)
    finish(odd, lons + 2)

    depth = t4.shape[0] // 3 // LANES
    for n in range(rows // step):
        r = n * step
        parts = [odd[t, pl.ds(r + SUB * d, step), :] for d in range(3) for t in range(depth)]
        force[pl.ds(r, step), :] = dot(jnp.concatenate(parts, axis=1), t4[...])

    ocean = sea[...].astype(f32)
    at_lat = iota((lons, lats), 1).astype(f32)
    lat_rows = (lat_index * lats).astype(f32) + at_lat
    turn = CORIOLIS * (2.0 * (lat_rows + 0.5) / (lats * lat_count) - 1.0)
    at_first = iota((lons, lats), 0) == 0
    at_last = iota((lons, lats), 0) == lons - 1
    at_south = iota((lons, lats), 1) == 0
    at_north = iota((lons, lats), 1) == lats - 1
    for m in range(members):
        pieces = []
        for q in range(chunks):
            size = min(blocks, lats - q * blocks)
            pieces.append(force[pl.ds(m * chunks + q, size, stride=SUB), :])
        forcing = jnp.transpose(jnp.concatenate(pieces, axis=0))

        def rims(c):
            row = (m * fields + c) * RIM
            west = left[pl.ds(row + RIM - 1, 1)]
            east = right[pl.ds(row, 1)]
            low, high = [], []
            for g in range(1, groups - 1):
                spot = (g * members + m) * RIM
                low.append(south[c * GROUP : (c + 1) * GROUP, spot + RIM - 1 : spot + RIM])
                high.append(north_rim[c * GROUP : (c + 1) * GROUP, spot : spot + 1])
            return west, east, jnp.concatenate(low, axis=0), jnp.concatenate(high, axis=0)

        def around(x, rim):
            west, east, low, high = rim
            return (
                jnp.where(at_first, west, pltpu.roll(x, 1, 0)),
                jnp.where(at_last, east, pltpu.roll(x, lons - 1, 0)),
                jnp.where(at_south, low, pltpu.roll(x, 1, 1)),
                jnp.where(at_north, high, pltpu.roll(x, lats - 1, 1)),
            )

        sets = []
        for level in range(levels):
            sets.append(
                [
                    (x[m, level], around(x[m, level], rims(noises + n * levels + level)))
                    for n, x in enumerate((u, v, h))
                ]
            )
        for level in range(levels):
            (cu, au), (cv, av), (ch, ah) = sets[level]
            upper, lower_h = sets[0][2][1], sets[1][2][1]
            pressure = [upper[i] + lower_h[i] for i in range(4)]
            if level == 1:
                pressure = [pressure[i] + REDUCED * lower_h[i] for i in range(4)]
            push_u = (forcing[level * lons : (level + 1) * lons] + bias_last[level]) * ocean
            wide_v = levels + level
            push_v = (forcing[wide_v * lons : (wide_v + 1) * lons] + bias_last[wide_v]) * ocean
            lap_u = au[1] + au[0] + au[3] + au[2] - 4.0 * cu
            lap_v = av[1] + av[0] + av[3] + av[2] - 4.0 * cv
            dx = 0.5 * (pressure[1] - pressure[0])
            dy = 0.5 * (pressure[3] - pressure[2])
            results[0, m, level] = ocean * (cu + TIME_STEP * (turn * cv - dx + push_u + VISCOSITY * lap_u))
            results[1, m, level] = ocean * (cv + TIME_STEP * (-turn * cu - dy + push_v + VISCOSITY * lap_v))
            flow = 0.5 * (ah[1] * au[1] - ah[0] * au[0]) + 0.5 * (ah[3] * av[3] - ah[2] * av[2])
            results[2, m, level] = ch - TIME_STEP * flow
        for n, out in enumerate((new_u, new_v, new_h)):
            pltpu.make_async_copy(results.at[n, m], out.at[m], done.at[n, m]).start()
    for m in range(members):
        for n, out in enumerate((new_u, new_v, new_h)):
            pltpu.make_async_copy(results.at[n, m], out.at[m], done.at[n, m]).wait()


def body(
    noise,
    velocity_u,
    velocity_v,
    thickness,
    land_sea,
    conv_first,
    bias_first,
    conv_second,
    bias_second,
    conv_third,
    bias_third,
    conv_last,
    bias_last,
):
    members, noises, lons, lats = noise.shape
    levels = velocity_u.shape[1]
    fields = noises + 3 * levels
    sizes = (members, noises, levels)
    hidden = conv_first.shape[0]
    outs = conv_last.shape[0]
    groups = lons // GROUP + 2
    rows = members * (lats + GAP)
    assert hidden * 4 == LANES and outs * lons == LANES and members * RIM * groups <= LANES
    assert lats % LANES == 0 and SUB % members == 0 and (lats + GAP) % (SUB // members) == 0
    lon_count, lat_count = lax.axis_size("lon"), lax.axis_size("lat")
    assert lon_count % 2 == 0 and lat_count % 2 == 0
    state = (noise, velocity_u, velocity_v, thickness, land_sea)
    whole = pl.BlockSpec(memory_space=pltpu.VMEM)

    tall = members * fields * RIM + GROUP
    head, tail = pl.pallas_call(
        functools.partial(pack_lon_kernel, sizes),
        out_shape=[pltpu.VMEM((tall, lats), f32)] * 2,
        in_specs=[pl.BlockSpec(memory_space=pltpu.HBM)] * 5,
        out_specs=[whole] * 2,
        scratch_shapes=[
            pltpu.VMEM(noise.shape, noise.dtype),
            pltpu.VMEM((2, 3, members, levels, GROUP, lats), f32),
            pltpu.VMEM((2, GROUP, lats), land_sea.dtype),
            pltpu.SemaphoreType.DMA((9,)),
        ],
        name="pack_lon",
    )(*state)
    ring = [(i, (i + 1) % lon_count) for i in range(lon_count)]
    left = lax.ppermute(tail, "lon", ring)
    right = lax.ppermute(head, "lon", [(b, a) for a, b in ring])

    wide = (fields + 2) * GROUP
    message = pltpu.VMEM((wide, LANES), f32)
    own, own_head, own_tail = pl.pallas_call(
        functools.partial(own_kernel, sizes),
        out_shape=[pltpu.VMEM((groups - 2, rows, LANES), bf16), message, message],
        in_specs=[whole] * 5,
        out_specs=[whole] * 3,
        scratch_shapes=[pltpu.VMEM((groups - 2, rows, LANES), f32)],
        compiler_params=pltpu.CompilerParams(vmem_limit_bytes=8 * 2**20),
        cost_estimate=pl.CostEstimate(flops=10**7, bytes_accessed=10**7, transcendentals=0),
        name="own_cells",
    )(*state)
    last = lat_count - 1
    smem = pl.BlockSpec(memory_space=pltpu.SMEM)
    to_even, to_odd = pl.pallas_call(
        functools.partial(join_kernel, sizes),
        out_shape=[message] * 2,
        in_specs=[whole] * 5,
        out_specs=[whole] * 2,
        compiler_params=pltpu.CompilerParams(vmem_limit_bytes=4 * 2**20),
        name="join_rims",
    )(land_sea, left, right, own_head, own_tail)
    even_rim = lax.ppermute(to_even, "lat", [(i, i ^ 1) for i in range(lat_count)])
    pairs = []
    for t in range(lon_count):
        at = t * lat_count
        pairs += [(at + k, at + k - 1 + 2 * (k % 2)) for k in range(1, last)]
        pairs += [(at, (t ^ 1) * lat_count), (at + last, (lon_count - 1 - t) * lat_count + last)]
    odd_rim = lax.ppermute(to_odd, ("lon", "lat"), pairs)

    deep = -(-(lons + 2) * hidden // LANES) * LANES
    t1, t2, t3, t4 = pl.pallas_call(
        weights_kernel,
        out_shape=[
            pltpu.VMEM((6 * LANES, 2 * LANES), bf16),
            pltpu.VMEM((8 * LANES, 2 * LANES), bf16),
            pltpu.VMEM((8 * LANES, 2 * LANES), bf16),
            pltpu.VMEM((3 * deep, LANES), bf16),
        ],
        in_specs=[whole] * 7,
        out_specs=[whole] * 4,
        compiler_params=pltpu.CompilerParams(vmem_limit_bytes=8 * 2**20),
        cost_estimate=pl.CostEstimate(flops=10**7, bytes_accessed=3 * 10**6, transcendentals=0),
        name="banded_matrices",
    )(
        conv_first.transpose(3, 2, 1, 0),
        conv_second.transpose(2, 3, 0, 1),
        conv_third.transpose(2, 3, 0, 1),
        conv_last.transpose(2, 3, 0, 1),
        bias_first[None],
        bias_second[None],
        bias_third[None],
    )

    padded = rows + 2 * SUB
    tiles = 2 * (groups - 1) + 1
    out = jax.ShapeDtypeStruct(velocity_u.shape, f32)
    return pl.pallas_call(
        functools.partial(main_kernel, sizes),
        out_shape=[out] * 3,
        in_specs=[smem] + [whole] * 14,
        out_specs=[pl.BlockSpec(memory_space=pltpu.HBM)] * 3,
        scratch_shapes=[
            pltpu.VMEM((2, rows, LANES), f32),
            pltpu.VMEM((groups, padded, LANES), bf16),
            pltpu.VMEM((tiles, padded, LANES), bf16),
            pltpu.VMEM((tiles, padded, LANES), bf16),
            pltpu.VMEM((rows, LANES), f32),
            pltpu.VMEM((4, LANES, LANES), f32),
            pltpu.VMEM((groups, 4 * RIM * SUB, LANES), f32),
            pltpu.VMEM((3, *velocity_u.shape), f32),
            pltpu.SemaphoreType.DMA((3, members)),
        ],
        compiler_params=pltpu.CompilerParams(vmem_limit_bytes=32 * 2**20),
        cost_estimate=pl.CostEstimate(flops=2 * 10**10, bytes_accessed=10**7, transcendentals=4 * 10**6),
        name="network_and_step",
    )(
        bias_last,
        own,
        *state[1:],
        left,
        right,
        even_rim,
        odd_rim,
        to_odd,
        t1,
        t2,
        t3,
        t4,
    )


def solution(mesh):
    tiles = P(None, None, "lon", "lat")
    return jax.shard_map(
        body,
        mesh=mesh,
        in_specs=(tiles,) * 4 + (P("lon", "lat"),) + (P(),) * 8,
        out_specs=(tiles,) * 3,
        check_vma=False,
    )
```

```python
import functools

import jax
import jax.numpy as jnp
from jax import lax
from jax.experimental import pallas as pl
from jax.experimental.pallas import tpu as pltpu
from jax.sharding import PartitionSpec as P

REDUCED = 0.5
TIME_STEP = 0.2
VISCOSITY = 0.05
CORIOLIS = 0.4

RIM = 4
GAP = 16
NORTH, STRIP, GHOST, SOUTH = 0, 4, 8, 12
SUB = 16
LANES = 128
GROUP = 8
LAND = 2.0**100

f32 = jnp.float32
bf16 = jnp.bfloat16


def iota(shape, dim):
    return lax.broadcasted_iota(jnp.int32, shape, dim)


def dot(a, b):
    return jnp.dot(a, b, preferred_element_type=f32)


def rest(x):
    return x - x.astype(bf16).astype(f32)


def pack_lon_kernel(sizes, noise, u, v, h, sea, head, tail, noises_in, states, seas, wide, done):
    members, noises, levels = sizes
    fields = noises + 3 * levels
    lons, lats = sea.shape
    copies = [pltpu.make_async_copy(noise, noises_in, done.at[0])]
    for side in range(2):
        at = pl.ds(side * (lons - GROUP), GROUP)
        copies.append(pltpu.make_async_copy(sea.at[at], seas.at[side], done.at[1 + 4 * side]))
        for n, x in enumerate((u, v, h)):
            copies.append(
                pltpu.make_async_copy(x.at[:, :, at], states.at[side, n], done.at[2 + 4 * side + n])
            )
    for copy in copies:
        copy.start()
    for copy in copies:
        copy.wait()
    upper = iota((GROUP, lats), 0) < RIM

    def field(m, c, side):
        if c < noises:
            full = noises_in[m, c].astype(f32)
            return full[-GROUP:] if side else full[:GROUP]
        c -= noises
        return states[side, c // levels, m, c % levels]

    rests = members * fields * RIM + GROUP
    for m in range(members):
        for c in range(0, fields, 2):
            rows = pl.ds((m * fields + c) * RIM, GROUP)
            wide[0, rows] = jnp.where(upper, field(m, c, 0), pltpu.roll(field(m, c + 1, 0), RIM, 0))
            wide[1, rows] = jnp.where(upper, pltpu.roll(field(m, c, 1), RIM, 0), field(m, c + 1, 1))
        for c in range(noises, fields):
            row = pl.ds(rests + m * (fields - noises) + c - noises, 1)
            wide[0, row] = rest(field(m, c, 0)[:1])
            wide[1, row] = rest(field(m, c, 1)[GROUP - 1 :])
    rows = pl.ds(members * fields * RIM, GROUP)
    wide[0, rows] = jnp.where(upper, seas[0].astype(f32), 0.0)
    wide[1, rows] = jnp.where(upper, pltpu.roll(seas[1].astype(f32), RIM, 0), 0.0)
    head[...] = wide[0].astype(bf16)
    tail[...] = wide[1].astype(bf16)


def rim_tile(sizes, m, c, side, rim):
    members, noises, levels = sizes
    fields = noises + 3 * levels
    row = (m * fields + c) * RIM if c < fields else members * fields * RIM
    tile = rim[pl.ds(row // GROUP * GROUP, GROUP)]
    if (row // RIM) % 2 == side:
        return tile
    return pltpu.roll(tile, RIM, 0)


def window(tiles, following, mask, next_mask):
    pair = iota(mask.shape, 0) // 2
    zero = jnp.zeros_like(mask)
    more = []
    for start in range(0, len(tiles), 4):
        total = zero
        for n in range(min(4, len(tiles) - start)):
            moved = pltpu.roll(following[start + n], 2 * n, 0) if n else following[start]
            total = jnp.where(pair == n, moved, total)
        more.append(total)
    return jnp.concatenate(
        tiles + more + [mask - 1.0, next_mask - 1.0, jnp.ones_like(mask)], axis=0
    )


def store_lats(block, t, dst, tile, m, lats, chunks, buffer):
    blocks = (lats + GAP) // chunks
    buffer[...] = jnp.transpose(block)
    for q in range(chunks):
        lo = max(q * blocks, t * LANES)
        hi = min((q + 1) * blocks, (t + 1) * LANES, lats)
        if lo < hi:
            start = (lo - q * blocks) * SUB + m * chunks + q
            dst[tile, pl.ds(start, hi - lo, stride=SUB), :] = buffer[pl.ds(lo - t * LANES, hi - lo), :]


def own_kernel(sizes, noise, u, v, h, sea, own, head, tail, cells, turned):
    members, noises, levels = sizes
    fields = noises + 3 * levels
    lons, lats = sea.shape
    groups = lons // GROUP + 1
    chunks = SUB // members
    gap_k = lats - (chunks - 1) * ((lats + GAP) // chunks)
    lane = iota((GROUP, LANES), 1)
    for m in range(members):
        for g in range(groups):
            empty = pl.ds(gap_k * SUB + (m + 1) * chunks - 1, GAP, stride=SUB)
            cells[g, empty, :] = jnp.zeros((GAP, LANES), f32)

    def tiles_of(m, c, t):
        lanes = slice(t * LANES, (t + 1) * LANES)
        if c == fields:
            full = sea[:, lanes].astype(f32)
        elif c < noises:
            full = noise[m, c, :, lanes].astype(f32)
        else:
            full = (u, v, h)[(c - noises) // levels][m, (c - noises) % levels, :, lanes]
        full = pltpu.roll(full, lons - RIM, 0)
        tiles = [full[g * GROUP : (g + 1) * GROUP] for g in range(groups - 1)]
        return tiles[-1:] + tiles

    last = lats // LANES - 1
    lows = [jnp.zeros((GROUP, LANES), f32)] * (fields + 1)
    highs = [jnp.zeros((GROUP, LANES), f32)] * (fields + 1)
    blank = jnp.zeros((GROUP, LANES), f32)
    for t in range(last + 1):
        for m in range(members):
            tiles = [tiles_of(m, c, t) for c in range(fields + 1)]
            for g in range(groups):
                after = g + 1 if g + 1 < groups else None
                block = window(
                    [tiles[c][g] for c in range(fields)],
                    [blank if after is None else tiles[c][after] for c in range(fields)],
                    tiles[fields][g],
                    blank if after is None else tiles[fields][after],
                )
                store_lats(block, t, cells, g, m, lats, chunks, turned.at[(t * members + m) * groups + g])
            for c in range(fields + 1):
                for g in range(groups):
                    place = (g * members + m) * RIM
                    spot = (lane >= place) & (lane < place + RIM)
                    other = groups * members * RIM + g * members + m
                    if t == 0:
                        lows[c] = jnp.where(spot, pltpu.roll(tiles[c][g], place, 1), lows[c])
                        moved = pltpu.roll(rest(tiles[c][g]), other, 1)
                        lows[c] = jnp.where(lane == other, moved, lows[c])
                    if t == last:
                        first = LANES - RIM
                        moved = pltpu.roll(tiles[c][g], (place - first) % LANES, 1)
                        highs[c] = jnp.where(spot, moved, highs[c])
                        moved = pltpu.roll(rest(tiles[c][g]), (other + 1) % LANES, 1)
                        highs[c] = jnp.where(lane == other, moved, highs[c])
    for c in range(fields + 1):
        head[pl.ds(c * GROUP, GROUP)] = lows[c]
        tail[pl.ds(c * GROUP, GROUP)] = highs[c]
    for c in range(fields + 1, head.shape[0] // GROUP):
        head[pl.ds(c * GROUP, GROUP)] = blank
        tail[pl.ds(c * GROUP, GROUP)] = blank
    for g in range(groups):
        own[g] = cells[g].astype(bf16)


def join_kernel(sizes, lons, left, right, head, tail, even, odd, rims, wide):
    members, noises, levels = sizes
    fields = noises + 3 * levels
    groups = lons // GROUP + 1
    lats = left.shape[1]
    for side, rim in enumerate((left, right)):
        rims[side, 0] = rim[:, :LANES].astype(f32)
        rims[side, 1] = rim[:, lats - LANES :].astype(f32)
    lane = iota((GROUP, LANES), 1)
    upper = iota((GROUP, LANES), 0) < RIM
    to_south = lax.axis_index("lat") % 2 == 1
    for c in range(fields + 1):
        rows = pl.ds(c * GROUP, GROUP)
        ends = []
        for n, (part, first) in enumerate(((head, 0), (tail, LANES - RIM))):
            total = part[rows]
            for side in range(2):
                held = upper if side == 0 else ~upper
                for m in range(members):
                    place = ((groups - 1) * side * members + m) * RIM
                    tile = rim_tile(sizes, m, c, side, rims.at[side, n])
                    moved = pltpu.roll(tile, (place - first) % LANES, 1)
                    total = jnp.where(held & (lane >= place) & (lane < place + RIM), moved, total)
            ends.append(total)
        wide[0, rows] = jnp.where(to_south, ends[0], ends[1])
        wide[1, rows] = jnp.where(to_south, ends[1], ends[0])
    rows = pl.ds((fields + 1) * GROUP, wide.shape[1] - (fields + 1) * GROUP)
    wide[:, rows] = jnp.zeros((2, wide.shape[1] - (fields + 1) * GROUP, LANES), f32)
    even[...] = wide[0].astype(bf16)
    odd[...] = wide[1].astype(bf16)


def weights_kernel(w1, w2, w3, w4, bias1, bias2, bias3, t1, t2, t3, t4):
    hidden = w2.shape[2]
    per = LANES // hidden
    lane = iota((hidden, LANES), 1)
    fields = w1.shape[2]
    rows = fields * GROUP
    out_lon = iota((GROUP, LANES), 1) // hidden
    in_row = iota((GROUP, LANES), 0)
    bias_row = iota((GROUP, LANES), 0)

    def bias_rows(layer):
        part = 0.5 * jnp.concatenate([(bias1, bias2, bias3)[layer][...]] * per, axis=1)
        b1 = part.astype(bf16).astype(f32)
        b2 = (part - b1).astype(bf16).astype(f32)
        b3 = part - b1 - b2
        zero = jnp.zeros((GROUP, LANES), f32)
        return jnp.where(
            bias_row == 0,
            b1,
            jnp.where(bias_row == 1, b2, jnp.where(bias_row == 2, b3, zero)),
        )

    def sea_rows(shift, tile):
        lon = iota((2 * GROUP, LANES), 0)
        out = iota((2 * GROUP, LANES), 1) // hidden + per * tile
        return jnp.where(lon == out + shift, LAND, 0.0)

    for dj in range(3):
        taps = [0.5 * jnp.concatenate([w1[dj, di].astype(f32)] * per, axis=1) for di in range(3)]
        for tile in range(2):
            parts = []
            for c in range(fields):
                total = jnp.zeros((GROUP, LANES), f32)
                for di in range(3):
                    hit = in_row == out_lon + per * tile + di
                    total = jnp.where(hit, jnp.broadcast_to(taps[di][c : c + 1], (GROUP, LANES)), total)
                parts.append(total)
            for start in range(0, fields, 4):
                total = jnp.zeros((GROUP, LANES), f32)
                for n in range(min(4, fields - start)):
                    for di in range(3):
                        hit = in_row % 2 + GROUP == out_lon + per * tile + di
                        row = jnp.broadcast_to(taps[di][start + n : start + n + 1], (GROUP, LANES))
                        total = jnp.where(hit & (in_row // 2 == n), row, total)
                parts.append(total)
            if dj == 1:
                parts += [sea_rows(1, tile), bias_rows(0)]
            else:
                parts.append(jnp.zeros((3 * GROUP, LANES), f32))
            block = jnp.concatenate(parts, axis=0)
            t1[pl.ds(dj * LANES, LANES), pl.ds(tile * LANES, LANES)] = block.astype(bf16)

    for layer, (w, t) in enumerate(((w2, t2), (w3, t3))):
        for dj in range(3):
            taps = []
            for di in range(3):
                cell = 0.5 * w[di, dj].astype(f32)
                wide = jnp.concatenate([cell, jnp.zeros((hidden, LANES - hidden), f32)], axis=1)
                square = jnp.concatenate([wide] * per, axis=0)
                taps.append(jnp.transpose(square)[:hidden])
            for lon in range(GROUP + 2):
                for tile in range(2):
                    total = jnp.zeros((hidden, LANES), f32)
                    for di in range(3):
                        total = jnp.where(lane // hidden + per * tile == lon - di, taps[di], total)
                    if lon < GROUP:
                        row = dj * GROUP * hidden + lon * hidden
                    else:
                        row = 3 * GROUP * hidden + dj * 2 * hidden + (lon - GROUP) * hidden
                    t[pl.ds(row, hidden), pl.ds(tile * LANES, LANES)] = total.astype(bf16)
        for tile in range(2):
            block = jnp.concatenate(
                [
                    jnp.zeros((5 * GROUP, LANES), f32),
                    sea_rows(2 + layer, tile),
                    bias_rows(1 + layer),
                ],
                axis=0,
            )
            row = 3 * GROUP * hidden + 6 * hidden
            t[pl.ds(row, 2 * hidden), pl.ds(tile * LANES, LANES)] = block.astype(bf16)

    outs = w4.shape[2]
    half = LANES // 2
    lons = half // outs
    slot = iota((hidden, LANES), 1) // half
    out_lon = iota((hidden, LANES), 1) % lons
    taps = {}
    for dj in range(3):
        for di in range(3):
            cell = w4[di, dj].astype(f32)
            wide = jnp.concatenate([cell, jnp.zeros((outs, LANES - hidden), f32)], axis=1)
            square = jnp.concatenate(
                [jnp.broadcast_to(wide[c : c + 1], (lons, LANES)) for c in range(outs)] * 2, axis=0
            )
            taps[dj, di] = jnp.transpose(square)[:hidden]
    order = ((0, 1, 2, None), (1, 0, None, 2))
    for side in range(2):
        for lon in range(t4.shape[1] // hidden):
            for tile in range(2):
                total = jnp.zeros((hidden, LANES), f32)
                for place in range(2):
                    dj = order[side][2 * tile + place]
                    if dj is None:
                        continue
                    for di in range(3):
                        total = jnp.where((slot == place) & (out_lon == lon - di), taps[dj, di], total)
                t4[side, pl.ds(lon * hidden, hidden), pl.ds(tile * LANES, LANES)] = total.astype(bf16)


def main_kernel(
    sizes,
    bias_last,
    own,
    u,
    v,
    h,
    sea,
    left_in,
    right_in,
    even_rim,
    odd_rim,
    own_tail,
    t1,
    t2,
    t3,
    t4,
    new_u,
    new_v,
    new_h,
    left,
    right,
    cells,
    first,
    odd,
    even,
    force,
    gathered,
    buffers,
    turned,
    gaps,
    results,
    done,
):
    members, noises, levels = sizes
    fields = noises + 3 * levels
    lons, lats = sea.shape
    groups = lons // GROUP + 1
    chunks = SUB // members
    blocks = (lats + GAP) // chunks
    rows = blocks * SUB
    gap_k = lats - (chunks - 1) * blocks
    lat_index, lat_count = lax.axis_index("lat"), lax.axis_size("lat")
    top = lat_index == lat_count - 1
    is_odd = lat_index % 2 == 1
    bottom = lat_index == 0
    left[...] = left_in[...].astype(f32)
    right[...] = right_in[...].astype(f32)
    strip = odd_rim[...].astype(f32)
    paired = even_rim[...].astype(f32)
    south = jnp.where(is_odd, paired, jnp.where(bottom, 0.0, strip))

    wide = strip.shape[0]
    span = members * RIM
    lane = iota((wide, LANES), 1)
    rests = groups * span
    border = ((lane % RIM == 0) & (lane < rests)) | (lane >= rests)
    row_to = iota((wide, wide), 0)
    row_from = iota((wide, wide), 1)
    channel = row_to // GROUP
    mirrored = (channel == row_from // GROUP) & (row_from % GROUP == GROUP - 1 - row_to % GROUP)
    odd_parity = (channel >= noises) & (channel < noises + 2 * levels)
    flip_rows = jnp.where(mirrored, jnp.where(odd_parity, -1.0, 1.0), 0.0).astype(bf16)
    lane_from = iota((LANES, LANES), 0)
    lane_to = iota((LANES, LANES), 1)
    source = (groups - 1 - lane_to // span) * span + lane_to % span + RIM - 1
    moves = (lane_to % RIM == 0) & (lane_to < rests) & (lane_from == source)
    other = lane_to - rests
    source = rests + (groups - 1 - other // members) * members + other % members
    moves = moves | ((other >= 0) & (other < groups * members) & (lane_from == source))
    flip_lanes = jnp.where(moves, 1.0, 0.0).astype(bf16)
    pair = dot(flip_rows, jnp.concatenate([odd_rim[...], own_tail[...]], axis=1)).astype(bf16)
    folded = dot(pair[:, :LANES], flip_lanes)
    ghost = dot(pair[:, LANES:], flip_lanes)
    north = jnp.where(is_odd, strip, paired)
    north_rim = jnp.where(border & top, folded, north)

    for n, message in enumerate((north_rim, strip, ghost, south)):
        after = pltpu.roll(message, LANES - span, 1)
        cut = [message[c * GROUP : (c + 1) * GROUP] for c in range(fields + 1)]
        after = [after[c * GROUP : (c + 1) * GROUP] for c in range(fields + 1)]
        turned[n] = jnp.transpose(window(cut[:fields], after[:fields], cut[fields], after[fields]))
        for g in range(groups):
            for m in range(members):
                gap = (m - 1) % members if n == 3 else m
                start = n * RIM * SUB + gap * chunks + chunks - 1
                gaps[g, pl.ds(start, RIM, stride=SUB), :] = turned[n, pl.ds((g * members + m) * RIM, RIM), :]

    blank = jnp.zeros((GROUP, LANES), f32)
    for t in range(lats // LANES):
        lanes = slice(t * LANES, (t + 1) * LANES)
        for side, rim in enumerate((left, right)):
            for m in range(members):
                tiles = [rim_tile(sizes, m, c, side, rim.at[:, lanes]) for c in range(fields + 1)]
                block = window(tiles[:fields], [blank] * fields, tiles[fields], blank)
                buffer = buffers.at[(t * 2 + side) * members + m]
                store_lats(block, t, cells, side, m, lats, chunks, buffer)

    in_gap = iota((GAP * SUB, LANES), 0) % chunks == chunks - 1
    at_lane = iota((rows, LANES), 1)
    holds_lon = (at_lane < fields * GROUP) | (at_lane // GROUP == LANES // GROUP - 3)
    for g in range(groups):
        if g in (0, groups - 1):
            side = g // (groups - 1)
            from_rim = holds_lon & ((at_lane % GROUP < RIM) if side == 0 else (at_lane % GROUP >= RIM))
            first[g, pl.ds(SUB, rows), :] = jnp.where(from_rim, cells[side], own[g].astype(f32)).astype(bf16)
        else:
            first[g, pl.ds(SUB, rows), :] = own[g]
        spot = pl.ds((1 + gap_k) * SUB, GAP * SUB)
        kept = first[g, spot, :].astype(f32)
        first[g, spot, :] = jnp.where(in_gap, gaps[g], kept).astype(bf16)
        end = first[g, pl.ds(rows, SUB), :].astype(f32)
        first[g, pl.ds(0, SUB), :] = pltpu.roll(end, 1, 0).astype(bf16)
        begin = first[g, pl.ds(SUB, SUB), :].astype(f32)
        first[g, pl.ds(SUB + rows, SUB), :] = pltpu.roll(begin, SUB - 1, 0).astype(bf16)

    hidden = LANES // 4
    per = LANES // hidden
    tiles = odd.shape[0]
    cuts = 2
    step = rows // cuts
    lower = iota((step, LANES), 1) < 2 * hidden

    def activate(pre):
        return (pre * jnp.tanh(pre) + pre).astype(bf16)

    def finish(x, valid):
        used = (valid + per - 1) // per

        @pl.when(top)
        def _():
            strip_top = SUB * (1 + gap_k + STRIP + RIM - 1)
            own_top = SUB * gap_k
            strip_ghost = SUB * (1 + gap_k + GHOST)
            own_ghost = SUB * (1 + gap_k + NORTH)
            last_chunk = iota((SUB, LANES), 0) % chunks == chunks - 1
            spot = iota((SUB, LANES), 1) // hidden
            for src, dst in ((strip_top, own_ghost), (own_top, strip_ghost)):
                found = [x[t, pl.ds(src, SUB), :].astype(f32) for t in range(used)]
                for t in range(used):
                    total = x[t, pl.ds(dst, SUB), :].astype(f32)
                    for i in range(per):
                        lon = valid - 1 - (per * t + i)
                        if lon < 0:
                            continue
                        moved = pltpu.roll(found[lon // per], (hidden * (i - lon % per)) % LANES, 1)
                        total = jnp.where(last_chunk & (spot == i), moved, total)
                    x[t, pl.ds(dst, SUB), :] = total.astype(bf16)

        for t in range(used):
            end = x[t, pl.ds(rows, SUB), :].astype(f32)
            x[t, pl.ds(0, SUB), :] = pltpu.roll(end, 1, 0).astype(bf16)
            begin = x[t, pl.ds(SUB, SUB), :].astype(f32)
            x[t, pl.ds(SUB + rows, SUB), :] = pltpu.roll(begin, SUB - 1, 0).astype(bf16)

    for x in (odd, even):
        x[tiles - 1] = jnp.zeros(x.shape[1:], bf16)
    even[tiles - 2] = jnp.zeros(even.shape[1:], bf16)

    def put(y, b, r, out):
        for e in range(out.shape[1] // LANES):
            y[2 * b + e, pl.ds(SUB + r, step), :] = out[:, e * LANES : (e + 1) * LANES]

    for b in range(groups):
        for n in range(cuts):
            r = n * step
            parts = [first[b, pl.ds(r + SUB * d, step), :] for d in range(3)]
            put(odd, b, r, activate(dot(jnp.concatenate(parts, axis=1), t1[...])))
    finish(odd, lons + 6)

    width = GROUP * hidden

    def layer(x, y, t, left_over):
        for b in range(groups):
            for n in range(cuts):
                r = n * step

                def cells_of(tile, d):
                    return x[tile, pl.ds(r + SUB * d, step), :]

                def packed(tile):
                    more = [cells_of(tile, d) for d in range(3)]
                    return [
                        jnp.where(lower, more[0], pltpu.roll(more[1], 2 * hidden, 1)),
                        jnp.where(lower, more[2], first[b, pl.ds(r + SUB, step), :]),
                    ]

                if b < groups - 1:
                    parts = [cells_of(2 * b + e, d) for d in range(3) for e in range(2)] + packed(2 * b + 2)
                    matrix = t[...]
                elif left_over == per:
                    parts = [cells_of(2 * b, d) for d in range(3)] + packed(2 * b + 1)
                    lanes = pl.ds(0, LANES)
                    matrix = jnp.concatenate(
                        [t[pl.ds(d * width, LANES), lanes] for d in range(3)]
                        + [t[pl.ds(d * width + LANES, 2 * hidden), lanes] for d in range(3)]
                        + [t[pl.ds(3 * width + 6 * hidden, 2 * hidden), lanes]],
                        axis=0,
                    )
                else:
                    parts = [cells_of(2 * b, d) for d in range(3)] + [first[b, pl.ds(r + SUB, step), :]]
                    lanes = pl.ds(0, LANES)
                    matrix = jnp.concatenate(
                        [t[pl.ds(d * width, LANES), lanes] for d in range(3)]
                        + [jnp.zeros((2 * hidden, LANES), bf16)]
                        + [t[pl.ds(3 * width + 6 * hidden, 2 * hidden), lanes]],
                        axis=0,
                    )
                put(y, b, r, activate(dot(jnp.concatenate(parts, axis=1), matrix)))

    layer(odd, even, t2, per)
    finish(even, lons + 4)
    layer(even, odd, t3, per // 2)
    finish(odd, lons + 2)

    depth = t4.shape[1] // LANES
    long = (rows + 2 * SUB) // 2
    before = iota((long, LANES), 1) < LANES // 2
    for n in range(2):
        span_rows = pl.ds(n * long, long)
        sides = []
        for side in range(2):
            parts = [odd[side * (depth - 1) + t, span_rows, :] for t in range(depth)]
            sides.append(dot(jnp.concatenate(parts, axis=1), t4[side]))
        force[0, span_rows, :] = jnp.where(before, sides[0][:, :LANES], sides[1][:, :LANES])
        swapped = jnp.where(before, sides[1][:, :LANES], sides[0][:, :LANES])
        force[1, span_rows, :] = pltpu.roll(swapped, LANES // 2, 1)
        force[2, span_rows, :] = jnp.where(before, sides[0][:, LANES:], sides[1][:, LANES:])

    ocean = sea[...].astype(f32)
    at_lat = iota((lons, lats), 1).astype(f32)
    lat_rows = (lat_index * lats).astype(f32) + at_lat
    turn = CORIOLIS * (2.0 * (lat_rows + 0.5) / (lats * lat_count) - 1.0)
    at_first = iota((lons, lats), 0) == 0
    at_last = iota((lons, lats), 0) == lons - 1
    at_south = iota((lons, lats), 1) == 0
    at_north = iota((lons, lats), 1) == lats - 1
    lon_rests = members * fields * RIM + GROUP
    halves = lons // 2
    for m in range(members):
        for q in range(chunks):
            size = min(blocks, lats - q * blocks)
            total = force[0, pl.ds(m * chunks + q, size, stride=SUB), :]
            for d in range(1, 3):
                total = total + force[d, pl.ds(d * SUB + m * chunks + q, size, stride=SUB), :]
            gathered[m, pl.ds(q * blocks, size), :] = total
        turned_force = jnp.transpose(gathered[m])

        def push(c):
            parts = [
                turned_force[side * LANES // 2 + c * halves : side * LANES // 2 + (c + 1) * halves]
                for side in range(2)
            ]
            return (jnp.concatenate(parts, axis=0) + bias_last[c]) * ocean

        def rims(c):
            row = (m * fields + c) * RIM
            more = lon_rests + m * (fields - noises) + c - noises
            west = left[pl.ds(row + RIM - 1, 1)] + left[pl.ds(more, 1)]
            east = right[pl.ds(row, 1)] + right[pl.ds(more, 1)]
            low, high = [], []
            for g in range(groups):
                spot = (g * members + m) * RIM
                more = rests + g * members + m
                some = slice(c * GROUP, (c + 1) * GROUP)
                low.append(south[some, spot + RIM - 1 : spot + RIM] + south[some, more : more + 1])
                high.append(north_rim[some, spot : spot + 1] + north_rim[some, more : more + 1])
            low = jnp.broadcast_to(jnp.concatenate(low, axis=0), (lons + GROUP, LANES))
            high = jnp.broadcast_to(jnp.concatenate(high, axis=0), (lons + GROUP, LANES))
            low = pltpu.roll(low, lons + GROUP - RIM, 0)[:lons]
            high = pltpu.roll(high, lons + GROUP - RIM, 0)[:lons]
            repeat = lats // LANES
            return west, east, jnp.concatenate([low] * repeat, axis=1), jnp.concatenate([high] * repeat, axis=1)

        def around(x, rim):
            west, east, low, high = rim
            return (
                jnp.where(at_first, west, pltpu.roll(x, 1, 0)),
                jnp.where(at_last, east, pltpu.roll(x, lons - 1, 0)),
                jnp.where(at_south, low, pltpu.roll(x, 1, 1)),
                jnp.where(at_north, high, pltpu.roll(x, lats - 1, 1)),
            )

        sets = []
        for level in range(levels):
            sets.append(
                [
                    (x[m, level], around(x[m, level], rims(noises + n * levels + level)))
                    for n, x in enumerate((u, v, h))
                ]
            )
        for level in range(levels):
            (cu, au), (cv, av), (ch, ah) = sets[level]
            upper, lower_h = sets[0][2][1], sets[1][2][1]
            pressure = [upper[i] + lower_h[i] for i in range(4)]
            if level == 1:
                pressure = [pressure[i] + REDUCED * lower_h[i] for i in range(4)]
            lap_u = au[1] + au[0] + au[3] + au[2] - 4.0 * cu
            lap_v = av[1] + av[0] + av[3] + av[2] - 4.0 * cv
            dx = 0.5 * (pressure[1] - pressure[0])
            dy = 0.5 * (pressure[3] - pressure[2])
            gain_u = turn * cv - dx + push(level) + VISCOSITY * lap_u
            gain_v = -turn * cu - dy + push(levels + level) + VISCOSITY * lap_v
            results[0, m, level] = ocean * (cu + TIME_STEP * gain_u)
            results[1, m, level] = ocean * (cv + TIME_STEP * gain_v)
            flow = 0.5 * (ah[1] * au[1] - ah[0] * au[0]) + 0.5 * (ah[3] * av[3] - ah[2] * av[2])
            results[2, m, level] = ch - TIME_STEP * flow
        for n, out in enumerate((new_u, new_v, new_h)):
            pltpu.make_async_copy(results.at[n, m], out.at[m], done.at[n, m]).start()
    for m in range(members):
        for n, out in enumerate((new_u, new_v, new_h)):
            pltpu.make_async_copy(results.at[n, m], out.at[m], done.at[n, m]).wait()


def body(
    noise,
    velocity_u,
    velocity_v,
    thickness,
    land_sea,
    conv_first,
    bias_first,
    conv_second,
    bias_second,
    conv_third,
    bias_third,
    conv_last,
    bias_last,
):
    members, noises, lons, lats = noise.shape
    levels = velocity_u.shape[1]
    fields = noises + 3 * levels
    sizes = (members, noises, levels)
    hidden = conv_first.shape[0]
    outs = conv_last.shape[0]
    groups = lons // GROUP + 1
    rows = members * (lats + GAP)
    assert hidden * 4 == LANES and outs * lons == LANES and members * (RIM + 1) * groups <= LANES
    assert fields % 2 == 0 and 4 * -(-fields // 4) == 12 and GROUP * (fields + 6) == LANES and lons % 16 == 0
    assert lats % LANES == 0 and SUB % members == 0 and (lats + GAP) % (SUB // members) == 0
    lon_count, lat_count = lax.axis_size("lon"), lax.axis_size("lat")
    assert lon_count % 2 == 0 and lat_count % 2 == 0
    state = (noise, velocity_u, velocity_v, thickness, land_sea)
    whole = pl.BlockSpec(memory_space=pltpu.VMEM)

    tall = members * fields * RIM + GROUP + members * 3 * levels
    assert tall % SUB == 0
    head, tail = pl.pallas_call(
        functools.partial(pack_lon_kernel, sizes),
        out_shape=[pltpu.VMEM((tall, lats), bf16)] * 2,
        in_specs=[pl.BlockSpec(memory_space=pltpu.HBM)] * 5,
        out_specs=[whole] * 2,
        scratch_shapes=[
            pltpu.VMEM(noise.shape, noise.dtype),
            pltpu.VMEM((2, 3, members, levels, GROUP, lats), f32),
            pltpu.VMEM((2, GROUP, lats), land_sea.dtype),
            pltpu.VMEM((2, tall, lats), f32),
            pltpu.SemaphoreType.DMA((9,)),
        ],
        name="pack_lon",
    )(*state)
    ring = [(i, (i + 1) % lon_count) for i in range(lon_count)]
    left = lax.ppermute(tail, "lon", ring)
    right = lax.ppermute(head, "lon", [(b, a) for a, b in ring])

    wide = -(-(fields + 1) * GROUP // SUB) * SUB
    part = pltpu.VMEM((wide, LANES), f32)
    message = pltpu.VMEM((wide, LANES), bf16)
    own, own_head, own_tail = pl.pallas_call(
        functools.partial(own_kernel, sizes),
        out_shape=[pltpu.VMEM((groups, rows, LANES), bf16), part, part],
        in_specs=[whole] * 5,
        out_specs=[whole] * 3,
        scratch_shapes=[
            pltpu.VMEM((groups, rows, LANES), f32),
            pltpu.VMEM((members * groups * lats // LANES, LANES, LANES), f32),
        ],
        compiler_params=pltpu.CompilerParams(vmem_limit_bytes=8 * 2**20),
        cost_estimate=pl.CostEstimate(flops=10**7, bytes_accessed=10**7, transcendentals=0),
        name="own_cells",
    )(*state)
    last = lat_count - 1
    smem = pl.BlockSpec(memory_space=pltpu.SMEM)
    to_even, to_odd = pl.pallas_call(
        functools.partial(join_kernel, sizes, lons),
        out_shape=[message] * 2,
        in_specs=[whole] * 4,
        out_specs=[whole] * 2,
        scratch_shapes=[
            pltpu.VMEM((2, 2, tall, LANES), f32),
            pltpu.VMEM((2, wide, LANES), f32),
        ],
        compiler_params=pltpu.CompilerParams(vmem_limit_bytes=4 * 2**20),
        name="join_rims",
    )(left, right, own_head, own_tail)
    even_rim = lax.ppermute(to_even, "lat", [(i, i ^ 1) for i in range(lat_count)])
    pairs = []
    for t in range(lon_count):
        at = t * lat_count
        pairs += [(at + k, at + k - 1 + 2 * (k % 2)) for k in range(1, last)]
        pairs += [(at, (t ^ 1) * lat_count), (at + last, (lon_count - 1 - t) * lat_count + last)]
    odd_rim = lax.ppermute(to_odd, ("lon", "lat"), pairs)

    deep = -(-(lons // 2 + 2) * hidden // LANES) * LANES
    t1, t2, t3, t4 = pl.pallas_call(
        weights_kernel,
        out_shape=[
            pltpu.VMEM((3 * LANES, 2 * LANES), bf16),
            pltpu.VMEM((8 * LANES, 2 * LANES), bf16),
            pltpu.VMEM((8 * LANES, 2 * LANES), bf16),
            pltpu.VMEM((2, deep, 2 * LANES), bf16),
        ],
        in_specs=[whole] * 7,
        out_specs=[whole] * 4,
        compiler_params=pltpu.CompilerParams(vmem_limit_bytes=8 * 2**20),
        cost_estimate=pl.CostEstimate(flops=10**7, bytes_accessed=3 * 10**6, transcendentals=0),
        name="banded_matrices",
    )(
        conv_first.transpose(3, 2, 1, 0),
        conv_second.transpose(2, 3, 0, 1),
        conv_third.transpose(2, 3, 0, 1),
        conv_last.transpose(2, 3, 0, 1),
        bias_first[None],
        bias_second[None],
        bias_third[None],
    )

    padded = rows + 2 * SUB
    tiles = 2 * groups + 1
    out = jax.ShapeDtypeStruct(velocity_u.shape, f32)
    return pl.pallas_call(
        functools.partial(main_kernel, sizes),
        out_shape=[out] * 3,
        in_specs=[smem] + [whole] * 14,
        out_specs=[pl.BlockSpec(memory_space=pltpu.HBM)] * 3,
        scratch_shapes=[
            pltpu.VMEM((tall, lats), f32),
            pltpu.VMEM((tall, lats), f32),
            pltpu.VMEM((2, rows, LANES), f32),
            pltpu.VMEM((groups, padded, LANES), bf16),
            pltpu.VMEM((tiles, padded, LANES), bf16),
            pltpu.VMEM((tiles, padded, LANES), bf16),
            pltpu.VMEM((3, padded, LANES), f32),
            pltpu.VMEM((members, lats, LANES), f32),
            pltpu.VMEM((2 * members * lats // LANES, LANES, LANES), f32),
            pltpu.VMEM((4, LANES, LANES), f32),
            pltpu.VMEM((groups, GAP * SUB, LANES), f32),
            pltpu.VMEM((3, *velocity_u.shape), f32),
            pltpu.SemaphoreType.DMA((3, members)),
        ],
        compiler_params=pltpu.CompilerParams(vmem_limit_bytes=32 * 2**20),
        cost_estimate=pl.CostEstimate(flops=2 * 10**10, bytes_accessed=10**7, transcendentals=4 * 10**6),
        name="network_and_step",
    )(
        bias_last,
        own,
        *state[1:],
        left,
        right,
        even_rim,
        odd_rim,
        to_odd,
        t1,
        t2,
        t3,
        t4,
    )


def solution(mesh):
    tiles = P(None, None, "lon", "lat")
    return jax.shard_map(
        body,
        mesh=mesh,
        in_specs=(tiles,) * 4 + (P("lon", "lat"),) + (P(),) * 8,
        out_specs=(tiles,) * 3,
        check_vma=False,
    )
```

```python
import functools

import jax
import jax.numpy as jnp
from jax import lax
from jax.experimental import pallas as pl
from jax.experimental.pallas import tpu as pltpu
from jax.sharding import PartitionSpec as P

REDUCED = 0.5
TIME_STEP = 0.2
VISCOSITY = 0.05
CORIOLIS = 0.4

RIM = 4
GAP = 16
NORTH, STRIP, GHOST, SOUTH = 0, 4, 8, 12
SUB = 16
LANES = 128
GROUP = 8
LAND = 2.0**100

f32 = jnp.float32
bf16 = jnp.bfloat16


def iota(shape, dim):
    return lax.broadcasted_iota(jnp.int32, shape, dim)


def dot(a, b):
    return jnp.dot(a, b, preferred_element_type=f32)


def rest(x):
    return x - x.astype(bf16).astype(f32)


def pack_lon_kernel(sizes, noise, u, v, h, sea, head, tail, noises_in, states, seas, wide, done):
    members, noises, levels = sizes
    fields = noises + 3 * levels
    lons, lats = sea.shape
    copies = [pltpu.make_async_copy(noise, noises_in, done.at[0])]
    for side in range(2):
        at = pl.ds(side * (lons - GROUP), GROUP)
        copies.append(pltpu.make_async_copy(sea.at[at], seas.at[side], done.at[1 + 4 * side]))
        for n, x in enumerate((u, v, h)):
            copies.append(
                pltpu.make_async_copy(x.at[:, :, at], states.at[side, n], done.at[2 + 4 * side + n])
            )
    for copy in copies:
        copy.start()
    for copy in copies:
        copy.wait()
    upper = iota((GROUP, lats), 0) < RIM

    def field(m, c, side):
        if c < noises:
            full = noises_in[m, c].astype(f32)
            return full[-GROUP:] if side else full[:GROUP]
        c -= noises
        return states[side, c // levels, m, c % levels]

    rests = members * fields * RIM + GROUP
    for m in range(members):
        for c in range(0, fields, 2):
            rows = pl.ds((m * fields + c) * RIM, GROUP)
            wide[0, rows] = jnp.where(upper, field(m, c, 0), pltpu.roll(field(m, c + 1, 0), RIM, 0))
            wide[1, rows] = jnp.where(upper, pltpu.roll(field(m, c, 1), RIM, 0), field(m, c + 1, 1))
        for c in range(noises, fields):
            row = pl.ds(rests + m * (fields - noises) + c - noises, 1)
            wide[0, row] = rest(field(m, c, 0)[:1])
            wide[1, row] = rest(field(m, c, 1)[GROUP - 1 :])
    rows = pl.ds(members * fields * RIM, GROUP)
    wide[0, rows] = jnp.where(upper, seas[0].astype(f32), 0.0)
    wide[1, rows] = jnp.where(upper, pltpu.roll(seas[1].astype(f32), RIM, 0), 0.0)
    head[...] = wide[0].astype(bf16)
    tail[...] = wide[1].astype(bf16)


def rim_tile(sizes, m, c, side, rim):
    members, noises, levels = sizes
    fields = noises + 3 * levels
    row = (m * fields + c) * RIM if c < fields else members * fields * RIM
    tile = rim[pl.ds(row // GROUP * GROUP, GROUP)]
    if (row // RIM) % 2 == side:
        return tile
    return pltpu.roll(tile, RIM, 0)


def window(tiles, following, mask, next_mask):
    pair = iota(mask.shape, 0) // 2
    zero = jnp.zeros_like(mask)
    more = []
    for start in range(0, len(tiles), 4):
        total = zero
        for n in range(min(4, len(tiles) - start)):
            moved = pltpu.roll(following[start + n], 2 * n, 0) if n else following[start]
            total = jnp.where(pair == n, moved, total)
        more.append(total)
    return jnp.concatenate(
        tiles + more + [mask - 1.0, next_mask - 1.0, jnp.ones_like(mask)], axis=0
    )


def store_lats(block, t, dst, tile, m, lats, chunks, buffer):
    blocks = (lats + GAP) // chunks
    buffer[...] = jnp.transpose(block)
    for q in range(chunks):
        lo = max(q * blocks, t * LANES)
        hi = min((q + 1) * blocks, (t + 1) * LANES, lats)
        if lo < hi:
            start = (lo - q * blocks) * SUB + m * chunks + q
            dst[tile, pl.ds(start, hi - lo, stride=SUB), :] = buffer[pl.ds(lo - t * LANES, hi - lo), :]


def shifted_tiles(sizes, refs, m, c, t):
    noise, u, v, h, sea = refs
    members, noises, levels = sizes
    fields = noises + 3 * levels
    lons = sea.shape[0]
    lanes = slice(t * LANES, (t + 1) * LANES)
    if c == fields:
        full = sea[:, lanes].astype(f32)
    elif c < noises:
        full = noise[m, c, :, lanes].astype(f32)
    else:
        full = (u, v, h)[(c - noises) // levels][m, (c - noises) % levels, :, lanes]
    full = pltpu.roll(full, lons - RIM, 0)
    tiles = [full[g * GROUP : (g + 1) * GROUP] for g in range(lons // GROUP)]
    return tiles[-1:] + tiles


def prepare_kernel(sizes, noise, u, v, h, sea, *refs):
    weights, refs = refs[:7], refs[7:]
    held, matrices, (head, tail, done) = refs[:5], refs[5:9], refs[9:]
    members, noises, levels = sizes
    fields = noises + 3 * levels
    lons, lats = sea.shape
    groups = lons // GROUP + 1
    copies = [
        pltpu.make_async_copy(x, y, done.at[n]) for n, (x, y) in enumerate(zip((noise, u, v, h, sea), held))
    ]
    for copy in copies:
        copy.start()
    weights_kernel(*weights, *matrices)
    for copy in copies:
        copy.wait()
    lane = iota((GROUP, LANES), 1)
    for out, t, first in ((head, 0, 0), (tail, lats // LANES - 1, LANES - RIM)):
        for c in range(fields + 1):
            total = jnp.zeros((GROUP, LANES), f32)
            for m in range(members):
                for g, tile in enumerate(shifted_tiles(sizes, held, m, c, t)):
                    place = (g * members + m) * RIM
                    moved = pltpu.roll(tile, (place - first) % LANES, 1)
                    total = jnp.where((lane >= place) & (lane < place + RIM), moved, total)
                    if noises <= c < fields:
                        place = groups * members * RIM + g * members + m
                        edge = 0 if out is head else LANES - 1
                        moved = pltpu.roll(rest(tile), (place - edge) % LANES, 1)
                        total = jnp.where(lane == place, moved, total)
            out[pl.ds(c * GROUP, GROUP)] = total
        for c in range(fields + 1, out.shape[0] // GROUP):
            out[pl.ds(c * GROUP, GROUP)] = jnp.zeros((GROUP, LANES), f32)


def cells_kernel(sizes, noise, u, v, h, sea, left, right, after, out, rims, cells, turned):
    members, noises, levels = sizes
    fields = noises + 3 * levels
    lons, lats = sea.shape
    groups = lons // GROUP + 1
    chunks = SUB // members
    rows = cells.shape[1]
    gap_k = lats - (chunks - 1) * ((lats + GAP) // chunks)
    rims[0] = left[...].astype(f32)
    rims[1] = right[...].astype(f32)
    for m in range(members):
        for g in range(groups):
            empty = pl.ds(gap_k * SUB + (m + 1) * chunks - 1, GAP, stride=SUB)
            cells[g, empty, :] = jnp.zeros((GAP, LANES), f32)
    blank = jnp.zeros((GROUP, LANES), f32)
    upper = iota((GROUP, LANES), 0) < RIM
    for t in range(lats // LANES):
        lanes = slice(t * LANES, (t + 1) * LANES)
        for m in range(members):
            tiles = []
            for c in range(fields + 1):
                groups_of = shifted_tiles(sizes, (noise, u, v, h, sea), m, c, t)
                ends = [rim_tile(sizes, m, c, side, rims.at[side, :, lanes]) for side in range(2)]
                groups_of[0] = jnp.where(upper, ends[0], groups_of[0])
                groups_of[-1] = jnp.where(upper, groups_of[-1], ends[1])
                tiles.append(groups_of)
            for g in range(groups):
                following = [x[g + 1] if g + 1 < groups else blank for x in tiles]
                block = window([x[g] for x in tiles[:fields]], following[:fields], tiles[fields][g], following[fields])
                store_lats(block, t, cells, g, m, lats, chunks, turned.at[(t * members + m) * groups + g])
    for g in range(groups):
        out[g] = cells[g].astype(bf16)


def join_kernel(sizes, lons, left, right, head, tail, even, odd, rims, wide):
    members, noises, levels = sizes
    fields = noises + 3 * levels
    groups = lons // GROUP + 1
    lats = left.shape[1]
    for side, rim in enumerate((left, right)):
        rims[side, 0] = rim[:, :LANES].astype(f32)
        rims[side, 1] = rim[:, lats - LANES :].astype(f32)
    lane = iota((GROUP, LANES), 1)
    upper = iota((GROUP, LANES), 0) < RIM
    to_south = lax.axis_index("lat") % 2 == 1
    for c in range(fields + 1):
        rows = pl.ds(c * GROUP, GROUP)
        ends = []
        for n, (part, first) in enumerate(((head, 0), (tail, LANES - RIM))):
            total = part[rows]
            for side in range(2):
                held = upper if side == 0 else ~upper
                for m in range(members):
                    place = ((groups - 1) * side * members + m) * RIM
                    tile = rim_tile(sizes, m, c, side, rims.at[side, n])
                    moved = pltpu.roll(tile, (place - first) % LANES, 1)
                    total = jnp.where(held & (lane >= place) & (lane < place + RIM), moved, total)
            ends.append(total)
        wide[0, rows] = jnp.where(to_south, ends[0], ends[1])
        wide[1, rows] = jnp.where(to_south, ends[1], ends[0])
    rows = pl.ds((fields + 1) * GROUP, wide.shape[1] - (fields + 1) * GROUP)
    wide[:, rows] = jnp.zeros((2, wide.shape[1] - (fields + 1) * GROUP, LANES), f32)
    even[...] = wide[0].astype(bf16)
    odd[...] = wide[1].astype(bf16)


def weights_kernel(w1, w2, w3, w4, bias1, bias2, bias3, t1, t2, t3, t4):
    hidden = w2.shape[2]
    per = LANES // hidden
    lane = iota((hidden, LANES), 1)
    fields = w1.shape[2]
    rows = fields * GROUP
    out_lon = iota((GROUP, LANES), 1) // hidden
    in_row = iota((GROUP, LANES), 0)
    bias_row = iota((GROUP, LANES), 0)

    def bias_rows(layer):
        part = 0.5 * jnp.concatenate([(bias1, bias2, bias3)[layer][...]] * per, axis=1)
        b1 = part.astype(bf16).astype(f32)
        b2 = (part - b1).astype(bf16).astype(f32)
        b3 = part - b1 - b2
        zero = jnp.zeros((GROUP, LANES), f32)
        return jnp.where(
            bias_row == 0,
            b1,
            jnp.where(bias_row == 1, b2, jnp.where(bias_row == 2, b3, zero)),
        )

    def sea_rows(shift, tile):
        lon = iota((2 * GROUP, LANES), 0)
        out = iota((2 * GROUP, LANES), 1) // hidden + per * tile
        return jnp.where(lon == out + shift, LAND, 0.0)

    for dj in range(3):
        taps = [0.5 * jnp.concatenate([w1[dj, di].astype(f32)] * per, axis=1) for di in range(3)]
        for tile in range(2):
            parts = []
            for c in range(fields):
                total = jnp.zeros((GROUP, LANES), f32)
                for di in range(3):
                    hit = in_row == out_lon + per * tile + di
                    total = jnp.where(hit, jnp.broadcast_to(taps[di][c : c + 1], (GROUP, LANES)), total)
                parts.append(total)
            for start in range(0, fields, 4):
                total = jnp.zeros((GROUP, LANES), f32)
                for n in range(min(4, fields - start)):
                    for di in range(3):
                        hit = in_row % 2 + GROUP == out_lon + per * tile + di
                        row = jnp.broadcast_to(taps[di][start + n : start + n + 1], (GROUP, LANES))
                        total = jnp.where(hit & (in_row // 2 == n), row, total)
                parts.append(total)
            if dj == 1:
                parts += [sea_rows(1, tile), bias_rows(0)]
            else:
                parts.append(jnp.zeros((3 * GROUP, LANES), f32))
            block = jnp.concatenate(parts, axis=0)
            t1[pl.ds(dj * LANES, LANES), pl.ds(tile * LANES, LANES)] = block.astype(bf16)

    for layer, (w, t) in enumerate(((w2, t2), (w3, t3))):
        for dj in range(3):
            taps = []
            for di in range(3):
                cell = 0.5 * w[di, dj].astype(f32)
                wide = jnp.concatenate([cell, jnp.zeros((hidden, LANES - hidden), f32)], axis=1)
                square = jnp.concatenate([wide] * per, axis=0)
                taps.append(jnp.transpose(square)[:hidden])
            for lon in range(GROUP + 2):
                for tile in range(2):
                    total = jnp.zeros((hidden, LANES), f32)
                    for di in range(3):
                        total = jnp.where(lane // hidden + per * tile == lon - di, taps[di], total)
                    if lon < GROUP:
                        row = dj * GROUP * hidden + lon * hidden
                    else:
                        row = 3 * GROUP * hidden + dj * 2 * hidden + (lon - GROUP) * hidden
                    t[pl.ds(row, hidden), pl.ds(tile * LANES, LANES)] = total.astype(bf16)
        for tile in range(2):
            block = jnp.concatenate(
                [
                    jnp.zeros((5 * GROUP, LANES), f32),
                    sea_rows(2 + layer, tile),
                    bias_rows(1 + layer),
                ],
                axis=0,
            )
            row = 3 * GROUP * hidden + 6 * hidden
            t[pl.ds(row, 2 * hidden), pl.ds(tile * LANES, LANES)] = block.astype(bf16)

    outs = w4.shape[2]
    half = LANES // 2
    lons = half // outs
    slot = iota((hidden, LANES), 1) // half
    out_lon = iota((hidden, LANES), 1) % lons
    taps = {}
    for dj in range(3):
        for di in range(3):
            cell = w4[di, dj].astype(f32)
            wide = jnp.concatenate([cell, jnp.zeros((outs, LANES - hidden), f32)], axis=1)
            square = jnp.concatenate(
                [jnp.broadcast_to(wide[c : c + 1], (lons, LANES)) for c in range(outs)] * 2, axis=0
            )
            taps[dj, di] = jnp.transpose(square)[:hidden]
    order = ((0, 1, 2, None), (1, 0, None, 2))
    for side in range(2):
        for lon in range(t4.shape[1] // hidden):
            for tile in range(2):
                total = jnp.zeros((hidden, LANES), f32)
                for place in range(2):
                    dj = order[side][2 * tile + place]
                    if dj is None:
                        continue
                    for di in range(3):
                        total = jnp.where((slot == place) & (out_lon == lon - di), taps[dj, di], total)
                t4[side, pl.ds(lon * hidden, hidden), pl.ds(tile * LANES, LANES)] = total.astype(bf16)


def main_kernel(
    sizes,
    bias_last,
    own,
    u,
    v,
    h,
    sea,
    left_in,
    right_in,
    even_rim,
    odd_rim,
    own_tail,
    t1,
    t2,
    t3,
    t4,
    new_u,
    new_v,
    new_h,
    left,
    right,
    first,
    odd,
    even,
    force,
    gathered,
    turned,
    gaps,
    results,
    done,
):
    members, noises, levels = sizes
    fields = noises + 3 * levels
    lons, lats = sea.shape
    groups = lons // GROUP + 1
    chunks = SUB // members
    blocks = (lats + GAP) // chunks
    rows = blocks * SUB
    gap_k = lats - (chunks - 1) * blocks
    lat_index, lat_count = lax.axis_index("lat"), lax.axis_size("lat")
    top = lat_index == lat_count - 1
    is_odd = lat_index % 2 == 1
    bottom = lat_index == 0
    left[...] = left_in[...].astype(f32)
    right[...] = right_in[...].astype(f32)
    strip = odd_rim[...].astype(f32)
    paired = even_rim[...].astype(f32)
    south = jnp.where(is_odd, paired, jnp.where(bottom, 0.0, strip))

    wide = strip.shape[0]
    span = members * RIM
    lane = iota((wide, LANES), 1)
    rests = groups * span
    border = ((lane % RIM == 0) & (lane < rests)) | (lane >= rests)
    row_to = iota((wide, wide), 0)
    row_from = iota((wide, wide), 1)
    channel = row_to // GROUP
    mirrored = (channel == row_from // GROUP) & (row_from % GROUP == GROUP - 1 - row_to % GROUP)
    odd_parity = (channel >= noises) & (channel < noises + 2 * levels)
    flip_rows = jnp.where(mirrored, jnp.where(odd_parity, -1.0, 1.0), 0.0).astype(bf16)
    lane_from = iota((LANES, LANES), 0)
    lane_to = iota((LANES, LANES), 1)
    source = (groups - 1 - lane_to // span) * span + lane_to % span + RIM - 1
    moves = (lane_to % RIM == 0) & (lane_to < rests) & (lane_from == source)
    other = lane_to - rests
    source = rests + (groups - 1 - other // members) * members + other % members
    moves = moves | ((other >= 0) & (other < groups * members) & (lane_from == source))
    flip_lanes = jnp.where(moves, 1.0, 0.0).astype(bf16)
    pair = dot(flip_rows, jnp.concatenate([odd_rim[...], own_tail[...]], axis=1)).astype(bf16)
    folded = dot(pair[:, :LANES], flip_lanes)
    ghost = dot(pair[:, LANES:], flip_lanes)
    north = jnp.where(is_odd, strip, paired)
    north_rim = jnp.where(border & top, folded, north)

    for n, message in enumerate((north_rim, strip, ghost, south)):
        after = pltpu.roll(message, LANES - span, 1)
        cut = [message[c * GROUP : (c + 1) * GROUP] for c in range(fields + 1)]
        after = [after[c * GROUP : (c + 1) * GROUP] for c in range(fields + 1)]
        turned[n] = jnp.transpose(window(cut[:fields], after[:fields], cut[fields], after[fields]))
        for g in range(groups):
            for m in range(members):
                gap = (m - 1) % members if n == 3 else m
                start = n * RIM * SUB + gap * chunks + chunks - 1
                gaps[g, pl.ds(start, RIM, stride=SUB), :] = turned[n, pl.ds((g * members + m) * RIM, RIM), :]

    in_gap = iota((GAP * SUB, LANES), 0) % chunks == chunks - 1
    for g in range(groups):
        first[g, pl.ds(SUB, rows), :] = own[g]
        spot = pl.ds((1 + gap_k) * SUB, GAP * SUB)
        kept = first[g, spot, :].astype(f32)
        first[g, spot, :] = jnp.where(in_gap, gaps[g], kept).astype(bf16)
        end = first[g, pl.ds(rows, SUB), :].astype(f32)
        first[g, pl.ds(0, SUB), :] = pltpu.roll(end, 1, 0).astype(bf16)
        begin = first[g, pl.ds(SUB, SUB), :].astype(f32)
        first[g, pl.ds(SUB + rows, SUB), :] = pltpu.roll(begin, SUB - 1, 0).astype(bf16)

    hidden = LANES // 4
    per = LANES // hidden
    tiles = odd.shape[0]
    cuts = 4
    step = rows // cuts
    lower = iota((step, LANES), 1) < 2 * hidden

    def activate(pre):
        return (pre * jnp.tanh(pre) + pre).astype(bf16)

    def finish(x, valid):
        used = (valid + per - 1) // per

        @pl.when(top)
        def _():
            strip_top = SUB * (1 + gap_k + STRIP + RIM - 1)
            own_top = SUB * gap_k
            strip_ghost = SUB * (1 + gap_k + GHOST)
            own_ghost = SUB * (1 + gap_k + NORTH)
            last_chunk = iota((SUB, LANES), 0) % chunks == chunks - 1
            spot = iota((SUB, LANES), 1) // hidden
            for src, dst in ((strip_top, own_ghost), (own_top, strip_ghost)):
                found = [x[t, pl.ds(src, SUB), :].astype(f32) for t in range(used)]
                for t in range(used):
                    total = x[t, pl.ds(dst, SUB), :].astype(f32)
                    for i in range(per):
                        lon = valid - 1 - (per * t + i)
                        if lon < 0:
                            continue
                        moved = pltpu.roll(found[lon // per], (hidden * (i - lon % per)) % LANES, 1)
                        total = jnp.where(last_chunk & (spot == i), moved, total)
                    x[t, pl.ds(dst, SUB), :] = total.astype(bf16)

        for t in range(used):
            end = x[t, pl.ds(rows, SUB), :].astype(f32)
            x[t, pl.ds(0, SUB), :] = pltpu.roll(end, 1, 0).astype(bf16)
            begin = x[t, pl.ds(SUB, SUB), :].astype(f32)
            x[t, pl.ds(SUB + rows, SUB), :] = pltpu.roll(begin, SUB - 1, 0).astype(bf16)

    for x in (odd, even):
        x[tiles - 1] = jnp.zeros(x.shape[1:], bf16)
    even[tiles - 2] = jnp.zeros(even.shape[1:], bf16)

    def put(y, b, r, out):
        for e in range(out.shape[1] // LANES):
            y[2 * b + e, pl.ds(SUB + r, step), :] = out[:, e * LANES : (e + 1) * LANES]

    for b in range(groups):
        for n in range(cuts):
            r = n * step
            parts = [first[b, pl.ds(r + SUB * d, step), :] for d in range(3)]
            put(odd, b, r, activate(dot(jnp.concatenate(parts, axis=1), t1[...])))
    finish(odd, lons + 6)

    width = GROUP * hidden

    def layer(x, y, t, left_over):
        for b in range(groups):
            for n in range(cuts):
                r = n * step

                def cells_of(tile, d):
                    return x[tile, pl.ds(r + SUB * d, step), :]

                def packed(tile):
                    more = [cells_of(tile, d) for d in range(3)]
                    return [
                        jnp.where(lower, more[0], pltpu.roll(more[1], 2 * hidden, 1)),
                        jnp.where(lower, more[2], first[b, pl.ds(r + SUB, step), :]),
                    ]

                if b < groups - 1:
                    parts = [cells_of(2 * b + e, d) for d in range(3) for e in range(2)] + packed(2 * b + 2)
                    matrix = t[...]
                elif left_over == per:
                    parts = [cells_of(2 * b, d) for d in range(3)] + packed(2 * b + 1)
                    lanes = pl.ds(0, LANES)
                    matrix = jnp.concatenate(
                        [t[pl.ds(d * width, LANES), lanes] for d in range(3)]
                        + [t[pl.ds(d * width + LANES, 2 * hidden), lanes] for d in range(3)]
                        + [t[pl.ds(3 * width + 6 * hidden, 2 * hidden), lanes]],
                        axis=0,
                    )
                else:
                    parts = [cells_of(2 * b, d) for d in range(3)] + [first[b, pl.ds(r + SUB, step), :]]
                    lanes = pl.ds(0, LANES)
                    matrix = jnp.concatenate(
                        [t[pl.ds(d * width, LANES), lanes] for d in range(3)]
                        + [jnp.zeros((2 * hidden, LANES), bf16)]
                        + [t[pl.ds(3 * width + 6 * hidden, 2 * hidden), lanes]],
                        axis=0,
                    )
                put(y, b, r, activate(dot(jnp.concatenate(parts, axis=1), matrix)))

    layer(odd, even, t2, per)
    finish(even, lons + 4)
    layer(even, odd, t3, per // 2)
    finish(odd, lons + 2)

    depth = t4.shape[1] // LANES
    long = (rows + 2 * SUB) // 2
    before = iota((long, LANES), 1) < LANES // 2
    for n in range(2):
        span_rows = pl.ds(n * long, long)
        sides = []
        for side in range(2):
            parts = [odd[side * (depth - 1) + t, span_rows, :] for t in range(depth)]
            sides.append(dot(jnp.concatenate(parts, axis=1), t4[side]))
        force[0, span_rows, :] = jnp.where(before, sides[0][:, :LANES], sides[1][:, :LANES])
        swapped = jnp.where(before, sides[1][:, :LANES], sides[0][:, :LANES])
        force[1, span_rows, :] = pltpu.roll(swapped, LANES // 2, 1)
        force[2, span_rows, :] = jnp.where(before, sides[0][:, LANES:], sides[1][:, LANES:])

    ocean = sea[...].astype(f32)
    at_lat = iota((lons, lats), 1).astype(f32)
    lat_rows = (lat_index * lats).astype(f32) + at_lat
    turn = CORIOLIS * (2.0 * (lat_rows + 0.5) / (lats * lat_count) - 1.0)
    at_first = iota((lons, lats), 0) == 0
    at_last = iota((lons, lats), 0) == lons - 1
    at_south = iota((lons, lats), 1) == 0
    at_north = iota((lons, lats), 1) == lats - 1
    lon_rests = members * fields * RIM + GROUP
    halves = lons // 2
    for m in range(members):
        for q in range(chunks):
            size = min(blocks, lats - q * blocks)
            total = force[0, pl.ds(m * chunks + q, size, stride=SUB), :]
            for d in range(1, 3):
                total = total + force[d, pl.ds(d * SUB + m * chunks + q, size, stride=SUB), :]
            gathered[m, pl.ds(q * blocks, size), :] = total
        turned_force = jnp.transpose(gathered[m])

        def push(c):
            parts = [
                turned_force[side * LANES // 2 + c * halves : side * LANES // 2 + (c + 1) * halves]
                for side in range(2)
            ]
            return (jnp.concatenate(parts, axis=0) + bias_last[c]) * ocean

        def rims(c):
            row = (m * fields + c) * RIM
            more = lon_rests + m * (fields - noises) + c - noises
            west = left[pl.ds(row + RIM - 1, 1)] + left[pl.ds(more, 1)]
            east = right[pl.ds(row, 1)] + right[pl.ds(more, 1)]
            low, high = [], []
            for g in range(groups):
                spot = (g * members + m) * RIM
                more = rests + g * members + m
                some = slice(c * GROUP, (c + 1) * GROUP)
                low.append(south[some, spot + RIM - 1 : spot + RIM] + south[some, more : more + 1])
                high.append(north_rim[some, spot : spot + 1] + north_rim[some, more : more + 1])
            low = jnp.broadcast_to(jnp.concatenate(low, axis=0), (lons + GROUP, LANES))
            high = jnp.broadcast_to(jnp.concatenate(high, axis=0), (lons + GROUP, LANES))
            low = pltpu.roll(low, lons + GROUP - RIM, 0)[:lons]
            high = pltpu.roll(high, lons + GROUP - RIM, 0)[:lons]
            repeat = lats // LANES
            return west, east, jnp.concatenate([low] * repeat, axis=1), jnp.concatenate([high] * repeat, axis=1)

        def around(x, rim):
            west, east, low, high = rim
            return (
                jnp.where(at_first, west, pltpu.roll(x, 1, 0)),
                jnp.where(at_last, east, pltpu.roll(x, lons - 1, 0)),
                jnp.where(at_south, low, pltpu.roll(x, 1, 1)),
                jnp.where(at_north, high, pltpu.roll(x, lats - 1, 1)),
            )

        sets = []
        for level in range(levels):
            sets.append(
                [
                    (x[m, level], around(x[m, level], rims(noises + n * levels + level)))
                    for n, x in enumerate((u, v, h))
                ]
            )
        for level in range(levels):
            (cu, au), (cv, av), (ch, ah) = sets[level]
            upper, lower_h = sets[0][2][1], sets[1][2][1]
            pressure = [upper[i] + lower_h[i] for i in range(4)]
            if level == 1:
                pressure = [pressure[i] + REDUCED * lower_h[i] for i in range(4)]
            lap_u = au[1] + au[0] + au[3] + au[2] - 4.0 * cu
            lap_v = av[1] + av[0] + av[3] + av[2] - 4.0 * cv
            dx = 0.5 * (pressure[1] - pressure[0])
            dy = 0.5 * (pressure[3] - pressure[2])
            gain_u = turn * cv - dx + push(level) + VISCOSITY * lap_u
            gain_v = -turn * cu - dy + push(levels + level) + VISCOSITY * lap_v
            results[0, m, level] = ocean * (cu + TIME_STEP * gain_u)
            results[1, m, level] = ocean * (cv + TIME_STEP * gain_v)
            flow = 0.5 * (ah[1] * au[1] - ah[0] * au[0]) + 0.5 * (ah[3] * av[3] - ah[2] * av[2])
            results[2, m, level] = ch - TIME_STEP * flow
        for n, out in enumerate((new_u, new_v, new_h)):
            pltpu.make_async_copy(results.at[n, m], out.at[m], done.at[n, m]).start()
    for m in range(members):
        for n, out in enumerate((new_u, new_v, new_h)):
            pltpu.make_async_copy(results.at[n, m], out.at[m], done.at[n, m]).wait()


def body(
    noise,
    velocity_u,
    velocity_v,
    thickness,
    land_sea,
    conv_first,
    bias_first,
    conv_second,
    bias_second,
    conv_third,
    bias_third,
    conv_last,
    bias_last,
):
    members, noises, lons, lats = noise.shape
    levels = velocity_u.shape[1]
    fields = noises + 3 * levels
    sizes = (members, noises, levels)
    hidden = conv_first.shape[0]
    outs = conv_last.shape[0]
    groups = lons // GROUP + 1
    rows = members * (lats + GAP)
    assert hidden * 4 == LANES and outs * lons == LANES and members * (RIM + 1) * groups <= LANES
    assert fields % 2 == 0 and 4 * -(-fields // 4) == 12 and GROUP * (fields + 6) == LANES and lons % 16 == 0
    assert lats % LANES == 0 and SUB % members == 0 and (lats + GAP) % (SUB // members) == 0
    lon_count, lat_count = lax.axis_size("lon"), lax.axis_size("lat")
    assert lon_count % 2 == 0 and lat_count % 2 == 0
    state = (noise, velocity_u, velocity_v, thickness, land_sea)
    whole = pl.BlockSpec(memory_space=pltpu.VMEM)

    tall = members * fields * RIM + GROUP + members * 3 * levels
    assert tall % SUB == 0
    head, tail = pl.pallas_call(
        functools.partial(pack_lon_kernel, sizes),
        out_shape=[pltpu.VMEM((tall, lats), bf16)] * 2,
        in_specs=[pl.BlockSpec(memory_space=pltpu.HBM)] * 5,
        out_specs=[whole] * 2,
        scratch_shapes=[
            pltpu.VMEM(noise.shape, noise.dtype),
            pltpu.VMEM((2, 3, members, levels, GROUP, lats), f32),
            pltpu.VMEM((2, GROUP, lats), land_sea.dtype),
            pltpu.VMEM((2, tall, lats), f32),
            pltpu.SemaphoreType.DMA((9,)),
        ],
        name="pack_lon",
    )(*state)
    ring = [(i, (i + 1) % lon_count) for i in range(lon_count)]
    left = lax.ppermute(tail, "lon", ring)
    right = lax.ppermute(head, "lon", [(b, a) for a, b in ring])

    wide = -(-(fields + 1) * GROUP // SUB) * SUB
    part = pltpu.VMEM((wide, LANES), f32)
    message = pltpu.VMEM((wide, LANES), bf16)
    deep = -(-(lons // 2 + 2) * hidden // LANES) * LANES
    noise, velocity_u, velocity_v, thickness, land_sea, t1, t2, t3, t4, own_head, own_tail = pl.pallas_call(
        functools.partial(prepare_kernel, sizes),
        out_shape=[pltpu.VMEM(x.shape, x.dtype) for x in state]
        + [
            pltpu.VMEM((3 * LANES, 2 * LANES), bf16),
            pltpu.VMEM((8 * LANES, 2 * LANES), bf16),
            pltpu.VMEM((8 * LANES, 2 * LANES), bf16),
            pltpu.VMEM((2, deep, 2 * LANES), bf16),
        ]
        + [part, part],
        in_specs=[pl.BlockSpec(memory_space=pltpu.HBM)] * 5 + [whole] * 7,
        out_specs=[whole] * 11,
        scratch_shapes=[pltpu.SemaphoreType.DMA((5,))],
        compiler_params=pltpu.CompilerParams(vmem_limit_bytes=8 * 2**20),
        cost_estimate=pl.CostEstimate(flops=10**7, bytes_accessed=10**7, transcendentals=0),
        name="prepare",
    )(
        *state,
        conv_first.transpose(3, 2, 1, 0),
        conv_second.transpose(2, 3, 0, 1),
        conv_third.transpose(2, 3, 0, 1),
        conv_last.transpose(2, 3, 0, 1),
        bias_first[None],
        bias_second[None],
        bias_third[None],
    )
    state = (noise, velocity_u, velocity_v, thickness, land_sea)
    last = lat_count - 1
    smem = pl.BlockSpec(memory_space=pltpu.SMEM)
    to_even, to_odd = pl.pallas_call(
        functools.partial(join_kernel, sizes, lons),
        out_shape=[message] * 2,
        in_specs=[whole] * 4,
        out_specs=[whole] * 2,
        scratch_shapes=[
            pltpu.VMEM((2, 2, tall, LANES), f32),
            pltpu.VMEM((2, wide, LANES), f32),
        ],
        compiler_params=pltpu.CompilerParams(vmem_limit_bytes=4 * 2**20),
        name="join_rims",
    )(left, right, own_head, own_tail)
    even_rim = lax.ppermute(to_even, "lat", [(i, i ^ 1) for i in range(lat_count)])
    pairs = []
    for t in range(lon_count):
        at = t * lat_count
        pairs += [(at + k, at + k - 1 + 2 * (k % 2)) for k in range(1, last)]
        pairs += [(at, (t ^ 1) * lat_count), (at + last, (lon_count - 1 - t) * lat_count + last)]
    odd_rim = lax.ppermute(to_odd, ("lon", "lat"), pairs)

    own = pl.pallas_call(
        functools.partial(cells_kernel, sizes),
        out_shape=pltpu.VMEM((groups, rows, LANES), bf16),
        in_specs=[whole] * 8,
        out_specs=whole,
        scratch_shapes=[
            pltpu.VMEM((2, tall, lats), f32),
            pltpu.VMEM((groups, rows, LANES), f32),
            pltpu.VMEM((members * groups * lats // LANES, LANES, LANES), f32),
        ],
        compiler_params=pltpu.CompilerParams(vmem_limit_bytes=12 * 2**20),
        cost_estimate=pl.CostEstimate(flops=10**7, bytes_accessed=10**7, transcendentals=0),
        name="cells",
    )(*state, left, right, to_even)

    padded = rows + 2 * SUB
    tiles = 2 * groups + 1
    out = jax.ShapeDtypeStruct(velocity_u.shape, f32)
    return pl.pallas_call(
        functools.partial(main_kernel, sizes),
        out_shape=[out] * 3,
        in_specs=[smem] + [whole] * 14,
        out_specs=[pl.BlockSpec(memory_space=pltpu.HBM)] * 3,
        scratch_shapes=[
            pltpu.VMEM((tall, lats), f32),
            pltpu.VMEM((tall, lats), f32),
            pltpu.VMEM((groups, padded, LANES), bf16),
            pltpu.VMEM((tiles, padded, LANES), bf16),
            pltpu.VMEM((tiles, padded, LANES), bf16),
            pltpu.VMEM((3, padded, LANES), f32),
            pltpu.VMEM((members, lats, LANES), f32),
            pltpu.VMEM((4, LANES, LANES), f32),
            pltpu.VMEM((groups, GAP * SUB, LANES), f32),
            pltpu.VMEM((3, *velocity_u.shape), f32),
            pltpu.SemaphoreType.DMA((3, members)),
        ],
        compiler_params=pltpu.CompilerParams(vmem_limit_bytes=32 * 2**20),
        cost_estimate=pl.CostEstimate(flops=2 * 10**10, bytes_accessed=10**7, transcendentals=4 * 10**6),
        name="network_and_step",
    )(
        bias_last,
        own,
        *state[1:],
        left,
        right,
        even_rim,
        odd_rim,
        to_odd,
        t1,
        t2,
        t3,
        t4,
    )


def solution(mesh):
    tiles = P(None, None, "lon", "lat")
    return jax.shard_map(
        body,
        mesh=mesh,
        in_specs=(tiles,) * 4 + (P("lon", "lat"),) + (P(),) * 8,
        out_specs=(tiles,) * 3,
        check_vma=False,
    )
```

```python
import functools

import jax
import jax.numpy as jnp
from jax import lax
from jax.experimental import pallas as pl
from jax.experimental.pallas import tpu as pltpu
from jax.sharding import PartitionSpec as P

REDUCED = 0.5
TIME_STEP = 0.2
VISCOSITY = 0.05
CORIOLIS = 0.4

RIM = 4
GAP = 16
NORTH, STRIP, GHOST, SOUTH = 0, 4, 8, 12
SUB = 16
LANES = 128
GROUP = 8
LAND = 2.0**100

f32 = jnp.float32
bf16 = jnp.bfloat16


def iota(shape, dim):
    return lax.broadcasted_iota(jnp.int32, shape, dim)


def dot(a, b):
    return jnp.dot(a, b, preferred_element_type=f32)


def rest(x):
    return x - x.astype(bf16).astype(f32)


def pack_lon_kernel(sizes, count, *refs):
    sources, held, (head, tail, wide, done) = refs[:count], refs[count : 2 * count], refs[2 * count :]
    members, noises, levels = sizes
    fields = noises + 3 * levels
    noise, u, v, h, sea = held[:5]
    lons, lats = sea.shape
    copies = [pltpu.make_async_copy(x, y, done.at[n]) for n, (x, y) in enumerate(zip(sources, held))]
    for copy in copies:
        copy.start()
    for copy in copies[:5]:
        copy.wait()
    upper = iota((GROUP, lats), 0) < RIM

    def field(m, c, side):
        if c < noises:
            full = noise[m, c].astype(f32)
            return full[-GROUP:] if side else full[:GROUP]
        c -= noises
        return (u, v, h)[c // levels][m, c % levels, pl.ds(side * (lons - GROUP), GROUP)]

    rests = members * fields * RIM + GROUP
    for m in range(members):
        for c in range(0, fields, 2):
            rows = pl.ds((m * fields + c) * RIM, GROUP)
            wide[0, rows] = jnp.where(upper, field(m, c, 0), pltpu.roll(field(m, c + 1, 0), RIM, 0))
            wide[1, rows] = jnp.where(upper, pltpu.roll(field(m, c, 1), RIM, 0), field(m, c + 1, 1))
        for c in range(noises, fields):
            row = pl.ds(rests + m * (fields - noises) + c - noises, 1)
            wide[0, row] = rest(field(m, c, 0)[:1])
            wide[1, row] = rest(field(m, c, 1)[GROUP - 1 :])
    rows = pl.ds(members * fields * RIM, GROUP)
    ends = [sea[pl.ds(side * (lons - GROUP), GROUP)].astype(f32) for side in range(2)]
    wide[0, rows] = jnp.where(upper, ends[0], 0.0)
    wide[1, rows] = jnp.where(upper, pltpu.roll(ends[1], RIM, 0), 0.0)
    head[...] = wide[0].astype(bf16)
    tail[...] = wide[1].astype(bf16)
    for copy in copies[5:]:
        copy.wait()


def rim_tile(sizes, m, c, side, rim):
    members, noises, levels = sizes
    fields = noises + 3 * levels
    row = (m * fields + c) * RIM if c < fields else members * fields * RIM
    tile = rim[pl.ds(row // GROUP * GROUP, GROUP)]
    if (row // RIM) % 2 == side:
        return tile
    return pltpu.roll(tile, RIM, 0)


def window(tiles, following, mask, next_mask):
    pair = iota(mask.shape, 0) // 2
    zero = jnp.zeros_like(mask)
    more = []
    for start in range(0, len(tiles), 4):
        total = zero
        for n in range(min(4, len(tiles) - start)):
            moved = pltpu.roll(following[start + n], 2 * n, 0) if n else following[start]
            total = jnp.where(pair == n, moved, total)
        more.append(total)
    return jnp.concatenate(
        tiles + more + [mask - 1.0, next_mask - 1.0, jnp.ones_like(mask)], axis=0
    )


def store_lats(block, t, dst, tile, m, lats, chunks, buffer):
    blocks = (lats + GAP) // chunks
    buffer[...] = jnp.transpose(block)
    for q in range(chunks):
        lo = max(q * blocks, t * LANES)
        hi = min((q + 1) * blocks, (t + 1) * LANES, lats)
        if lo < hi:
            start = (lo - q * blocks) * SUB + m * chunks + q
            dst[tile, pl.ds(start, hi - lo, stride=SUB), :] = buffer[pl.ds(lo - t * LANES, hi - lo), :]


def shifted_tiles(sizes, refs, m, c, t):
    noise, u, v, h, sea = refs
    members, noises, levels = sizes
    fields = noises + 3 * levels
    lons = sea.shape[0]
    lanes = slice(t * LANES, (t + 1) * LANES)
    if c == fields:
        full = sea[:, lanes].astype(f32)
    elif c < noises:
        full = noise[m, c, :, lanes].astype(f32)
    else:
        full = (u, v, h)[(c - noises) // levels][m, (c - noises) % levels, :, lanes]
    full = pltpu.roll(full, lons - RIM, 0)
    tiles = [full[g * GROUP : (g + 1) * GROUP] for g in range(lons // GROUP)]
    return tiles[-1:] + tiles


def prepare_kernel(sizes, noise, u, v, h, sea, *refs):
    weights, matrices, (head, tail) = refs[:7], refs[7:11], refs[11:]
    held = (noise, u, v, h, sea)
    members, noises, levels = sizes
    fields = noises + 3 * levels
    lons, lats = sea.shape
    groups = lons // GROUP + 1
    weights_kernel(*weights, *matrices)
    lane = iota((GROUP, LANES), 1)
    for out, t, first in ((head, 0, 0), (tail, lats // LANES - 1, LANES - RIM)):
        for c in range(fields + 1):
            total = jnp.zeros((GROUP, LANES), f32)
            for m in range(members):
                for g, tile in enumerate(shifted_tiles(sizes, held, m, c, t)):
                    place = (g * members + m) * RIM
                    moved = pltpu.roll(tile, (place - first) % LANES, 1)
                    total = jnp.where((lane >= place) & (lane < place + RIM), moved, total)
                    if noises <= c < fields:
                        place = groups * members * RIM + g * members + m
                        edge = 0 if out is head else LANES - 1
                        moved = pltpu.roll(rest(tile), (place - edge) % LANES, 1)
                        total = jnp.where(lane == place, moved, total)
            out[pl.ds(c * GROUP, GROUP)] = total
        for c in range(fields + 1, out.shape[0] // GROUP):
            out[pl.ds(c * GROUP, GROUP)] = jnp.zeros((GROUP, LANES), f32)


def cells_kernel(sizes, noise, u, v, h, sea, left, right, after, out, base, rims, cells, turned):
    members, noises, levels = sizes
    fields = noises + 3 * levels
    lons, lats = sea.shape
    groups = lons // GROUP + 1
    chunks = SUB // members
    rows = cells.shape[1]
    gap_k = lats - (chunks - 1) * ((lats + GAP) // chunks)
    rims[0] = left[...].astype(f32)
    rims[1] = right[...].astype(f32)
    for m in range(members):
        for g in range(groups):
            empty = pl.ds(gap_k * SUB + (m + 1) * chunks - 1, GAP, stride=SUB)
            cells[g, empty, :] = jnp.zeros((GAP, LANES), f32)
    blank = jnp.zeros((GROUP, LANES), f32)
    upper = iota((GROUP, LANES), 0) < RIM
    for t in range(lats // LANES):
        lanes = slice(t * LANES, (t + 1) * LANES)
        for m in range(members):
            tiles = []
            for c in range(fields + 1):
                groups_of = shifted_tiles(sizes, (noise, u, v, h, sea), m, c, t)
                ends = [rim_tile(sizes, m, c, side, rims.at[side, :, lanes]) for side in range(2)]
                groups_of[0] = jnp.where(upper, ends[0], groups_of[0])
                groups_of[-1] = jnp.where(upper, groups_of[-1], ends[1])
                tiles.append(groups_of)
            for g in range(groups):
                following = [x[g + 1] if g + 1 < groups else blank for x in tiles]
                block = window([x[g] for x in tiles[:fields]], following[:fields], tiles[fields][g], following[fields])
                store_lats(block, t, cells, g, m, lats, chunks, turned.at[(t * members + m) * groups + g])
    for g in range(groups):
        out[g] = cells[g].astype(bf16)
    step_kernel(sizes, u, v, h, sea, rims, base)


def step_kernel(sizes, u, v, h, sea, rims, base):
    members, noises, levels = sizes
    fields = noises + 3 * levels
    lons, lats = sea.shape
    ocean = sea[...].astype(f32)
    lat_count = lax.axis_size("lat")
    lat_rows = (lax.axis_index("lat") * lats).astype(f32) + iota((lons, lats), 1).astype(f32)
    turn = CORIOLIS * (2.0 * (lat_rows + 0.5) / (lats * lat_count) - 1.0)
    at_first = iota((lons, lats), 0) == 0
    at_last = iota((lons, lats), 0) == lons - 1
    at_south = iota((lons, lats), 1) == 0
    at_north = iota((lons, lats), 1) == lats - 1
    lon_rests = members * fields * RIM + GROUP

    def around(x, m, c):
        row = (m * fields + c) * RIM
        more = lon_rests + m * (fields - noises) + c - noises
        west = rims[0, pl.ds(row + RIM - 1, 1)] + rims[0, pl.ds(more, 1)]
        east = rims[1, pl.ds(row, 1)] + rims[1, pl.ds(more, 1)]
        return (
            jnp.where(at_first, west, pltpu.roll(x, 1, 0)),
            jnp.where(at_last, east, pltpu.roll(x, lons - 1, 0)),
            jnp.where(at_south, 0.0, pltpu.roll(x, 1, 1)),
            jnp.where(at_north, 0.0, pltpu.roll(x, lats - 1, 1)),
        )

    for m in range(members):
        sets = []
        for level in range(levels):
            sets.append(
                [
                    (x[m, level], around(x[m, level], m, noises + n * levels + level))
                    for n, x in enumerate((u, v, h))
                ]
            )
        for level in range(levels):
            (cu, au), (cv, av), (ch, ah) = sets[level]
            upper, lower = sets[0][2][1], sets[1][2][1]
            pressure = [upper[i] + lower[i] for i in range(4)]
            if level == 1:
                pressure = [pressure[i] + REDUCED * lower[i] for i in range(4)]
            lap_u = au[1] + au[0] + au[3] + au[2] - 4.0 * cu
            lap_v = av[1] + av[0] + av[3] + av[2] - 4.0 * cv
            dx = 0.5 * (pressure[1] - pressure[0])
            dy = 0.5 * (pressure[3] - pressure[2])
            base[0, m, level] = ocean * (cu + TIME_STEP * (turn * cv - dx + VISCOSITY * lap_u))
            base[1, m, level] = ocean * (cv + TIME_STEP * (-turn * cu - dy + VISCOSITY * lap_v))
            flow = 0.5 * (ah[1] * au[1] - ah[0] * au[0]) + 0.5 * (ah[3] * av[3] - ah[2] * av[2])
            base[2, m, level] = ch - TIME_STEP * flow


def join_kernel(sizes, lons, left, right, head, tail, even, odd, rims, wide):
    members, noises, levels = sizes
    fields = noises + 3 * levels
    groups = lons // GROUP + 1
    lats = left.shape[1]
    for side, rim in enumerate((left, right)):
        rims[side, 0] = rim[:, :LANES].astype(f32)
        rims[side, 1] = rim[:, lats - LANES :].astype(f32)
    lane = iota((GROUP, LANES), 1)
    upper = iota((GROUP, LANES), 0) < RIM
    to_south = lax.axis_index("lat") % 2 == 1
    for c in range(fields + 1):
        rows = pl.ds(c * GROUP, GROUP)
        ends = []
        for n, (part, first) in enumerate(((head, 0), (tail, LANES - RIM))):
            total = part[rows]
            for side in range(2):
                held = upper if side == 0 else ~upper
                for m in range(members):
                    place = ((groups - 1) * side * members + m) * RIM
                    tile = rim_tile(sizes, m, c, side, rims.at[side, n])
                    moved = pltpu.roll(tile, (place - first) % LANES, 1)
                    total = jnp.where(held & (lane >= place) & (lane < place + RIM), moved, total)
            ends.append(total)
        wide[0, rows] = jnp.where(to_south, ends[0], ends[1])
        wide[1, rows] = jnp.where(to_south, ends[1], ends[0])
    rows = pl.ds((fields + 1) * GROUP, wide.shape[1] - (fields + 1) * GROUP)
    wide[:, rows] = jnp.zeros((2, wide.shape[1] - (fields + 1) * GROUP, LANES), f32)
    even[...] = wide[0].astype(bf16)
    odd[...] = wide[1].astype(bf16)


def weights_kernel(w1, w2, w3, w4, bias1, bias2, bias3, t1, t2, t3, t4):
    hidden = w2.shape[2]
    per = LANES // hidden
    lane = iota((hidden, LANES), 1)
    fields = w1.shape[0]
    out_lon = iota((GROUP, LANES), 1) // hidden
    in_row = iota((GROUP, LANES), 0)
    bias_row = iota((GROUP, LANES), 0)

    def bias_rows(layer):
        part = 0.5 * jnp.concatenate([(bias1, bias2, bias3)[layer][...]] * per, axis=1)
        b1 = part.astype(bf16).astype(f32)
        b2 = (part - b1).astype(bf16).astype(f32)
        b3 = part - b1 - b2
        zero = jnp.zeros((GROUP, LANES), f32)
        return jnp.where(
            bias_row == 0,
            b1,
            jnp.where(bias_row == 1, b2, jnp.where(bias_row == 2, b3, zero)),
        )

    def sea_rows(shift, tile):
        lon = iota((2 * GROUP, LANES), 0)
        out = iota((2 * GROUP, LANES), 1) // hidden + per * tile
        return jnp.where(lon == out + shift, LAND, 0.0)

    for dj in range(3):
        taps = []
        for di in range(3):
            cells = [w1[c, di].astype(f32)[dj : dj + 1] for c in range(fields)]
            taps.append(
                [jnp.broadcast_to(0.5 * jnp.concatenate([x] * per, axis=1), (GROUP, LANES)) for x in cells]
            )
        for tile in range(2):
            parts = []
            for c in range(fields):
                total = jnp.zeros((GROUP, LANES), f32)
                for di in range(3):
                    hit = in_row == out_lon + per * tile + di
                    total = jnp.where(hit, taps[di][c], total)
                parts.append(total)
            for start in range(0, fields, 4):
                total = jnp.zeros((GROUP, LANES), f32)
                for n in range(min(4, fields - start)):
                    for di in range(3):
                        hit = in_row % 2 + GROUP == out_lon + per * tile + di
                        total = jnp.where(hit & (in_row // 2 == n), taps[di][start + n], total)
                parts.append(total)
            if dj == 1:
                parts += [sea_rows(1, tile), bias_rows(0)]
            else:
                parts.append(jnp.zeros((3 * GROUP, LANES), f32))
            block = jnp.concatenate(parts, axis=0)
            t1[pl.ds(dj * LANES, LANES), pl.ds(tile * LANES, LANES)] = block.astype(bf16)

    for layer, (w, t) in enumerate(((w2, t2), (w3, t3))):
        for dj in range(3):
            taps = []
            for di in range(3):
                cell = 0.5 * w[di, dj].astype(f32)
                wide = jnp.concatenate([cell, jnp.zeros((hidden, LANES - hidden), f32)], axis=1)
                square = jnp.concatenate([wide] * per, axis=0)
                taps.append(jnp.transpose(square)[:hidden])
            for lon in range(GROUP + 2):
                for tile in range(2):
                    total = jnp.zeros((hidden, LANES), f32)
                    for di in range(3):
                        total = jnp.where(lane // hidden + per * tile == lon - di, taps[di], total)
                    if lon < GROUP:
                        row = dj * GROUP * hidden + lon * hidden
                    else:
                        row = 3 * GROUP * hidden + dj * 2 * hidden + (lon - GROUP) * hidden
                    t[pl.ds(row, hidden), pl.ds(tile * LANES, LANES)] = total.astype(bf16)
        for tile in range(2):
            block = jnp.concatenate(
                [
                    jnp.zeros((5 * GROUP, LANES), f32),
                    sea_rows(2 + layer, tile),
                    bias_rows(1 + layer),
                ],
                axis=0,
            )
            row = 3 * GROUP * hidden + 6 * hidden
            t[pl.ds(row, 2 * hidden), pl.ds(tile * LANES, LANES)] = block.astype(bf16)

    outs = w4.shape[2]
    half = LANES // 2
    lons = half // outs
    slot = iota((hidden, LANES), 1) // half
    out_lon = iota((hidden, LANES), 1) % lons
    taps = {}
    for dj in range(3):
        for di in range(3):
            cell = w4[di, dj].astype(f32)
            wide = jnp.concatenate([cell, jnp.zeros((outs, LANES - hidden), f32)], axis=1)
            square = jnp.concatenate(
                [jnp.broadcast_to(wide[c : c + 1], (lons, LANES)) for c in range(outs)] * 2, axis=0
            )
            taps[dj, di] = jnp.transpose(square)[:hidden]
    order = ((0, 1, 2, None), (1, 0, None, 2))
    for side in range(2):
        for lon in range(t4.shape[1] // hidden):
            for tile in range(2):
                total = jnp.zeros((hidden, LANES), f32)
                for place in range(2):
                    dj = order[side][2 * tile + place]
                    if dj is None:
                        continue
                    for di in range(3):
                        total = jnp.where((slot == place) & (out_lon == lon - di), taps[dj, di], total)
                t4[side, pl.ds(lon * hidden, hidden), pl.ds(tile * LANES, LANES)] = total.astype(bf16)


def main_kernel(
    sizes,
    bias_last,
    own,
    base,
    sea,
    even_rim,
    odd_rim,
    own_tail,
    t1,
    t2,
    t3,
    t4,
    new_u,
    new_v,
    new_h,
    first,
    odd,
    even,
    force,
    gathered,
    turned,
    gaps,
    results,
    done,
):
    members, noises, levels = sizes
    fields = noises + 3 * levels
    lons, lats = sea.shape
    groups = lons // GROUP + 1
    chunks = SUB // members
    blocks = (lats + GAP) // chunks
    rows = blocks * SUB
    gap_k = lats - (chunks - 1) * blocks
    lat_index, lat_count = lax.axis_index("lat"), lax.axis_size("lat")
    top = lat_index == lat_count - 1
    is_odd = lat_index % 2 == 1
    bottom = lat_index == 0
    strip = odd_rim[...].astype(f32)
    paired = even_rim[...].astype(f32)
    south = jnp.where(is_odd, paired, jnp.where(bottom, 0.0, strip))

    wide = strip.shape[0]
    span = members * RIM
    lane = iota((wide, LANES), 1)
    rests = groups * span
    border = ((lane % RIM == 0) & (lane < rests)) | (lane >= rests)
    row_to = iota((wide, wide), 0)
    row_from = iota((wide, wide), 1)
    channel = row_to // GROUP
    mirrored = (channel == row_from // GROUP) & (row_from % GROUP == GROUP - 1 - row_to % GROUP)
    odd_parity = (channel >= noises) & (channel < noises + 2 * levels)
    flip_rows = jnp.where(mirrored, jnp.where(odd_parity, -1.0, 1.0), 0.0).astype(bf16)
    lane_from = iota((LANES, LANES), 0)
    lane_to = iota((LANES, LANES), 1)
    source = (groups - 1 - lane_to // span) * span + lane_to % span + RIM - 1
    moves = (lane_to % RIM == 0) & (lane_to < rests) & (lane_from == source)
    other = lane_to - rests
    source = rests + (groups - 1 - other // members) * members + other % members
    moves = moves | ((other >= 0) & (other < groups * members) & (lane_from == source))
    flip_lanes = jnp.where(moves, 1.0, 0.0).astype(bf16)
    pair = dot(flip_rows, jnp.concatenate([odd_rim[...], own_tail[...]], axis=1)).astype(bf16)
    folded = dot(pair[:, :LANES], flip_lanes)
    ghost = dot(pair[:, LANES:], flip_lanes)
    north = jnp.where(is_odd, strip, paired)
    north_rim = jnp.where(border & top, folded, north)

    for n, message in enumerate((north_rim, strip, ghost, south)):
        after = pltpu.roll(message, LANES - span, 1)
        cut = [message[c * GROUP : (c + 1) * GROUP] for c in range(fields + 1)]
        after = [after[c * GROUP : (c + 1) * GROUP] for c in range(fields + 1)]
        turned[n] = jnp.transpose(window(cut[:fields], after[:fields], cut[fields], after[fields]))
        for g in range(groups):
            for m in range(members):
                gap = (m - 1) % members if n == 3 else m
                start = n * RIM * SUB + gap * chunks + chunks - 1
                gaps[g, pl.ds(start, RIM, stride=SUB), :] = turned[n, pl.ds((g * members + m) * RIM, RIM), :]

    in_gap = iota((GAP * SUB, LANES), 0) % chunks == chunks - 1
    for g in range(groups):
        first[g, pl.ds(SUB, rows), :] = own[g]
        spot = pl.ds((1 + gap_k) * SUB, GAP * SUB)
        kept = first[g, spot, :].astype(f32)
        first[g, spot, :] = jnp.where(in_gap, gaps[g], kept).astype(bf16)
        end = first[g, pl.ds(rows, SUB), :].astype(f32)
        first[g, pl.ds(0, SUB), :] = pltpu.roll(end, 1, 0).astype(bf16)
        begin = first[g, pl.ds(SUB, SUB), :].astype(f32)
        first[g, pl.ds(SUB + rows, SUB), :] = pltpu.roll(begin, SUB - 1, 0).astype(bf16)

    hidden = LANES // 4
    per = LANES // hidden
    tiles = odd.shape[0]
    cuts = 1
    step = rows // cuts
    lower = iota((step, LANES), 1) < 2 * hidden

    def activate(pre):
        return (pre * jnp.tanh(pre) + pre).astype(bf16)

    def finish(x, valid):
        used = (valid + per - 1) // per

        @pl.when(top)
        def _():
            strip_top = SUB * (1 + gap_k + STRIP + RIM - 1)
            own_top = SUB * gap_k
            strip_ghost = SUB * (1 + gap_k + GHOST)
            own_ghost = SUB * (1 + gap_k + NORTH)
            last_chunk = iota((SUB, LANES), 0) % chunks == chunks - 1
            spot = iota((SUB, LANES), 1) // hidden
            for src, dst in ((strip_top, own_ghost), (own_top, strip_ghost)):
                found = [x[t, pl.ds(src, SUB), :].astype(f32) for t in range(used)]
                for t in range(used):
                    total = x[t, pl.ds(dst, SUB), :].astype(f32)
                    for i in range(per):
                        lon = valid - 1 - (per * t + i)
                        if lon < 0:
                            continue
                        moved = pltpu.roll(found[lon // per], (hidden * (i - lon % per)) % LANES, 1)
                        total = jnp.where(last_chunk & (spot == i), moved, total)
                    x[t, pl.ds(dst, SUB), :] = total.astype(bf16)

        for t in range(used):
            end = x[t, pl.ds(rows, SUB), :].astype(f32)
            x[t, pl.ds(0, SUB), :] = pltpu.roll(end, 1, 0).astype(bf16)
            begin = x[t, pl.ds(SUB, SUB), :].astype(f32)
            x[t, pl.ds(SUB + rows, SUB), :] = pltpu.roll(begin, SUB - 1, 0).astype(bf16)

    for x in (odd, even):
        x[tiles - 1] = jnp.zeros(x.shape[1:], bf16)
    even[tiles - 2] = jnp.zeros(even.shape[1:], bf16)

    def put(y, b, r, out):
        for e in range(out.shape[1] // LANES):
            y[2 * b + e, pl.ds(SUB + r, step), :] = out[:, e * LANES : (e + 1) * LANES]

    for b in range(groups):
        for n in range(cuts):
            r = n * step
            parts = [first[b, pl.ds(r + SUB * d, step), :] for d in range(3)]
            put(odd, b, r, activate(dot(jnp.concatenate(parts, axis=1), t1[...])))
    finish(odd, lons + 6)

    width = GROUP * hidden

    def layer(x, y, t, left_over):
        for b in range(groups):
            for n in range(cuts):
                r = n * step

                def cells_of(tile, d):
                    return x[tile, pl.ds(r + SUB * d, step), :]

                def packed(tile):
                    more = [cells_of(tile, d) for d in range(3)]
                    return [
                        jnp.where(lower, more[0], pltpu.roll(more[1], 2 * hidden, 1)),
                        jnp.where(lower, more[2], first[b, pl.ds(r + SUB, step), :]),
                    ]

                if b < groups - 1:
                    parts = [cells_of(2 * b + e, d) for d in range(3) for e in range(2)] + packed(2 * b + 2)
                    matrix = t[...]
                elif left_over == per:
                    parts = [cells_of(2 * b, d) for d in range(3)] + packed(2 * b + 1)
                    lanes = pl.ds(0, LANES)
                    matrix = jnp.concatenate(
                        [t[pl.ds(d * width, LANES), lanes] for d in range(3)]
                        + [t[pl.ds(d * width + LANES, 2 * hidden), lanes] for d in range(3)]
                        + [t[pl.ds(3 * width + 6 * hidden, 2 * hidden), lanes]],
                        axis=0,
                    )
                else:
                    parts = [cells_of(2 * b, d) for d in range(3)] + [first[b, pl.ds(r + SUB, step), :]]
                    lanes = pl.ds(0, LANES)
                    matrix = jnp.concatenate(
                        [t[pl.ds(d * width, LANES), lanes] for d in range(3)]
                        + [jnp.zeros((2 * hidden, LANES), bf16)]
                        + [t[pl.ds(3 * width + 6 * hidden, 2 * hidden), lanes]],
                        axis=0,
                    )
                put(y, b, r, activate(dot(jnp.concatenate(parts, axis=1), matrix)))

    layer(odd, even, t2, per)
    finish(even, lons + 4)
    layer(even, odd, t3, per // 2)
    finish(odd, lons + 2)

    depth = t4.shape[1] // LANES
    long = (rows + 2 * SUB) // 2
    before = iota((long, LANES), 1) < LANES // 2
    for n in range(2):
        span_rows = pl.ds(n * long, long)
        sides = []
        for side in range(2):
            parts = [odd[side * (depth - 1) + t, span_rows, :] for t in range(depth)]
            sides.append(dot(jnp.concatenate(parts, axis=1), t4[side]))
        force[0, span_rows, :] = jnp.where(before, sides[0][:, :LANES], sides[1][:, :LANES])
        swapped = jnp.where(before, sides[1][:, :LANES], sides[0][:, :LANES])
        force[1, span_rows, :] = pltpu.roll(swapped, LANES // 2, 1)
        force[2, span_rows, :] = jnp.where(before, sides[0][:, LANES:], sides[1][:, LANES:])

    ocean = sea[...].astype(f32)
    narrow = iota((lons, LANES), 1)
    at_south = narrow == 0
    at_north = narrow == LANES - 1
    halves = lons // 2

    def beyond(message, m, c, offset):
        cells = []
        some = slice(c * GROUP, (c + 1) * GROUP)
        for g in range(groups):
            spot = (g * members + m) * RIM + offset
            more = rests + g * members + m
            cells.append(message[some, spot : spot + 1] + message[some, more : more + 1])
        whole = jnp.broadcast_to(jnp.concatenate(cells, axis=0), (lons + GROUP, LANES))
        return pltpu.roll(whole, lons + GROUP - RIM, 0)[:lons]

    for m in range(members):
        for q in range(chunks):
            size = min(blocks, lats - q * blocks)
            total = force[0, pl.ds(m * chunks + q, size, stride=SUB), :]
            for d in range(1, 3):
                total = total + force[d, pl.ds(d * SUB + m * chunks + q, size, stride=SUB), :]
            gathered[m, pl.ds(q * blocks, size), :] = total
        turned_force = jnp.transpose(gathered[m])
        rims = [
            [beyond(message, m, c, offset) for c in range(noises, fields)]
            for message, offset in ((south, RIM - 1), (north_rim, 0))
        ]
        for level in range(levels):
            gains = []
            for (sign, spot), rim in zip(((1.0, at_south), (-1.0, at_north)), rims):
                ru, rv, rh = rim[level], rim[levels + level], rim[2 * levels + level]
                pressure = rim[2 * levels] + rim[2 * levels + 1]
                if level == 1:
                    pressure = pressure + REDUCED * rh
                gains.append(
                    [
                        jnp.where(spot, TIME_STEP * VISCOSITY * ru, 0.0),
                        jnp.where(spot, TIME_STEP * (VISCOSITY * rv + sign * 0.5 * pressure), 0.0),
                        jnp.where(spot, TIME_STEP * sign * 0.5 * (rh * rv), 0.0),
                    ]
                )
            middle = [jnp.zeros((lons, lats - 2 * LANES), f32)] if lats > 2 * LANES else []
            gains = [jnp.concatenate([gains[0][n]] + middle + [gains[1][n]], axis=1) for n in range(3)]

            def push(c):
                parts = [
                    turned_force[side * LANES // 2 + c * halves : side * LANES // 2 + (c + 1) * halves]
                    for side in range(2)
                ]
                return TIME_STEP * (jnp.concatenate(parts, axis=0) + bias_last[c])

            results[0, m, level] = base[0, m, level] + ocean * (gains[0] + push(level))
            results[1, m, level] = base[1, m, level] + ocean * (gains[1] + push(levels + level))
            results[2, m, level] = base[2, m, level] + gains[2]
        for n, out in enumerate((new_u, new_v, new_h)):
            pltpu.make_async_copy(results.at[n, m], out.at[m], done.at[n, m]).start()
    for m in range(members):
        for n, out in enumerate((new_u, new_v, new_h)):
            pltpu.make_async_copy(results.at[n, m], out.at[m], done.at[n, m]).wait()


def body(
    noise,
    velocity_u,
    velocity_v,
    thickness,
    land_sea,
    conv_first,
    bias_first,
    conv_second,
    bias_second,
    conv_third,
    bias_third,
    conv_last,
    bias_last,
):
    members, noises, lons, lats = noise.shape
    levels = velocity_u.shape[1]
    fields = noises + 3 * levels
    sizes = (members, noises, levels)
    hidden = conv_first.shape[0]
    outs = conv_last.shape[0]
    groups = lons // GROUP + 1
    rows = members * (lats + GAP)
    assert hidden * 4 == LANES and outs * lons == LANES and members * (RIM + 1) * groups <= LANES
    assert fields % 2 == 0 and 4 * -(-fields // 4) == 12 and GROUP * (fields + 6) == LANES and lons % 16 == 0
    assert lats % LANES == 0 and SUB % members == 0 and (lats + GAP) % (SUB // members) == 0
    lon_count, lat_count = lax.axis_size("lon"), lax.axis_size("lat")
    assert lon_count % 2 == 0 and lat_count % 2 == 0
    state = (noise, velocity_u, velocity_v, thickness, land_sea)
    whole = pl.BlockSpec(memory_space=pltpu.VMEM)

    tall = members * fields * RIM + GROUP + members * 3 * levels
    assert tall % SUB == 0
    args = state + (
        conv_first.transpose(1, 2, 3, 0),
        conv_second.transpose(2, 3, 0, 1),
        conv_third.transpose(2, 3, 0, 1),
        conv_last.transpose(2, 3, 0, 1),
        bias_first[None],
        bias_second[None],
        bias_third[None],
    )
    count = len(args)
    *held, head, tail = pl.pallas_call(
        functools.partial(pack_lon_kernel, sizes, count),
        out_shape=[pltpu.VMEM(x.shape, x.dtype) for x in args] + [pltpu.VMEM((tall, lats), bf16)] * 2,
        in_specs=[pl.BlockSpec(memory_space=pltpu.HBM)] * count,
        out_specs=[whole] * (count + 2),
        scratch_shapes=[pltpu.VMEM((2, tall, lats), f32), pltpu.SemaphoreType.DMA((count,))],
        compiler_params=pltpu.CompilerParams(vmem_limit_bytes=62 * 2**20),
        name="pack_lon",
    )(*args)
    state = tuple(held[:5])
    ring = [(i, (i + 1) % lon_count) for i in range(lon_count)]
    left = lax.ppermute(tail, "lon", ring)
    right = lax.ppermute(head, "lon", [(b, a) for a, b in ring])

    wide = -(-(fields + 1) * GROUP // SUB) * SUB
    part = pltpu.VMEM((wide, LANES), f32)
    message = pltpu.VMEM((wide, LANES), bf16)
    deep = -(-(lons // 2 + 2) * hidden // LANES) * LANES
    t1, t2, t3, t4, own_head, own_tail = pl.pallas_call(
        functools.partial(prepare_kernel, sizes),
        out_shape=[
            pltpu.VMEM((3 * LANES, 2 * LANES), bf16),
            pltpu.VMEM((8 * LANES, 2 * LANES), bf16),
            pltpu.VMEM((8 * LANES, 2 * LANES), bf16),
            pltpu.VMEM((2, deep, 2 * LANES), bf16),
            part,
            part,
        ],
        in_specs=[whole] * count,
        out_specs=[whole] * 6,
        compiler_params=pltpu.CompilerParams(vmem_limit_bytes=8 * 2**20),
        cost_estimate=pl.CostEstimate(flops=10**7, bytes_accessed=10**7, transcendentals=0),
        name="prepare",
    )(*held)
    last = lat_count - 1
    smem = pl.BlockSpec(memory_space=pltpu.SMEM)
    to_even, to_odd = pl.pallas_call(
        functools.partial(join_kernel, sizes, lons),
        out_shape=[message] * 2,
        in_specs=[whole] * 4,
        out_specs=[whole] * 2,
        scratch_shapes=[
            pltpu.VMEM((2, 2, tall, LANES), f32),
            pltpu.VMEM((2, wide, LANES), f32),
        ],
        compiler_params=pltpu.CompilerParams(vmem_limit_bytes=4 * 2**20),
        name="join_rims",
    )(left, right, own_head, own_tail)
    even_rim = lax.ppermute(to_even, "lat", [(i, i ^ 1) for i in range(lat_count)])
    pairs = []
    for t in range(lon_count):
        at = t * lat_count
        pairs += [(at + k, at + k - 1 + 2 * (k % 2)) for k in range(1, last)]
        pairs += [(at, (t ^ 1) * lat_count), (at + last, (lon_count - 1 - t) * lat_count + last)]
    odd_rim = lax.ppermute(to_odd, ("lon", "lat"), pairs)

    own, base = pl.pallas_call(
        functools.partial(cells_kernel, sizes),
        out_shape=[pltpu.VMEM((groups, rows, LANES), bf16), pltpu.VMEM((3, *velocity_u.shape), f32)],
        in_specs=[whole] * 8,
        out_specs=[whole] * 2,
        scratch_shapes=[
            pltpu.VMEM((2, tall, lats), f32),
            pltpu.VMEM((groups, rows, LANES), f32),
            pltpu.VMEM((members * groups * lats // LANES, LANES, LANES), f32),
        ],
        compiler_params=pltpu.CompilerParams(vmem_limit_bytes=12 * 2**20),
        cost_estimate=pl.CostEstimate(flops=10**7, bytes_accessed=10**7, transcendentals=0),
        name="cells",
    )(*state, left, right, to_even)

    padded = rows + 2 * SUB
    tiles = 2 * groups + 1
    out = jax.ShapeDtypeStruct(velocity_u.shape, f32)
    return pl.pallas_call(
        functools.partial(main_kernel, sizes),
        out_shape=[out] * 3,
        in_specs=[smem] + [whole] * 10,
        out_specs=[pl.BlockSpec(memory_space=pltpu.HBM)] * 3,
        scratch_shapes=[
            pltpu.VMEM((groups, padded, LANES), bf16),
            pltpu.VMEM((tiles, padded, LANES), bf16),
            pltpu.VMEM((tiles, padded, LANES), bf16),
            pltpu.VMEM((3, padded, LANES), f32),
            pltpu.VMEM((members, lats, LANES), f32),
            pltpu.VMEM((4, LANES, LANES), f32),
            pltpu.VMEM((groups, GAP * SUB, LANES), f32),
            pltpu.VMEM((3, *velocity_u.shape), f32),
            pltpu.SemaphoreType.DMA((3, members)),
        ],
        compiler_params=pltpu.CompilerParams(vmem_limit_bytes=32 * 2**20),
        cost_estimate=pl.CostEstimate(flops=2 * 10**10, bytes_accessed=10**7, transcendentals=4 * 10**6),
        name="network_and_step",
    )(
        bias_last,
        own,
        base,
        state[4],
        even_rim,
        odd_rim,
        to_odd,
        t1,
        t2,
        t3,
        t4,
    )


def solution(mesh):
    tiles = P(None, None, "lon", "lat")
    return jax.shard_map(
        body,
        mesh=mesh,
        in_specs=(tiles,) * 4 + (P("lon", "lat"),) + (P(),) * 8,
        out_specs=(tiles,) * 3,
        check_vma=False,
    )
```

```python
import functools

import jax
import jax.numpy as jnp
from jax import lax
from jax.experimental import pallas as pl
from jax.experimental.pallas import tpu as pltpu
from jax.sharding import PartitionSpec as P

REDUCED = 0.5
TIME_STEP = 0.2
VISCOSITY = 0.05
CORIOLIS = 0.4

RIM = 4
GAP = 16
NORTH, STRIP, GHOST, SOUTH = 0, 4, 8, 12
SUB = 16
LANES = 128
GROUP = 8
LAND = 2.0**100

f32 = jnp.float32
bf16 = jnp.bfloat16


def iota(shape, dim):
    return lax.broadcasted_iota(jnp.int32, shape, dim)


def dot(a, b):
    return jnp.dot(a, b, preferred_element_type=f32)


def rest(x):
    return x - x.astype(bf16).astype(f32)


def pack_lon_kernel(sizes, count, *refs):
    sources, held, (head, tail, wide, done) = refs[:count], refs[count : 2 * count], refs[2 * count :]
    members, noises, levels = sizes
    fields = noises + 3 * levels
    noise, u, v, h, sea = held[:5]
    lons, lats = sea.shape
    copies = [pltpu.make_async_copy(x, y, done.at[n]) for n, (x, y) in enumerate(zip(sources, held))]
    for copy in copies:
        copy.start()
    for copy in copies[:5]:
        copy.wait()
    upper = iota((GROUP, lats), 0) < RIM

    def field(m, c, side):
        if c < noises:
            full = noise[m, c].astype(f32)
            return full[-GROUP:] if side else full[:GROUP]
        c -= noises
        return (u, v, h)[c // levels][m, c % levels, pl.ds(side * (lons - GROUP), GROUP)]

    rests = members * fields * RIM + GROUP
    for m in range(members):
        for c in range(0, fields, 2):
            rows = pl.ds((m * fields + c) * RIM, GROUP)
            wide[0, rows] = jnp.where(upper, field(m, c, 0), pltpu.roll(field(m, c + 1, 0), RIM, 0))
            wide[1, rows] = jnp.where(upper, pltpu.roll(field(m, c, 1), RIM, 0), field(m, c + 1, 1))
        for c in range(noises, fields):
            row = pl.ds(rests + m * (fields - noises) + c - noises, 1)
            wide[0, row] = rest(field(m, c, 0)[:1])
            wide[1, row] = rest(field(m, c, 1)[GROUP - 1 :])
    rows = pl.ds(members * fields * RIM, GROUP)
    ends = [sea[pl.ds(side * (lons - GROUP), GROUP)].astype(f32) for side in range(2)]
    wide[0, rows] = jnp.where(upper, ends[0], 0.0)
    wide[1, rows] = jnp.where(upper, pltpu.roll(ends[1], RIM, 0), 0.0)
    head[...] = wide[0].astype(bf16)
    tail[...] = wide[1].astype(bf16)
    for copy in copies[5:]:
        copy.wait()


def rim_tile(sizes, m, c, side, rim):
    members, noises, levels = sizes
    fields = noises + 3 * levels
    row = (m * fields + c) * RIM if c < fields else members * fields * RIM
    tile = rim[pl.ds(row // GROUP * GROUP, GROUP)]
    if (row // RIM) % 2 == side:
        return tile
    return pltpu.roll(tile, RIM, 0)


def window(tiles, following, mask, next_mask):
    pair = iota(mask.shape, 0) // 2
    zero = jnp.zeros_like(mask)
    more = []
    for start in range(0, len(tiles), 4):
        total = zero
        for n in range(min(4, len(tiles) - start)):
            moved = pltpu.roll(following[start + n], 2 * n, 0) if n else following[start]
            total = jnp.where(pair == n, moved, total)
        more.append(total)
    return jnp.concatenate(
        tiles + more + [mask - 1.0, next_mask - 1.0, jnp.ones_like(mask)], axis=0
    )


def store_lats(block, t, dst, tile, m, lats, chunks, buffer):
    blocks = (lats + GAP) // chunks
    buffer[...] = jnp.transpose(block)
    for q in range(chunks):
        lo = max(q * blocks, t * LANES)
        hi = min((q + 1) * blocks, (t + 1) * LANES, lats)
        if lo < hi:
            start = (lo - q * blocks) * SUB + m * chunks + q
            dst[tile, pl.ds(start, hi - lo, stride=SUB), :] = buffer[pl.ds(lo - t * LANES, hi - lo), :]


def shifted_tiles(sizes, refs, m, c, t):
    noise, u, v, h, sea = refs
    members, noises, levels = sizes
    fields = noises + 3 * levels
    lons = sea.shape[0]
    lanes = slice(t * LANES, (t + 1) * LANES)
    if c == fields:
        full = sea[:, lanes].astype(f32)
    elif c < noises:
        full = noise[m, c, :, lanes].astype(f32)
    else:
        full = (u, v, h)[(c - noises) // levels][m, (c - noises) % levels, :, lanes]
    full = pltpu.roll(full, lons - RIM, 0)
    tiles = [full[g * GROUP : (g + 1) * GROUP] for g in range(lons // GROUP)]
    return tiles[-1:] + tiles


def prepare_kernel(sizes, noise, u, v, h, sea, *refs):
    weights, matrices, (head, tail) = refs[:7], refs[7:11], refs[11:]
    held = (noise, u, v, h, sea)
    members, noises, levels = sizes
    fields = noises + 3 * levels
    lons, lats = sea.shape
    groups = lons // GROUP + 1
    weights_kernel(*weights, *matrices)
    lane = iota((GROUP, LANES), 1)
    for out, t, first in ((head, 0, 0), (tail, lats // LANES - 1, LANES - RIM)):
        for c in range(fields + 1):
            total = jnp.zeros((GROUP, LANES), f32)
            for m in range(members):
                for g, tile in enumerate(shifted_tiles(sizes, held, m, c, t)):
                    place = (g * members + m) * RIM
                    moved = pltpu.roll(tile, (place - first) % LANES, 1)
                    total = jnp.where((lane >= place) & (lane < place + RIM), moved, total)
                    if noises <= c < fields:
                        place = groups * members * RIM + g * members + m
                        edge = 0 if out is head else LANES - 1
                        moved = pltpu.roll(rest(tile), (place - edge) % LANES, 1)
                        total = jnp.where(lane == place, moved, total)
            out[pl.ds(c * GROUP, GROUP)] = total
        for c in range(fields + 1, out.shape[0] // GROUP):
            out[pl.ds(c * GROUP, GROUP)] = jnp.zeros((GROUP, LANES), f32)


def cells_kernel(sizes, noise, u, v, h, sea, left, right, after, out, base, rims, cells, turned):
    members, noises, levels = sizes
    fields = noises + 3 * levels
    lons, lats = sea.shape
    groups = lons // GROUP + 1
    chunks = SUB // members
    rows = cells.shape[1]
    gap_k = lats - (chunks - 1) * ((lats + GAP) // chunks)
    rims[0] = left[...].astype(f32)
    rims[1] = right[...].astype(f32)
    for m in range(members):
        for g in range(groups):
            empty = pl.ds(gap_k * SUB + (m + 1) * chunks - 1, GAP, stride=SUB)
            cells[g, empty, :] = jnp.zeros((GAP, LANES), f32)
    blank = jnp.zeros((GROUP, LANES), f32)
    upper = iota((GROUP, LANES), 0) < RIM
    for t in range(lats // LANES):
        lanes = slice(t * LANES, (t + 1) * LANES)
        for m in range(members):
            tiles = []
            for c in range(fields + 1):
                groups_of = shifted_tiles(sizes, (noise, u, v, h, sea), m, c, t)
                ends = [rim_tile(sizes, m, c, side, rims.at[side, :, lanes]) for side in range(2)]
                groups_of[0] = jnp.where(upper, ends[0], groups_of[0])
                groups_of[-1] = jnp.where(upper, groups_of[-1], ends[1])
                tiles.append(groups_of)
            for g in range(groups):
                following = [x[g + 1] if g + 1 < groups else blank for x in tiles]
                block = window([x[g] for x in tiles[:fields]], following[:fields], tiles[fields][g], following[fields])
                store_lats(block, t, cells, g, m, lats, chunks, turned.at[(t * members + m) * groups + g])
    for g in range(groups):
        out[g] = cells[g].astype(bf16)
    step_kernel(sizes, u, v, h, sea, rims, base)


def step_kernel(sizes, u, v, h, sea, rims, base):
    members, noises, levels = sizes
    fields = noises + 3 * levels
    lons, lats = sea.shape
    ocean = sea[...].astype(f32)
    lat_count = lax.axis_size("lat")
    lat_rows = (lax.axis_index("lat") * lats).astype(f32) + iota((lons, lats), 1).astype(f32)
    turn = CORIOLIS * (2.0 * (lat_rows + 0.5) / (lats * lat_count) - 1.0)
    at_first = iota((lons, lats), 0) == 0
    at_last = iota((lons, lats), 0) == lons - 1
    at_south = iota((lons, lats), 1) == 0
    at_north = iota((lons, lats), 1) == lats - 1
    lon_rests = members * fields * RIM + GROUP

    def around(x, m, c):
        row = (m * fields + c) * RIM
        more = lon_rests + m * (fields - noises) + c - noises
        west = rims[0, pl.ds(row + RIM - 1, 1)] + rims[0, pl.ds(more, 1)]
        east = rims[1, pl.ds(row, 1)] + rims[1, pl.ds(more, 1)]
        return (
            jnp.where(at_first, west, pltpu.roll(x, 1, 0)),
            jnp.where(at_last, east, pltpu.roll(x, lons - 1, 0)),
            jnp.where(at_south, 0.0, pltpu.roll(x, 1, 1)),
            jnp.where(at_north, 0.0, pltpu.roll(x, lats - 1, 1)),
        )

    for m in range(members):
        sets = []
        for level in range(levels):
            sets.append(
                [
                    (x[m, level], around(x[m, level], m, noises + n * levels + level))
                    for n, x in enumerate((u, v, h))
                ]
            )
        for level in range(levels):
            (cu, au), (cv, av), (ch, ah) = sets[level]
            upper, lower = sets[0][2][1], sets[1][2][1]
            pressure = [upper[i] + lower[i] for i in range(4)]
            if level == 1:
                pressure = [pressure[i] + REDUCED * lower[i] for i in range(4)]
            lap_u = au[1] + au[0] + au[3] + au[2] - 4.0 * cu
            lap_v = av[1] + av[0] + av[3] + av[2] - 4.0 * cv
            dx = 0.5 * (pressure[1] - pressure[0])
            dy = 0.5 * (pressure[3] - pressure[2])
            base[0, m, level] = ocean * (cu + TIME_STEP * (turn * cv - dx + VISCOSITY * lap_u))
            base[1, m, level] = ocean * (cv + TIME_STEP * (-turn * cu - dy + VISCOSITY * lap_v))
            flow = 0.5 * (ah[1] * au[1] - ah[0] * au[0]) + 0.5 * (ah[3] * av[3] - ah[2] * av[2])
            base[2, m, level] = ch - TIME_STEP * flow


def join_kernel(sizes, lons, left, right, head, tail, even, odd, rims, wide):
    members, noises, levels = sizes
    fields = noises + 3 * levels
    groups = lons // GROUP + 1
    lats = left.shape[1]
    for side, rim in enumerate((left, right)):
        rims[side, 0] = rim[:, :LANES].astype(f32)
        rims[side, 1] = rim[:, lats - LANES :].astype(f32)
    lane = iota((GROUP, LANES), 1)
    upper = iota((GROUP, LANES), 0) < RIM
    to_south = lax.axis_index("lat") % 2 == 1
    for c in range(fields + 1):
        rows = pl.ds(c * GROUP, GROUP)
        ends = []
        for n, (part, first) in enumerate(((head, 0), (tail, LANES - RIM))):
            total = part[rows]
            for side in range(2):
                held = upper if side == 0 else ~upper
                for m in range(members):
                    place = ((groups - 1) * side * members + m) * RIM
                    tile = rim_tile(sizes, m, c, side, rims.at[side, n])
                    moved = pltpu.roll(tile, (place - first) % LANES, 1)
                    total = jnp.where(held & (lane >= place) & (lane < place + RIM), moved, total)
            ends.append(total)
        wide[0, rows] = jnp.where(to_south, ends[0], ends[1])
        wide[1, rows] = jnp.where(to_south, ends[1], ends[0])
    rows = pl.ds((fields + 1) * GROUP, wide.shape[1] - (fields + 1) * GROUP)
    wide[:, rows] = jnp.zeros((2, wide.shape[1] - (fields + 1) * GROUP, LANES), f32)
    even[...] = wide[0].astype(bf16)
    odd[...] = wide[1].astype(bf16)


def weights_kernel(w1, w2, w3, w4, bias1, bias2, bias3, t1, t2, t3, t4):
    hidden = w2.shape[2]
    per = LANES // hidden
    lane = iota((hidden, LANES), 1)
    fields = w1.shape[0]
    out_lon = iota((GROUP, LANES), 1) // hidden
    in_row = iota((GROUP, LANES), 0)
    bias_row = iota((GROUP, LANES), 0)

    def bias_rows(layer):
        part = 0.5 * jnp.concatenate([(bias1, bias2, bias3)[layer][...]] * per, axis=1)
        b1 = part.astype(bf16).astype(f32)
        b2 = (part - b1).astype(bf16).astype(f32)
        b3 = part - b1 - b2
        zero = jnp.zeros((GROUP, LANES), f32)
        return jnp.where(
            bias_row == 0,
            b1,
            jnp.where(bias_row == 1, b2, jnp.where(bias_row == 2, b3, zero)),
        )

    def sea_rows(shift, tile):
        lon = iota((2 * GROUP, LANES), 0)
        out = iota((2 * GROUP, LANES), 1) // hidden + per * tile
        return jnp.where(lon == out + shift, LAND, 0.0)

    for dj in range(3):
        taps = []
        for di in range(3):
            cells = [w1[c, di].astype(f32)[dj : dj + 1] for c in range(fields)]
            taps.append(
                [jnp.broadcast_to(0.5 * jnp.concatenate([x] * per, axis=1), (GROUP, LANES)) for x in cells]
            )
        for tile in range(2):
            parts = []
            for c in range(fields):
                total = jnp.zeros((GROUP, LANES), f32)
                for di in range(3):
                    hit = in_row == out_lon + per * tile + di
                    total = jnp.where(hit, taps[di][c], total)
                parts.append(total)
            for start in range(0, fields, 4):
                total = jnp.zeros((GROUP, LANES), f32)
                for n in range(min(4, fields - start)):
                    for di in range(3):
                        hit = in_row % 2 + GROUP == out_lon + per * tile + di
                        total = jnp.where(hit & (in_row // 2 == n), taps[di][start + n], total)
                parts.append(total)
            if dj == 1:
                parts += [sea_rows(1, tile), bias_rows(0)]
            else:
                parts.append(jnp.zeros((3 * GROUP, LANES), f32))
            block = jnp.concatenate(parts, axis=0)
            t1[pl.ds(dj * LANES, LANES), pl.ds(tile * LANES, LANES)] = block.astype(bf16)

    for layer, (w, t) in enumerate(((w2, t2), (w3, t3))):
        for dj in range(3):
            taps = []
            for di in range(3):
                cell = 0.5 * w[di, dj].astype(f32)
                wide = jnp.concatenate([cell, jnp.zeros((hidden, LANES - hidden), f32)], axis=1)
                square = jnp.concatenate([wide] * per, axis=0)
                taps.append(jnp.transpose(square)[:hidden])
            for lon in range(GROUP + 2):
                for tile in range(2):
                    total = jnp.zeros((hidden, LANES), f32)
                    for di in range(3):
                        total = jnp.where(lane // hidden + per * tile == lon - di, taps[di], total)
                    if lon < GROUP:
                        row = dj * GROUP * hidden + lon * hidden
                    else:
                        row = 3 * GROUP * hidden + dj * 2 * hidden + (lon - GROUP) * hidden
                    t[pl.ds(row, hidden), pl.ds(tile * LANES, LANES)] = total.astype(bf16)
        for tile in range(2):
            block = jnp.concatenate(
                [
                    jnp.zeros((5 * GROUP, LANES), f32),
                    sea_rows(2 + layer, tile),
                    bias_rows(1 + layer),
                ],
                axis=0,
            )
            row = 3 * GROUP * hidden + 6 * hidden
            t[pl.ds(row, 2 * hidden), pl.ds(tile * LANES, LANES)] = block.astype(bf16)

    outs = w4.shape[2]
    half = LANES // 2
    lons = half // outs
    slot = iota((hidden, LANES), 1) // half
    out_lon = iota((hidden, LANES), 1) % lons
    taps = {}
    for dj in range(3):
        for di in range(3):
            cell = w4[di, dj].astype(f32)
            wide = jnp.concatenate([cell, jnp.zeros((outs, LANES - hidden), f32)], axis=1)
            square = jnp.concatenate(
                [jnp.broadcast_to(wide[c : c + 1], (lons, LANES)) for c in range(outs)] * 2, axis=0
            )
            taps[dj, di] = jnp.transpose(square)[:hidden]
    order = ((0, 1, 2, None), (1, 0, None, 2))
    for side in range(2):
        for lon in range(t4.shape[1] // hidden):
            for tile in range(2):
                total = jnp.zeros((hidden, LANES), f32)
                for place in range(2):
                    dj = order[side][2 * tile + place]
                    if dj is None:
                        continue
                    for di in range(3):
                        total = jnp.where((slot == place) & (out_lon == lon - di), taps[dj, di], total)
                t4[side, pl.ds(lon * hidden, hidden), pl.ds(tile * LANES, LANES)] = total.astype(bf16)


def main_kernel(
    sizes,
    bias_last,
    own,
    base,
    sea,
    even_rim,
    odd_rim,
    own_tail,
    t1,
    t2,
    t3,
    t4,
    new_u,
    new_v,
    new_h,
    first,
    odd,
    even,
    force,
    gathered,
    turned,
    gaps,
    results,
    done,
):
    members, noises, levels = sizes
    fields = noises + 3 * levels
    lons, lats = sea.shape
    groups = lons // GROUP + 1
    chunks = SUB // members
    blocks = (lats + GAP) // chunks
    rows = blocks * SUB
    gap_k = lats - (chunks - 1) * blocks
    lat_index, lat_count = lax.axis_index("lat"), lax.axis_size("lat")
    top = lat_index == lat_count - 1
    is_odd = lat_index % 2 == 1
    bottom = lat_index == 0
    strip = odd_rim[...].astype(f32)
    paired = even_rim[...].astype(f32)
    south = jnp.where(is_odd, paired, jnp.where(bottom, 0.0, strip))

    wide = strip.shape[0]
    span = members * RIM
    lane = iota((wide, LANES), 1)
    rests = groups * span
    border = ((lane % RIM == 0) & (lane < rests)) | (lane >= rests)
    row_to = iota((wide, wide), 0)
    row_from = iota((wide, wide), 1)
    channel = row_to // GROUP
    mirrored = (channel == row_from // GROUP) & (row_from % GROUP == GROUP - 1 - row_to % GROUP)
    odd_parity = (channel >= noises) & (channel < noises + 2 * levels)
    flip_rows = jnp.where(mirrored, jnp.where(odd_parity, -1.0, 1.0), 0.0).astype(bf16)
    lane_from = iota((LANES, LANES), 0)
    lane_to = iota((LANES, LANES), 1)
    source = (groups - 1 - lane_to // span) * span + lane_to % span + RIM - 1
    moves = (lane_to % RIM == 0) & (lane_to < rests) & (lane_from == source)
    other = lane_to - rests
    source = rests + (groups - 1 - other // members) * members + other % members
    moves = moves | ((other >= 0) & (other < groups * members) & (lane_from == source))
    flip_lanes = jnp.where(moves, 1.0, 0.0).astype(bf16)
    pair = dot(flip_rows, jnp.concatenate([odd_rim[...], own_tail[...]], axis=1)).astype(bf16)
    folded = dot(pair[:, :LANES], flip_lanes)
    ghost = dot(pair[:, LANES:], flip_lanes)
    north = jnp.where(is_odd, strip, paired)
    north_rim = jnp.where(border & top, folded, north)

    for n, message in enumerate((north_rim, strip, ghost, south)):
        after = pltpu.roll(message, LANES - span, 1)
        cut = [message[c * GROUP : (c + 1) * GROUP] for c in range(fields + 1)]
        after = [after[c * GROUP : (c + 1) * GROUP] for c in range(fields + 1)]
        turned[n] = jnp.transpose(window(cut[:fields], after[:fields], cut[fields], after[fields]))
        for g in range(groups):
            for m in range(members):
                gap = (m - 1) % members if n == 3 else m
                start = n * RIM * SUB + gap * chunks + chunks - 1
                gaps[g, pl.ds(start, RIM, stride=SUB), :] = turned[n, pl.ds((g * members + m) * RIM, RIM), :]

    in_gap = iota((GAP * SUB, LANES), 0) % chunks == chunks - 1
    for g in range(groups):
        first[g, pl.ds(SUB, rows), :] = own[g]
        spot = pl.ds((1 + gap_k) * SUB, GAP * SUB)
        kept = first[g, spot, :].astype(f32)
        first[g, spot, :] = jnp.where(in_gap, gaps[g], kept).astype(bf16)
        end = first[g, pl.ds(rows, SUB), :].astype(f32)
        first[g, pl.ds(0, SUB), :] = pltpu.roll(end, 1, 0).astype(bf16)
        begin = first[g, pl.ds(SUB, SUB), :].astype(f32)
        first[g, pl.ds(SUB + rows, SUB), :] = pltpu.roll(begin, SUB - 1, 0).astype(bf16)

    hidden = LANES // 4
    per = LANES // hidden
    tiles = odd.shape[0]
    piece = 8 * SUB
    pieces = [(r, min(piece, rows - r)) for r in range(0, rows, piece)]

    def activate(pre):
        return (pre * jnp.tanh(pre) + pre).astype(bf16)

    def finish(x, valid):
        used = (valid + per - 1) // per

        @pl.when(top)
        def _():
            strip_top = SUB * (1 + gap_k + STRIP + RIM - 1)
            own_top = SUB * gap_k
            strip_ghost = SUB * (1 + gap_k + GHOST)
            own_ghost = SUB * (1 + gap_k + NORTH)
            last_chunk = iota((SUB, LANES), 0) % chunks == chunks - 1
            spot = iota((SUB, LANES), 1) // hidden
            for src, dst in ((strip_top, own_ghost), (own_top, strip_ghost)):
                found = [x[t, pl.ds(src, SUB), :].astype(f32) for t in range(used)]
                for t in range(used):
                    total = x[t, pl.ds(dst, SUB), :].astype(f32)
                    for i in range(per):
                        lon = valid - 1 - (per * t + i)
                        if lon < 0:
                            continue
                        moved = pltpu.roll(found[lon // per], (hidden * (i - lon % per)) % LANES, 1)
                        total = jnp.where(last_chunk & (spot == i), moved, total)
                    x[t, pl.ds(dst, SUB), :] = total.astype(bf16)

        for t in range(used):
            end = x[t, pl.ds(rows, SUB), :].astype(f32)
            x[t, pl.ds(0, SUB), :] = pltpu.roll(end, 1, 0).astype(bf16)
            begin = x[t, pl.ds(SUB, SUB), :].astype(f32)
            x[t, pl.ds(SUB + rows, SUB), :] = pltpu.roll(begin, SUB - 1, 0).astype(bf16)

    for x in (odd, even):
        x[tiles - 1] = jnp.zeros(x.shape[1:], bf16)
    even[tiles - 2] = jnp.zeros(even.shape[1:], bf16)

    def put(y, b, r, out):
        step = out.shape[0]
        for e in range(out.shape[1] // LANES):
            y[2 * b + e, pl.ds(SUB + r, step), :] = out[:, e * LANES : (e + 1) * LANES]

    for b in range(groups):
        for r, step in pieces:
            parts = [first[b, pl.ds(r + SUB * d, step), :] for d in range(3)]
            put(odd, b, r, activate(dot(jnp.concatenate(parts, axis=1), t1[...])))
    finish(odd, lons + 6)

    width = GROUP * hidden

    def layer(x, y, t, left_over):
        for b in range(groups):
            for r, step in pieces:
                lower = iota((step, LANES), 1) < 2 * hidden

                def cells_of(tile, d):
                    return x[tile, pl.ds(r + SUB * d, step), :]

                def packed(tile):
                    more = [cells_of(tile, d) for d in range(3)]
                    return [
                        jnp.where(lower, more[0], pltpu.roll(more[1], 2 * hidden, 1)),
                        jnp.where(lower, more[2], first[b, pl.ds(r + SUB, step), :]),
                    ]

                if b < groups - 1:
                    parts = [cells_of(2 * b + e, d) for d in range(3) for e in range(2)] + packed(2 * b + 2)
                    matrix = t[...]
                elif left_over == per:
                    parts = [cells_of(2 * b, d) for d in range(3)] + packed(2 * b + 1)
                    lanes = pl.ds(0, LANES)
                    matrix = jnp.concatenate(
                        [t[pl.ds(d * width, LANES), lanes] for d in range(3)]
                        + [t[pl.ds(d * width + LANES, 2 * hidden), lanes] for d in range(3)]
                        + [t[pl.ds(3 * width + 6 * hidden, 2 * hidden), lanes]],
                        axis=0,
                    )
                else:
                    parts = [cells_of(2 * b, d) for d in range(3)] + [first[b, pl.ds(r + SUB, step), :]]
                    lanes = pl.ds(0, LANES)
                    matrix = jnp.concatenate(
                        [t[pl.ds(d * width, LANES), lanes] for d in range(3)]
                        + [jnp.zeros((2 * hidden, LANES), bf16)]
                        + [t[pl.ds(3 * width + 6 * hidden, 2 * hidden), lanes]],
                        axis=0,
                    )
                put(y, b, r, activate(dot(jnp.concatenate(parts, axis=1), matrix)))

    layer(odd, even, t2, per)
    finish(even, lons + 4)
    layer(even, odd, t3, per // 2)
    finish(odd, lons + 2)

    depth = t4.shape[1] // LANES
    padded = rows + 2 * SUB
    for r in range(0, padded, piece):
        long = min(piece, padded - r)
        before = iota((long, LANES), 1) < LANES // 2
        span_rows = pl.ds(r, long)
        sides = []
        for side in range(2):
            parts = [odd[side * (depth - 1) + t, span_rows, :] for t in range(depth)]
            sides.append(dot(jnp.concatenate(parts, axis=1), t4[side]))
        force[0, span_rows, :] = jnp.where(before, sides[0][:, :LANES], sides[1][:, :LANES])
        swapped = jnp.where(before, sides[1][:, :LANES], sides[0][:, :LANES])
        force[1, span_rows, :] = pltpu.roll(swapped, LANES // 2, 1)
        force[2, span_rows, :] = jnp.where(before, sides[0][:, LANES:], sides[1][:, LANES:])

    ocean = sea[...].astype(f32)
    narrow = iota((lons, LANES), 1)
    at_south = narrow == 0
    at_north = narrow == LANES - 1
    halves = lons // 2

    def beyond(message, m, c, offset):
        cells = []
        some = slice(c * GROUP, (c + 1) * GROUP)
        for g in range(groups):
            spot = (g * members + m) * RIM + offset
            more = rests + g * members + m
            cells.append(message[some, spot : spot + 1] + message[some, more : more + 1])
        whole = jnp.broadcast_to(jnp.concatenate(cells, axis=0), (lons + GROUP, LANES))
        return pltpu.roll(whole, lons + GROUP - RIM, 0)[:lons]

    for m in range(members):
        for q in range(chunks):
            size = min(blocks, lats - q * blocks)
            total = force[0, pl.ds(m * chunks + q, size, stride=SUB), :]
            for d in range(1, 3):
                total = total + force[d, pl.ds(d * SUB + m * chunks + q, size, stride=SUB), :]
            gathered[m, pl.ds(q * blocks, size), :] = total
        turned_force = jnp.transpose(gathered[m])
        rims = [
            [beyond(message, m, c, offset) for c in range(noises, fields)]
            for message, offset in ((south, RIM - 1), (north_rim, 0))
        ]
        for level in range(levels):
            gains = []
            for (sign, spot), rim in zip(((1.0, at_south), (-1.0, at_north)), rims):
                ru, rv, rh = rim[level], rim[levels + level], rim[2 * levels + level]
                pressure = rim[2 * levels] + rim[2 * levels + 1]
                if level == 1:
                    pressure = pressure + REDUCED * rh
                gains.append(
                    [
                        jnp.where(spot, TIME_STEP * VISCOSITY * ru, 0.0),
                        jnp.where(spot, TIME_STEP * (VISCOSITY * rv + sign * 0.5 * pressure), 0.0),
                        jnp.where(spot, TIME_STEP * sign * 0.5 * (rh * rv), 0.0),
                    ]
                )
            middle = [jnp.zeros((lons, lats - 2 * LANES), f32)] if lats > 2 * LANES else []
            gains = [jnp.concatenate([gains[0][n]] + middle + [gains[1][n]], axis=1) for n in range(3)]

            def push(c):
                parts = [
                    turned_force[side * LANES // 2 + c * halves : side * LANES // 2 + (c + 1) * halves]
                    for side in range(2)
                ]
                return TIME_STEP * (jnp.concatenate(parts, axis=0) + bias_last[c])

            results[0, m, level] = base[0, m, level] + ocean * (gains[0] + push(level))
            results[1, m, level] = base[1, m, level] + ocean * (gains[1] + push(levels + level))
            results[2, m, level] = base[2, m, level] + gains[2]
        for n, out in enumerate((new_u, new_v, new_h)):
            pltpu.make_async_copy(results.at[n, m], out.at[m], done.at[n, m]).start()
    for m in range(members):
        for n, out in enumerate((new_u, new_v, new_h)):
            pltpu.make_async_copy(results.at[n, m], out.at[m], done.at[n, m]).wait()


def body(
    noise,
    velocity_u,
    velocity_v,
    thickness,
    land_sea,
    conv_first,
    bias_first,
    conv_second,
    bias_second,
    conv_third,
    bias_third,
    conv_last,
    bias_last,
):
    members, noises, lons, lats = noise.shape
    levels = velocity_u.shape[1]
    fields = noises + 3 * levels
    sizes = (members, noises, levels)
    hidden = conv_first.shape[0]
    outs = conv_last.shape[0]
    groups = lons // GROUP + 1
    rows = members * (lats + GAP)
    assert hidden * 4 == LANES and outs * lons == LANES and members * (RIM + 1) * groups <= LANES
    assert fields % 2 == 0 and 4 * -(-fields // 4) == 12 and GROUP * (fields + 6) == LANES and lons % 16 == 0
    assert lats % LANES == 0 and SUB % members == 0 and (lats + GAP) % (SUB // members) == 0
    lon_count, lat_count = lax.axis_size("lon"), lax.axis_size("lat")
    assert lon_count % 2 == 0 and lat_count % 2 == 0
    state = (noise, velocity_u, velocity_v, thickness, land_sea)
    whole = pl.BlockSpec(memory_space=pltpu.VMEM)

    tall = members * fields * RIM + GROUP + members * 3 * levels
    assert tall % SUB == 0
    args = state + (
        conv_first.transpose(1, 2, 3, 0),
        conv_second.transpose(2, 3, 0, 1),
        conv_third.transpose(2, 3, 0, 1),
        conv_last.transpose(2, 3, 0, 1),
        bias_first[None],
        bias_second[None],
        bias_third[None],
    )
    count = len(args)
    *held, head, tail = pl.pallas_call(
        functools.partial(pack_lon_kernel, sizes, count),
        out_shape=[pltpu.VMEM(x.shape, x.dtype) for x in args] + [pltpu.VMEM((tall, lats), bf16)] * 2,
        in_specs=[pl.BlockSpec(memory_space=pltpu.HBM)] * count,
        out_specs=[whole] * (count + 2),
        scratch_shapes=[pltpu.VMEM((2, tall, lats), f32), pltpu.SemaphoreType.DMA((count,))],
        compiler_params=pltpu.CompilerParams(vmem_limit_bytes=62 * 2**20),
        name="pack_lon",
    )(*args)
    state = tuple(held[:5])
    ring = [(i, (i + 1) % lon_count) for i in range(lon_count)]
    left = lax.ppermute(tail, "lon", ring)
    right = lax.ppermute(head, "lon", [(b, a) for a, b in ring])

    wide = -(-(fields + 1) * GROUP // SUB) * SUB
    part = pltpu.VMEM((wide, LANES), f32)
    message = pltpu.VMEM((wide, LANES), bf16)
    deep = -(-(lons // 2 + 2) * hidden // LANES) * LANES
    t1, t2, t3, t4, own_head, own_tail = pl.pallas_call(
        functools.partial(prepare_kernel, sizes),
        out_shape=[
            pltpu.VMEM((3 * LANES, 2 * LANES), bf16),
            pltpu.VMEM((8 * LANES, 2 * LANES), bf16),
            pltpu.VMEM((8 * LANES, 2 * LANES), bf16),
            pltpu.VMEM((2, deep, 2 * LANES), bf16),
            part,
            part,
        ],
        in_specs=[whole] * count,
        out_specs=[whole] * 6,
        compiler_params=pltpu.CompilerParams(vmem_limit_bytes=8 * 2**20),
        cost_estimate=pl.CostEstimate(flops=10**7, bytes_accessed=10**7, transcendentals=0),
        name="prepare",
    )(*held)
    last = lat_count - 1
    smem = pl.BlockSpec(memory_space=pltpu.SMEM)
    to_even, to_odd = pl.pallas_call(
        functools.partial(join_kernel, sizes, lons),
        out_shape=[message] * 2,
        in_specs=[whole] * 4,
        out_specs=[whole] * 2,
        scratch_shapes=[
            pltpu.VMEM((2, 2, tall, LANES), f32),
            pltpu.VMEM((2, wide, LANES), f32),
        ],
        compiler_params=pltpu.CompilerParams(vmem_limit_bytes=4 * 2**20),
        name="join_rims",
    )(left, right, own_head, own_tail)
    even_rim = lax.ppermute(to_even, "lat", [(i, i ^ 1) for i in range(lat_count)])
    pairs = []
    for t in range(lon_count):
        at = t * lat_count
        pairs += [(at + k, at + k - 1 + 2 * (k % 2)) for k in range(1, last)]
        pairs += [(at, (t ^ 1) * lat_count), (at + last, (lon_count - 1 - t) * lat_count + last)]
    odd_rim = lax.ppermute(to_odd, ("lon", "lat"), pairs)

    own, base = pl.pallas_call(
        functools.partial(cells_kernel, sizes),
        out_shape=[pltpu.VMEM((groups, rows, LANES), bf16), pltpu.VMEM((3, *velocity_u.shape), f32)],
        in_specs=[whole] * 8,
        out_specs=[whole] * 2,
        scratch_shapes=[
            pltpu.VMEM((2, tall, lats), f32),
            pltpu.VMEM((groups, rows, LANES), f32),
            pltpu.VMEM((members * groups * lats // LANES, LANES, LANES), f32),
        ],
        compiler_params=pltpu.CompilerParams(vmem_limit_bytes=12 * 2**20),
        cost_estimate=pl.CostEstimate(flops=10**7, bytes_accessed=10**7, transcendentals=0),
        name="cells",
    )(*state, left, right, to_even)

    padded = rows + 2 * SUB
    tiles = 2 * groups + 1
    out = jax.ShapeDtypeStruct(velocity_u.shape, f32)
    return pl.pallas_call(
        functools.partial(main_kernel, sizes),
        out_shape=[out] * 3,
        in_specs=[smem] + [whole] * 10,
        out_specs=[pl.BlockSpec(memory_space=pltpu.HBM)] * 3,
        scratch_shapes=[
            pltpu.VMEM((groups, padded, LANES), bf16),
            pltpu.VMEM((tiles, padded, LANES), bf16),
            pltpu.VMEM((tiles, padded, LANES), bf16),
            pltpu.VMEM((3, padded, LANES), f32),
            pltpu.VMEM((members, lats, LANES), f32),
            pltpu.VMEM((4, LANES, LANES), f32),
            pltpu.VMEM((groups, GAP * SUB, LANES), f32),
            pltpu.VMEM((3, *velocity_u.shape), f32),
            pltpu.SemaphoreType.DMA((3, members)),
        ],
        compiler_params=pltpu.CompilerParams(vmem_limit_bytes=32 * 2**20),
        cost_estimate=pl.CostEstimate(flops=2 * 10**10, bytes_accessed=10**7, transcendentals=4 * 10**6),
        name="network_and_step",
    )(
        bias_last,
        own,
        base,
        state[4],
        even_rim,
        odd_rim,
        to_odd,
        t1,
        t2,
        t3,
        t4,
    )


def solution(mesh):
    tiles = P(None, None, "lon", "lat")
    return jax.shard_map(
        body,
        mesh=mesh,
        in_specs=(tiles,) * 4 + (P("lon", "lat"),) + (P(),) * 8,
        out_specs=(tiles,) * 3,
        check_vma=False,
    )
```

```python
import functools

import jax
import jax.numpy as jnp
from jax import lax
from jax.experimental import pallas as pl
from jax.experimental.pallas import tpu as pltpu
from jax.sharding import PartitionSpec as P

REDUCED = 0.5
TIME_STEP = 0.2
VISCOSITY = 0.05
CORIOLIS = 0.4

RIM = 4
GAP = 16
NORTH, STRIP, GHOST, SOUTH = 0, 4, 8, 12
SUB = 16
LANES = 128
GROUP = 8
LAND = 2.0**100

f32 = jnp.float32
bf16 = jnp.bfloat16


def iota(shape, dim):
    return lax.broadcasted_iota(jnp.int32, shape, dim)


def dot(a, b):
    return jnp.dot(a, b, preferred_element_type=f32)


def rest(x):
    return x - x.astype(bf16).astype(f32)


def pack_lon_kernel(sizes, count, *refs):
    sources, held, (even, odd, wide, done) = refs[:count], refs[count : 2 * count], refs[2 * count :]
    members, noises, levels = sizes
    fields = noises + 3 * levels
    noise, u, v, h, sea = held[:5]
    lons, lats = sea.shape
    copies = [pltpu.make_async_copy(x, y, done.at[n]) for n, (x, y) in enumerate(zip(sources, held))]
    for copy in copies:
        copy.start()
    for copy in copies[:5]:
        copy.wait()
    upper = iota((GROUP, lats), 0) < RIM

    def field(m, c, side):
        if c < noises:
            full = noise[m, c].astype(f32)
            return full[-GROUP:] if side else full[:GROUP]
        c -= noises
        return (u, v, h)[c // levels][m, c % levels, pl.ds(side * (lons - GROUP), GROUP)]

    rests = members * fields * RIM + GROUP
    for m in range(members):
        for c in range(0, fields, 2):
            rows = pl.ds((m * fields + c) * RIM, GROUP)
            wide[0, rows] = jnp.where(upper, field(m, c, 0), pltpu.roll(field(m, c + 1, 0), RIM, 0))
            wide[1, rows] = jnp.where(upper, pltpu.roll(field(m, c, 1), RIM, 0), field(m, c + 1, 1))
        for c in range(noises, fields):
            row = pl.ds(rests + m * (fields - noises) + c - noises, 1)
            wide[0, row] = rest(field(m, c, 0)[:1])
            wide[1, row] = rest(field(m, c, 1)[GROUP - 1 :])
    rows = pl.ds(members * fields * RIM, GROUP)
    ends = [sea[pl.ds(side * (lons - GROUP), GROUP)].astype(f32) for side in range(2)]
    wide[0, rows] = jnp.where(upper, ends[0], 0.0)
    wide[1, rows] = jnp.where(upper, pltpu.roll(ends[1], RIM, 0), 0.0)
    is_odd = lax.axis_index("lon") % 2 == 1
    even[...] = jnp.where(is_odd, wide[0], wide[1]).astype(bf16)
    odd[...] = jnp.where(is_odd, wide[1], wide[0]).astype(bf16)
    for copy in copies[5:]:
        copy.wait()


def lon_rims(even, odd, lanes=slice(None)):
    is_odd = lax.axis_index("lon") % 2 == 1
    a, b = even[:, lanes].astype(f32), odd[:, lanes].astype(f32)
    return jnp.where(is_odd, a, b), jnp.where(is_odd, b, a)


def rim_tile(sizes, m, c, side, rim):
    members, noises, levels = sizes
    fields = noises + 3 * levels
    row = (m * fields + c) * RIM if c < fields else members * fields * RIM
    tile = rim[pl.ds(row // GROUP * GROUP, GROUP)]
    if (row // RIM) % 2 == side:
        return tile
    return pltpu.roll(tile, RIM, 0)


def window(tiles, following, mask, next_mask):
    pair = iota(mask.shape, 0) // 2
    zero = jnp.zeros_like(mask)
    more = []
    for start in range(0, len(tiles), 4):
        total = zero
        for n in range(min(4, len(tiles) - start)):
            moved = pltpu.roll(following[start + n], 2 * n, 0) if n else following[start]
            total = jnp.where(pair == n, moved, total)
        more.append(total)
    return jnp.concatenate(
        tiles + more + [mask - 1.0, next_mask - 1.0, jnp.ones_like(mask)], axis=0
    )


def store_lats(block, t, dst, tile, m, lats, chunks, buffer):
    blocks = (lats + GAP) // chunks
    buffer[...] = jnp.transpose(block)
    for q in range(chunks):
        lo = max(q * blocks, t * LANES)
        hi = min((q + 1) * blocks, (t + 1) * LANES, lats)
        if lo < hi:
            start = (lo - q * blocks) * SUB + m * chunks + q
            dst[tile, pl.ds(start, hi - lo, stride=SUB), :] = buffer[pl.ds(lo - t * LANES, hi - lo), :]


def shifted_tiles(sizes, refs, m, c, t):
    noise, u, v, h, sea = refs
    members, noises, levels = sizes
    fields = noises + 3 * levels
    lons = sea.shape[0]
    lanes = slice(t * LANES, (t + 1) * LANES)
    if c == fields:
        full = sea[:, lanes].astype(f32)
    elif c < noises:
        full = noise[m, c, :, lanes].astype(f32)
    else:
        full = (u, v, h)[(c - noises) // levels][m, (c - noises) % levels, :, lanes]
    full = pltpu.roll(full, lons - RIM, 0)
    tiles = [full[g * GROUP : (g + 1) * GROUP] for g in range(lons // GROUP)]
    return tiles[-1:] + tiles


def prepare_kernel(sizes, noise, u, v, h, sea, *refs):
    weights, matrices, (head, tail, middle, pre, cells, turned) = refs[:7], refs[7:11], refs[11:]
    held = (noise, u, v, h, sea)
    members, noises, levels = sizes
    fields = noises + 3 * levels
    lons, lats = sea.shape
    groups = lons // GROUP + 1
    weights_kernel(*weights, *matrices)
    lane = iota((GROUP, LANES), 1)
    for out, t, first in ((head, 0, 0), (tail, lats // LANES - 1, LANES - RIM)):
        for c in range(fields + 1):
            total = jnp.zeros((GROUP, LANES), f32)
            for m in range(members):
                for g, tile in enumerate(shifted_tiles(sizes, held, m, c, t)):
                    place = (g * members + m) * RIM
                    moved = pltpu.roll(tile, (place - first) % LANES, 1)
                    total = jnp.where((lane >= place) & (lane < place + RIM), moved, total)
                    if noises <= c < fields:
                        place = groups * members * RIM + g * members + m
                        edge = 0 if out is head else LANES - 1
                        moved = pltpu.roll(rest(tile), (place - edge) % LANES, 1)
                        total = jnp.where(lane == place, moved, total)
            out[pl.ds(c * GROUP, GROUP)] = total
        for c in range(fields + 1, out.shape[0] // GROUP):
            out[pl.ds(c * GROUP, GROUP)] = jnp.zeros((GROUP, LANES), f32)
    chunks = SUB // members
    rows = cells.shape[1]
    gap_k = lats - (chunks - 1) * ((lats + GAP) // chunks)
    inner = groups - 2
    for m in range(members):
        for g in range(inner):
            empty = pl.ds(gap_k * SUB + (m + 1) * chunks - 1, GAP, stride=SUB)
            cells[g, empty, :] = jnp.zeros((GAP, LANES), f32)
    for t in range(lats // LANES):
        for m in range(members):
            tiles = [shifted_tiles(sizes, held, m, c, t) for c in range(fields + 1)]
            for g in range(1, inner + 1):
                following = [x[g + 1] for x in tiles]
                block = window([x[g] for x in tiles[:fields]], following[:fields], tiles[fields][g], following[fields])
                buffer = turned.at[(t * members + m) * inner + g - 1]
                store_lats(block, t, cells, g - 1, m, lats, chunks, buffer)
    for g in range(inner):
        middle[g, pl.ds(SUB, rows), :] = cells[g].astype(bf16)
        wrap(middle.at[g], rows)
    for g in range(inner):
        for r, step in row_pieces(rows):
            parts = [middle[g, pl.ds(r + SUB * d, step), :] for d in range(3)]
            put(pre, g + 1, r, activate(dot(jnp.concatenate(parts, axis=1), matrices[0][...])))


def row_pieces(rows):
    half = rows // 2 // SUB * SUB
    return [(0, half), (half, rows - half)]


def activate(pre):
    return (pre * jnp.tanh(pre) + pre).astype(bf16)


def put(y, b, r, out):
    for e in range(out.shape[1] // LANES):
        y[2 * b + e, pl.ds(SUB + r, out.shape[0]), :] = out[:, e * LANES : (e + 1) * LANES]


def wrap(x, rows):
    end = x[pl.ds(rows, SUB), :].astype(f32)
    x[pl.ds(0, SUB), :] = pltpu.roll(end, 1, 0).astype(bf16)
    begin = x[pl.ds(SUB, SUB), :].astype(f32)
    x[pl.ds(SUB + rows, SUB), :] = pltpu.roll(begin, SUB - 1, 0).astype(bf16)


def cells_kernel(sizes, noise, u, v, h, sea, lon_even, lon_odd, after, out, base, rims, cells, turned):
    members, noises, levels = sizes
    fields = noises + 3 * levels
    lons, lats = sea.shape
    groups = lons // GROUP + 1
    chunks = SUB // members
    rows = cells.shape[1]
    gap_k = lats - (chunks - 1) * ((lats + GAP) // chunks)
    rims[0], rims[1] = lon_rims(lon_even, lon_odd)
    for m in range(members):
        for side in range(2):
            empty = pl.ds(gap_k * SUB + (m + 1) * chunks - 1, GAP, stride=SUB)
            cells[side, empty, :] = jnp.zeros((GAP, LANES), f32)
    blank = jnp.zeros((GROUP, LANES), f32)
    upper = iota((GROUP, LANES), 0) < RIM
    for t in range(lats // LANES):
        lanes = slice(t * LANES, (t + 1) * LANES)
        for m in range(members):
            tiles = []
            for c in range(fields + 1):
                groups_of = shifted_tiles(sizes, (noise, u, v, h, sea), m, c, t)
                ends = [rim_tile(sizes, m, c, side, rims.at[side, :, lanes]) for side in range(2)]
                groups_of[0] = jnp.where(upper, ends[0], groups_of[0])
                groups_of[-1] = jnp.where(upper, groups_of[-1], ends[1])
                tiles.append(groups_of)
            for side, g in enumerate((0, groups - 1)):
                following = [x[g + 1] if g + 1 < groups else blank for x in tiles]
                block = window([x[g] for x in tiles[:fields]], following[:fields], tiles[fields][g], following[fields])
                store_lats(block, t, cells, side, m, lats, chunks, turned.at[(t * members + m) * 2 + side])
    for side in range(2):
        out[side, pl.ds(SUB, rows), :] = cells[side].astype(bf16)
    step_kernel(sizes, u, v, h, sea, rims, base)


def step_kernel(sizes, u, v, h, sea, rims, base):
    members, noises, levels = sizes
    fields = noises + 3 * levels
    lons, lats = sea.shape
    ocean = sea[...].astype(f32)
    lat_count = lax.axis_size("lat")
    lat_rows = (lax.axis_index("lat") * lats).astype(f32) + iota((lons, lats), 1).astype(f32)
    turn = CORIOLIS * (2.0 * (lat_rows + 0.5) / (lats * lat_count) - 1.0)
    at_first = iota((lons, lats), 0) == 0
    at_last = iota((lons, lats), 0) == lons - 1
    at_south = iota((lons, lats), 1) == 0
    at_north = iota((lons, lats), 1) == lats - 1
    lon_rests = members * fields * RIM + GROUP

    def around(x, m, c):
        row = (m * fields + c) * RIM
        more = lon_rests + m * (fields - noises) + c - noises
        west = rims[0, pl.ds(row + RIM - 1, 1)] + rims[0, pl.ds(more, 1)]
        east = rims[1, pl.ds(row, 1)] + rims[1, pl.ds(more, 1)]
        return (
            jnp.where(at_first, west, pltpu.roll(x, 1, 0)),
            jnp.where(at_last, east, pltpu.roll(x, lons - 1, 0)),
            jnp.where(at_south, 0.0, pltpu.roll(x, 1, 1)),
            jnp.where(at_north, 0.0, pltpu.roll(x, lats - 1, 1)),
        )

    for m in range(members):
        sets = []
        for level in range(levels):
            sets.append(
                [
                    (x[m, level], around(x[m, level], m, noises + n * levels + level))
                    for n, x in enumerate((u, v, h))
                ]
            )
        for level in range(levels):
            (cu, au), (cv, av), (ch, ah) = sets[level]
            upper, lower = sets[0][2][1], sets[1][2][1]
            pressure = [upper[i] + lower[i] for i in range(4)]
            if level == 1:
                pressure = [pressure[i] + REDUCED * lower[i] for i in range(4)]
            lap_u = au[1] + au[0] + au[3] + au[2] - 4.0 * cu
            lap_v = av[1] + av[0] + av[3] + av[2] - 4.0 * cv
            dx = 0.5 * (pressure[1] - pressure[0])
            dy = 0.5 * (pressure[3] - pressure[2])
            base[0, m, level] = ocean * (cu + TIME_STEP * (turn * cv - dx + VISCOSITY * lap_u))
            base[1, m, level] = ocean * (cv + TIME_STEP * (-turn * cu - dy + VISCOSITY * lap_v))
            flow = 0.5 * (ah[1] * au[1] - ah[0] * au[0]) + 0.5 * (ah[3] * av[3] - ah[2] * av[2])
            base[2, m, level] = ch - TIME_STEP * flow


def join_kernel(sizes, lons, lon_even, lon_odd, head, tail, even, odd, rims, wide):
    members, noises, levels = sizes
    fields = noises + 3 * levels
    groups = lons // GROUP + 1
    lats = lon_even.shape[1]
    for n, lanes in enumerate((slice(0, LANES), slice(lats - LANES, lats))):
        rims[0, n], rims[1, n] = lon_rims(lon_even, lon_odd, lanes)
    lane = iota((GROUP, LANES), 1)
    upper = iota((GROUP, LANES), 0) < RIM
    to_south = lax.axis_index("lat") % 2 == 1
    for c in range(fields + 1):
        rows = pl.ds(c * GROUP, GROUP)
        ends = []
        for n, (part, first) in enumerate(((head, 0), (tail, LANES - RIM))):
            total = part[rows]
            for side in range(2):
                held = upper if side == 0 else ~upper
                for m in range(members):
                    place = ((groups - 1) * side * members + m) * RIM
                    tile = rim_tile(sizes, m, c, side, rims.at[side, n])
                    moved = pltpu.roll(tile, (place - first) % LANES, 1)
                    total = jnp.where(held & (lane >= place) & (lane < place + RIM), moved, total)
            ends.append(total)
        wide[0, rows] = jnp.where(to_south, ends[0], ends[1])
        wide[1, rows] = jnp.where(to_south, ends[1], ends[0])
    rows = pl.ds((fields + 1) * GROUP, wide.shape[1] - (fields + 1) * GROUP)
    wide[:, rows] = jnp.zeros((2, wide.shape[1] - (fields + 1) * GROUP, LANES), f32)
    even[...] = wide[0].astype(bf16)
    odd[...] = wide[1].astype(bf16)


def weights_kernel(w1, w2, w3, w4, bias1, bias2, bias3, t1, t2, t3, t4):
    hidden = w2.shape[2]
    per = LANES // hidden
    lane = iota((hidden, LANES), 1)
    fields = w1.shape[0]
    out_lon = iota((GROUP, LANES), 1) // hidden
    in_row = iota((GROUP, LANES), 0)
    bias_row = iota((GROUP, LANES), 0)

    def bias_rows(layer):
        part = 0.5 * jnp.concatenate([(bias1, bias2, bias3)[layer][...]] * per, axis=1)
        b1 = part.astype(bf16).astype(f32)
        b2 = (part - b1).astype(bf16).astype(f32)
        b3 = part - b1 - b2
        zero = jnp.zeros((GROUP, LANES), f32)
        return jnp.where(
            bias_row == 0,
            b1,
            jnp.where(bias_row == 1, b2, jnp.where(bias_row == 2, b3, zero)),
        )

    def sea_rows(shift, tile):
        lon = iota((2 * GROUP, LANES), 0)
        out = iota((2 * GROUP, LANES), 1) // hidden + per * tile
        return jnp.where(lon == out + shift, LAND, 0.0)

    for dj in range(3):
        taps = []
        for di in range(3):
            cells = [w1[c, di].astype(f32)[dj : dj + 1] for c in range(fields)]
            taps.append(
                [jnp.broadcast_to(0.5 * jnp.concatenate([x] * per, axis=1), (GROUP, LANES)) for x in cells]
            )
        for tile in range(2):
            parts = []
            for c in range(fields):
                total = jnp.zeros((GROUP, LANES), f32)
                for di in range(3):
                    hit = in_row == out_lon + per * tile + di
                    total = jnp.where(hit, taps[di][c], total)
                parts.append(total)
            for start in range(0, fields, 4):
                total = jnp.zeros((GROUP, LANES), f32)
                for n in range(min(4, fields - start)):
                    for di in range(3):
                        hit = in_row % 2 + GROUP == out_lon + per * tile + di
                        total = jnp.where(hit & (in_row // 2 == n), taps[di][start + n], total)
                parts.append(total)
            if dj == 1:
                parts += [sea_rows(1, tile), bias_rows(0)]
            else:
                parts.append(jnp.zeros((3 * GROUP, LANES), f32))
            block = jnp.concatenate(parts, axis=0)
            t1[pl.ds(dj * LANES, LANES), pl.ds(tile * LANES, LANES)] = block.astype(bf16)

    for layer, (w, t) in enumerate(((w2, t2), (w3, t3))):
        for dj in range(3):
            taps = []
            for di in range(3):
                cell = 0.5 * w[di, dj].astype(f32)
                wide = jnp.concatenate([cell, jnp.zeros((hidden, LANES - hidden), f32)], axis=1)
                square = jnp.concatenate([wide] * per, axis=0)
                taps.append(jnp.transpose(square)[:hidden])
            for lon in range(GROUP + 2):
                for tile in range(2):
                    total = jnp.zeros((hidden, LANES), f32)
                    for di in range(3):
                        total = jnp.where(lane // hidden + per * tile == lon - di, taps[di], total)
                    if lon < GROUP:
                        row = dj * GROUP * hidden + lon * hidden
                    else:
                        row = 3 * GROUP * hidden + dj * 2 * hidden + (lon - GROUP) * hidden
                    t[pl.ds(row, hidden), pl.ds(tile * LANES, LANES)] = total.astype(bf16)
        for tile in range(2):
            block = jnp.concatenate(
                [
                    jnp.zeros((5 * GROUP, LANES), f32),
                    sea_rows(2 + layer, tile),
                    bias_rows(1 + layer),
                ],
                axis=0,
            )
            row = 3 * GROUP * hidden + 6 * hidden
            t[pl.ds(row, 2 * hidden), pl.ds(tile * LANES, LANES)] = block.astype(bf16)

    outs = w4.shape[2]
    half = LANES // 2
    lons = half // outs
    slot = iota((hidden, LANES), 1) // half
    out_lon = iota((hidden, LANES), 1) % lons
    taps = {}
    for dj in range(3):
        for di in range(3):
            cell = w4[di, dj].astype(f32)
            wide = jnp.concatenate([cell, jnp.zeros((outs, LANES - hidden), f32)], axis=1)
            square = jnp.concatenate(
                [jnp.broadcast_to(wide[c : c + 1], (lons, LANES)) for c in range(outs)] * 2, axis=0
            )
            taps[dj, di] = jnp.transpose(square)[:hidden]
    order = ((0, 1, 2, None), (1, 0, None, 2))
    for side in range(2):
        for lon in range(t4.shape[1] // hidden):
            for tile in range(2):
                total = jnp.zeros((hidden, LANES), f32)
                for place in range(2):
                    dj = order[side][2 * tile + place]
                    if dj is None:
                        continue
                    for di in range(3):
                        total = jnp.where((slot == place) & (out_lon == lon - di), taps[dj, di], total)
                t4[side, pl.ds(lon * hidden, hidden), pl.ds(tile * LANES, LANES)] = total.astype(bf16)


def main_kernel(
    sizes,
    bias_last,
    middle_in,
    ends_in,
    pre_in,
    base,
    sea,
    even_rim,
    odd_rim,
    own_tail,
    t1,
    t2,
    t3,
    t4,
    new_u,
    new_v,
    new_h,
    middle,
    ends,
    odd,
    even,
    force,
    gathered,
    turned,
    gaps,
    results,
    done,
):
    members, noises, levels = sizes
    fields = noises + 3 * levels
    lons, lats = sea.shape
    groups = lons // GROUP + 1
    chunks = SUB // members
    blocks = (lats + GAP) // chunks
    rows = blocks * SUB
    gap_k = lats - (chunks - 1) * blocks
    lat_index, lat_count = lax.axis_index("lat"), lax.axis_size("lat")
    top = lat_index == lat_count - 1
    is_odd = lat_index % 2 == 1
    bottom = lat_index == 0
    strip = odd_rim[...].astype(f32)
    paired = even_rim[...].astype(f32)
    south = jnp.where(is_odd, paired, jnp.where(bottom, 0.0, strip))

    wide = strip.shape[0]
    span = members * RIM
    lane = iota((wide, LANES), 1)
    rests = groups * span
    border = ((lane % RIM == 0) & (lane < rests)) | (lane >= rests)
    row_to = iota((wide, wide), 0)
    row_from = iota((wide, wide), 1)
    channel = row_to // GROUP
    mirrored = (channel == row_from // GROUP) & (row_from % GROUP == GROUP - 1 - row_to % GROUP)
    odd_parity = (channel >= noises) & (channel < noises + 2 * levels)
    flip_rows = jnp.where(mirrored, jnp.where(odd_parity, -1.0, 1.0), 0.0).astype(bf16)
    lane_from = iota((LANES, LANES), 0)
    lane_to = iota((LANES, LANES), 1)
    source = (groups - 1 - lane_to // span) * span + lane_to % span + RIM - 1
    moves = (lane_to % RIM == 0) & (lane_to < rests) & (lane_from == source)
    other = lane_to - rests
    source = rests + (groups - 1 - other // members) * members + other % members
    moves = moves | ((other >= 0) & (other < groups * members) & (lane_from == source))
    flip_lanes = jnp.where(moves, 1.0, 0.0).astype(bf16)
    pair = dot(flip_rows, jnp.concatenate([odd_rim[...], own_tail[...]], axis=1)).astype(bf16)
    folded = dot(pair[:, :LANES], flip_lanes)
    ghost = dot(pair[:, LANES:], flip_lanes)
    north = jnp.where(is_odd, strip, paired)
    north_rim = jnp.where(border & top, folded, north)

    for n, message in enumerate((north_rim, strip, ghost, south)):
        after = pltpu.roll(message, LANES - span, 1)
        cut = [message[c * GROUP : (c + 1) * GROUP] for c in range(fields + 1)]
        after = [after[c * GROUP : (c + 1) * GROUP] for c in range(fields + 1)]
        turned[n] = jnp.transpose(window(cut[:fields], after[:fields], cut[fields], after[fields]))
        for g in range(groups):
            for m in range(members):
                gap = (m - 1) % members if n == 3 else m
                start = n * RIM * SUB + gap * chunks + chunks - 1
                gaps[g, pl.ds(start, RIM, stride=SUB), :] = turned[n, pl.ds((g * members + m) * RIM, RIM), :]

    first = [ends.at[0]] + [middle.at[g] for g in range(groups - 2)] + [ends.at[1]]
    in_gap = iota((GAP * SUB, LANES), 0) % chunks == chunks - 1
    for g in range(groups):
        spot = pl.ds((1 + gap_k) * SUB, GAP * SUB)
        kept = first[g][spot, :].astype(f32)
        first[g][spot, :] = jnp.where(in_gap, gaps[g], kept).astype(bf16)
        wrap(first[g], rows)

    hidden = LANES // 4
    per = LANES // hidden
    tiles = odd.shape[0]
    pieces = row_pieces(rows)

    def finish(x, valid):
        used = (valid + per - 1) // per

        @pl.when(top)
        def _():
            strip_top = SUB * (1 + gap_k + STRIP + RIM - 1)
            own_top = SUB * gap_k
            strip_ghost = SUB * (1 + gap_k + GHOST)
            own_ghost = SUB * (1 + gap_k + NORTH)
            last_chunk = iota((SUB, LANES), 0) % chunks == chunks - 1
            spot = iota((SUB, LANES), 1) // hidden
            for src, dst in ((strip_top, own_ghost), (own_top, strip_ghost)):
                found = [x[t, pl.ds(src, SUB), :].astype(f32) for t in range(used)]
                for t in range(used):
                    total = x[t, pl.ds(dst, SUB), :].astype(f32)
                    for i in range(per):
                        lon = valid - 1 - (per * t + i)
                        if lon < 0:
                            continue
                        moved = pltpu.roll(found[lon // per], (hidden * (i - lon % per)) % LANES, 1)
                        total = jnp.where(last_chunk & (spot == i), moved, total)
                    x[t, pl.ds(dst, SUB), :] = total.astype(bf16)

        for t in range(used):
            wrap(x.at[t], rows)

    for x in (odd, even):
        x[tiles - 1] = jnp.zeros(x.shape[1:], bf16)
    even[tiles - 2] = jnp.zeros(even.shape[1:], bf16)

    for b in (0, groups - 1):
        for r, step in pieces:
            parts = [first[b][pl.ds(r + SUB * d, step), :] for d in range(3)]
            put(odd, b, r, activate(dot(jnp.concatenate(parts, axis=1), t1[...])))
    near = (gap_k - 1) * SUB
    for b in range(1, groups - 1):
        parts = []
        for d in range(3):
            some = [first[b][pl.ds(near + SUB * d, rows - near), :], first[b][pl.ds(SUB * d, SUB), :]]
            parts.append(jnp.concatenate(some, axis=0))
        out = activate(dot(jnp.concatenate(parts, axis=1), t1[...]))
        put(odd, b, near, out[: rows - near])
        put(odd, b, 0, out[rows - near :])
    finish(odd, lons + 6)

    width = GROUP * hidden

    def layer(x, y, t, left_over):
        for b in range(groups):
            for r, step in pieces:
                lower = iota((step, LANES), 1) < 2 * hidden

                def cells_of(tile, d):
                    return x[tile, pl.ds(r + SUB * d, step), :]

                def packed(tile):
                    more = [cells_of(tile, d) for d in range(3)]
                    return [
                        jnp.where(lower, more[0], pltpu.roll(more[1], 2 * hidden, 1)),
                        jnp.where(lower, more[2], first[b][pl.ds(r + SUB, step), :]),
                    ]

                if b < groups - 1:
                    parts = [cells_of(2 * b + e, d) for d in range(3) for e in range(2)] + packed(2 * b + 2)
                    matrix = t[...]
                elif left_over == per:
                    parts = [cells_of(2 * b, d) for d in range(3)] + packed(2 * b + 1)
                    lanes = pl.ds(0, LANES)
                    matrix = jnp.concatenate(
                        [t[pl.ds(d * width, LANES), lanes] for d in range(3)]
                        + [t[pl.ds(d * width + LANES, 2 * hidden), lanes] for d in range(3)]
                        + [t[pl.ds(3 * width + 6 * hidden, 2 * hidden), lanes]],
                        axis=0,
                    )
                else:
                    parts = [cells_of(2 * b, d) for d in range(3)] + [first[b][pl.ds(r + SUB, step), :]]
                    lanes = pl.ds(0, LANES)
                    matrix = jnp.concatenate(
                        [t[pl.ds(d * width, LANES), lanes] for d in range(3)]
                        + [jnp.zeros((2 * hidden, LANES), bf16)]
                        + [t[pl.ds(3 * width + 6 * hidden, 2 * hidden), lanes]],
                        axis=0,
                    )
                put(y, b, r, activate(dot(jnp.concatenate(parts, axis=1), matrix)))

    layer(odd, even, t2, per)
    finish(even, lons + 4)
    layer(even, odd, t3, per // 2)
    finish(odd, lons + 2)

    depth = t4.shape[1] // LANES
    padded = rows + 2 * SUB
    for r, long in row_pieces(padded):
        before = iota((long, LANES), 1) < LANES // 2
        span_rows = pl.ds(r, long)
        sides = []
        for side in range(2):
            parts = [odd[side * (depth - 1) + t, span_rows, :] for t in range(depth)]
            sides.append(dot(jnp.concatenate(parts, axis=1), t4[side]))
        force[0, span_rows, :] = jnp.where(before, sides[0][:, :LANES], sides[1][:, :LANES])
        swapped = jnp.where(before, sides[1][:, :LANES], sides[0][:, :LANES])
        force[1, span_rows, :] = pltpu.roll(swapped, LANES // 2, 1)
        force[2, span_rows, :] = jnp.where(before, sides[0][:, LANES:], sides[1][:, LANES:])

    ocean = sea[...].astype(f32)
    narrow = iota((lons, LANES), 1)
    at_south = narrow == 0
    at_north = narrow == LANES - 1
    halves = lons // 2

    def beyond(message, m, c, offset):
        cells = []
        some = slice(c * GROUP, (c + 1) * GROUP)
        for g in range(groups):
            spot = (g * members + m) * RIM + offset
            more = rests + g * members + m
            cells.append(message[some, spot : spot + 1] + message[some, more : more + 1])
        whole = jnp.broadcast_to(jnp.concatenate(cells, axis=0), (lons + GROUP, LANES))
        return pltpu.roll(whole, lons + GROUP - RIM, 0)[:lons]

    for m in range(members):
        for q in range(chunks):
            size = min(blocks, lats - q * blocks)
            total = force[0, pl.ds(m * chunks + q, size, stride=SUB), :]
            for d in range(1, 3):
                total = total + force[d, pl.ds(d * SUB + m * chunks + q, size, stride=SUB), :]
            gathered[m, pl.ds(q * blocks, size), :] = total
        turned_force = jnp.transpose(gathered[m])
        rims = [
            [beyond(message, m, c, offset) for c in range(noises, fields)]
            for message, offset in ((south, RIM - 1), (north_rim, 0))
        ]
        for level in range(levels):
            gains = []
            for (sign, spot), rim in zip(((1.0, at_south), (-1.0, at_north)), rims):
                ru, rv, rh = rim[level], rim[levels + level], rim[2 * levels + level]
                pressure = rim[2 * levels] + rim[2 * levels + 1]
                if level == 1:
                    pressure = pressure + REDUCED * rh
                gains.append(
                    [
                        jnp.where(spot, TIME_STEP * VISCOSITY * ru, 0.0),
                        jnp.where(spot, TIME_STEP * (VISCOSITY * rv + sign * 0.5 * pressure), 0.0),
                        jnp.where(spot, TIME_STEP * sign * 0.5 * (rh * rv), 0.0),
                    ]
                )
            middle = [jnp.zeros((lons, lats - 2 * LANES), f32)] if lats > 2 * LANES else []
            gains = [jnp.concatenate([gains[0][n]] + middle + [gains[1][n]], axis=1) for n in range(3)]

            def push(c):
                parts = [
                    turned_force[side * LANES // 2 + c * halves : side * LANES // 2 + (c + 1) * halves]
                    for side in range(2)
                ]
                return TIME_STEP * (jnp.concatenate(parts, axis=0) + bias_last[c])

            results[0, m, level] = base[0, m, level] + ocean * (gains[0] + push(level))
            results[1, m, level] = base[1, m, level] + ocean * (gains[1] + push(levels + level))
            results[2, m, level] = base[2, m, level] + gains[2]
        for n, out in enumerate((new_u, new_v, new_h)):
            pltpu.make_async_copy(results.at[n, m], out.at[m], done.at[n, m]).start()
    for m in range(members):
        for n, out in enumerate((new_u, new_v, new_h)):
            pltpu.make_async_copy(results.at[n, m], out.at[m], done.at[n, m]).wait()


def body(
    noise,
    velocity_u,
    velocity_v,
    thickness,
    land_sea,
    conv_first,
    bias_first,
    conv_second,
    bias_second,
    conv_third,
    bias_third,
    conv_last,
    bias_last,
):
    members, noises, lons, lats = noise.shape
    levels = velocity_u.shape[1]
    fields = noises + 3 * levels
    sizes = (members, noises, levels)
    hidden = conv_first.shape[0]
    outs = conv_last.shape[0]
    groups = lons // GROUP + 1
    rows = members * (lats + GAP)
    assert hidden * 4 == LANES and outs * lons == LANES and members * (RIM + 1) * groups <= LANES
    assert fields % 2 == 0 and 4 * -(-fields // 4) == 12 and GROUP * (fields + 6) == LANES and lons % 16 == 0
    assert lats % LANES == 0 and SUB % members == 0 and (lats + GAP) % (SUB // members) == 0
    lon_count, lat_count = lax.axis_size("lon"), lax.axis_size("lat")
    assert lon_count % 2 == 0 and lat_count % 2 == 0
    state = (noise, velocity_u, velocity_v, thickness, land_sea)
    whole = pl.BlockSpec(memory_space=pltpu.VMEM)

    tall = members * fields * RIM + GROUP + members * 3 * levels
    assert tall % SUB == 0
    args = state + (
        conv_first.transpose(1, 2, 3, 0),
        conv_second.transpose(2, 3, 0, 1),
        conv_third.transpose(2, 3, 0, 1),
        conv_last.transpose(2, 3, 0, 1),
        bias_first[None],
        bias_second[None],
        bias_third[None],
    )
    count = len(args)
    *held, to_even, to_odd = pl.pallas_call(
        functools.partial(pack_lon_kernel, sizes, count),
        out_shape=[pltpu.VMEM(x.shape, x.dtype) for x in args] + [pltpu.VMEM((tall, lats), bf16)] * 2,
        in_specs=[pl.BlockSpec(memory_space=pltpu.HBM)] * count,
        out_specs=[whole] * (count + 2),
        scratch_shapes=[pltpu.VMEM((2, tall, lats), f32), pltpu.SemaphoreType.DMA((count,))],
        compiler_params=pltpu.CompilerParams(vmem_limit_bytes=62 * 2**20),
        name="pack_lon",
    )(*args)
    state = tuple(held[:5])
    lon_even = lax.ppermute(to_even, "lon", [(i, i ^ 1) for i in range(lon_count)])
    lon_odd = lax.ppermute(to_odd, "lon", [(i, (i - 1 + 2 * (i % 2)) % lon_count) for i in range(lon_count)])

    wide = -(-(fields + 1) * GROUP // SUB) * SUB
    part = pltpu.VMEM((wide, LANES), f32)
    message = pltpu.VMEM((wide, LANES), bf16)
    deep = -(-(lons // 2 + 2) * hidden // LANES) * LANES
    padded = rows + 2 * SUB
    tiles = 2 * groups + 1
    t1, t2, t3, t4, own_head, own_tail, middle, pre = pl.pallas_call(
        functools.partial(prepare_kernel, sizes),
        out_shape=[
            pltpu.VMEM((3 * LANES, 2 * LANES), bf16),
            pltpu.VMEM((8 * LANES, 2 * LANES), bf16),
            pltpu.VMEM((8 * LANES, 2 * LANES), bf16),
            pltpu.VMEM((2, deep, 2 * LANES), bf16),
            part,
            part,
            pltpu.VMEM((groups - 2, padded, LANES), bf16),
            pltpu.VMEM((tiles, padded, LANES), bf16),
        ],
        in_specs=[whole] * count,
        out_specs=[whole] * 8,
        scratch_shapes=[
            pltpu.VMEM((groups - 2, rows, LANES), f32),
            pltpu.VMEM((members * (groups - 2) * lats // LANES, LANES, LANES), f32),
        ],
        compiler_params=pltpu.CompilerParams(vmem_limit_bytes=12 * 2**20),
        cost_estimate=pl.CostEstimate(flops=10**7, bytes_accessed=10**7, transcendentals=0),
        name="prepare",
    )(*held)
    last = lat_count - 1
    smem = pl.BlockSpec(memory_space=pltpu.SMEM)
    to_even, to_odd = pl.pallas_call(
        functools.partial(join_kernel, sizes, lons),
        out_shape=[message] * 2,
        in_specs=[whole] * 4,
        out_specs=[whole] * 2,
        scratch_shapes=[
            pltpu.VMEM((2, 2, tall, LANES), f32),
            pltpu.VMEM((2, wide, LANES), f32),
        ],
        compiler_params=pltpu.CompilerParams(vmem_limit_bytes=4 * 2**20),
        name="join_rims",
    )(lon_even, lon_odd, own_head, own_tail)
    even_rim = lax.ppermute(to_even, "lat", [(i, i ^ 1) for i in range(lat_count)])
    pairs = []
    for t in range(lon_count):
        at = t * lat_count
        pairs += [(at + k, at + k - 1 + 2 * (k % 2)) for k in range(1, last)]
        pairs += [(at, (t ^ 1) * lat_count), (at + last, (lon_count - 1 - t) * lat_count + last)]
    odd_rim = lax.ppermute(to_odd, ("lon", "lat"), pairs)

    ends, base = pl.pallas_call(
        functools.partial(cells_kernel, sizes),
        out_shape=[pltpu.VMEM((2, padded, LANES), bf16), pltpu.VMEM((3, *velocity_u.shape), f32)],
        in_specs=[whole] * 8,
        out_specs=[whole] * 2,
        scratch_shapes=[
            pltpu.VMEM((2, tall, lats), f32),
            pltpu.VMEM((2, rows, LANES), f32),
            pltpu.VMEM((2 * members * lats // LANES, LANES, LANES), f32),
        ],
        compiler_params=pltpu.CompilerParams(vmem_limit_bytes=12 * 2**20),
        cost_estimate=pl.CostEstimate(flops=10**7, bytes_accessed=10**7, transcendentals=0),
        name="cells",
    )(*state, lon_even, lon_odd, to_even)

    out = jax.ShapeDtypeStruct(velocity_u.shape, f32)
    return pl.pallas_call(
        functools.partial(main_kernel, sizes),
        out_shape=[out] * 3 + [pltpu.VMEM(x.shape, x.dtype) for x in (middle, ends, pre)],
        in_specs=[smem] + [whole] * 12,
        out_specs=[pl.BlockSpec(memory_space=pltpu.HBM)] * 3 + [whole] * 3,
        input_output_aliases={1: 3, 2: 4, 3: 5},
        scratch_shapes=[
            pltpu.VMEM((tiles, padded, LANES), bf16),
            pltpu.VMEM((3, padded, LANES), f32),
            pltpu.VMEM((members, lats, LANES), f32),
            pltpu.VMEM((4, LANES, LANES), f32),
            pltpu.VMEM((groups, GAP * SUB, LANES), f32),
            pltpu.VMEM((3, *velocity_u.shape), f32),
            pltpu.SemaphoreType.DMA((3, members)),
        ],
        compiler_params=pltpu.CompilerParams(vmem_limit_bytes=32 * 2**20),
        cost_estimate=pl.CostEstimate(flops=2 * 10**10, bytes_accessed=10**7, transcendentals=4 * 10**6),
        name="network_and_step",
    )(
        bias_last,
        middle,
        ends,
        pre,
        base,
        state[4],
        even_rim,
        odd_rim,
        to_odd,
        t1,
        t2,
        t3,
        t4,
    )[:3]


def solution(mesh):
    tiles = P(None, None, "lon", "lat")
    return jax.shard_map(
        body,
        mesh=mesh,
        in_specs=(tiles,) * 4 + (P("lon", "lat"),) + (P(),) * 8,
        out_specs=(tiles,) * 3,
        check_vma=False,
    )
```

```python
import functools

import jax
import jax.numpy as jnp
from jax import lax
from jax.experimental import pallas as pl
from jax.experimental.pallas import tpu as pltpu
from jax.sharding import PartitionSpec as P

REDUCED = 0.5
TIME_STEP = 0.2
VISCOSITY = 0.05
CORIOLIS = 0.4

RIM = 4
GAP = 16
NORTH, STRIP, GHOST, SOUTH = 0, 4, 8, 12
SUB = 16
LANES = 128
GROUP = 8
LAND = 2.0**100

f32 = jnp.float32
bf16 = jnp.bfloat16


def iota(shape, dim):
    return lax.broadcasted_iota(jnp.int32, shape, dim)


def dot(a, b):
    return jnp.dot(a, b, preferred_element_type=f32)


def rest(x):
    return x - x.astype(bf16).astype(f32)


def pack_lon_kernel(sizes, count, *refs):
    sources, held, (even, odd, wide, done) = refs[:count], refs[count : 2 * count], refs[2 * count :]
    members, noises, levels = sizes
    fields = noises + 3 * levels
    noise, u, v, h, sea = held[:5]
    lons, lats = sea.shape
    copies = [pltpu.make_async_copy(x, y, done.at[n]) for n, (x, y) in enumerate(zip(sources, held))]
    for copy in copies:
        copy.start()
    for copy in copies[:5]:
        copy.wait()
    upper = iota((GROUP, lats), 0) < RIM

    def field(m, c, side):
        if c < noises:
            full = noise[m, c].astype(f32)
            return full[-GROUP:] if side else full[:GROUP]
        c -= noises
        return (u, v, h)[c // levels][m, c % levels, pl.ds(side * (lons - GROUP), GROUP)]

    rests = members * fields * RIM + GROUP
    for m in range(members):
        for c in range(0, fields, 2):
            rows = pl.ds((m * fields + c) * RIM, GROUP)
            wide[0, rows] = jnp.where(upper, field(m, c, 0), pltpu.roll(field(m, c + 1, 0), RIM, 0))
            wide[1, rows] = jnp.where(upper, pltpu.roll(field(m, c, 1), RIM, 0), field(m, c + 1, 1))
        for c in range(noises, fields):
            row = pl.ds(rests + m * (fields - noises) + c - noises, 1)
            wide[0, row] = rest(field(m, c, 0)[:1])
            wide[1, row] = rest(field(m, c, 1)[GROUP - 1 :])
    rows = pl.ds(members * fields * RIM, GROUP)
    ends = [sea[pl.ds(side * (lons - GROUP), GROUP)].astype(f32) for side in range(2)]
    wide[0, rows] = jnp.where(upper, ends[0], 0.0)
    wide[1, rows] = jnp.where(upper, pltpu.roll(ends[1], RIM, 0), 0.0)
    is_odd = lax.axis_index("lon") % 2 == 1
    even[...] = jnp.where(is_odd, wide[0], wide[1]).astype(bf16)
    odd[...] = jnp.where(is_odd, wide[1], wide[0]).astype(bf16)
    for copy in copies[5:]:
        copy.wait()


def lon_rims(even, odd, lanes=slice(None)):
    is_odd = lax.axis_index("lon") % 2 == 1
    a, b = even[:, lanes].astype(f32), odd[:, lanes].astype(f32)
    return jnp.where(is_odd, a, b), jnp.where(is_odd, b, a)


def rim_tile(sizes, m, c, side, rim):
    members, noises, levels = sizes
    fields = noises + 3 * levels
    if c < fields:
        start = m * (fields * RIM) + c * RIM // GROUP * GROUP
    else:
        start = members * fields * RIM
    tile = rim[pl.ds(pl.multiple_of(start, GROUP), GROUP)]
    if (c if c < fields else 0) % 2 == side:
        return tile
    return pltpu.roll(tile, RIM, 0)


def window(tiles, following, mask, next_mask):
    pair = iota(mask.shape, 0) // 2
    zero = jnp.zeros_like(mask)
    more = []
    for start in range(0, len(tiles), 4):
        total = zero
        for n in range(min(4, len(tiles) - start)):
            moved = pltpu.roll(following[start + n], 2 * n, 0) if n else following[start]
            total = jnp.where(pair == n, moved, total)
        more.append(total)
    return jnp.concatenate(
        tiles + more + [mask - 1.0, next_mask - 1.0, jnp.ones_like(mask)], axis=0
    )


def store_lats(block, t, dst, tile, m, lats, chunks, buffer):
    blocks = (lats + GAP) // chunks
    buffer[...] = jnp.transpose(block)
    for q in range(chunks):
        lo = max(q * blocks, t * LANES)
        hi = min((q + 1) * blocks, (t + 1) * LANES, lats)
        if lo < hi:
            start = (lo - q * blocks) * SUB + m * chunks + q
            dst[tile, pl.ds(start, hi - lo, stride=SUB), :] = buffer[pl.ds(lo - t * LANES, hi - lo), :]


def shifted_tiles(sizes, refs, m, c, t):
    noise, u, v, h, sea = refs
    members, noises, levels = sizes
    fields = noises + 3 * levels
    lons = sea.shape[0]
    lanes = slice(t * LANES, (t + 1) * LANES)
    if c == fields:
        full = sea[:, lanes].astype(f32)
    elif c < noises:
        full = noise[m, c, :, lanes].astype(f32)
    else:
        full = (u, v, h)[(c - noises) // levels][m, (c - noises) % levels, :, lanes]
    full = pltpu.roll(full, lons - RIM, 0)
    tiles = [full[g * GROUP : (g + 1) * GROUP] for g in range(lons // GROUP)]
    return tiles[-1:] + tiles


def prepare_kernel(sizes, noise, u, v, h, sea, *refs):
    weights, matrices, (head, tail, middle, pre, cells, turned) = refs[:7], refs[7:11], refs[11:]
    held = (noise, u, v, h, sea)
    members, noises, levels = sizes
    fields = noises + 3 * levels
    lons, lats = sea.shape
    groups = lons // GROUP + 1
    weights_kernel(*weights, *matrices)
    lane = iota((GROUP, LANES), 1)
    zero = jnp.zeros((GROUP, LANES), f32)
    for out, t, first in ((head, 0, 0), (tail, lats // LANES - 1, LANES - RIM)):
        edge = 0 if first == 0 else LANES - 1

        def add_member(m, totals):
            totals = list(totals)
            for c in range(fields + 1):
                for g, tile in enumerate(shifted_tiles(sizes, held, m, c, t)):
                    place = (g * members + m) * RIM
                    moved = pltpu.roll(tile, lax.rem(place + LANES - first, LANES), 1)
                    totals[c] = jnp.where((lane >= place) & (lane < place + RIM), moved, totals[c])
                    if noises <= c < fields:
                        place = groups * members * RIM + g * members + m
                        moved = pltpu.roll(rest(tile), lax.rem(place + LANES - edge, LANES), 1)
                        totals[c] = jnp.where(lane == place, moved, totals[c])
            return tuple(totals)

        totals = lax.fori_loop(0, members, add_member, (zero,) * (fields + 1))
        for c in range(out.shape[0] // GROUP):
            out[pl.ds(c * GROUP, GROUP)] = totals[c] if c < len(totals) else zero
    chunks = SUB // members
    rows = cells.shape[1]
    gap_k = lats - (chunks - 1) * ((lats + GAP) // chunks)
    inner = groups - 2
    for m in range(members):
        for g in range(inner):
            empty = pl.ds(gap_k * SUB + (m + 1) * chunks - 1, GAP, stride=SUB)
            cells[g, empty, :] = jnp.zeros((GAP, LANES), f32)
    for t in range(lats // LANES):

        def lay_out(m, carry):
            tiles = [shifted_tiles(sizes, held, m, c, t) for c in range(fields + 1)]
            for g in range(1, inner + 1):
                following = [x[g + 1] for x in tiles]
                block = window([x[g] for x in tiles[:fields]], following[:fields], tiles[fields][g], following[fields])
                store_lats(block, t, cells, g - 1, m, lats, chunks, turned.at[g - 1])
            return carry

        lax.fori_loop(0, members, lay_out, 0)
    for g in range(inner):
        middle[g + 1, pl.ds(SUB, rows), :] = cells[g].astype(bf16)
        wrap(middle.at[g + 1], rows)

    def first_layer(g, carry):
        for r, step in row_pieces(rows):
            parts = [middle[g, pl.ds(r + SUB * d, step), :] for d in range(3)]
            put(pre, g, r, activate(dot(jnp.concatenate(parts, axis=1), matrices[0][...])))
        return carry

    lax.fori_loop(1, inner + 1, first_layer, 0)


def row_pieces(rows):
    half = rows // 2 // SUB * SUB
    return [(0, half), (half, rows - half)]


def activate(pre):
    return (pre * jnp.tanh(pre) + pre).astype(bf16)


def put(y, b, r, out):
    for e in range(out.shape[1] // LANES):
        y[2 * b + e, pl.ds(SUB + r, out.shape[0]), :] = out[:, e * LANES : (e + 1) * LANES]


def wrap(x, rows):
    end = x[pl.ds(rows, SUB), :].astype(f32)
    x[pl.ds(0, SUB), :] = pltpu.roll(end, 1, 0).astype(bf16)
    begin = x[pl.ds(SUB, SUB), :].astype(f32)
    x[pl.ds(SUB + rows, SUB), :] = pltpu.roll(begin, SUB - 1, 0).astype(bf16)


def cells_kernel(sizes, noise, u, v, h, sea, lon_even, lon_odd, after, given, out, base, rims, cells, turned):
    members, noises, levels = sizes
    fields = noises + 3 * levels
    lons, lats = sea.shape
    groups = lons // GROUP + 1
    chunks = SUB // members
    rows = cells.shape[1]
    gap_k = lats - (chunks - 1) * ((lats + GAP) // chunks)
    rims[0], rims[1] = lon_rims(lon_even, lon_odd)
    for m in range(members):
        for side in range(2):
            empty = pl.ds(gap_k * SUB + (m + 1) * chunks - 1, GAP, stride=SUB)
            cells[side, empty, :] = jnp.zeros((GAP, LANES), f32)
    blank = jnp.zeros((GROUP, LANES), f32)
    upper = iota((GROUP, LANES), 0) < RIM
    for t in range(lats // LANES):
        lanes = slice(t * LANES, (t + 1) * LANES)

        def lay_out(m, carry):
            tiles = []
            for c in range(fields + 1):
                groups_of = shifted_tiles(sizes, (noise, u, v, h, sea), m, c, t)
                ends = [rim_tile(sizes, m, c, side, rims.at[side, :, lanes]) for side in range(2)]
                groups_of[0] = jnp.where(upper, ends[0], groups_of[0])
                groups_of[-1] = jnp.where(upper, groups_of[-1], ends[1])
                tiles.append(groups_of)
            for side, g in enumerate((0, groups - 1)):
                following = [x[g + 1] if g + 1 < groups else blank for x in tiles]
                block = window([x[g] for x in tiles[:fields]], following[:fields], tiles[fields][g], following[fields])
                store_lats(block, t, cells, side, m, lats, chunks, turned.at[side])
            return carry

        lax.fori_loop(0, members, lay_out, 0)
    for side, g in enumerate((0, groups - 1)):
        out[g, pl.ds(SUB, rows), :] = cells[side].astype(bf16)
    step_kernel(sizes, u, v, h, sea, rims, base)


def step_kernel(sizes, u, v, h, sea, rims, base):
    members, noises, levels = sizes
    fields = noises + 3 * levels
    lons, lats = sea.shape
    ocean = sea[...].astype(f32)
    lat_count = lax.axis_size("lat")
    lat_rows = (lax.axis_index("lat") * lats).astype(f32) + iota((lons, lats), 1).astype(f32)
    turn = CORIOLIS * (2.0 * (lat_rows + 0.5) / (lats * lat_count) - 1.0)
    at_first = iota((lons, lats), 0) == 0
    at_last = iota((lons, lats), 0) == lons - 1
    at_south = iota((lons, lats), 1) == 0
    at_north = iota((lons, lats), 1) == lats - 1
    lon_rests = members * fields * RIM + GROUP

    def around(x, m, c):
        row = (m * fields + c) * RIM
        more = lon_rests + m * (fields - noises) + c - noises
        west = rims[0, pl.ds(row + RIM - 1, 1)] + rims[0, pl.ds(more, 1)]
        east = rims[1, pl.ds(row, 1)] + rims[1, pl.ds(more, 1)]
        return (
            jnp.where(at_first, west, pltpu.roll(x, 1, 0)),
            jnp.where(at_last, east, pltpu.roll(x, lons - 1, 0)),
            jnp.where(at_south, 0.0, pltpu.roll(x, 1, 1)),
            jnp.where(at_north, 0.0, pltpu.roll(x, lats - 1, 1)),
        )

    def member(m, carry):
        sets = []
        for level in range(levels):
            sets.append(
                [
                    (x[m, level], around(x[m, level], m, noises + n * levels + level))
                    for n, x in enumerate((u, v, h))
                ]
            )
        for level in range(levels):
            (cu, au), (cv, av), (ch, ah) = sets[level]
            upper, lower = sets[0][2][1], sets[1][2][1]
            pressure = [upper[i] + lower[i] for i in range(4)]
            if level == 1:
                pressure = [pressure[i] + REDUCED * lower[i] for i in range(4)]
            lap_u = au[1] + au[0] + au[3] + au[2] - 4.0 * cu
            lap_v = av[1] + av[0] + av[3] + av[2] - 4.0 * cv
            dx = 0.5 * (pressure[1] - pressure[0])
            dy = 0.5 * (pressure[3] - pressure[2])
            base[0, m, level] = ocean * (cu + TIME_STEP * (turn * cv - dx + VISCOSITY * lap_u))
            base[1, m, level] = ocean * (cv + TIME_STEP * (-turn * cu - dy + VISCOSITY * lap_v))
            flow = 0.5 * (ah[1] * au[1] - ah[0] * au[0]) + 0.5 * (ah[3] * av[3] - ah[2] * av[2])
            base[2, m, level] = ch - TIME_STEP * flow
        return carry

    lax.fori_loop(0, members, member, 0)


def join_kernel(sizes, lons, lon_even, lon_odd, head, tail, even, odd, rims, wide):
    members, noises, levels = sizes
    fields = noises + 3 * levels
    groups = lons // GROUP + 1
    lats = lon_even.shape[1]
    for n, lanes in enumerate((slice(0, LANES), slice(lats - LANES, lats))):
        rims[0, n], rims[1, n] = lon_rims(lon_even, lon_odd, lanes)
    lane = iota((GROUP, LANES), 1)
    upper = iota((GROUP, LANES), 0) < RIM
    to_south = lax.axis_index("lat") % 2 == 1
    for c in range(fields + 1):
        rows = pl.ds(c * GROUP, GROUP)
        ends = []
        for n, (part, first) in enumerate(((head, 0), (tail, LANES - RIM))):
            total = part[rows]
            for side in range(2):
                held = upper if side == 0 else ~upper
                for m in range(members):
                    place = ((groups - 1) * side * members + m) * RIM
                    tile = rim_tile(sizes, m, c, side, rims.at[side, n])
                    moved = pltpu.roll(tile, (place - first) % LANES, 1)
                    total = jnp.where(held & (lane >= place) & (lane < place + RIM), moved, total)
            ends.append(total)
        wide[0, rows] = jnp.where(to_south, ends[0], ends[1])
        wide[1, rows] = jnp.where(to_south, ends[1], ends[0])
    rows = pl.ds((fields + 1) * GROUP, wide.shape[1] - (fields + 1) * GROUP)
    wide[:, rows] = jnp.zeros((2, wide.shape[1] - (fields + 1) * GROUP, LANES), f32)
    even[...] = wide[0].astype(bf16)
    odd[...] = wide[1].astype(bf16)


def weights_kernel(w1, w2, w3, w4, bias1, bias2, bias3, t1, t2, t3, t4):
    hidden = w2.shape[2]
    per = LANES // hidden
    lane = iota((hidden, LANES), 1)
    fields = w1.shape[0]
    out_lon = iota((GROUP, LANES), 1) // hidden
    in_row = iota((GROUP, LANES), 0)
    bias_row = iota((GROUP, LANES), 0)

    def bias_rows(layer):
        part = 0.5 * jnp.concatenate([(bias1, bias2, bias3)[layer][...]] * per, axis=1)
        b1 = part.astype(bf16).astype(f32)
        b2 = (part - b1).astype(bf16).astype(f32)
        b3 = part - b1 - b2
        zero = jnp.zeros((GROUP, LANES), f32)
        return jnp.where(
            bias_row == 0,
            b1,
            jnp.where(bias_row == 1, b2, jnp.where(bias_row == 2, b3, zero)),
        )

    def sea_rows(shift, tile):
        lon = iota((2 * GROUP, LANES), 0)
        out = iota((2 * GROUP, LANES), 1) // hidden + per * tile
        return jnp.where(lon == out + shift, LAND, 0.0)

    for dj in range(3):
        taps = []
        for di in range(3):
            cells = [w1[c, di].astype(f32)[dj : dj + 1] for c in range(fields)]
            taps.append(
                [jnp.broadcast_to(0.5 * jnp.concatenate([x] * per, axis=1), (GROUP, LANES)) for x in cells]
            )
        for tile in range(2):
            parts = []
            for c in range(fields):
                total = jnp.zeros((GROUP, LANES), f32)
                for di in range(3):
                    hit = in_row == out_lon + per * tile + di
                    total = jnp.where(hit, taps[di][c], total)
                parts.append(total)
            for start in range(0, fields, 4):
                total = jnp.zeros((GROUP, LANES), f32)
                for n in range(min(4, fields - start)):
                    for di in range(3):
                        hit = in_row % 2 + GROUP == out_lon + per * tile + di
                        total = jnp.where(hit & (in_row // 2 == n), taps[di][start + n], total)
                parts.append(total)
            if dj == 1:
                parts += [sea_rows(1, tile), bias_rows(0)]
            else:
                parts.append(jnp.zeros((3 * GROUP, LANES), f32))
            block = jnp.concatenate(parts, axis=0)
            t1[pl.ds(dj * LANES, LANES), pl.ds(tile * LANES, LANES)] = block.astype(bf16)

    for layer, (w, t) in enumerate(((w2, t2), (w3, t3))):
        for dj in range(3):
            taps = []
            for di in range(3):
                cell = 0.5 * w[di, dj].astype(f32)
                wide = jnp.concatenate([cell, jnp.zeros((hidden, LANES - hidden), f32)], axis=1)
                square = jnp.concatenate([wide] * per, axis=0)
                taps.append(jnp.transpose(square)[:hidden])
            for lon in range(GROUP + 2):
                for tile in range(2):
                    total = jnp.zeros((hidden, LANES), f32)
                    for di in range(3):
                        total = jnp.where(lane // hidden + per * tile == lon - di, taps[di], total)
                    if lon < GROUP:
                        row = dj * GROUP * hidden + lon * hidden
                    else:
                        row = 3 * GROUP * hidden + dj * 2 * hidden + (lon - GROUP) * hidden
                    t[pl.ds(row, hidden), pl.ds(tile * LANES, LANES)] = total.astype(bf16)
        for tile in range(2):
            block = jnp.concatenate(
                [
                    jnp.zeros((5 * GROUP, LANES), f32),
                    sea_rows(2 + layer, tile),
                    bias_rows(1 + layer),
                ],
                axis=0,
            )
            row = 3 * GROUP * hidden + 6 * hidden
            t[pl.ds(row, 2 * hidden), pl.ds(tile * LANES, LANES)] = block.astype(bf16)

    outs = w4.shape[2]
    half = LANES // 2
    lons = half // outs
    slot = iota((hidden, LANES), 1) // half
    out_lon = iota((hidden, LANES), 1) % lons
    taps = {}
    for dj in range(3):
        for di in range(3):
            cell = w4[di, dj].astype(f32)
            wide = jnp.concatenate([cell, jnp.zeros((outs, LANES - hidden), f32)], axis=1)
            square = jnp.concatenate(
                [jnp.broadcast_to(wide[c : c + 1], (lons, LANES)) for c in range(outs)] * 2, axis=0
            )
            taps[dj, di] = jnp.transpose(square)[:hidden]
    order = ((0, 1, 2, None), (1, 0, None, 2))
    for side in range(2):
        for lon in range(t4.shape[1] // hidden):
            for tile in range(2):
                total = jnp.zeros((hidden, LANES), f32)
                for place in range(2):
                    dj = order[side][2 * tile + place]
                    if dj is None:
                        continue
                    for di in range(3):
                        total = jnp.where((slot == place) & (out_lon == lon - di), taps[dj, di], total)
                t4[side, pl.ds(lon * hidden, hidden), pl.ds(tile * LANES, LANES)] = total.astype(bf16)


def main_kernel(
    sizes,
    bias_last,
    first_in,
    pre_in,
    base,
    sea,
    even_rim,
    odd_rim,
    own_tail,
    t1,
    t2,
    t3,
    t4,
    new_u,
    new_v,
    new_h,
    first,
    odd,
    even,
    force,
    gathered,
    turned,
    gaps,
    messages,
    results,
    done,
):
    members, noises, levels = sizes
    fields = noises + 3 * levels
    lons, lats = sea.shape
    groups = lons // GROUP + 1
    chunks = SUB // members
    blocks = (lats + GAP) // chunks
    rows = blocks * SUB
    gap_k = lats - (chunks - 1) * blocks
    lat_index, lat_count = lax.axis_index("lat"), lax.axis_size("lat")
    top = lat_index == lat_count - 1
    is_odd = lat_index % 2 == 1
    bottom = lat_index == 0
    strip = odd_rim[...].astype(f32)
    paired = even_rim[...].astype(f32)
    south = jnp.where(is_odd, paired, jnp.where(bottom, 0.0, strip))

    wide = strip.shape[0]
    span = members * RIM
    lane = iota((wide, LANES), 1)
    rests = groups * span
    border = ((lane % RIM == 0) & (lane < rests)) | (lane >= rests)
    row_to = iota((wide, wide), 0)
    row_from = iota((wide, wide), 1)
    channel = row_to // GROUP
    mirrored = (channel == row_from // GROUP) & (row_from % GROUP == GROUP - 1 - row_to % GROUP)
    odd_parity = (channel >= noises) & (channel < noises + 2 * levels)
    flip_rows = jnp.where(mirrored, jnp.where(odd_parity, -1.0, 1.0), 0.0).astype(bf16)
    lane_from = iota((LANES, LANES), 0)
    lane_to = iota((LANES, LANES), 1)
    source = (groups - 1 - lane_to // span) * span + lane_to % span + RIM - 1
    moves = (lane_to % RIM == 0) & (lane_to < rests) & (lane_from == source)
    other = lane_to - rests
    source = rests + (groups - 1 - other // members) * members + other % members
    moves = moves | ((other >= 0) & (other < groups * members) & (lane_from == source))
    flip_lanes = jnp.where(moves, 1.0, 0.0).astype(bf16)
    pair = dot(flip_rows, jnp.concatenate([odd_rim[...], own_tail[...]], axis=1)).astype(bf16)
    folded = dot(pair[:, :LANES], flip_lanes)
    ghost = dot(pair[:, LANES:], flip_lanes)
    north = jnp.where(is_odd, strip, paired)
    north_rim = jnp.where(border & top, folded, north)

    for n, message in enumerate((north_rim, strip, ghost, south)):
        messages[n] = message

    def lay_out(n, carry):
        message = messages[n]
        after = pltpu.roll(message, LANES - span, 1)
        cut = [message[c * GROUP : (c + 1) * GROUP] for c in range(fields + 1)]
        after = [after[c * GROUP : (c + 1) * GROUP] for c in range(fields + 1)]
        turned[...] = jnp.transpose(window(cut[:fields], after[:fields], cut[fields], after[fields]))
        for g in range(groups):
            for m in range(members):
                gap = jnp.where(n == 3, (m - 1) % members, m)
                start = n * (RIM * SUB) + gap * chunks + chunks - 1
                gaps[g, pl.ds(start, RIM, stride=SUB), :] = turned[pl.ds((g * members + m) * RIM, RIM), :]
        return carry

    lax.fori_loop(0, 4, lay_out, 0)

    in_gap = iota((GAP * SUB, LANES), 0) % chunks == chunks - 1

    def fill_gap(g, carry):
        spot = pl.ds((1 + gap_k) * SUB, GAP * SUB)
        kept = first[g, spot, :].astype(f32)
        first[g, spot, :] = jnp.where(in_gap, gaps[g], kept).astype(bf16)
        wrap(first.at[g], rows)
        return carry

    lax.fori_loop(0, groups, fill_gap, 0)

    hidden = LANES // 4
    per = LANES // hidden
    tiles = odd.shape[0]
    pieces = row_pieces(rows)

    def finish(x, valid):
        used = (valid + per - 1) // per

        @pl.when(top)
        def _():
            strip_top = SUB * (1 + gap_k + STRIP + RIM - 1)
            own_top = SUB * gap_k
            strip_ghost = SUB * (1 + gap_k + GHOST)
            own_ghost = SUB * (1 + gap_k + NORTH)
            last_chunk = iota((SUB, LANES), 0) % chunks == chunks - 1
            spot = iota((SUB, LANES), 1) // hidden
            edge = (valid - 1) % per

            def turn_tile(t, carry):
                high = (valid - 1) // per - t
                low = jnp.maximum(high - 1, 0)
                for src, dst in ((strip_top, own_ghost), (own_top, strip_ghost)):
                    found = [x[n, pl.ds(src, SUB), :].astype(f32) for n in (high, low)]
                    total = x[t, pl.ds(dst, SUB), :].astype(f32)
                    for i in range(per):
                        lon = edge - i
                        moved = pltpu.roll(found[0 if lon >= 0 else 1], (hidden * (i - lon % per)) % LANES, 1)
                        total = jnp.where(last_chunk & (spot == i), moved, total)
                    x[t, pl.ds(dst, SUB), :] = total.astype(bf16)
                return carry

            lax.fori_loop(0, used, turn_tile, 0)

        def wrap_tile(t, carry):
            wrap(x.at[t], rows)
            return carry

        lax.fori_loop(0, used, wrap_tile, 0)

    for x in (odd, even):
        x[tiles - 1] = jnp.zeros(x.shape[1:], bf16)
    even[tiles - 2] = jnp.zeros(even.shape[1:], bf16)

    def first_ends(side, carry):
        b = side * (groups - 1)
        for r, step in pieces:
            parts = [first[b, pl.ds(r + SUB * d, step), :] for d in range(3)]
            put(odd, b, r, activate(dot(jnp.concatenate(parts, axis=1), t1[...])))
        return carry

    lax.fori_loop(0, 2, first_ends, 0)
    near = (gap_k - 1) * SUB

    def first_middle(b, carry):
        parts = []
        for d in range(3):
            some = [first[b, pl.ds(near + SUB * d, rows - near), :], first[b, pl.ds(SUB * d, SUB), :]]
            parts.append(jnp.concatenate(some, axis=0))
        out = activate(dot(jnp.concatenate(parts, axis=1), t1[...]))
        put(odd, b, near, out[: rows - near])
        put(odd, b, 0, out[rows - near :])
        return carry

    lax.fori_loop(1, groups - 1, first_middle, 0)
    finish(odd, lons + 6)

    width = GROUP * hidden

    def layer(x, y, t, left_over):
        def block(b, last=False):
            for r, step in pieces:
                lower = iota((step, LANES), 1) < 2 * hidden

                def cells_of(tile, d):
                    return x[tile, pl.ds(r + SUB * d, step), :]

                def packed(tile):
                    more = [cells_of(tile, d) for d in range(3)]
                    return [
                        jnp.where(lower, more[0], pltpu.roll(more[1], 2 * hidden, 1)),
                        jnp.where(lower, more[2], first[b, pl.ds(r + SUB, step), :]),
                    ]

                if not last:
                    parts = [cells_of(2 * b + e, d) for d in range(3) for e in range(2)] + packed(2 * b + 2)
                    matrix = t[...]
                elif left_over == per:
                    parts = [cells_of(2 * b, d) for d in range(3)] + packed(2 * b + 1)
                    lanes = pl.ds(0, LANES)
                    matrix = jnp.concatenate(
                        [t[pl.ds(d * width, LANES), lanes] for d in range(3)]
                        + [t[pl.ds(d * width + LANES, 2 * hidden), lanes] for d in range(3)]
                        + [t[pl.ds(3 * width + 6 * hidden, 2 * hidden), lanes]],
                        axis=0,
                    )
                else:
                    parts = [cells_of(2 * b, d) for d in range(3)] + [first[b, pl.ds(r + SUB, step), :]]
                    lanes = pl.ds(0, LANES)
                    matrix = jnp.concatenate(
                        [t[pl.ds(d * width, LANES), lanes] for d in range(3)]
                        + [jnp.zeros((2 * hidden, LANES), bf16)]
                        + [t[pl.ds(3 * width + 6 * hidden, 2 * hidden), lanes]],
                        axis=0,
                    )
                put(y, b, r, activate(dot(jnp.concatenate(parts, axis=1), matrix)))

        def turn(b, carry):
            block(b)
            return carry

        lax.fori_loop(0, groups - 1, turn, 0)
        block(groups - 1, last=True)

    layer(odd, even, t2, per)
    finish(even, lons + 4)
    layer(even, odd, t3, per // 2)
    finish(odd, lons + 2)

    depth = t4.shape[1] // LANES
    padded = rows + 2 * SUB
    long = padded // 2
    before = iota((long, LANES), 1) < LANES // 2

    def last_layer(n, carry):
        span_rows = pl.ds(pl.multiple_of(n * long, SUB), long)
        sides = []
        for side in range(2):
            parts = [odd[side * (depth - 1) + t, span_rows, :] for t in range(depth)]
            sides.append(dot(jnp.concatenate(parts, axis=1), t4[side]))
        force[0, span_rows, :] = jnp.where(before, sides[0][:, :LANES], sides[1][:, :LANES])
        swapped = jnp.where(before, sides[1][:, :LANES], sides[0][:, :LANES])
        force[1, span_rows, :] = pltpu.roll(swapped, LANES // 2, 1)
        force[2, span_rows, :] = jnp.where(before, sides[0][:, LANES:], sides[1][:, LANES:])
        return carry

    lax.fori_loop(0, 2, last_layer, 0)

    ocean = sea[...].astype(f32)
    narrow = iota((lons, LANES), 1)
    at_south = narrow == 0
    at_north = narrow == LANES - 1
    halves = lons // 2

    def beyond(n, m, offset, to):
        some = pl.ds(noises * GROUP, (fields - noises) * GROUP)
        columns = []
        for g in range(groups):
            spot = (g * members + m) * RIM + offset
            more = rests + g * members + m
            tall = messages[n, some, :]
            column = pltpu.roll(tall, lax.rem(LANES + to - spot, LANES), 1)
            columns.append(column + pltpu.roll(tall, lax.rem(LANES + to - more, LANES), 1))
        cells = []
        for c in range(fields - noises):
            whole = jnp.concatenate([x[c * GROUP : (c + 1) * GROUP] for x in columns], axis=0)
            cells.append(pltpu.roll(whole, lons + GROUP - RIM, 0)[:lons])
        return cells

    def member(m, carry):
        for q in range(chunks):
            size = min(blocks, lats - q * blocks)
            total = force[0, pl.ds(m * chunks + q, size, stride=SUB), :]
            for d in range(1, 3):
                total = total + force[d, pl.ds(d * SUB + m * chunks + q, size, stride=SUB), :]
            gathered[pl.ds(q * blocks, size), :] = total
        turned_force = jnp.transpose(gathered[...])
        rims = [beyond(3, m, RIM - 1, 0), beyond(0, m, 0, LANES - 1)]
        for level in range(levels):
            gains = []
            for (sign, spot), rim in zip(((1.0, at_south), (-1.0, at_north)), rims):
                ru, rv, rh = rim[level], rim[levels + level], rim[2 * levels + level]
                pressure = rim[2 * levels] + rim[2 * levels + 1]
                if level == 1:
                    pressure = pressure + REDUCED * rh
                gains.append(
                    [
                        jnp.where(spot, TIME_STEP * VISCOSITY * ru, 0.0),
                        jnp.where(spot, TIME_STEP * (VISCOSITY * rv + sign * 0.5 * pressure), 0.0),
                        jnp.where(spot, TIME_STEP * sign * 0.5 * (rh * rv), 0.0),
                    ]
                )
            middle = [jnp.zeros((lons, lats - 2 * LANES), f32)] if lats > 2 * LANES else []
            gains = [jnp.concatenate([gains[0][n]] + middle + [gains[1][n]], axis=1) for n in range(3)]

            def push(c):
                parts = [
                    turned_force[side * LANES // 2 + c * halves : side * LANES // 2 + (c + 1) * halves]
                    for side in range(2)
                ]
                return TIME_STEP * (jnp.concatenate(parts, axis=0) + bias_last[c])

            results[0, m, level] = base[0, m, level] + ocean * (gains[0] + push(level))
            results[1, m, level] = base[1, m, level] + ocean * (gains[1] + push(levels + level))
            results[2, m, level] = base[2, m, level] + gains[2]
        for n, out in enumerate((new_u, new_v, new_h)):
            pltpu.make_async_copy(results.at[n, m], out.at[m], done.at[n, m]).start()
        return carry

    lax.fori_loop(0, members, member, 0)
    for m in range(members):
        for n, out in enumerate((new_u, new_v, new_h)):
            pltpu.make_async_copy(results.at[n, m], out.at[m], done.at[n, m]).wait()


def body(
    noise,
    velocity_u,
    velocity_v,
    thickness,
    land_sea,
    conv_first,
    bias_first,
    conv_second,
    bias_second,
    conv_third,
    bias_third,
    conv_last,
    bias_last,
):
    members, noises, lons, lats = noise.shape
    levels = velocity_u.shape[1]
    fields = noises + 3 * levels
    sizes = (members, noises, levels)
    hidden = conv_first.shape[0]
    outs = conv_last.shape[0]
    groups = lons // GROUP + 1
    rows = members * (lats + GAP)
    assert hidden * 4 == LANES and outs * lons == LANES and members * (RIM + 1) * groups <= LANES
    assert fields % 2 == 0 and 4 * -(-fields // 4) == 12 and GROUP * (fields + 6) == LANES and lons % 16 == 0
    assert lats % LANES == 0 and SUB % members == 0 and (lats + GAP) % (SUB // members) == 0
    lon_count, lat_count = lax.axis_size("lon"), lax.axis_size("lat")
    assert lon_count % 2 == 0 and lat_count % 2 == 0
    state = (noise, velocity_u, velocity_v, thickness, land_sea)
    whole = pl.BlockSpec(memory_space=pltpu.VMEM)

    tall = members * fields * RIM + GROUP + members * 3 * levels
    assert tall % SUB == 0
    args = state + (
        conv_first.transpose(1, 2, 3, 0),
        conv_second.transpose(2, 3, 0, 1),
        conv_third.transpose(2, 3, 0, 1),
        conv_last.transpose(2, 3, 0, 1),
        bias_first[None],
        bias_second[None],
        bias_third[None],
    )
    count = len(args)
    *held, to_even, to_odd = pl.pallas_call(
        functools.partial(pack_lon_kernel, sizes, count),
        out_shape=[pltpu.VMEM(x.shape, x.dtype) for x in args] + [pltpu.VMEM((tall, lats), bf16)] * 2,
        in_specs=[pl.BlockSpec(memory_space=pltpu.HBM)] * count,
        out_specs=[whole] * (count + 2),
        scratch_shapes=[pltpu.VMEM((2, tall, lats), f32), pltpu.SemaphoreType.DMA((count,))],
        compiler_params=pltpu.CompilerParams(vmem_limit_bytes=62 * 2**20),
        name="pack_lon",
    )(*args)
    state = tuple(held[:5])
    lon_even = lax.ppermute(to_even, "lon", [(i, i ^ 1) for i in range(lon_count)])
    lon_odd = lax.ppermute(to_odd, "lon", [(i, (i - 1 + 2 * (i % 2)) % lon_count) for i in range(lon_count)])

    wide = -(-(fields + 1) * GROUP // SUB) * SUB
    part = pltpu.VMEM((wide, LANES), f32)
    message = pltpu.VMEM((wide, LANES), bf16)
    deep = -(-(lons // 2 + 2) * hidden // LANES) * LANES
    padded = rows + 2 * SUB
    tiles = 2 * groups + 1
    t1, t2, t3, t4, own_head, own_tail, windows, pre = pl.pallas_call(
        functools.partial(prepare_kernel, sizes),
        out_shape=[
            pltpu.VMEM((3 * LANES, 2 * LANES), bf16),
            pltpu.VMEM((8 * LANES, 2 * LANES), bf16),
            pltpu.VMEM((8 * LANES, 2 * LANES), bf16),
            pltpu.VMEM((2, deep, 2 * LANES), bf16),
            part,
            part,
            pltpu.VMEM((groups, padded, LANES), bf16),
            pltpu.VMEM((tiles, padded, LANES), bf16),
        ],
        in_specs=[whole] * count,
        out_specs=[whole] * 8,
        scratch_shapes=[
            pltpu.VMEM((groups - 2, rows, LANES), f32),
            pltpu.VMEM((groups - 2, LANES, LANES), f32),
        ],
        compiler_params=pltpu.CompilerParams(vmem_limit_bytes=12 * 2**20),
        cost_estimate=pl.CostEstimate(flops=10**7, bytes_accessed=10**7, transcendentals=0),
        name="prepare",
    )(*held)
    last = lat_count - 1
    smem = pl.BlockSpec(memory_space=pltpu.SMEM)
    to_even, to_odd = pl.pallas_call(
        functools.partial(join_kernel, sizes, lons),
        out_shape=[message] * 2,
        in_specs=[whole] * 4,
        out_specs=[whole] * 2,
        scratch_shapes=[
            pltpu.VMEM((2, 2, tall, LANES), f32),
            pltpu.VMEM((2, wide, LANES), f32),
        ],
        compiler_params=pltpu.CompilerParams(vmem_limit_bytes=4 * 2**20),
        name="join_rims",
    )(lon_even, lon_odd, own_head, own_tail)
    even_rim = lax.ppermute(to_even, "lat", [(i, i ^ 1) for i in range(lat_count)])
    pairs = []
    for t in range(lon_count):
        at = t * lat_count
        pairs += [(at + k, at + k - 1 + 2 * (k % 2)) for k in range(1, last)]
        pairs += [(at, (t ^ 1) * lat_count), (at + last, (lon_count - 1 - t) * lat_count + last)]
    odd_rim = lax.ppermute(to_odd, ("lon", "lat"), pairs)

    windows, base = pl.pallas_call(
        functools.partial(cells_kernel, sizes),
        out_shape=[pltpu.VMEM(windows.shape, bf16), pltpu.VMEM((3, *velocity_u.shape), f32)],
        in_specs=[whole] * 9,
        out_specs=[whole] * 2,
        input_output_aliases={8: 0},
        scratch_shapes=[
            pltpu.VMEM((2, tall, lats), f32),
            pltpu.VMEM((2, rows, LANES), f32),
            pltpu.VMEM((2, LANES, LANES), f32),
        ],
        compiler_params=pltpu.CompilerParams(vmem_limit_bytes=12 * 2**20),
        cost_estimate=pl.CostEstimate(flops=10**7, bytes_accessed=10**7, transcendentals=0),
        name="cells",
    )(*state, lon_even, lon_odd, to_even, windows)

    out = jax.ShapeDtypeStruct(velocity_u.shape, f32)
    return pl.pallas_call(
        functools.partial(main_kernel, sizes),
        out_shape=[out] * 3 + [pltpu.VMEM(x.shape, x.dtype) for x in (windows, pre)],
        in_specs=[smem] + [whole] * 11,
        out_specs=[pl.BlockSpec(memory_space=pltpu.HBM)] * 3 + [whole] * 2,
        input_output_aliases={1: 3, 2: 4},
        scratch_shapes=[
            pltpu.VMEM((tiles, padded, LANES), bf16),
            pltpu.VMEM((3, padded, LANES), f32),
            pltpu.VMEM((lats, LANES), f32),
            pltpu.VMEM((LANES, LANES), f32),
            pltpu.VMEM((groups, GAP * SUB, LANES), f32),
            pltpu.VMEM((4, wide, LANES), f32),
            pltpu.VMEM((3, *velocity_u.shape), f32),
            pltpu.SemaphoreType.DMA((3, members)),
        ],
        compiler_params=pltpu.CompilerParams(vmem_limit_bytes=32 * 2**20),
        cost_estimate=pl.CostEstimate(flops=2 * 10**10, bytes_accessed=10**7, transcendentals=4 * 10**6),
        name="network_and_step",
    )(
        bias_last,
        windows,
        pre,
        base,
        state[4],
        even_rim,
        odd_rim,
        to_odd,
        t1,
        t2,
        t3,
        t4,
    )[:3]


def solution(mesh):
    tiles = P(None, None, "lon", "lat")
    return jax.shard_map(
        body,
        mesh=mesh,
        in_specs=(tiles,) * 4 + (P("lon", "lat"),) + (P(),) * 8,
        out_specs=(tiles,) * 3,
        check_vma=False,
    )
```

```python
import functools

import jax
import jax.numpy as jnp
from jax import lax
from jax.experimental import pallas as pl
from jax.experimental.pallas import tpu as pltpu
from jax.sharding import PartitionSpec as P

REDUCED = 0.5
TIME_STEP = 0.2
VISCOSITY = 0.05
CORIOLIS = 0.4

RIM = 4
GAP = 16
NORTH, STRIP, GHOST, SOUTH = 0, 4, 8, 12
SUB = 16
LANES = 128
GROUP = 8
LAND = 2.0**100

f32 = jnp.float32
bf16 = jnp.bfloat16


def iota(shape, dim):
    return lax.broadcasted_iota(jnp.int32, shape, dim)


def dot(a, b):
    return jnp.dot(a, b, preferred_element_type=f32)


def rest(x):
    return x - x.astype(bf16).astype(f32)


def pack_lon_kernel(sizes, count, *refs):
    sources, held, (even, odd, wide, done) = refs[:count], refs[count : 2 * count], refs[2 * count :]
    members, noises, levels = sizes
    fields = noises + 3 * levels
    noise, u, v, h, sea = held[:5]
    lons, lats = sea.shape
    copies = [pltpu.make_async_copy(x, y, done.at[n]) for n, (x, y) in enumerate(zip(sources, held))]
    for copy in copies:
        copy.start()
    for copy in copies[:5]:
        copy.wait()
    upper = iota((GROUP, lats), 0) < RIM

    def field(m, c, side):
        if c < noises:
            full = noise[m, c].astype(f32)
            return full[-GROUP:] if side else full[:GROUP]
        c -= noises
        return (u, v, h)[c // levels][m, c % levels, pl.ds(side * (lons - GROUP), GROUP)]

    rests = members * fields * RIM + GROUP
    for m in range(members):
        for c in range(0, fields, 2):
            rows = pl.ds((m * fields + c) * RIM, GROUP)
            wide[0, rows] = jnp.where(upper, field(m, c, 0), pltpu.roll(field(m, c + 1, 0), RIM, 0))
            wide[1, rows] = jnp.where(upper, pltpu.roll(field(m, c, 1), RIM, 0), field(m, c + 1, 1))
        for c in range(noises, fields):
            row = pl.ds(rests + m * (fields - noises) + c - noises, 1)
            wide[0, row] = rest(field(m, c, 0)[:1])
            wide[1, row] = rest(field(m, c, 1)[GROUP - 1 :])
    rows = pl.ds(members * fields * RIM, GROUP)
    ends = [sea[pl.ds(side * (lons - GROUP), GROUP)].astype(f32) for side in range(2)]
    wide[0, rows] = jnp.where(upper, ends[0], 0.0)
    wide[1, rows] = jnp.where(upper, pltpu.roll(ends[1], RIM, 0), 0.0)
    is_odd = lax.axis_index("lon") % 2 == 1
    even[...] = jnp.where(is_odd, wide[0], wide[1]).astype(bf16)
    odd[...] = jnp.where(is_odd, wide[1], wide[0]).astype(bf16)
    for copy in copies[5:]:
        copy.wait()


def lon_rims(even, odd, lanes=slice(None)):
    is_odd = lax.axis_index("lon") % 2 == 1
    a, b = even[:, lanes].astype(f32), odd[:, lanes].astype(f32)
    return jnp.where(is_odd, a, b), jnp.where(is_odd, b, a)


def rim_tile(sizes, m, c, side, rim):
    members, noises, levels = sizes
    fields = noises + 3 * levels
    row = (m * fields + c) * RIM if c < fields else members * fields * RIM
    tile = rim[pl.ds(row // GROUP * GROUP, GROUP)]
    if (row // RIM) % 2 == side:
        return tile
    return pltpu.roll(tile, RIM, 0)


def window(tiles, following, mask, next_mask):
    pair = iota(mask.shape, 0) // 2
    zero = jnp.zeros_like(mask)
    more = []
    for start in range(0, len(tiles), 4):
        total = zero
        for n in range(min(4, len(tiles) - start)):
            moved = pltpu.roll(following[start + n], 2 * n, 0) if n else following[start]
            total = jnp.where(pair == n, moved, total)
        more.append(total)
    return jnp.concatenate(
        tiles + more + [mask - 1.0, next_mask - 1.0, jnp.ones_like(mask)], axis=0
    )


def store_lats(block, t, dst, tile, m, lats, chunks, buffer):
    blocks = (lats + GAP) // chunks
    buffer[...] = jnp.transpose(block)
    for q in range(chunks):
        lo = max(q * blocks, t * LANES)
        hi = min((q + 1) * blocks, (t + 1) * LANES, lats)
        if lo < hi:
            start = (lo - q * blocks) * SUB + m * chunks + q
            dst[tile, pl.ds(start, hi - lo, stride=SUB), :] = buffer[pl.ds(lo - t * LANES, hi - lo), :]


def shifted_tiles(sizes, refs, m, c, t):
    noise, u, v, h, sea = refs
    members, noises, levels = sizes
    fields = noises + 3 * levels
    lons = sea.shape[0]
    lanes = slice(t * LANES, (t + 1) * LANES)
    if c == fields:
        full = sea[:, lanes].astype(f32)
    elif c < noises:
        full = noise[m, c, :, lanes].astype(f32)
    else:
        full = (u, v, h)[(c - noises) // levels][m, (c - noises) % levels, :, lanes]
    full = pltpu.roll(full, lons - RIM, 0)
    tiles = [full[g * GROUP : (g + 1) * GROUP] for g in range(lons // GROUP)]
    return tiles[-1:] + tiles


def prepare_kernel(sizes, noise, u, v, h, sea, *refs):
    weights, matrices, (head, tail, middle, pre, cells, turned) = refs[:7], refs[7:11], refs[11:]
    held = (noise, u, v, h, sea)
    members, noises, levels = sizes
    fields = noises + 3 * levels
    lons, lats = sea.shape
    groups = lons // GROUP + 1
    weights_kernel(*weights, *matrices)
    lane = iota((GROUP, LANES), 1)
    for out, t, first in ((head, 0, 0), (tail, lats // LANES - 1, LANES - RIM)):
        for c in range(fields + 1):
            total = jnp.zeros((GROUP, LANES), f32)
            for m in range(members):
                for g, tile in enumerate(shifted_tiles(sizes, held, m, c, t)):
                    place = (g * members + m) * RIM
                    moved = pltpu.roll(tile, (place - first) % LANES, 1)
                    total = jnp.where((lane >= place) & (lane < place + RIM), moved, total)
                    if noises <= c < fields:
                        place = groups * members * RIM + g * members + m
                        edge = 0 if out is head else LANES - 1
                        moved = pltpu.roll(rest(tile), (place - edge) % LANES, 1)
                        total = jnp.where(lane == place, moved, total)
            out[pl.ds(c * GROUP, GROUP)] = total
        for c in range(fields + 1, out.shape[0] // GROUP):
            out[pl.ds(c * GROUP, GROUP)] = jnp.zeros((GROUP, LANES), f32)
    chunks = SUB // members
    rows = cells.shape[1]
    gap_k = lats - (chunks - 1) * ((lats + GAP) // chunks)
    inner = groups - 2
    for m in range(members):
        for g in range(inner):
            empty = pl.ds(gap_k * SUB + (m + 1) * chunks - 1, GAP, stride=SUB)
            cells[g, empty, :] = jnp.zeros((GAP, LANES), f32)
    for t in range(lats // LANES):
        for m in range(members):
            tiles = [shifted_tiles(sizes, held, m, c, t) for c in range(fields + 1)]
            for g in range(1, inner + 1):
                following = [x[g + 1] for x in tiles]
                block = window([x[g] for x in tiles[:fields]], following[:fields], tiles[fields][g], following[fields])
                buffer = turned.at[(t * members + m) * inner + g - 1]
                store_lats(block, t, cells, g - 1, m, lats, chunks, buffer)
    for g in range(inner):
        middle[g, pl.ds(SUB, rows), :] = cells[g].astype(bf16)
        wrap(middle.at[g], rows)
    for g in range(inner):
        for r, step in row_pieces(rows):
            parts = [middle[g, pl.ds(r + SUB * d, step), :] for d in range(3)]
            put(pre, g + 1, r, activate(dot(jnp.concatenate(parts, axis=1), matrices[0][...])))


def row_pieces(rows):
    half = rows // 2 // SUB * SUB
    return [(0, half), (half, rows - half)]


def activate(pre):
    return (pre * jnp.tanh(pre) + pre).astype(bf16)


def put(y, b, r, out):
    for e in range(out.shape[1] // LANES):
        y[2 * b + e, pl.ds(SUB + r, out.shape[0]), :] = out[:, e * LANES : (e + 1) * LANES]


def wrap(x, rows):
    end = x[pl.ds(rows, SUB), :].astype(f32)
    x[pl.ds(0, SUB), :] = pltpu.roll(end, 1, 0).astype(bf16)
    begin = x[pl.ds(SUB, SUB), :].astype(f32)
    x[pl.ds(SUB + rows, SUB), :] = pltpu.roll(begin, SUB - 1, 0).astype(bf16)


def cells_kernel(sizes, noise, u, v, h, sea, lon_even, lon_odd, after, out, base, rims, cells, turned):
    members, noises, levels = sizes
    fields = noises + 3 * levels
    lons, lats = sea.shape
    groups = lons // GROUP + 1
    chunks = SUB // members
    rows = cells.shape[1]
    gap_k = lats - (chunks - 1) * ((lats + GAP) // chunks)
    rims[0], rims[1] = lon_rims(lon_even, lon_odd)
    for m in range(members):
        for side in range(2):
            empty = pl.ds(gap_k * SUB + (m + 1) * chunks - 1, GAP, stride=SUB)
            cells[side, empty, :] = jnp.zeros((GAP, LANES), f32)
    blank = jnp.zeros((GROUP, LANES), f32)
    upper = iota((GROUP, LANES), 0) < RIM
    for t in range(lats // LANES):
        lanes = slice(t * LANES, (t + 1) * LANES)
        for m in range(members):
            tiles = []
            for c in range(fields + 1):
                groups_of = shifted_tiles(sizes, (noise, u, v, h, sea), m, c, t)
                ends = [rim_tile(sizes, m, c, side, rims.at[side, :, lanes]) for side in range(2)]
                groups_of[0] = jnp.where(upper, ends[0], groups_of[0])
                groups_of[-1] = jnp.where(upper, groups_of[-1], ends[1])
                tiles.append(groups_of)
            for side, g in enumerate((0, groups - 1)):
                following = [x[g + 1] if g + 1 < groups else blank for x in tiles]
                block = window([x[g] for x in tiles[:fields]], following[:fields], tiles[fields][g], following[fields])
                store_lats(block, t, cells, side, m, lats, chunks, turned.at[(t * members + m) * 2 + side])
    for side in range(2):
        out[side, pl.ds(SUB, rows), :] = cells[side].astype(bf16)
    step_kernel(sizes, u, v, h, sea, rims, base)


def step_kernel(sizes, u, v, h, sea, rims, base):
    members, noises, levels = sizes
    fields = noises + 3 * levels
    lons, lats = sea.shape
    ocean = sea[...].astype(f32)
    lat_count = lax.axis_size("lat")
    lat_rows = (lax.axis_index("lat") * lats).astype(f32) + iota((lons, lats), 1).astype(f32)
    turn = CORIOLIS * (2.0 * (lat_rows + 0.5) / (lats * lat_count) - 1.0)
    at_first = iota((lons, lats), 0) == 0
    at_last = iota((lons, lats), 0) == lons - 1
    at_south = iota((lons, lats), 1) == 0
    at_north = iota((lons, lats), 1) == lats - 1
    lon_rests = members * fields * RIM + GROUP

    def around(x, m, c):
        row = (m * fields + c) * RIM
        more = lon_rests + m * (fields - noises) + c - noises
        west = rims[0, pl.ds(row + RIM - 1, 1)] + rims[0, pl.ds(more, 1)]
        east = rims[1, pl.ds(row, 1)] + rims[1, pl.ds(more, 1)]
        return (
            jnp.where(at_first, west, pltpu.roll(x, 1, 0)),
            jnp.where(at_last, east, pltpu.roll(x, lons - 1, 0)),
            jnp.where(at_south, 0.0, pltpu.roll(x, 1, 1)),
            jnp.where(at_north, 0.0, pltpu.roll(x, lats - 1, 1)),
        )

    for m in range(members):
        sets = []
        for level in range(levels):
            sets.append(
                [
                    (x[m, level], around(x[m, level], m, noises + n * levels + level))
                    for n, x in enumerate((u, v, h))
                ]
            )
        for level in range(levels):
            (cu, au), (cv, av), (ch, ah) = sets[level]
            upper, lower = sets[0][2][1], sets[1][2][1]
            pressure = [upper[i] + lower[i] for i in range(4)]
            if level == 1:
                pressure = [pressure[i] + REDUCED * lower[i] for i in range(4)]
            lap_u = au[1] + au[0] + au[3] + au[2] - 4.0 * cu
            lap_v = av[1] + av[0] + av[3] + av[2] - 4.0 * cv
            dx = 0.5 * (pressure[1] - pressure[0])
            dy = 0.5 * (pressure[3] - pressure[2])
            base[0, m, level] = ocean * (cu + TIME_STEP * (turn * cv - dx + VISCOSITY * lap_u))
            base[1, m, level] = ocean * (cv + TIME_STEP * (-turn * cu - dy + VISCOSITY * lap_v))
            flow = 0.5 * (ah[1] * au[1] - ah[0] * au[0]) + 0.5 * (ah[3] * av[3] - ah[2] * av[2])
            base[2, m, level] = ch - TIME_STEP * flow


def join_kernel(sizes, lons, lon_even, lon_odd, head, tail, even, odd, rims, wide):
    members, noises, levels = sizes
    fields = noises + 3 * levels
    groups = lons // GROUP + 1
    lats = lon_even.shape[1]
    for n, lanes in enumerate((slice(0, LANES), slice(lats - LANES, lats))):
        rims[0, n], rims[1, n] = lon_rims(lon_even, lon_odd, lanes)
    lane = iota((GROUP, LANES), 1)
    upper = iota((GROUP, LANES), 0) < RIM
    to_south = lax.axis_index("lat") % 2 == 1
    for c in range(fields + 1):
        rows = pl.ds(c * GROUP, GROUP)
        ends = []
        for n, (part, first) in enumerate(((head, 0), (tail, LANES - RIM))):
            total = part[rows]
            for side in range(2):
                held = upper if side == 0 else ~upper
                for m in range(members):
                    place = ((groups - 1) * side * members + m) * RIM
                    tile = rim_tile(sizes, m, c, side, rims.at[side, n])
                    moved = pltpu.roll(tile, (place - first) % LANES, 1)
                    total = jnp.where(held & (lane >= place) & (lane < place + RIM), moved, total)
            ends.append(total)
        wide[0, rows] = jnp.where(to_south, ends[0], ends[1])
        wide[1, rows] = jnp.where(to_south, ends[1], ends[0])
    rows = pl.ds((fields + 1) * GROUP, wide.shape[1] - (fields + 1) * GROUP)
    wide[:, rows] = jnp.zeros((2, wide.shape[1] - (fields + 1) * GROUP, LANES), f32)
    even[...] = wide[0].astype(bf16)
    odd[...] = wide[1].astype(bf16)


def weights_kernel(w1, w2, w3, w4, bias1, bias2, bias3, t1, t2, t3, t4):
    hidden = w2.shape[2]
    per = LANES // hidden
    lane = iota((hidden, LANES), 1)
    fields = w1.shape[0]
    out_lon = iota((GROUP, LANES), 1) // hidden
    in_row = iota((GROUP, LANES), 0)
    bias_row = iota((GROUP, LANES), 0)

    def bias_rows(layer):
        part = 0.5 * jnp.concatenate([(bias1, bias2, bias3)[layer][...]] * per, axis=1)
        b1 = part.astype(bf16).astype(f32)
        b2 = (part - b1).astype(bf16).astype(f32)
        b3 = part - b1 - b2
        zero = jnp.zeros((GROUP, LANES), f32)
        return jnp.where(
            bias_row == 0,
            b1,
            jnp.where(bias_row == 1, b2, jnp.where(bias_row == 2, b3, zero)),
        )

    def sea_rows(shift, tile):
        lon = iota((2 * GROUP, LANES), 0)
        out = iota((2 * GROUP, LANES), 1) // hidden + per * tile
        return jnp.where(lon == out + shift, LAND, 0.0)

    for dj in range(3):
        taps = []
        for di in range(3):
            cells = [w1[c, di].astype(f32)[dj : dj + 1] for c in range(fields)]
            taps.append(
                [jnp.broadcast_to(0.5 * jnp.concatenate([x] * per, axis=1), (GROUP, LANES)) for x in cells]
            )
        for tile in range(2):
            parts = []
            for c in range(fields):
                total = jnp.zeros((GROUP, LANES), f32)
                for di in range(3):
                    hit = in_row == out_lon + per * tile + di
                    total = jnp.where(hit, taps[di][c], total)
                parts.append(total)
            for start in range(0, fields, 4):
                total = jnp.zeros((GROUP, LANES), f32)
                for n in range(min(4, fields - start)):
                    for di in range(3):
                        hit = in_row % 2 + GROUP == out_lon + per * tile + di
                        total = jnp.where(hit & (in_row // 2 == n), taps[di][start + n], total)
                parts.append(total)
            if dj == 1:
                parts += [sea_rows(1, tile), bias_rows(0)]
            else:
                parts.append(jnp.zeros((3 * GROUP, LANES), f32))
            block = jnp.concatenate(parts, axis=0)
            t1[pl.ds(dj * LANES, LANES), pl.ds(tile * LANES, LANES)] = block.astype(bf16)

    for layer, (w, t) in enumerate(((w2, t2), (w3, t3))):
        for dj in range(3):
            taps = []
            for di in range(3):
                cell = 0.5 * w[di, dj].astype(f32)
                wide = jnp.concatenate([cell, jnp.zeros((hidden, LANES - hidden), f32)], axis=1)
                square = jnp.concatenate([wide] * per, axis=0)
                taps.append(jnp.transpose(square)[:hidden])
            for lon in range(GROUP + 2):
                for tile in range(2):
                    total = jnp.zeros((hidden, LANES), f32)
                    for di in range(3):
                        total = jnp.where(lane // hidden + per * tile == lon - di, taps[di], total)
                    if lon < GROUP:
                        row = dj * GROUP * hidden + lon * hidden
                    else:
                        row = 3 * GROUP * hidden + dj * 2 * hidden + (lon - GROUP) * hidden
                    t[pl.ds(row, hidden), pl.ds(tile * LANES, LANES)] = total.astype(bf16)
        for tile in range(2):
            block = jnp.concatenate(
                [
                    jnp.zeros((5 * GROUP, LANES), f32),
                    sea_rows(2 + layer, tile),
                    bias_rows(1 + layer),
                ],
                axis=0,
            )
            row = 3 * GROUP * hidden + 6 * hidden
            t[pl.ds(row, 2 * hidden), pl.ds(tile * LANES, LANES)] = block.astype(bf16)

    outs = w4.shape[2]
    half = LANES // 2
    lons = half // outs
    slot = iota((hidden, LANES), 1) // half
    out_lon = iota((hidden, LANES), 1) % lons
    taps = {}
    for dj in range(3):
        for di in range(3):
            cell = w4[di, dj].astype(f32)
            wide = jnp.concatenate([cell, jnp.zeros((outs, LANES - hidden), f32)], axis=1)
            square = jnp.concatenate(
                [jnp.broadcast_to(wide[c : c + 1], (lons, LANES)) for c in range(outs)] * 2, axis=0
            )
            taps[dj, di] = jnp.transpose(square)[:hidden]
    order = ((0, 1, 2, None), (1, 0, None, 2))
    for side in range(2):
        for lon in range(t4.shape[1] // hidden):
            for tile in range(2):
                total = jnp.zeros((hidden, LANES), f32)
                for place in range(2):
                    dj = order[side][2 * tile + place]
                    if dj is None:
                        continue
                    for di in range(3):
                        total = jnp.where((slot == place) & (out_lon == lon - di), taps[dj, di], total)
                t4[side, pl.ds(lon * hidden, hidden), pl.ds(tile * LANES, LANES)] = total.astype(bf16)


def main_kernel(
    sizes,
    bias_last,
    middle_in,
    ends_in,
    pre_in,
    base,
    sea,
    even_rim,
    odd_rim,
    own_tail,
    t1,
    t2,
    t3,
    t4,
    new_u,
    new_v,
    new_h,
    middle,
    ends,
    odd,
    even,
    force,
    gathered,
    turned,
    gaps,
    results,
    done,
):
    members, noises, levels = sizes
    fields = noises + 3 * levels
    lons, lats = sea.shape
    groups = lons // GROUP + 1
    chunks = SUB // members
    blocks = (lats + GAP) // chunks
    rows = blocks * SUB
    gap_k = lats - (chunks - 1) * blocks
    lat_index, lat_count = lax.axis_index("lat"), lax.axis_size("lat")
    top = lat_index == lat_count - 1
    is_odd = lat_index % 2 == 1
    bottom = lat_index == 0
    strip = odd_rim[...].astype(f32)
    paired = even_rim[...].astype(f32)
    south = jnp.where(is_odd, paired, jnp.where(bottom, 0.0, strip))

    wide = strip.shape[0]
    span = members * RIM
    lane = iota((wide, LANES), 1)
    rests = groups * span
    border = ((lane % RIM == 0) & (lane < rests)) | (lane >= rests)
    row_to = iota((wide, wide), 0)
    row_from = iota((wide, wide), 1)
    channel = row_to // GROUP
    mirrored = (channel == row_from // GROUP) & (row_from % GROUP == GROUP - 1 - row_to % GROUP)
    odd_parity = (channel >= noises) & (channel < noises + 2 * levels)
    flip_rows = jnp.where(mirrored, jnp.where(odd_parity, -1.0, 1.0), 0.0).astype(bf16)
    lane_from = iota((LANES, LANES), 0)
    lane_to = iota((LANES, LANES), 1)
    source = (groups - 1 - lane_to // span) * span + lane_to % span + RIM - 1
    moves = (lane_to % RIM == 0) & (lane_to < rests) & (lane_from == source)
    other = lane_to - rests
    source = rests + (groups - 1 - other // members) * members + other % members
    moves = moves | ((other >= 0) & (other < groups * members) & (lane_from == source))
    flip_lanes = jnp.where(moves, 1.0, 0.0).astype(bf16)
    pair = dot(flip_rows, jnp.concatenate([odd_rim[...], own_tail[...]], axis=1)).astype(bf16)
    folded = dot(pair[:, :LANES], flip_lanes)
    ghost = dot(pair[:, LANES:], flip_lanes)
    north = jnp.where(is_odd, strip, paired)
    north_rim = jnp.where(border & top, folded, north)

    for n, message in enumerate((north_rim, strip, ghost, south)):
        after = pltpu.roll(message, LANES - span, 1)
        cut = [message[c * GROUP : (c + 1) * GROUP] for c in range(fields + 1)]
        after = [after[c * GROUP : (c + 1) * GROUP] for c in range(fields + 1)]
        turned[n] = jnp.transpose(window(cut[:fields], after[:fields], cut[fields], after[fields]))
        for g in range(groups):
            for m in range(members):
                gap = (m - 1) % members if n == 3 else m
                start = n * RIM * SUB + gap * chunks + chunks - 1
                gaps[g, pl.ds(start, RIM, stride=SUB), :] = turned[n, pl.ds((g * members + m) * RIM, RIM), :]

    first = [ends.at[0]] + [middle.at[g] for g in range(groups - 2)] + [ends.at[1]]
    in_gap = iota((GAP * SUB, LANES), 0) % chunks == chunks - 1
    for g in range(groups):
        spot = pl.ds((1 + gap_k) * SUB, GAP * SUB)
        kept = first[g][spot, :].astype(f32)
        first[g][spot, :] = jnp.where(in_gap, gaps[g], kept).astype(bf16)
        wrap(first[g], rows)

    hidden = LANES // 4
    per = LANES // hidden
    tiles = odd.shape[0]
    pieces = row_pieces(rows)

    def finish(x, valid):
        used = (valid + per - 1) // per

        @pl.when(top)
        def _():
            strip_top = SUB * (1 + gap_k + STRIP + RIM - 1)
            own_top = SUB * gap_k
            strip_ghost = SUB * (1 + gap_k + GHOST)
            own_ghost = SUB * (1 + gap_k + NORTH)
            last_chunk = iota((SUB, LANES), 0) % chunks == chunks - 1
            spot = iota((SUB, LANES), 1) // hidden
            for src, dst in ((strip_top, own_ghost), (own_top, strip_ghost)):
                found = [x[t, pl.ds(src, SUB), :].astype(f32) for t in range(used)]
                for t in range(used):
                    total = x[t, pl.ds(dst, SUB), :].astype(f32)
                    for i in range(per):
                        lon = valid - 1 - (per * t + i)
                        if lon < 0:
                            continue
                        moved = pltpu.roll(found[lon // per], (hidden * (i - lon % per)) % LANES, 1)
                        total = jnp.where(last_chunk & (spot == i), moved, total)
                    x[t, pl.ds(dst, SUB), :] = total.astype(bf16)

        for t in range(used):
            wrap(x.at[t], rows)

    for x in (odd, even):
        x[tiles - 1] = jnp.zeros(x.shape[1:], bf16)
    even[tiles - 2] = jnp.zeros(even.shape[1:], bf16)

    for b in (0, groups - 1):
        for r, step in pieces:
            parts = [first[b][pl.ds(r + SUB * d, step), :] for d in range(3)]
            put(odd, b, r, activate(dot(jnp.concatenate(parts, axis=1), t1[...])))
    near = (gap_k - 1) * SUB
    for b in range(1, groups - 1):
        parts = []
        for d in range(3):
            some = [first[b][pl.ds(near + SUB * d, rows - near), :], first[b][pl.ds(SUB * d, SUB), :]]
            parts.append(jnp.concatenate(some, axis=0))
        out = activate(dot(jnp.concatenate(parts, axis=1), t1[...]))
        put(odd, b, near, out[: rows - near])
        put(odd, b, 0, out[rows - near :])
    finish(odd, lons + 6)

    ocean = sea[...].astype(f32)
    narrow = iota((lons, LANES), 1)
    at_south = narrow == 0
    at_north = narrow == LANES - 1

    def beyond(message, m, offset, to):
        tall = message[noises * GROUP : fields * GROUP]
        columns = []
        for g in range(groups):
            spot = (g * members + m) * RIM + offset
            more = rests + g * members + m
            column = pltpu.roll(tall, (to - spot) % LANES, 1)
            columns.append(column + pltpu.roll(tall, (to - more) % LANES, 1))
        cells = []
        for c in range(fields - noises):
            whole = jnp.concatenate([x[c * GROUP : (c + 1) * GROUP] for x in columns], axis=0)
            cells.append(pltpu.roll(whole, lons + GROUP - RIM, 0)[:lons])
        return cells

    def step_rims(m):
        rims = [beyond(south, m, RIM - 1, 0), beyond(north_rim, m, 0, LANES - 1)]
        for level in range(levels):
            gains = []
            for (sign, spot), rim in zip(((1.0, at_south), (-1.0, at_north)), rims):
                ru, rv, rh = rim[level], rim[levels + level], rim[2 * levels + level]
                pressure = rim[2 * levels] + rim[2 * levels + 1]
                if level == 1:
                    pressure = pressure + REDUCED * rh
                gains.append(
                    [
                        jnp.where(spot, TIME_STEP * VISCOSITY * ru, 0.0),
                        jnp.where(spot, TIME_STEP * (VISCOSITY * rv + sign * 0.5 * pressure), 0.0),
                        jnp.where(spot, TIME_STEP * sign * 0.5 * (rh * rv), 0.0),
                    ]
                )
            middle = [jnp.zeros((lons, lats - 2 * LANES), f32)] if lats > 2 * LANES else []
            gains = [jnp.concatenate([gains[0][n]] + middle + [gains[1][n]], axis=1) for n in range(3)]
            results[0, m, level] = base[0, m, level] + ocean * gains[0]
            results[1, m, level] = base[1, m, level] + ocean * gains[1]
            results[2, m, level] = base[2, m, level] + gains[2]
        pltpu.make_async_copy(results.at[2, m], new_h.at[m], done.at[2, m]).start()

    width = GROUP * hidden

    def layer(x, y, t, left_over, beside):
        for b in range(groups):
            for r, step in pieces:
                lower = iota((step, LANES), 1) < 2 * hidden

                def cells_of(tile, d):
                    return x[tile, pl.ds(r + SUB * d, step), :]

                def packed(tile):
                    more = [cells_of(tile, d) for d in range(3)]
                    return [
                        jnp.where(lower, more[0], pltpu.roll(more[1], 2 * hidden, 1)),
                        jnp.where(lower, more[2], first[b][pl.ds(r + SUB, step), :]),
                    ]

                if b < groups - 1:
                    parts = [cells_of(2 * b + e, d) for d in range(3) for e in range(2)] + packed(2 * b + 2)
                    matrix = t[...]
                elif left_over == per:
                    parts = [cells_of(2 * b, d) for d in range(3)] + packed(2 * b + 1)
                    lanes = pl.ds(0, LANES)
                    matrix = jnp.concatenate(
                        [t[pl.ds(d * width, LANES), lanes] for d in range(3)]
                        + [t[pl.ds(d * width + LANES, 2 * hidden), lanes] for d in range(3)]
                        + [t[pl.ds(3 * width + 6 * hidden, 2 * hidden), lanes]],
                        axis=0,
                    )
                else:
                    parts = [cells_of(2 * b, d) for d in range(3)] + [first[b][pl.ds(r + SUB, step), :]]
                    lanes = pl.ds(0, LANES)
                    matrix = jnp.concatenate(
                        [t[pl.ds(d * width, LANES), lanes] for d in range(3)]
                        + [jnp.zeros((2 * hidden, LANES), bf16)]
                        + [t[pl.ds(3 * width + 6 * hidden, 2 * hidden), lanes]],
                        axis=0,
                    )
                put(y, b, r, activate(dot(jnp.concatenate(parts, axis=1), matrix)))
            for m in beside.get(b, ()):
                step_rims(m)

    beside = {}
    for m in range(members):
        beside.setdefault(min(m, groups - 1), []).append(m)
    layer(odd, even, t2, per, beside)
    finish(even, lons + 4)
    layer(even, odd, t3, per // 2, {})
    finish(odd, lons + 2)

    depth = t4.shape[1] // LANES
    padded = rows + 2 * SUB
    for r, long in row_pieces(padded):
        before = iota((long, LANES), 1) < LANES // 2
        span_rows = pl.ds(r, long)
        sides = []
        for side in range(2):
            parts = [odd[side * (depth - 1) + t, span_rows, :] for t in range(depth)]
            sides.append(dot(jnp.concatenate(parts, axis=1), t4[side]))
        force[0, span_rows, :] = jnp.where(before, sides[0][:, :LANES], sides[1][:, :LANES])
        swapped = jnp.where(before, sides[1][:, :LANES], sides[0][:, :LANES])
        force[1, span_rows, :] = pltpu.roll(swapped, LANES // 2, 1)
        force[2, span_rows, :] = jnp.where(before, sides[0][:, LANES:], sides[1][:, LANES:])

    halves = lons // 2
    for m in range(members):
        for q in range(chunks):
            size = min(blocks, lats - q * blocks)
            total = force[0, pl.ds(m * chunks + q, size, stride=SUB), :]
            for d in range(1, 3):
                total = total + force[d, pl.ds(d * SUB + m * chunks + q, size, stride=SUB), :]
            gathered[m, pl.ds(q * blocks, size), :] = total
        turned_force = jnp.transpose(gathered[m])
        for n, out in enumerate((new_u, new_v)):
            for level in range(levels):
                c = n * levels + level
                parts = [
                    turned_force[side * LANES // 2 + c * halves : side * LANES // 2 + (c + 1) * halves]
                    for side in range(2)
                ]
                push = TIME_STEP * (jnp.concatenate(parts, axis=0) + bias_last[c])
                results[n, m, level] = results[n, m, level] + ocean * push
            pltpu.make_async_copy(results.at[n, m], out.at[m], done.at[n, m]).start()
    for m in range(members):
        for n, out in enumerate((new_u, new_v, new_h)):
            pltpu.make_async_copy(results.at[n, m], out.at[m], done.at[n, m]).wait()


def body(
    noise,
    velocity_u,
    velocity_v,
    thickness,
    land_sea,
    conv_first,
    bias_first,
    conv_second,
    bias_second,
    conv_third,
    bias_third,
    conv_last,
    bias_last,
):
    members, noises, lons, lats = noise.shape
    levels = velocity_u.shape[1]
    fields = noises + 3 * levels
    sizes = (members, noises, levels)
    hidden = conv_first.shape[0]
    outs = conv_last.shape[0]
    groups = lons // GROUP + 1
    rows = members * (lats + GAP)
    assert hidden * 4 == LANES and outs * lons == LANES and members * (RIM + 1) * groups <= LANES
    assert fields % 2 == 0 and 4 * -(-fields // 4) == 12 and GROUP * (fields + 6) == LANES and lons % 16 == 0
    assert lats % LANES == 0 and SUB % members == 0 and (lats + GAP) % (SUB // members) == 0
    lon_count, lat_count = lax.axis_size("lon"), lax.axis_size("lat")
    assert lon_count % 2 == 0 and lat_count % 2 == 0
    state = (noise, velocity_u, velocity_v, thickness, land_sea)
    whole = pl.BlockSpec(memory_space=pltpu.VMEM)

    tall = members * fields * RIM + GROUP + members * 3 * levels
    assert tall % SUB == 0
    args = state + (
        conv_first.transpose(1, 2, 3, 0),
        conv_second.transpose(2, 3, 0, 1),
        conv_third.transpose(2, 3, 0, 1),
        conv_last.transpose(2, 3, 0, 1),
        bias_first[None],
        bias_second[None],
        bias_third[None],
    )
    count = len(args)
    *held, to_even, to_odd = pl.pallas_call(
        functools.partial(pack_lon_kernel, sizes, count),
        out_shape=[pltpu.VMEM(x.shape, x.dtype) for x in args] + [pltpu.VMEM((tall, lats), bf16)] * 2,
        in_specs=[pl.BlockSpec(memory_space=pltpu.HBM)] * count,
        out_specs=[whole] * (count + 2),
        scratch_shapes=[pltpu.VMEM((2, tall, lats), f32), pltpu.SemaphoreType.DMA((count,))],
        compiler_params=pltpu.CompilerParams(vmem_limit_bytes=62 * 2**20),
        name="pack_lon",
    )(*args)
    state = tuple(held[:5])
    lon_even = lax.ppermute(to_even, "lon", [(i, i ^ 1) for i in range(lon_count)])
    lon_odd = lax.ppermute(to_odd, "lon", [(i, (i - 1 + 2 * (i % 2)) % lon_count) for i in range(lon_count)])

    wide = -(-(fields + 1) * GROUP // SUB) * SUB
    part = pltpu.VMEM((wide, LANES), f32)
    message = pltpu.VMEM((wide, LANES), bf16)
    deep = -(-(lons // 2 + 2) * hidden // LANES) * LANES
    padded = rows + 2 * SUB
    tiles = 2 * groups + 1
    t1, t2, t3, t4, own_head, own_tail, middle, pre = pl.pallas_call(
        functools.partial(prepare_kernel, sizes),
        out_shape=[
            pltpu.VMEM((3 * LANES, 2 * LANES), bf16),
            pltpu.VMEM((8 * LANES, 2 * LANES), bf16),
            pltpu.VMEM((8 * LANES, 2 * LANES), bf16),
            pltpu.VMEM((2, deep, 2 * LANES), bf16),
            part,
            part,
            pltpu.VMEM((groups - 2, padded, LANES), bf16),
            pltpu.VMEM((tiles, padded, LANES), bf16),
        ],
        in_specs=[whole] * count,
        out_specs=[whole] * 8,
        scratch_shapes=[
            pltpu.VMEM((groups - 2, rows, LANES), f32),
            pltpu.VMEM((members * (groups - 2) * lats // LANES, LANES, LANES), f32),
        ],
        compiler_params=pltpu.CompilerParams(vmem_limit_bytes=12 * 2**20),
        cost_estimate=pl.CostEstimate(flops=10**7, bytes_accessed=10**7, transcendentals=0),
        name="prepare",
    )(*held)
    last = lat_count - 1
    smem = pl.BlockSpec(memory_space=pltpu.SMEM)
    to_even, to_odd = pl.pallas_call(
        functools.partial(join_kernel, sizes, lons),
        out_shape=[message] * 2,
        in_specs=[whole] * 4,
        out_specs=[whole] * 2,
        scratch_shapes=[
            pltpu.VMEM((2, 2, tall, LANES), f32),
            pltpu.VMEM((2, wide, LANES), f32),
        ],
        compiler_params=pltpu.CompilerParams(vmem_limit_bytes=4 * 2**20),
        name="join_rims",
    )(lon_even, lon_odd, own_head, own_tail)
    even_rim = lax.ppermute(to_even, "lat", [(i, i ^ 1) for i in range(lat_count)])
    pairs = []
    for t in range(lon_count):
        at = t * lat_count
        pairs += [(at + k, at + k - 1 + 2 * (k % 2)) for k in range(1, last)]
        pairs += [(at, (t ^ 1) * lat_count), (at + last, (lon_count - 1 - t) * lat_count + last)]
    odd_rim = lax.ppermute(to_odd, ("lon", "lat"), pairs)

    ends, base = pl.pallas_call(
        functools.partial(cells_kernel, sizes),
        out_shape=[pltpu.VMEM((2, padded, LANES), bf16), pltpu.VMEM((3, *velocity_u.shape), f32)],
        in_specs=[whole] * 8,
        out_specs=[whole] * 2,
        scratch_shapes=[
            pltpu.VMEM((2, tall, lats), f32),
            pltpu.VMEM((2, rows, LANES), f32),
            pltpu.VMEM((2 * members * lats // LANES, LANES, LANES), f32),
        ],
        compiler_params=pltpu.CompilerParams(vmem_limit_bytes=12 * 2**20),
        cost_estimate=pl.CostEstimate(flops=10**7, bytes_accessed=10**7, transcendentals=0),
        name="cells",
    )(*state, lon_even, lon_odd, to_even)

    out = jax.ShapeDtypeStruct(velocity_u.shape, f32)
    return pl.pallas_call(
        functools.partial(main_kernel, sizes),
        out_shape=[out] * 3 + [pltpu.VMEM(x.shape, x.dtype) for x in (middle, ends, pre)],
        in_specs=[smem] + [whole] * 12,
        out_specs=[pl.BlockSpec(memory_space=pltpu.HBM)] * 3 + [whole] * 3,
        input_output_aliases={1: 3, 2: 4, 3: 5},
        scratch_shapes=[
            pltpu.VMEM((tiles, padded, LANES), bf16),
            pltpu.VMEM((3, padded, LANES), f32),
            pltpu.VMEM((members, lats, LANES), f32),
            pltpu.VMEM((4, LANES, LANES), f32),
            pltpu.VMEM((groups, GAP * SUB, LANES), f32),
            pltpu.VMEM((3, *velocity_u.shape), f32),
            pltpu.SemaphoreType.DMA((3, members)),
        ],
        compiler_params=pltpu.CompilerParams(vmem_limit_bytes=32 * 2**20),
        cost_estimate=pl.CostEstimate(flops=2 * 10**10, bytes_accessed=10**7, transcendentals=4 * 10**6),
        name="network_and_step",
    )(
        bias_last,
        middle,
        ends,
        pre,
        base,
        state[4],
        even_rim,
        odd_rim,
        to_odd,
        t1,
        t2,
        t3,
        t4,
    )[:3]


def solution(mesh):
    tiles = P(None, None, "lon", "lat")
    return jax.shard_map(
        body,
        mesh=mesh,
        in_specs=(tiles,) * 4 + (P("lon", "lat"),) + (P(),) * 8,
        out_specs=(tiles,) * 3,
        check_vma=False,
    )
```

```python
import functools

import jax
import jax.numpy as jnp
from jax import lax
from jax.experimental import pallas as pl
from jax.experimental.pallas import tpu as pltpu
from jax.sharding import PartitionSpec as P

REDUCED = 0.5
TIME_STEP = 0.2
VISCOSITY = 0.05
CORIOLIS = 0.4

RIM = 4
GAP = 16
NORTH, STRIP, GHOST, SOUTH = 0, 4, 8, 12
SUB = 16
LANES = 128
GROUP = 8
LAND = 2.0**100

f32 = jnp.float32
bf16 = jnp.bfloat16


def iota(shape, dim):
    return lax.broadcasted_iota(jnp.int32, shape, dim)


def dot(a, b):
    return jnp.dot(a, b, preferred_element_type=f32)


def rest(x):
    return x - x.astype(bf16).astype(f32)


def pack_lon_kernel(sizes, count, *refs):
    sources, held, (even, odd, wide, done) = refs[:count], refs[count : 2 * count], refs[2 * count :]
    members, noises, levels = sizes
    fields = noises + 3 * levels
    noise, u, v, h, sea = held[:5]
    lons, lats = sea.shape
    copies = [pltpu.make_async_copy(x, y, done.at[n]) for n, (x, y) in enumerate(zip(sources, held))]
    for copy in copies:
        copy.start()
    for copy in copies[:5]:
        copy.wait()
    upper = iota((GROUP, lats), 0) < RIM

    def field(m, c, side):
        if c < noises:
            full = noise[m, c].astype(f32)
            return full[-GROUP:] if side else full[:GROUP]
        c -= noises
        return (u, v, h)[c // levels][m, c % levels, pl.ds(side * (lons - GROUP), GROUP)]

    rests = members * fields * RIM + GROUP
    for m in range(members):
        for c in range(0, fields, 2):
            rows = pl.ds((m * fields + c) * RIM, GROUP)
            wide[0, rows] = jnp.where(upper, field(m, c, 0), pltpu.roll(field(m, c + 1, 0), RIM, 0))
            wide[1, rows] = jnp.where(upper, pltpu.roll(field(m, c, 1), RIM, 0), field(m, c + 1, 1))
        for c in range(noises, fields):
            row = pl.ds(rests + m * (fields - noises) + c - noises, 1)
            wide[0, row] = rest(field(m, c, 0)[:1])
            wide[1, row] = rest(field(m, c, 1)[GROUP - 1 :])
    rows = pl.ds(members * fields * RIM, GROUP)
    ends = [sea[pl.ds(side * (lons - GROUP), GROUP)].astype(f32) for side in range(2)]
    wide[0, rows] = jnp.where(upper, ends[0], 0.0)
    wide[1, rows] = jnp.where(upper, pltpu.roll(ends[1], RIM, 0), 0.0)
    is_odd = lax.axis_index("lon") % 2 == 1
    even[...] = jnp.where(is_odd, wide[0], wide[1]).astype(bf16)
    odd[...] = jnp.where(is_odd, wide[1], wide[0]).astype(bf16)
    for copy in copies[5:]:
        copy.wait()


def lon_rims(even, odd, lanes=slice(None)):
    is_odd = lax.axis_index("lon") % 2 == 1
    a, b = even[:, lanes].astype(f32), odd[:, lanes].astype(f32)
    return jnp.where(is_odd, a, b), jnp.where(is_odd, b, a)


def rim_tile(sizes, m, c, side, rim):
    members, noises, levels = sizes
    fields = noises + 3 * levels
    row = (m * fields + c) * RIM if c < fields else members * fields * RIM
    tile = rim[pl.ds(row // GROUP * GROUP, GROUP)]
    if (row // RIM) % 2 == side:
        return tile
    return pltpu.roll(tile, RIM, 0)


def window(tiles, following, mask, next_mask):
    pair = iota(mask.shape, 0) // 2
    zero = jnp.zeros_like(mask)
    more = []
    for start in range(0, len(tiles), 4):
        total = zero
        for n in range(min(4, len(tiles) - start)):
            moved = pltpu.roll(following[start + n], 2 * n, 0) if n else following[start]
            total = jnp.where(pair == n, moved, total)
        more.append(total)
    return jnp.concatenate(
        tiles + more + [mask - 1.0, next_mask - 1.0, jnp.ones_like(mask)], axis=0
    )


def store_lats(block, t, dst, tile, m, lats, chunks, buffer):
    blocks = (lats + GAP) // chunks
    buffer[...] = jnp.transpose(block)
    for q in range(chunks):
        lo = max(q * blocks, t * LANES)
        hi = min((q + 1) * blocks, (t + 1) * LANES, lats)
        if lo < hi:
            start = (lo - q * blocks) * SUB + m * chunks + q
            dst[tile, pl.ds(start, hi - lo, stride=SUB), :] = buffer[pl.ds(lo - t * LANES, hi - lo), :]


def shifted_tiles(sizes, refs, m, c, t):
    noise, u, v, h, sea = refs
    members, noises, levels = sizes
    fields = noises + 3 * levels
    lons = sea.shape[0]
    lanes = slice(t * LANES, (t + 1) * LANES)
    if c == fields:
        full = sea[:, lanes].astype(f32)
    elif c < noises:
        full = noise[m, c, :, lanes].astype(f32)
    else:
        full = (u, v, h)[(c - noises) // levels][m, (c - noises) % levels, :, lanes]
    full = pltpu.roll(full, lons - RIM, 0)
    tiles = [full[g * GROUP : (g + 1) * GROUP] for g in range(lons // GROUP)]
    return tiles[-1:] + tiles


def prepare_kernel(sizes, noise, u, v, h, sea, *refs):
    weights, matrices, (head, tail, middle, pre, cells, turned) = refs[:7], refs[7:11], refs[11:]
    held = (noise, u, v, h, sea)
    members, noises, levels = sizes
    fields = noises + 3 * levels
    lons, lats = sea.shape
    groups = lons // GROUP + 1
    weights_kernel(*weights, *matrices)
    lane = iota((GROUP, LANES), 1)
    for out, t, first in ((head, 0, 0), (tail, lats // LANES - 1, LANES - RIM)):
        for c in range(fields + 1):
            total = jnp.zeros((GROUP, LANES), f32)
            for m in range(members):
                for g, tile in enumerate(shifted_tiles(sizes, held, m, c, t)):
                    place = (g * members + m) * RIM
                    moved = pltpu.roll(tile, (place - first) % LANES, 1)
                    total = jnp.where((lane >= place) & (lane < place + RIM), moved, total)
                    if noises <= c < fields:
                        place = groups * members * RIM + g * members + m
                        edge = 0 if out is head else LANES - 1
                        moved = pltpu.roll(rest(tile), (place - edge) % LANES, 1)
                        total = jnp.where(lane == place, moved, total)
            out[pl.ds(c * GROUP, GROUP)] = total
        for c in range(fields + 1, out.shape[0] // GROUP):
            out[pl.ds(c * GROUP, GROUP)] = jnp.zeros((GROUP, LANES), f32)
    chunks = SUB // members
    rows = cells.shape[1]
    gap_k = lats - (chunks - 1) * ((lats + GAP) // chunks)
    inner = groups - 2
    for m in range(members):
        for g in range(inner):
            empty = pl.ds(gap_k * SUB + (m + 1) * chunks - 1, GAP, stride=SUB)
            cells[g, empty, :] = jnp.zeros((GAP, LANES), f32)
    for t in range(lats // LANES):
        for m in range(members):
            tiles = [shifted_tiles(sizes, held, m, c, t) for c in range(fields + 1)]
            for g in range(1, inner + 1):
                following = [x[g + 1] for x in tiles]
                block = window([x[g] for x in tiles[:fields]], following[:fields], tiles[fields][g], following[fields])
                buffer = turned.at[(t * members + m) * inner + g - 1]
                store_lats(block, t, cells, g - 1, m, lats, chunks, buffer)
    for g in range(inner):
        middle[g, pl.ds(SUB, rows), :] = cells[g].astype(bf16)
        wrap(middle.at[g], rows)
    for g in range(inner):
        for r, step in row_pieces(rows):
            parts = [middle[g, pl.ds(r + SUB * d, step), :] for d in range(3)]
            put(pre, g + 1, r, activate(dot(jnp.concatenate(parts, axis=1), matrices[0][...])))


def row_pieces(rows):
    half = rows // 2 // SUB * SUB
    return [(0, half), (half, rows - half)]


def activate(pre):
    return (pre * jnp.tanh(pre) + pre).astype(bf16)


def put(y, b, r, out):
    for e in range(out.shape[1] // LANES):
        y[2 * b + e, pl.ds(SUB + r, out.shape[0]), :] = out[:, e * LANES : (e + 1) * LANES]


def wrap(x, rows):
    end = x[pl.ds(rows, SUB), :].astype(f32)
    x[pl.ds(0, SUB), :] = pltpu.roll(end, 1, 0).astype(bf16)
    begin = x[pl.ds(SUB, SUB), :].astype(f32)
    x[pl.ds(SUB + rows, SUB), :] = pltpu.roll(begin, SUB - 1, 0).astype(bf16)


def cells_kernel(sizes, noise, u, v, h, sea, lon_odd, lon_even, after, out, base, rims, cells, turned):
    members, noises, levels = sizes
    fields = noises + 3 * levels
    lons, lats = sea.shape
    groups = lons // GROUP + 1
    chunks = SUB // members
    rows = cells.shape[1]
    gap_k = lats - (chunks - 1) * ((lats + GAP) // chunks)
    rims[0], rims[1] = lon_rims(lon_even, lon_odd)
    for m in range(members):
        for side in range(2):
            empty = pl.ds(gap_k * SUB + (m + 1) * chunks - 1, GAP, stride=SUB)
            cells[side, empty, :] = jnp.zeros((GAP, LANES), f32)
    blank = jnp.zeros((GROUP, LANES), f32)
    upper = iota((GROUP, LANES), 0) < RIM
    for t in range(lats // LANES):
        lanes = slice(t * LANES, (t + 1) * LANES)
        for m in range(members):
            tiles = []
            for c in range(fields + 1):
                groups_of = shifted_tiles(sizes, (noise, u, v, h, sea), m, c, t)
                ends = [rim_tile(sizes, m, c, side, rims.at[side, :, lanes]) for side in range(2)]
                groups_of[0] = jnp.where(upper, ends[0], groups_of[0])
                groups_of[-1] = jnp.where(upper, groups_of[-1], ends[1])
                tiles.append(groups_of)
            for side, g in enumerate((0, groups - 1)):
                following = [x[g + 1] if g + 1 < groups else blank for x in tiles]
                block = window([x[g] for x in tiles[:fields]], following[:fields], tiles[fields][g], following[fields])
                store_lats(block, t, cells, side, m, lats, chunks, turned.at[(t * members + m) * 2 + side])
    for side in range(2):
        out[side, pl.ds(SUB, rows), :] = cells[side].astype(bf16)
    step_kernel(sizes, u, v, h, sea, rims, base)


def step_kernel(sizes, u, v, h, sea, rims, base):
    members, noises, levels = sizes
    fields = noises + 3 * levels
    lons, lats = sea.shape
    ocean = sea[...].astype(f32)
    lat_count = lax.axis_size("lat")
    lat_rows = (lax.axis_index("lat") * lats).astype(f32) + iota((lons, lats), 1).astype(f32)
    turn = CORIOLIS * (2.0 * (lat_rows + 0.5) / (lats * lat_count) - 1.0)
    at_first = iota((lons, lats), 0) == 0
    at_last = iota((lons, lats), 0) == lons - 1
    at_south = iota((lons, lats), 1) == 0
    at_north = iota((lons, lats), 1) == lats - 1
    lon_rests = members * fields * RIM + GROUP

    def around(x, m, c):
        row = (m * fields + c) * RIM
        more = lon_rests + m * (fields - noises) + c - noises
        west = rims[0, pl.ds(row + RIM - 1, 1)] + rims[0, pl.ds(more, 1)]
        east = rims[1, pl.ds(row, 1)] + rims[1, pl.ds(more, 1)]
        return (
            jnp.where(at_first, west, pltpu.roll(x, 1, 0)),
            jnp.where(at_last, east, pltpu.roll(x, lons - 1, 0)),
            jnp.where(at_south, 0.0, pltpu.roll(x, 1, 1)),
            jnp.where(at_north, 0.0, pltpu.roll(x, lats - 1, 1)),
        )

    for m in range(members):
        sets = []
        for level in range(levels):
            sets.append(
                [
                    (x[m, level], around(x[m, level], m, noises + n * levels + level))
                    for n, x in enumerate((u, v, h))
                ]
            )
        for level in range(levels):
            (cu, au), (cv, av), (ch, ah) = sets[level]
            upper, lower = sets[0][2][1], sets[1][2][1]
            pressure = [upper[i] + lower[i] for i in range(4)]
            if level == 1:
                pressure = [pressure[i] + REDUCED * lower[i] for i in range(4)]
            lap_u = au[1] + au[0] + au[3] + au[2] - 4.0 * cu
            lap_v = av[1] + av[0] + av[3] + av[2] - 4.0 * cv
            dx = 0.5 * (pressure[1] - pressure[0])
            dy = 0.5 * (pressure[3] - pressure[2])
            base[0, m, level] = ocean * (cu + TIME_STEP * (turn * cv - dx + VISCOSITY * lap_u))
            base[1, m, level] = ocean * (cv + TIME_STEP * (-turn * cu - dy + VISCOSITY * lap_v))
            flow = 0.5 * (ah[1] * au[1] - ah[0] * au[0]) + 0.5 * (ah[3] * av[3] - ah[2] * av[2])
            base[2, m, level] = ch - TIME_STEP * flow


def join_kernel(sizes, lons, lon_odd, lon_even, head, tail, even, odd, rims, wide):
    members, noises, levels = sizes
    fields = noises + 3 * levels
    groups = lons // GROUP + 1
    lats = lon_even.shape[1]
    for n, lanes in enumerate((slice(0, LANES), slice(lats - LANES, lats))):
        rims[0, n], rims[1, n] = lon_rims(lon_even, lon_odd, lanes)
    lane = iota((GROUP, LANES), 1)
    upper = iota((GROUP, LANES), 0) < RIM
    to_south = lax.axis_index("lat") % 2 == 1
    for c in range(fields + 1):
        rows = pl.ds(c * GROUP, GROUP)
        ends = []
        for n, (part, first) in enumerate(((head, 0), (tail, LANES - RIM))):
            total = part[rows]
            for side in range(2):
                held = upper if side == 0 else ~upper
                for m in range(members):
                    place = ((groups - 1) * side * members + m) * RIM
                    tile = rim_tile(sizes, m, c, side, rims.at[side, n])
                    moved = pltpu.roll(tile, (place - first) % LANES, 1)
                    total = jnp.where(held & (lane >= place) & (lane < place + RIM), moved, total)
            ends.append(total)
        wide[0, rows] = jnp.where(to_south, ends[0], ends[1])
        wide[1, rows] = jnp.where(to_south, ends[1], ends[0])
    rows = pl.ds((fields + 1) * GROUP, wide.shape[1] - (fields + 1) * GROUP)
    wide[:, rows] = jnp.zeros((2, wide.shape[1] - (fields + 1) * GROUP, LANES), f32)
    even[...] = wide[0].astype(bf16)
    odd[...] = wide[1].astype(bf16)


def weights_kernel(w1, w2, w3, w4, bias1, bias2, bias3, t1, t2, t3, t4):
    hidden = w2.shape[2]
    per = LANES // hidden
    lane = iota((hidden, LANES), 1)
    fields = w1.shape[0]
    out_lon = iota((GROUP, LANES), 1) // hidden
    in_row = iota((GROUP, LANES), 0)
    bias_row = iota((GROUP, LANES), 0)

    def bias_rows(layer):
        part = 0.5 * jnp.concatenate([(bias1, bias2, bias3)[layer][...]] * per, axis=1)
        b1 = part.astype(bf16).astype(f32)
        b2 = (part - b1).astype(bf16).astype(f32)
        b3 = part - b1 - b2
        zero = jnp.zeros((GROUP, LANES), f32)
        return jnp.where(
            bias_row == 0,
            b1,
            jnp.where(bias_row == 1, b2, jnp.where(bias_row == 2, b3, zero)),
        )

    def sea_rows(shift, tile):
        lon = iota((2 * GROUP, LANES), 0)
        out = iota((2 * GROUP, LANES), 1) // hidden + per * tile
        return jnp.where(lon == out + shift, LAND, 0.0)

    for dj in range(3):
        taps = []
        for di in range(3):
            cells = [w1[c, di].astype(f32)[dj : dj + 1] for c in range(fields)]
            taps.append(
                [jnp.broadcast_to(0.5 * jnp.concatenate([x] * per, axis=1), (GROUP, LANES)) for x in cells]
            )
        for tile in range(2):
            parts = []
            for c in range(fields):
                total = jnp.zeros((GROUP, LANES), f32)
                for di in range(3):
                    hit = in_row == out_lon + per * tile + di
                    total = jnp.where(hit, taps[di][c], total)
                parts.append(total)
            for start in range(0, fields, 4):
                total = jnp.zeros((GROUP, LANES), f32)
                for n in range(min(4, fields - start)):
                    for di in range(3):
                        hit = in_row % 2 + GROUP == out_lon + per * tile + di
                        total = jnp.where(hit & (in_row // 2 == n), taps[di][start + n], total)
                parts.append(total)
            if dj == 1:
                parts += [sea_rows(1, tile), bias_rows(0)]
            else:
                parts.append(jnp.zeros((3 * GROUP, LANES), f32))
            block = jnp.concatenate(parts, axis=0)
            t1[pl.ds(dj * LANES, LANES), pl.ds(tile * LANES, LANES)] = block.astype(bf16)

    for layer, (w, t) in enumerate(((w2, t2), (w3, t3))):
        for dj in range(3):
            taps = []
            for di in range(3):
                cell = 0.5 * w[di, dj].astype(f32)
                wide = jnp.concatenate([cell, jnp.zeros((hidden, LANES - hidden), f32)], axis=1)
                square = jnp.concatenate([wide] * per, axis=0)
                taps.append(jnp.transpose(square)[:hidden])
            for lon in range(GROUP + 2):
                for tile in range(2):
                    total = jnp.zeros((hidden, LANES), f32)
                    for di in range(3):
                        total = jnp.where(lane // hidden + per * tile == lon - di, taps[di], total)
                    if lon < GROUP:
                        row = dj * GROUP * hidden + lon * hidden
                    else:
                        row = 3 * GROUP * hidden + dj * 2 * hidden + (lon - GROUP) * hidden
                    t[pl.ds(row, hidden), pl.ds(tile * LANES, LANES)] = total.astype(bf16)
        for tile in range(2):
            block = jnp.concatenate(
                [
                    jnp.zeros((5 * GROUP, LANES), f32),
                    sea_rows(2 + layer, tile),
                    bias_rows(1 + layer),
                ],
                axis=0,
            )
            row = 3 * GROUP * hidden + 6 * hidden
            t[pl.ds(row, 2 * hidden), pl.ds(tile * LANES, LANES)] = block.astype(bf16)

    outs = w4.shape[2]
    half = LANES // 2
    lons = half // outs
    slot = iota((hidden, LANES), 1) // half
    out_lon = iota((hidden, LANES), 1) % lons
    taps = {}
    for dj in range(3):
        for di in range(3):
            cell = w4[di, dj].astype(f32)
            wide = jnp.concatenate([cell, jnp.zeros((outs, LANES - hidden), f32)], axis=1)
            square = jnp.concatenate(
                [jnp.broadcast_to(wide[c : c + 1], (lons, LANES)) for c in range(outs)] * 2, axis=0
            )
            taps[dj, di] = jnp.transpose(square)[:hidden]
    order = ((0, 1, 2, None), (1, 0, None, 2))
    for side in range(2):
        for lon in range(t4.shape[1] // hidden):
            for tile in range(2):
                total = jnp.zeros((hidden, LANES), f32)
                for place in range(2):
                    dj = order[side][2 * tile + place]
                    if dj is None:
                        continue
                    for di in range(3):
                        total = jnp.where((slot == place) & (out_lon == lon - di), taps[dj, di], total)
                t4[side, pl.ds(lon * hidden, hidden), pl.ds(tile * LANES, LANES)] = total.astype(bf16)


def main_kernel(
    sizes,
    bias_last,
    middle_in,
    ends_in,
    pre_in,
    base,
    sea,
    odd_rim,
    even_rim,
    own_tail,
    t1,
    t2,
    t3,
    t4,
    new_u,
    new_v,
    new_h,
    middle,
    ends,
    odd,
    even,
    force,
    gathered,
    results,
    done,
):
    members, noises, levels = sizes
    fields = noises + 3 * levels
    lons, lats = sea.shape
    groups = lons // GROUP + 1
    chunks = SUB // members
    blocks = (lats + GAP) // chunks
    rows = blocks * SUB
    gap_k = lats - (chunks - 1) * blocks
    lat_index, lat_count = lax.axis_index("lat"), lax.axis_size("lat")
    top = lat_index == lat_count - 1
    is_odd = lat_index % 2 == 1
    bottom = lat_index == 0
    strip = odd_rim[...].astype(f32)
    paired = even_rim[...].astype(f32)
    south = jnp.where(is_odd, paired, jnp.where(bottom, 0.0, strip))

    wide = strip.shape[0]
    span = members * RIM
    lane = iota((wide, LANES), 1)
    rests = groups * span
    border = ((lane % RIM == 0) & (lane < rests)) | (lane >= rests)
    row_to = iota((wide, wide), 0)
    row_from = iota((wide, wide), 1)
    channel = row_to // GROUP
    mirrored = (channel == row_from // GROUP) & (row_from % GROUP == GROUP - 1 - row_to % GROUP)
    odd_parity = (channel >= noises) & (channel < noises + 2 * levels)
    flip_rows = jnp.where(mirrored, jnp.where(odd_parity, -1.0, 1.0), 0.0).astype(bf16)
    lane_from = iota((LANES, LANES), 0)
    lane_to = iota((LANES, LANES), 1)
    source = (groups - 1 - lane_to // span) * span + lane_to % span + RIM - 1
    moves = (lane_to % RIM == 0) & (lane_to < rests) & (lane_from == source)
    other = lane_to - rests
    source = rests + (groups - 1 - other // members) * members + other % members
    moves = moves | ((other >= 0) & (other < groups * members) & (lane_from == source))
    flip_lanes = jnp.where(moves, 1.0, 0.0).astype(bf16)
    pair = dot(flip_rows, jnp.concatenate([odd_rim[...], own_tail[...]], axis=1)).astype(bf16)
    folded = dot(pair[:, :LANES], flip_lanes)
    ghost = dot(pair[:, LANES:], flip_lanes)
    north = jnp.where(is_odd, strip, paired)
    north_rim = jnp.where(border & top, folded, north)

    spread_row = iota((groups * RIM * SUB, LANES), 0)
    spread_lane = iota((groups * RIM * SUB, LANES), 1)
    line = spread_row // (RIM * SUB) * span + spread_row // SUB % RIM
    of_member = spread_row % SUB // chunks
    next_member = jnp.where(of_member == members - 1, 0, of_member + 1)
    spreads = [
        jnp.where(spread_lane == line + member * RIM, 1.0, 0.0).astype(bf16) for member in (of_member, next_member)
    ]
    gaps = []
    for n, message in enumerate((north_rim, strip, ghost, south)):
        after = pltpu.roll(message, LANES - span, 1)
        cut = [message[c * GROUP : (c + 1) * GROUP] for c in range(fields + 1)]
        after = [after[c * GROUP : (c + 1) * GROUP] for c in range(fields + 1)]
        block = window(cut[:fields], after[:fields], cut[fields], after[fields]).astype(bf16)
        gaps.append(
            lax.dot_general(spreads[n // 3], block, (((1,), (1,)), ((), ())), preferred_element_type=f32)
        )

    first = [ends.at[0]] + [middle.at[g] for g in range(groups - 2)] + [ends.at[1]]
    in_gap = iota((RIM * SUB, LANES), 0) % chunks == chunks - 1
    for g in range(groups):
        for n in range(4):
            spot = pl.ds((1 + gap_k + n * RIM) * SUB, RIM * SUB)
            kept = first[g][spot, :].astype(f32)
            filled = gaps[n][g * RIM * SUB : (g + 1) * RIM * SUB]
            first[g][spot, :] = jnp.where(in_gap, filled, kept).astype(bf16)
        wrap(first[g], rows)

    hidden = LANES // 4
    per = LANES // hidden
    tiles = odd.shape[0]
    pieces = row_pieces(rows)

    def finish(x, valid):
        used = (valid + per - 1) // per

        @pl.when(top)
        def _():
            strip_top = SUB * (1 + gap_k + STRIP + RIM - 1)
            own_top = SUB * gap_k
            strip_ghost = SUB * (1 + gap_k + GHOST)
            own_ghost = SUB * (1 + gap_k + NORTH)
            last_chunk = iota((SUB, LANES), 0) % chunks == chunks - 1
            spot = iota((SUB, LANES), 1) // hidden
            for src, dst in ((strip_top, own_ghost), (own_top, strip_ghost)):
                found = [x[t, pl.ds(src, SUB), :].astype(f32) for t in range(used)]
                for t in range(used):
                    total = x[t, pl.ds(dst, SUB), :].astype(f32)
                    for i in range(per):
                        lon = valid - 1 - (per * t + i)
                        if lon < 0:
                            continue
                        moved = pltpu.roll(found[lon // per], (hidden * (i - lon % per)) % LANES, 1)
                        total = jnp.where(last_chunk & (spot == i), moved, total)
                    x[t, pl.ds(dst, SUB), :] = total.astype(bf16)

        for t in range(used):
            wrap(x.at[t], rows)

    for x in (odd, even):
        x[tiles - 1] = jnp.zeros(x.shape[1:], bf16)
    even[tiles - 2] = jnp.zeros(even.shape[1:], bf16)

    for b in (0, groups - 1):
        for r, step in pieces:
            parts = [first[b][pl.ds(r + SUB * d, step), :] for d in range(3)]
            put(odd, b, r, activate(dot(jnp.concatenate(parts, axis=1), t1[...])))
    near = (gap_k - 1) * SUB
    for b in range(1, groups - 1):
        parts = []
        for d in range(3):
            some = [first[b][pl.ds(near + SUB * d, rows - near), :], first[b][pl.ds(SUB * d, SUB), :]]
            parts.append(jnp.concatenate(some, axis=0))
        out = activate(dot(jnp.concatenate(parts, axis=1), t1[...]))
        put(odd, b, near, out[: rows - near])
        put(odd, b, 0, out[rows - near :])
    finish(odd, lons + 6)

    ocean = sea[...].astype(f32)
    narrow = iota((lons, LANES), 1)
    at_south = narrow == 0
    at_north = narrow == LANES - 1

    def beyond(message, m, offset, to):
        tall = message[noises * GROUP : fields * GROUP]
        columns = []
        for g in range(groups):
            spot = (g * members + m) * RIM + offset
            more = rests + g * members + m
            column = pltpu.roll(tall, (to - spot) % LANES, 1)
            columns.append(column + pltpu.roll(tall, (to - more) % LANES, 1))
        cells = []
        for c in range(fields - noises):
            whole = jnp.concatenate([x[c * GROUP : (c + 1) * GROUP] for x in columns], axis=0)
            cells.append(pltpu.roll(whole, lons + GROUP - RIM, 0)[:lons])
        return cells

    def step_rims(m):
        rims = [beyond(south, m, RIM - 1, 0), beyond(north_rim, m, 0, LANES - 1)]
        for level in range(levels):
            gains = []
            for (sign, spot), rim in zip(((1.0, at_south), (-1.0, at_north)), rims):
                ru, rv, rh = rim[level], rim[levels + level], rim[2 * levels + level]
                pressure = rim[2 * levels] + rim[2 * levels + 1]
                if level == 1:
                    pressure = pressure + REDUCED * rh
                gains.append(
                    [
                        jnp.where(spot, TIME_STEP * VISCOSITY * ru, 0.0),
                        jnp.where(spot, TIME_STEP * (VISCOSITY * rv + sign * 0.5 * pressure), 0.0),
                        jnp.where(spot, TIME_STEP * sign * 0.5 * (rh * rv), 0.0),
                    ]
                )
            middle = [jnp.zeros((lons, lats - 2 * LANES), f32)] if lats > 2 * LANES else []
            gains = [jnp.concatenate([gains[0][n]] + middle + [gains[1][n]], axis=1) for n in range(3)]
            results[0, m, level] = base[0, m, level] + ocean * gains[0]
            results[1, m, level] = base[1, m, level] + ocean * gains[1]
            results[2, m, level] = base[2, m, level] + gains[2]
        pltpu.make_async_copy(results.at[2, m], new_h.at[m], done.at[2, m]).start()

    width = GROUP * hidden

    def layer(x, y, t, left_over, beside):
        for b in range(groups):
            for r, step in pieces:
                lower = iota((step, LANES), 1) < 2 * hidden

                def cells_of(tile, d):
                    return x[tile, pl.ds(r + SUB * d, step), :]

                def packed(tile):
                    more = [cells_of(tile, d) for d in range(3)]
                    return [
                        jnp.where(lower, more[0], pltpu.roll(more[1], 2 * hidden, 1)),
                        jnp.where(lower, more[2], first[b][pl.ds(r + SUB, step), :]),
                    ]

                if b < groups - 1:
                    parts = [cells_of(2 * b + e, d) for d in range(3) for e in range(2)] + packed(2 * b + 2)
                    matrix = t[...]
                elif left_over == per:
                    parts = [cells_of(2 * b, d) for d in range(3)] + packed(2 * b + 1)
                    lanes = pl.ds(0, LANES)
                    matrix = jnp.concatenate(
                        [t[pl.ds(d * width, LANES), lanes] for d in range(3)]
                        + [t[pl.ds(d * width + LANES, 2 * hidden), lanes] for d in range(3)]
                        + [t[pl.ds(3 * width + 6 * hidden, 2 * hidden), lanes]],
                        axis=0,
                    )
                else:
                    parts = [cells_of(2 * b, d) for d in range(3)] + [first[b][pl.ds(r + SUB, step), :]]
                    lanes = pl.ds(0, LANES)
                    matrix = jnp.concatenate(
                        [t[pl.ds(d * width, LANES), lanes] for d in range(3)]
                        + [jnp.zeros((2 * hidden, LANES), bf16)]
                        + [t[pl.ds(3 * width + 6 * hidden, 2 * hidden), lanes]],
                        axis=0,
                    )
                put(y, b, r, activate(dot(jnp.concatenate(parts, axis=1), matrix)))
            for m in beside.get(b, ()):
                step_rims(m)

    beside = {}
    for m in range(members):
        beside.setdefault(min(m, groups - 1), []).append(m)
    layer(odd, even, t2, per, beside)
    finish(even, lons + 4)
    layer(even, odd, t3, per // 2, {})
    finish(odd, lons + 2)

    depth = t4.shape[1] // LANES
    padded = rows + 2 * SUB
    for r, long in row_pieces(padded):
        before = iota((long, LANES), 1) < LANES // 2
        span_rows = pl.ds(r, long)
        sides = []
        for side in range(2):
            parts = [odd[side * (depth - 1) + t, span_rows, :] for t in range(depth)]
            sides.append(dot(jnp.concatenate(parts, axis=1), t4[side]))
        force[0, span_rows, :] = jnp.where(before, sides[0][:, :LANES], sides[1][:, :LANES])
        swapped = jnp.where(before, sides[1][:, :LANES], sides[0][:, :LANES])
        force[1, span_rows, :] = pltpu.roll(swapped, LANES // 2, 1)
        force[2, span_rows, :] = jnp.where(before, sides[0][:, LANES:], sides[1][:, LANES:])

    halves = lons // 2
    for m in range(members):
        for q in range(chunks):
            size = min(blocks, lats - q * blocks)
            total = force[0, pl.ds(m * chunks + q, size, stride=SUB), :]
            for d in range(1, 3):
                total = total + force[d, pl.ds(d * SUB + m * chunks + q, size, stride=SUB), :]
            gathered[m, pl.ds(q * blocks, size), :] = total
        turned_force = jnp.transpose(gathered[m])
        for n, out in enumerate((new_u, new_v)):
            for level in range(levels):
                c = n * levels + level
                parts = [
                    turned_force[side * LANES // 2 + c * halves : side * LANES // 2 + (c + 1) * halves]
                    for side in range(2)
                ]
                push = TIME_STEP * (jnp.concatenate(parts, axis=0) + bias_last[c])
                results[n, m, level] = results[n, m, level] + ocean * push
            pltpu.make_async_copy(results.at[n, m], out.at[m], done.at[n, m]).start()
    for m in range(members):
        for n, out in enumerate((new_u, new_v, new_h)):
            pltpu.make_async_copy(results.at[n, m], out.at[m], done.at[n, m]).wait()


def body(
    noise,
    velocity_u,
    velocity_v,
    thickness,
    land_sea,
    conv_first,
    bias_first,
    conv_second,
    bias_second,
    conv_third,
    bias_third,
    conv_last,
    bias_last,
):
    members, noises, lons, lats = noise.shape
    levels = velocity_u.shape[1]
    fields = noises + 3 * levels
    sizes = (members, noises, levels)
    hidden = conv_first.shape[0]
    outs = conv_last.shape[0]
    groups = lons // GROUP + 1
    rows = members * (lats + GAP)
    assert hidden * 4 == LANES and outs * lons == LANES and members * (RIM + 1) * groups <= LANES
    assert fields % 2 == 0 and 4 * -(-fields // 4) == 12 and GROUP * (fields + 6) == LANES and lons % 16 == 0
    assert lats % LANES == 0 and SUB % members == 0 and (lats + GAP) % (SUB // members) == 0
    lon_count, lat_count = lax.axis_size("lon"), lax.axis_size("lat")
    assert lon_count % 2 == 0 and lat_count % 2 == 0
    state = (noise, velocity_u, velocity_v, thickness, land_sea)
    whole = pl.BlockSpec(memory_space=pltpu.VMEM)

    tall = members * fields * RIM + GROUP + members * 3 * levels
    assert tall % SUB == 0
    args = state + (
        conv_first.transpose(1, 2, 3, 0),
        conv_second.transpose(2, 3, 0, 1),
        conv_third.transpose(2, 3, 0, 1),
        conv_last.transpose(2, 3, 0, 1),
        bias_first[None],
        bias_second[None],
        bias_third[None],
    )
    count = len(args)
    *held, to_even, to_odd = pl.pallas_call(
        functools.partial(pack_lon_kernel, sizes, count),
        out_shape=[pltpu.VMEM(x.shape, x.dtype) for x in args] + [pltpu.VMEM((tall, lats), bf16)] * 2,
        in_specs=[pl.BlockSpec(memory_space=pltpu.HBM)] * count,
        out_specs=[whole] * (count + 2),
        scratch_shapes=[pltpu.VMEM((2, tall, lats), f32), pltpu.SemaphoreType.DMA((count,))],
        compiler_params=pltpu.CompilerParams(vmem_limit_bytes=62 * 2**20),
        name="pack_lon",
    )(*args)
    state = tuple(held[:5])
    lon_odd = lax.ppermute(to_odd, "lon", [(i, (i - 1 + 2 * (i % 2)) % lon_count) for i in range(lon_count)])
    lon_even = lax.ppermute(to_even, "lon", [(i, i ^ 1) for i in range(lon_count)])

    wide = -(-(fields + 1) * GROUP // SUB) * SUB
    part = pltpu.VMEM((wide, LANES), f32)
    message = pltpu.VMEM((wide, LANES), bf16)
    deep = -(-(lons // 2 + 2) * hidden // LANES) * LANES
    padded = rows + 2 * SUB
    tiles = 2 * groups + 1
    t1, t2, t3, t4, own_head, own_tail, middle, pre = pl.pallas_call(
        functools.partial(prepare_kernel, sizes),
        out_shape=[
            pltpu.VMEM((3 * LANES, 2 * LANES), bf16),
            pltpu.VMEM((8 * LANES, 2 * LANES), bf16),
            pltpu.VMEM((8 * LANES, 2 * LANES), bf16),
            pltpu.VMEM((2, deep, 2 * LANES), bf16),
            part,
            part,
            pltpu.VMEM((groups - 2, padded, LANES), bf16),
            pltpu.VMEM((tiles, padded, LANES), bf16),
        ],
        in_specs=[whole] * count,
        out_specs=[whole] * 8,
        scratch_shapes=[
            pltpu.VMEM((groups - 2, rows, LANES), f32),
            pltpu.VMEM((members * (groups - 2) * lats // LANES, LANES, LANES), f32),
        ],
        compiler_params=pltpu.CompilerParams(vmem_limit_bytes=12 * 2**20),
        cost_estimate=pl.CostEstimate(flops=10**7, bytes_accessed=10**7, transcendentals=0),
        name="prepare",
    )(*held)
    last = lat_count - 1
    smem = pl.BlockSpec(memory_space=pltpu.SMEM)
    to_even, to_odd = pl.pallas_call(
        functools.partial(join_kernel, sizes, lons),
        out_shape=[message] * 2,
        in_specs=[whole] * 4,
        out_specs=[whole] * 2,
        scratch_shapes=[
            pltpu.VMEM((2, 2, tall, LANES), f32),
            pltpu.VMEM((2, wide, LANES), f32),
        ],
        compiler_params=pltpu.CompilerParams(vmem_limit_bytes=4 * 2**20),
        name="join_rims",
    )(lon_odd, lon_even, own_head, own_tail)
    pairs = []
    for t in range(lon_count):
        at = t * lat_count
        pairs += [(at + k, at + k - 1 + 2 * (k % 2)) for k in range(1, last)]
        pairs += [(at, (t ^ 1) * lat_count), (at + last, (lon_count - 1 - t) * lat_count + last)]
    odd_rim = lax.ppermute(to_odd, ("lon", "lat"), pairs)
    even_rim = lax.ppermute(to_even, "lat", [(i, i ^ 1) for i in range(lat_count)])

    ends, base = pl.pallas_call(
        functools.partial(cells_kernel, sizes),
        out_shape=[pltpu.VMEM((2, padded, LANES), bf16), pltpu.VMEM((3, *velocity_u.shape), f32)],
        in_specs=[whole] * 8,
        out_specs=[whole] * 2,
        scratch_shapes=[
            pltpu.VMEM((2, tall, lats), f32),
            pltpu.VMEM((2, rows, LANES), f32),
            pltpu.VMEM((2 * members * lats // LANES, LANES, LANES), f32),
        ],
        compiler_params=pltpu.CompilerParams(vmem_limit_bytes=12 * 2**20),
        cost_estimate=pl.CostEstimate(flops=10**7, bytes_accessed=10**7, transcendentals=0),
        name="cells",
    )(*state, lon_odd, lon_even, to_even)

    out = jax.ShapeDtypeStruct(velocity_u.shape, f32)
    return pl.pallas_call(
        functools.partial(main_kernel, sizes),
        out_shape=[out] * 3 + [pltpu.VMEM(x.shape, x.dtype) for x in (middle, ends, pre)],
        in_specs=[smem] + [whole] * 12,
        out_specs=[pl.BlockSpec(memory_space=pltpu.HBM)] * 3 + [whole] * 3,
        input_output_aliases={1: 3, 2: 4, 3: 5},
        scratch_shapes=[
            pltpu.VMEM((tiles, padded, LANES), bf16),
            pltpu.VMEM((3, padded, LANES), f32),
            pltpu.VMEM((members, lats, LANES), f32),
            pltpu.VMEM((3, *velocity_u.shape), f32),
            pltpu.SemaphoreType.DMA((3, members)),
        ],
        compiler_params=pltpu.CompilerParams(vmem_limit_bytes=32 * 2**20),
        cost_estimate=pl.CostEstimate(flops=2 * 10**10, bytes_accessed=10**7, transcendentals=4 * 10**6),
        name="network_and_step",
    )(
        bias_last,
        middle,
        ends,
        pre,
        base,
        state[4],
        odd_rim,
        even_rim,
        to_odd,
        t1,
        t2,
        t3,
        t4,
    )[:3]


def solution(mesh):
    tiles = P(None, None, "lon", "lat")
    return jax.shard_map(
        body,
        mesh=mesh,
        in_specs=(tiles,) * 4 + (P("lon", "lat"),) + (P(),) * 8,
        out_specs=(tiles,) * 3,
        check_vma=False,
    )
```

```python
import functools

import jax
import jax.numpy as jnp
from jax import lax
from jax.experimental import pallas as pl
from jax.experimental.pallas import tpu as pltpu
from jax.sharding import PartitionSpec as P

REDUCED = 0.5
TIME_STEP = 0.2
VISCOSITY = 0.05
CORIOLIS = 0.4

RIM = 4
GAP = 16
NORTH, STRIP, GHOST, SOUTH = 0, 4, 8, 12
SUB = 16
LANES = 128
GROUP = 8
LAND = 2.0**100

f32 = jnp.float32
bf16 = jnp.bfloat16


def iota(shape, dim):
    return lax.broadcasted_iota(jnp.int32, shape, dim)


def dot(a, b):
    return jnp.dot(a, b, preferred_element_type=f32)


def rest(x):
    return x - x.astype(bf16).astype(f32)


def pack_lon_kernel(sizes, count, *refs):
    sources, held, (even, odd, wide, done) = refs[:count], refs[count : 2 * count], refs[2 * count :]
    members, noises, levels = sizes
    fields = noises + 3 * levels
    noise, u, v, h, sea = held[:5]
    lons, lats = sea.shape
    copies = [pltpu.make_async_copy(x, y, done.at[n]) for n, (x, y) in enumerate(zip(sources, held))]
    for copy in copies:
        copy.start()
    for copy in copies[:5]:
        copy.wait()
    upper = iota((GROUP, lats), 0) < RIM

    def field(m, c, side):
        if c < noises:
            full = noise[m, c].astype(f32)
            return full[-GROUP:] if side else full[:GROUP]
        c -= noises
        return (u, v, h)[c // levels][m, c % levels, pl.ds(side * (lons - GROUP), GROUP)]

    rests = members * fields * RIM + GROUP
    for m in range(members):
        for c in range(0, fields, 2):
            rows = pl.ds((m * fields + c) * RIM, GROUP)
            wide[0, rows] = jnp.where(upper, field(m, c, 0), pltpu.roll(field(m, c + 1, 0), RIM, 0))
            wide[1, rows] = jnp.where(upper, pltpu.roll(field(m, c, 1), RIM, 0), field(m, c + 1, 1))
        for c in range(noises, fields):
            row = pl.ds(rests + m * (fields - noises) + c - noises, 1)
            wide[0, row] = rest(field(m, c, 0)[:1])
            wide[1, row] = rest(field(m, c, 1)[GROUP - 1 :])
    rows = pl.ds(members * fields * RIM, GROUP)
    ends = [sea[pl.ds(side * (lons - GROUP), GROUP)].astype(f32) for side in range(2)]
    wide[0, rows] = jnp.where(upper, ends[0], 0.0)
    wide[1, rows] = jnp.where(upper, pltpu.roll(ends[1], RIM, 0), 0.0)
    is_odd = lax.axis_index("lon") % 2 == 1
    even[...] = jnp.where(is_odd, wide[0], wide[1]).astype(bf16)
    odd[...] = jnp.where(is_odd, wide[1], wide[0]).astype(bf16)
    for copy in copies[5:]:
        copy.wait()


def lon_rims(even, odd, lanes=slice(None)):
    is_odd = lax.axis_index("lon") % 2 == 1
    a, b = even[:, lanes].astype(f32), odd[:, lanes].astype(f32)
    return jnp.where(is_odd, a, b), jnp.where(is_odd, b, a)


def rim_tile(sizes, m, c, side, rim):
    members, noises, levels = sizes
    fields = noises + 3 * levels
    row = (m * fields + c) * RIM if c < fields else members * fields * RIM
    tile = rim[pl.ds(row // GROUP * GROUP, GROUP)]
    if (row // RIM) % 2 == side:
        return tile
    return pltpu.roll(tile, RIM, 0)


def window(tiles, following, mask, next_mask):
    pair = iota(mask.shape, 0) // 2
    zero = jnp.zeros_like(mask)
    more = []
    for start in range(0, len(tiles), 4):
        total = zero
        for n in range(min(4, len(tiles) - start)):
            moved = pltpu.roll(following[start + n], 2 * n, 0) if n else following[start]
            total = jnp.where(pair == n, moved, total)
        more.append(total)
    return jnp.concatenate(
        tiles + more + [mask - 1.0, next_mask - 1.0, jnp.ones_like(mask)], axis=0
    )


def store_lats(block, t, dst, tile, m, lats, chunks, buffer):
    blocks = (lats + GAP) // chunks
    buffer[...] = jnp.transpose(block)
    for q in range(chunks):
        lo = max(q * blocks, t * LANES)
        hi = min((q + 1) * blocks, (t + 1) * LANES, lats)
        if lo < hi:
            start = (lo - q * blocks) * SUB + m * chunks + q
            dst[tile, pl.ds(start, hi - lo, stride=SUB), :] = buffer[pl.ds(lo - t * LANES, hi - lo), :]


def shifted_tiles(sizes, refs, m, c, t):
    noise, u, v, h, sea = refs
    members, noises, levels = sizes
    fields = noises + 3 * levels
    lons = sea.shape[0]
    lanes = slice(t * LANES, (t + 1) * LANES)
    if c == fields:
        full = sea[:, lanes].astype(f32)
    elif c < noises:
        full = noise[m, c, :, lanes].astype(f32)
    else:
        full = (u, v, h)[(c - noises) // levels][m, (c - noises) % levels, :, lanes]
    full = pltpu.roll(full, lons - RIM, 0)
    tiles = [full[g * GROUP : (g + 1) * GROUP] for g in range(lons // GROUP)]
    return tiles[-1:] + tiles


def prepare_kernel(sizes, noise, u, v, h, sea, *refs):
    w1, bias1, t1, head, tail, middle, pre, cells, turned = refs
    held = (noise, u, v, h, sea)
    members, noises, levels = sizes
    fields = noises + 3 * levels
    lons, lats = sea.shape
    groups = lons // GROUP + 1
    first_weights(w1, bias1, t1)
    lane = iota((GROUP, LANES), 1)
    for out, t, first in ((head, 0, 0), (tail, lats // LANES - 1, LANES - RIM)):
        for c in range(fields + 1):
            total = jnp.zeros((GROUP, LANES), f32)
            for m in range(members):
                for g, tile in enumerate(shifted_tiles(sizes, held, m, c, t)):
                    place = (g * members + m) * RIM
                    moved = pltpu.roll(tile, (place - first) % LANES, 1)
                    total = jnp.where((lane >= place) & (lane < place + RIM), moved, total)
                    if noises <= c < fields:
                        place = groups * members * RIM + g * members + m
                        edge = 0 if out is head else LANES - 1
                        moved = pltpu.roll(rest(tile), (place - edge) % LANES, 1)
                        total = jnp.where(lane == place, moved, total)
            out[pl.ds(c * GROUP, GROUP)] = total
        for c in range(fields + 1, out.shape[0] // GROUP):
            out[pl.ds(c * GROUP, GROUP)] = jnp.zeros((GROUP, LANES), f32)
    chunks = SUB // members
    rows = cells.shape[1]
    gap_k = lats - (chunks - 1) * ((lats + GAP) // chunks)
    inner = groups - 2
    for m in range(members):
        for g in range(inner):
            empty = pl.ds(gap_k * SUB + (m + 1) * chunks - 1, GAP, stride=SUB)
            cells[g, empty, :] = jnp.zeros((GAP, LANES), f32)
    for t in range(lats // LANES):
        for m in range(members):
            tiles = [shifted_tiles(sizes, held, m, c, t) for c in range(fields + 1)]
            for g in range(1, inner + 1):
                following = [x[g + 1] for x in tiles]
                block = window([x[g] for x in tiles[:fields]], following[:fields], tiles[fields][g], following[fields])
                buffer = turned.at[(t * members + m) * inner + g - 1]
                store_lats(block, t, cells, g - 1, m, lats, chunks, buffer)
    for g in range(inner):
        middle[g, pl.ds(SUB, rows), :] = cells[g].astype(bf16)
        wrap(middle.at[g], rows)
    for g in range(inner):
        for r, step in row_pieces(rows):
            parts = [middle[g, pl.ds(r + SUB * d, step), :] for d in range(3)]
            put(pre, g + 1, r, activate(dot(jnp.concatenate(parts, axis=1), t1[...])))


def row_pieces(rows):
    half = rows // 2 // SUB * SUB
    return [(0, half), (half, rows - half)]


def activate(pre):
    return (pre * jnp.tanh(pre) + pre).astype(bf16)


def put(y, b, r, out):
    for e in range(out.shape[1] // LANES):
        y[2 * b + e, pl.ds(SUB + r, out.shape[0]), :] = out[:, e * LANES : (e + 1) * LANES]


def wrap(x, rows):
    end = x[pl.ds(rows, SUB), :].astype(f32)
    x[pl.ds(0, SUB), :] = pltpu.roll(end, 1, 0).astype(bf16)
    begin = x[pl.ds(SUB, SUB), :].astype(f32)
    x[pl.ds(SUB + rows, SUB), :] = pltpu.roll(begin, SUB - 1, 0).astype(bf16)


def cells_kernel(sizes, noise, u, v, h, sea, lon_even, lon_odd, after, *refs):
    weights, (t1, _, out, base, pre, *matrices, rims, cells, turned) = refs[:5], refs[5:]
    members, noises, levels = sizes
    fields = noises + 3 * levels
    lons, lats = sea.shape
    groups = lons // GROUP + 1
    chunks = SUB // members
    rows = cells.shape[1]
    gap_k = lats - (chunks - 1) * ((lats + GAP) // chunks)
    rims[0], rims[1] = lon_rims(lon_even, lon_odd)
    for m in range(members):
        for side in range(2):
            empty = pl.ds(gap_k * SUB + (m + 1) * chunks - 1, GAP, stride=SUB)
            cells[side, empty, :] = jnp.zeros((GAP, LANES), f32)
    blank = jnp.zeros((GROUP, LANES), f32)
    upper = iota((GROUP, LANES), 0) < RIM
    for t in range(lats // LANES):
        lanes = slice(t * LANES, (t + 1) * LANES)
        for m in range(members):
            tiles = []
            for c in range(fields + 1):
                groups_of = shifted_tiles(sizes, (noise, u, v, h, sea), m, c, t)
                ends = [rim_tile(sizes, m, c, side, rims.at[side, :, lanes]) for side in range(2)]
                groups_of[0] = jnp.where(upper, ends[0], groups_of[0])
                groups_of[-1] = jnp.where(upper, groups_of[-1], ends[1])
                tiles.append(groups_of)
            for side, g in enumerate((0, groups - 1)):
                following = [x[g + 1] if g + 1 < groups else blank for x in tiles]
                block = window([x[g] for x in tiles[:fields]], following[:fields], tiles[fields][g], following[fields])
                store_lats(block, t, cells, side, m, lats, chunks, turned.at[(t * members + m) * 2 + side])
    for side in range(2):
        out[side, pl.ds(SUB, rows), :] = cells[side].astype(bf16)
        wrap(out.at[side], rows)
    for side in range(2):
        for r, step in row_pieces(rows):
            parts = [out[side, pl.ds(r + SUB * d, step), :] for d in range(3)]
            put(pre, side * (groups - 1), r, activate(dot(jnp.concatenate(parts, axis=1), t1[...])))
    other_weights(*weights, *matrices)
    step_kernel(sizes, u, v, h, sea, rims, base)


def step_kernel(sizes, u, v, h, sea, rims, base):
    members, noises, levels = sizes
    fields = noises + 3 * levels
    lons, lats = sea.shape
    ocean = sea[...].astype(f32)
    lat_count = lax.axis_size("lat")
    lat_rows = (lax.axis_index("lat") * lats).astype(f32) + iota((lons, lats), 1).astype(f32)
    turn = CORIOLIS * (2.0 * (lat_rows + 0.5) / (lats * lat_count) - 1.0)
    at_first = iota((lons, lats), 0) == 0
    at_last = iota((lons, lats), 0) == lons - 1
    at_south = iota((lons, lats), 1) == 0
    at_north = iota((lons, lats), 1) == lats - 1
    lon_rests = members * fields * RIM + GROUP

    def around(x, m, c):
        row = (m * fields + c) * RIM
        more = lon_rests + m * (fields - noises) + c - noises
        west = rims[0, pl.ds(row + RIM - 1, 1)] + rims[0, pl.ds(more, 1)]
        east = rims[1, pl.ds(row, 1)] + rims[1, pl.ds(more, 1)]
        return (
            jnp.where(at_first, west, pltpu.roll(x, 1, 0)),
            jnp.where(at_last, east, pltpu.roll(x, lons - 1, 0)),
            jnp.where(at_south, 0.0, pltpu.roll(x, 1, 1)),
            jnp.where(at_north, 0.0, pltpu.roll(x, lats - 1, 1)),
        )

    for m in range(members):
        sets = []
        for level in range(levels):
            sets.append(
                [
                    (x[m, level], around(x[m, level], m, noises + n * levels + level))
                    for n, x in enumerate((u, v, h))
                ]
            )
        for level in range(levels):
            (cu, au), (cv, av), (ch, ah) = sets[level]
            upper, lower = sets[0][2][1], sets[1][2][1]
            pressure = [upper[i] + lower[i] for i in range(4)]
            if level == 1:
                pressure = [pressure[i] + REDUCED * lower[i] for i in range(4)]
            lap_u = au[1] + au[0] + au[3] + au[2] - 4.0 * cu
            lap_v = av[1] + av[0] + av[3] + av[2] - 4.0 * cv
            dx = 0.5 * (pressure[1] - pressure[0])
            dy = 0.5 * (pressure[3] - pressure[2])
            base[0, m, level] = ocean * (cu + TIME_STEP * (turn * cv - dx + VISCOSITY * lap_u))
            base[1, m, level] = ocean * (cv + TIME_STEP * (-turn * cu - dy + VISCOSITY * lap_v))
            flow = 0.5 * (ah[1] * au[1] - ah[0] * au[0]) + 0.5 * (ah[3] * av[3] - ah[2] * av[2])
            base[2, m, level] = ch - TIME_STEP * flow


def join_kernel(sizes, lons, lon_even, lon_odd, head, tail, even, odd, rims, wide):
    members, noises, levels = sizes
    fields = noises + 3 * levels
    groups = lons // GROUP + 1
    lats = lon_even.shape[1]
    for n, lanes in enumerate((slice(0, LANES), slice(lats - LANES, lats))):
        rims[0, n], rims[1, n] = lon_rims(lon_even, lon_odd, lanes)
    lane = iota((GROUP, LANES), 1)
    upper = iota((GROUP, LANES), 0) < RIM
    to_south = lax.axis_index("lat") % 2 == 1
    for c in range(fields + 1):
        rows = pl.ds(c * GROUP, GROUP)
        ends = []
        for n, (part, first) in enumerate(((head, 0), (tail, LANES - RIM))):
            total = part[rows]
            for side in range(2):
                held = upper if side == 0 else ~upper
                for m in range(members):
                    place = ((groups - 1) * side * members + m) * RIM
                    tile = rim_tile(sizes, m, c, side, rims.at[side, n])
                    moved = pltpu.roll(tile, (place - first) % LANES, 1)
                    total = jnp.where(held & (lane >= place) & (lane < place + RIM), moved, total)
            ends.append(total)
        wide[0, rows] = jnp.where(to_south, ends[0], ends[1])
        wide[1, rows] = jnp.where(to_south, ends[1], ends[0])
    rows = pl.ds((fields + 1) * GROUP, wide.shape[1] - (fields + 1) * GROUP)
    wide[:, rows] = jnp.zeros((2, wide.shape[1] - (fields + 1) * GROUP, LANES), f32)
    even[...] = wide[0].astype(bf16)
    odd[...] = wide[1].astype(bf16)


def extra_rows(hidden):
    per = LANES // hidden
    bias_row = iota((GROUP, LANES), 0)

    def bias_rows(bias):
        part = 0.5 * jnp.concatenate([bias[...]] * per, axis=1)
        b1 = part.astype(bf16).astype(f32)
        b2 = (part - b1).astype(bf16).astype(f32)
        b3 = part - b1 - b2
        zero = jnp.zeros((GROUP, LANES), f32)
        return jnp.where(
            bias_row == 0,
            b1,
            jnp.where(bias_row == 1, b2, jnp.where(bias_row == 2, b3, zero)),
        )

    def sea_rows(shift, tile):
        lon = iota((2 * GROUP, LANES), 0)
        out = iota((2 * GROUP, LANES), 1) // hidden + per * tile
        return jnp.where(lon == out + shift, LAND, 0.0)

    return sea_rows, bias_rows


def first_weights(w1, bias1, t1):
    hidden = w1.shape[3]
    per = LANES // hidden
    sea_rows, bias_rows = extra_rows(hidden)
    fields = w1.shape[0]
    out_lon = iota((GROUP, LANES), 1) // hidden
    in_row = iota((GROUP, LANES), 0)
    for dj in range(3):
        taps = []
        for di in range(3):
            cells = [w1[c, di].astype(f32)[dj : dj + 1] for c in range(fields)]
            taps.append(
                [jnp.broadcast_to(0.5 * jnp.concatenate([x] * per, axis=1), (GROUP, LANES)) for x in cells]
            )
        for tile in range(2):
            parts = []
            for c in range(fields):
                total = jnp.zeros((GROUP, LANES), f32)
                for di in range(3):
                    hit = in_row == out_lon + per * tile + di
                    total = jnp.where(hit, taps[di][c], total)
                parts.append(total)
            for start in range(0, fields, 4):
                total = jnp.zeros((GROUP, LANES), f32)
                for n in range(min(4, fields - start)):
                    for di in range(3):
                        hit = in_row % 2 + GROUP == out_lon + per * tile + di
                        total = jnp.where(hit & (in_row // 2 == n), taps[di][start + n], total)
                parts.append(total)
            if dj == 1:
                parts += [sea_rows(1, tile), bias_rows(bias1)]
            else:
                parts.append(jnp.zeros((3 * GROUP, LANES), f32))
            block = jnp.concatenate(parts, axis=0)
            t1[pl.ds(dj * LANES, LANES), pl.ds(tile * LANES, LANES)] = block.astype(bf16)


def other_weights(w2, w3, w4, bias2, bias3, t2, t3, t4):
    hidden = w2.shape[2]
    per = LANES // hidden
    lane = iota((hidden, LANES), 1)
    sea_rows, bias_rows = extra_rows(hidden)
    for layer, (w, bias, t) in enumerate(((w2, bias2, t2), (w3, bias3, t3))):
        for dj in range(3):
            taps = []
            for di in range(3):
                cell = 0.5 * w[di, dj].astype(f32)
                wide = jnp.concatenate([cell, jnp.zeros((hidden, LANES - hidden), f32)], axis=1)
                square = jnp.concatenate([wide] * per, axis=0)
                taps.append(jnp.transpose(square)[:hidden])
            for lon in range(GROUP + 2):
                for tile in range(2):
                    total = jnp.zeros((hidden, LANES), f32)
                    for di in range(3):
                        total = jnp.where(lane // hidden + per * tile == lon - di, taps[di], total)
                    if lon < GROUP:
                        row = dj * GROUP * hidden + lon * hidden
                    else:
                        row = 3 * GROUP * hidden + dj * 2 * hidden + (lon - GROUP) * hidden
                    t[pl.ds(row, hidden), pl.ds(tile * LANES, LANES)] = total.astype(bf16)
        for tile in range(2):
            block = jnp.concatenate(
                [
                    jnp.zeros((5 * GROUP, LANES), f32),
                    sea_rows(2 + layer, tile),
                    bias_rows(bias),
                ],
                axis=0,
            )
            row = 3 * GROUP * hidden + 6 * hidden
            t[pl.ds(row, 2 * hidden), pl.ds(tile * LANES, LANES)] = block.astype(bf16)

    outs = w4.shape[2]
    half = LANES // 2
    lons = half // outs
    slot = iota((hidden, LANES), 1) // half
    out_lon = iota((hidden, LANES), 1) % lons
    taps = {}
    for dj in range(3):
        for di in range(3):
            cell = w4[di, dj].astype(f32)
            wide = jnp.concatenate([cell, jnp.zeros((outs, LANES - hidden), f32)], axis=1)
            square = jnp.concatenate(
                [jnp.broadcast_to(wide[c : c + 1], (lons, LANES)) for c in range(outs)] * 2, axis=0
            )
            taps[dj, di] = jnp.transpose(square)[:hidden]
    order = ((0, 1, 2, None), (1, 0, None, 2))
    for side in range(2):
        for lon in range(t4.shape[1] // hidden):
            for tile in range(2):
                total = jnp.zeros((hidden, LANES), f32)
                for place in range(2):
                    dj = order[side][2 * tile + place]
                    if dj is None:
                        continue
                    for di in range(3):
                        total = jnp.where((slot == place) & (out_lon == lon - di), taps[dj, di], total)
                t4[side, pl.ds(lon * hidden, hidden), pl.ds(tile * LANES, LANES)] = total.astype(bf16)


def main_kernel(
    sizes,
    bias_last,
    middle_in,
    ends_in,
    pre_in,
    base,
    sea,
    even_rim,
    odd_rim,
    own_tail,
    t1,
    t2,
    t3,
    t4,
    new_u,
    new_v,
    new_h,
    middle,
    ends,
    odd,
    even,
    force,
    gathered,
    turned,
    gaps,
    results,
    done,
):
    members, noises, levels = sizes
    fields = noises + 3 * levels
    lons, lats = sea.shape
    groups = lons // GROUP + 1
    chunks = SUB // members
    blocks = (lats + GAP) // chunks
    rows = blocks * SUB
    gap_k = lats - (chunks - 1) * blocks
    lat_index, lat_count = lax.axis_index("lat"), lax.axis_size("lat")
    top = lat_index == lat_count - 1
    is_odd = lat_index % 2 == 1
    bottom = lat_index == 0
    strip = odd_rim[...].astype(f32)
    paired = even_rim[...].astype(f32)
    south = jnp.where(is_odd, paired, jnp.where(bottom, 0.0, strip))

    wide = strip.shape[0]
    span = members * RIM
    lane = iota((wide, LANES), 1)
    rests = groups * span
    border = ((lane % RIM == 0) & (lane < rests)) | (lane >= rests)
    row_to = iota((wide, wide), 0)
    row_from = iota((wide, wide), 1)
    channel = row_to // GROUP
    mirrored = (channel == row_from // GROUP) & (row_from % GROUP == GROUP - 1 - row_to % GROUP)
    odd_parity = (channel >= noises) & (channel < noises + 2 * levels)
    flip_rows = jnp.where(mirrored, jnp.where(odd_parity, -1.0, 1.0), 0.0).astype(bf16)
    lane_from = iota((LANES, LANES), 0)
    lane_to = iota((LANES, LANES), 1)
    source = (groups - 1 - lane_to // span) * span + lane_to % span + RIM - 1
    moves = (lane_to % RIM == 0) & (lane_to < rests) & (lane_from == source)
    other = lane_to - rests
    source = rests + (groups - 1 - other // members) * members + other % members
    moves = moves | ((other >= 0) & (other < groups * members) & (lane_from == source))
    flip_lanes = jnp.where(moves, 1.0, 0.0).astype(bf16)
    pair = dot(flip_rows, jnp.concatenate([odd_rim[...], own_tail[...]], axis=1)).astype(bf16)
    folded = dot(pair[:, :LANES], flip_lanes)
    ghost = dot(pair[:, LANES:], flip_lanes)
    north = jnp.where(is_odd, strip, paired)
    north_rim = jnp.where(border & top, folded, north)

    for n, message in enumerate((north_rim, strip, ghost, south)):
        after = pltpu.roll(message, LANES - span, 1)
        cut = [message[c * GROUP : (c + 1) * GROUP] for c in range(fields + 1)]
        after = [after[c * GROUP : (c + 1) * GROUP] for c in range(fields + 1)]
        turned[n] = jnp.transpose(window(cut[:fields], after[:fields], cut[fields], after[fields]))
        for g in range(groups):
            for m in range(members):
                gap = (m - 1) % members if n == 3 else m
                start = n * RIM * SUB + gap * chunks + chunks - 1
                gaps[g, pl.ds(start, RIM, stride=SUB), :] = turned[n, pl.ds((g * members + m) * RIM, RIM), :]

    first = [ends.at[0]] + [middle.at[g] for g in range(groups - 2)] + [ends.at[1]]
    in_gap = iota((GAP * SUB, LANES), 0) % chunks == chunks - 1
    for g in range(groups):
        spot = pl.ds((1 + gap_k) * SUB, GAP * SUB)
        kept = first[g][spot, :].astype(f32)
        first[g][spot, :] = jnp.where(in_gap, gaps[g], kept).astype(bf16)
        wrap(first[g], rows)

    hidden = LANES // 4
    per = LANES // hidden
    tiles = odd.shape[0]
    pieces = row_pieces(rows)

    def finish(x, valid):
        used = (valid + per - 1) // per

        @pl.when(top)
        def _():
            strip_top = SUB * (1 + gap_k + STRIP + RIM - 1)
            own_top = SUB * gap_k
            strip_ghost = SUB * (1 + gap_k + GHOST)
            own_ghost = SUB * (1 + gap_k + NORTH)
            last_chunk = iota((SUB, LANES), 0) % chunks == chunks - 1
            spot = iota((SUB, LANES), 1) // hidden
            for src, dst in ((strip_top, own_ghost), (own_top, strip_ghost)):
                found = [x[t, pl.ds(src, SUB), :].astype(f32) for t in range(used)]
                for t in range(used):
                    total = x[t, pl.ds(dst, SUB), :].astype(f32)
                    for i in range(per):
                        lon = valid - 1 - (per * t + i)
                        if lon < 0:
                            continue
                        moved = pltpu.roll(found[lon // per], (hidden * (i - lon % per)) % LANES, 1)
                        total = jnp.where(last_chunk & (spot == i), moved, total)
                    x[t, pl.ds(dst, SUB), :] = total.astype(bf16)

        for t in range(used):
            wrap(x.at[t], rows)

    for x in (odd, even):
        x[tiles - 1] = jnp.zeros(x.shape[1:], bf16)
    even[tiles - 2] = jnp.zeros(even.shape[1:], bf16)

    near = (gap_k - 1) * SUB
    for b in range(groups):
        parts = []
        for d in range(3):
            some = [first[b][pl.ds(near + SUB * d, rows - near), :], first[b][pl.ds(SUB * d, SUB), :]]
            parts.append(jnp.concatenate(some, axis=0))
        out = activate(dot(jnp.concatenate(parts, axis=1), t1[...]))
        put(odd, b, near, out[: rows - near])
        put(odd, b, 0, out[rows - near :])
    finish(odd, lons + 6)

    ocean = sea[...].astype(f32)
    narrow = iota((lons, LANES), 1)
    at_south = narrow == 0
    at_north = narrow == LANES - 1

    def beyond(message, m, offset, to):
        tall = message[noises * GROUP : fields * GROUP]
        columns = []
        for g in range(groups):
            spot = (g * members + m) * RIM + offset
            more = rests + g * members + m
            column = pltpu.roll(tall, (to - spot) % LANES, 1)
            columns.append(column + pltpu.roll(tall, (to - more) % LANES, 1))
        cells = []
        for c in range(fields - noises):
            whole = jnp.concatenate([x[c * GROUP : (c + 1) * GROUP] for x in columns], axis=0)
            cells.append(pltpu.roll(whole, lons + GROUP - RIM, 0)[:lons])
        return cells

    def step_rims(m):
        rims = [beyond(south, m, RIM - 1, 0), beyond(north_rim, m, 0, LANES - 1)]
        for level in range(levels):
            gains = []
            for (sign, spot), rim in zip(((1.0, at_south), (-1.0, at_north)), rims):
                ru, rv, rh = rim[level], rim[levels + level], rim[2 * levels + level]
                pressure = rim[2 * levels] + rim[2 * levels + 1]
                if level == 1:
                    pressure = pressure + REDUCED * rh
                gains.append(
                    [
                        jnp.where(spot, TIME_STEP * VISCOSITY * ru, 0.0),
                        jnp.where(spot, TIME_STEP * (VISCOSITY * rv + sign * 0.5 * pressure), 0.0),
                        jnp.where(spot, TIME_STEP * sign * 0.5 * (rh * rv), 0.0),
                    ]
                )
            middle = [jnp.zeros((lons, lats - 2 * LANES), f32)] if lats > 2 * LANES else []
            gains = [jnp.concatenate([gains[0][n]] + middle + [gains[1][n]], axis=1) for n in range(3)]
            results[0, m, level] = base[0, m, level] + ocean * gains[0]
            results[1, m, level] = base[1, m, level] + ocean * gains[1]
            results[2, m, level] = base[2, m, level] + gains[2]
        pltpu.make_async_copy(results.at[2, m], new_h.at[m], done.at[2, m]).start()

    width = GROUP * hidden

    def layer(x, y, t, left_over, beside):
        for b in range(groups):
            for r, step in pieces:
                lower = iota((step, LANES), 1) < 2 * hidden

                def cells_of(tile, d):
                    return x[tile, pl.ds(r + SUB * d, step), :]

                def packed(tile):
                    more = [cells_of(tile, d) for d in range(3)]
                    return [
                        jnp.where(lower, more[0], pltpu.roll(more[1], 2 * hidden, 1)),
                        jnp.where(lower, more[2], first[b][pl.ds(r + SUB, step), :]),
                    ]

                if b < groups - 1:
                    parts = [cells_of(2 * b + e, d) for d in range(3) for e in range(2)] + packed(2 * b + 2)
                    matrix = t[...]
                elif left_over == per:
                    parts = [cells_of(2 * b, d) for d in range(3)] + packed(2 * b + 1)
                    lanes = pl.ds(0, LANES)
                    matrix = jnp.concatenate(
                        [t[pl.ds(d * width, LANES), lanes] for d in range(3)]
                        + [t[pl.ds(d * width + LANES, 2 * hidden), lanes] for d in range(3)]
                        + [t[pl.ds(3 * width + 6 * hidden, 2 * hidden), lanes]],
                        axis=0,
                    )
                else:
                    parts = [cells_of(2 * b, d) for d in range(3)] + [first[b][pl.ds(r + SUB, step), :]]
                    lanes = pl.ds(0, LANES)
                    matrix = jnp.concatenate(
                        [t[pl.ds(d * width, LANES), lanes] for d in range(3)]
                        + [jnp.zeros((2 * hidden, LANES), bf16)]
                        + [t[pl.ds(3 * width + 6 * hidden, 2 * hidden), lanes]],
                        axis=0,
                    )
                put(y, b, r, activate(dot(jnp.concatenate(parts, axis=1), matrix)))
            for m in beside.get(b, ()):
                step_rims(m)

    beside = {}
    for m in range(members):
        beside.setdefault(min(m, groups - 1), []).append(m)
    layer(odd, even, t2, per, beside)
    finish(even, lons + 4)
    layer(even, odd, t3, per // 2, {})
    finish(odd, lons + 2)

    depth = t4.shape[1] // LANES
    padded = rows + 2 * SUB
    for r, long in row_pieces(padded):
        before = iota((long, LANES), 1) < LANES // 2
        span_rows = pl.ds(r, long)
        sides = []
        for side in range(2):
            parts = [odd[side * (depth - 1) + t, span_rows, :] for t in range(depth)]
            sides.append(dot(jnp.concatenate(parts, axis=1), t4[side]))
        force[0, span_rows, :] = jnp.where(before, sides[0][:, :LANES], sides[1][:, :LANES])
        swapped = jnp.where(before, sides[1][:, :LANES], sides[0][:, :LANES])
        force[1, span_rows, :] = pltpu.roll(swapped, LANES // 2, 1)
        force[2, span_rows, :] = jnp.where(before, sides[0][:, LANES:], sides[1][:, LANES:])

    halves = lons // 2
    for r, step in pieces:
        total = force[0, pl.ds(r, step), :] + force[1, pl.ds(r + SUB, step), :]
        force[0, pl.ds(r, step), :] = total + force[2, pl.ds(r + 2 * SUB, step), :]
    for m in range(members):
        for q in range(chunks):
            size = min(blocks, lats - q * blocks)
            gathered[m, pl.ds(q * blocks, size), :] = force[0, pl.ds(m * chunks + q, size, stride=SUB), :]
        turned_force = jnp.transpose(gathered[m])
        for n, out in enumerate((new_u, new_v)):
            for level in range(levels):
                c = n * levels + level
                parts = [
                    turned_force[side * LANES // 2 + c * halves : side * LANES // 2 + (c + 1) * halves]
                    for side in range(2)
                ]
                push = TIME_STEP * (jnp.concatenate(parts, axis=0) + bias_last[c])
                results[n, m, level] = results[n, m, level] + ocean * push
            pltpu.make_async_copy(results.at[n, m], out.at[m], done.at[n, m]).start()
    for m in range(members):
        for n, out in enumerate((new_u, new_v, new_h)):
            pltpu.make_async_copy(results.at[n, m], out.at[m], done.at[n, m]).wait()


def body(
    noise,
    velocity_u,
    velocity_v,
    thickness,
    land_sea,
    conv_first,
    bias_first,
    conv_second,
    bias_second,
    conv_third,
    bias_third,
    conv_last,
    bias_last,
):
    members, noises, lons, lats = noise.shape
    levels = velocity_u.shape[1]
    fields = noises + 3 * levels
    sizes = (members, noises, levels)
    hidden = conv_first.shape[0]
    outs = conv_last.shape[0]
    groups = lons // GROUP + 1
    rows = members * (lats + GAP)
    assert hidden * 4 == LANES and outs * lons == LANES and members * (RIM + 1) * groups <= LANES
    assert fields % 2 == 0 and 4 * -(-fields // 4) == 12 and GROUP * (fields + 6) == LANES and lons % 16 == 0
    assert lats % LANES == 0 and SUB % members == 0 and (lats + GAP) % (SUB // members) == 0
    lon_count, lat_count = lax.axis_size("lon"), lax.axis_size("lat")
    assert lon_count % 2 == 0 and lat_count % 2 == 0
    state = (noise, velocity_u, velocity_v, thickness, land_sea)
    whole = pl.BlockSpec(memory_space=pltpu.VMEM)

    tall = members * fields * RIM + GROUP + members * 3 * levels
    assert tall % SUB == 0
    args = state + (
        conv_first.transpose(1, 2, 3, 0),
        conv_second.transpose(2, 3, 0, 1),
        conv_third.transpose(2, 3, 0, 1),
        conv_last.transpose(2, 3, 0, 1),
        bias_first[None],
        bias_second[None],
        bias_third[None],
    )
    count = len(args)
    *held, to_even, to_odd = pl.pallas_call(
        functools.partial(pack_lon_kernel, sizes, count),
        out_shape=[pltpu.VMEM(x.shape, x.dtype) for x in args] + [pltpu.VMEM((tall, lats), bf16)] * 2,
        in_specs=[pl.BlockSpec(memory_space=pltpu.HBM)] * count,
        out_specs=[whole] * (count + 2),
        scratch_shapes=[pltpu.VMEM((2, tall, lats), f32), pltpu.SemaphoreType.DMA((count,))],
        compiler_params=pltpu.CompilerParams(vmem_limit_bytes=62 * 2**20),
        name="pack_lon",
    )(*args)
    state = tuple(held[:5])
    lon_even = lax.ppermute(to_even, "lon", [(i, i ^ 1) for i in range(lon_count)])
    lon_odd = lax.ppermute(to_odd, "lon", [(i, (i - 1 + 2 * (i % 2)) % lon_count) for i in range(lon_count)])

    wide = -(-(fields + 1) * GROUP // SUB) * SUB
    part = pltpu.VMEM((wide, LANES), f32)
    message = pltpu.VMEM((wide, LANES), bf16)
    deep = -(-(lons // 2 + 2) * hidden // LANES) * LANES
    padded = rows + 2 * SUB
    tiles = 2 * groups + 1
    t1, own_head, own_tail, middle, pre = pl.pallas_call(
        functools.partial(prepare_kernel, sizes),
        out_shape=[
            pltpu.VMEM((3 * LANES, 2 * LANES), bf16),
            part,
            part,
            pltpu.VMEM((groups - 2, padded, LANES), bf16),
            pltpu.VMEM((tiles, padded, LANES), bf16),
        ],
        in_specs=[whole] * 7,
        out_specs=[whole] * 5,
        scratch_shapes=[
            pltpu.VMEM((groups - 2, rows, LANES), f32),
            pltpu.VMEM((members * (groups - 2) * lats // LANES, LANES, LANES), f32),
        ],
        compiler_params=pltpu.CompilerParams(vmem_limit_bytes=12 * 2**20),
        cost_estimate=pl.CostEstimate(flops=10**7, bytes_accessed=10**7, transcendentals=0),
        name="prepare",
    )(*held[:6], held[9])
    last = lat_count - 1
    smem = pl.BlockSpec(memory_space=pltpu.SMEM)
    to_even, to_odd = pl.pallas_call(
        functools.partial(join_kernel, sizes, lons),
        out_shape=[message] * 2,
        in_specs=[whole] * 4,
        out_specs=[whole] * 2,
        scratch_shapes=[
            pltpu.VMEM((2, 2, tall, LANES), f32),
            pltpu.VMEM((2, wide, LANES), f32),
        ],
        compiler_params=pltpu.CompilerParams(vmem_limit_bytes=4 * 2**20),
        name="join_rims",
    )(lon_even, lon_odd, own_head, own_tail)
    even_rim = lax.ppermute(to_even, "lat", [(i, i ^ 1) for i in range(lat_count)])
    pairs = []
    for t in range(lon_count):
        at = t * lat_count
        pairs += [(at + k, at + k - 1 + 2 * (k % 2)) for k in range(1, last)]
        pairs += [(at, (t ^ 1) * lat_count), (at + last, (lon_count - 1 - t) * lat_count + last)]
    odd_rim = lax.ppermute(to_odd, ("lon", "lat"), pairs)

    ends, base, pre, t2, t3, t4 = pl.pallas_call(
        functools.partial(cells_kernel, sizes),
        out_shape=[
            pltpu.VMEM((2, padded, LANES), bf16),
            pltpu.VMEM((3, *velocity_u.shape), f32),
            pltpu.VMEM(pre.shape, bf16),
            pltpu.VMEM((8 * LANES, 2 * LANES), bf16),
            pltpu.VMEM((8 * LANES, 2 * LANES), bf16),
            pltpu.VMEM((2, deep, 2 * LANES), bf16),
        ],
        in_specs=[whole] * 15,
        out_specs=[whole] * 6,
        input_output_aliases={14: 2},
        scratch_shapes=[
            pltpu.VMEM((2, tall, lats), f32),
            pltpu.VMEM((2, rows, LANES), f32),
            pltpu.VMEM((2 * members * lats // LANES, LANES, LANES), f32),
        ],
        compiler_params=pltpu.CompilerParams(vmem_limit_bytes=12 * 2**20),
        cost_estimate=pl.CostEstimate(flops=10**7, bytes_accessed=10**7, transcendentals=0),
        name="cells",
    )(*state, lon_even, lon_odd, to_even, *held[6:9], *held[10:12], t1, pre)

    out = jax.ShapeDtypeStruct(velocity_u.shape, f32)
    return pl.pallas_call(
        functools.partial(main_kernel, sizes),
        out_shape=[out] * 3 + [pltpu.VMEM(x.shape, x.dtype) for x in (middle, ends, pre)],
        in_specs=[smem] + [whole] * 12,
        out_specs=[pl.BlockSpec(memory_space=pltpu.HBM)] * 3 + [whole] * 3,
        input_output_aliases={1: 3, 2: 4, 3: 5},
        scratch_shapes=[
            pltpu.VMEM((tiles, padded, LANES), bf16),
            pltpu.VMEM((3, padded, LANES), f32),
            pltpu.VMEM((members, lats, LANES), f32),
            pltpu.VMEM((4, LANES, LANES), f32),
            pltpu.VMEM((groups, GAP * SUB, LANES), f32),
            pltpu.VMEM((3, *velocity_u.shape), f32),
            pltpu.SemaphoreType.DMA((3, members)),
        ],
        compiler_params=pltpu.CompilerParams(vmem_limit_bytes=32 * 2**20),
        cost_estimate=pl.CostEstimate(flops=2 * 10**10, bytes_accessed=10**7, transcendentals=4 * 10**6),
        name="network_and_step",
    )(
        bias_last,
        middle,
        ends,
        pre,
        base,
        state[4],
        even_rim,
        odd_rim,
        to_odd,
        t1,
        t2,
        t3,
        t4,
    )[:3]


def solution(mesh):
    tiles = P(None, None, "lon", "lat")
    return jax.shard_map(
        body,
        mesh=mesh,
        in_specs=(tiles,) * 4 + (P("lon", "lat"),) + (P(),) * 8,
        out_specs=(tiles,) * 3,
        check_vma=False,
    )
```

```python
import functools

import jax
import jax.numpy as jnp
from jax import lax
from jax.experimental import pallas as pl
from jax.experimental.pallas import tpu as pltpu
from jax.sharding import PartitionSpec as P

REDUCED = 0.5
TIME_STEP = 0.2
VISCOSITY = 0.05
CORIOLIS = 0.4

RIM = 4
GAP = 16
NORTH, STRIP, GHOST, SOUTH = 0, 4, 8, 12
SUB = 16
LANES = 128
GROUP = 8
LAND = 2.0**100

f32 = jnp.float32
bf16 = jnp.bfloat16


def iota(shape, dim):
    return lax.broadcasted_iota(jnp.int32, shape, dim)


def dot(a, b):
    return jnp.dot(a, b, preferred_element_type=f32)


def rest(x):
    return x - x.astype(bf16).astype(f32)


def pack_lon_kernel(sizes, count, *refs):
    sources, held, (even, odd, wide, done) = refs[:count], refs[count : 2 * count], refs[2 * count :]
    members, noises, levels = sizes
    fields = noises + 3 * levels
    noise, u, v, h, sea = held[:5]
    lons, lats = sea.shape
    copies = [pltpu.make_async_copy(x, y, done.at[n]) for n, (x, y) in enumerate(zip(sources, held))]
    for copy in copies:
        copy.start()
    for copy in copies[:5]:
        copy.wait()
    upper = iota((GROUP, lats), 0) < RIM

    def field(m, c, side):
        if c < noises:
            full = noise[m, c].astype(f32)
            return full[-GROUP:] if side else full[:GROUP]
        c -= noises
        return (u, v, h)[c // levels][m, c % levels, pl.ds(side * (lons - GROUP), GROUP)]

    rests = members * fields * RIM + GROUP
    for m in range(members):
        for c in range(0, fields, 2):
            rows = pl.ds((m * fields + c) * RIM, GROUP)
            wide[0, rows] = jnp.where(upper, field(m, c, 0), pltpu.roll(field(m, c + 1, 0), RIM, 0))
            wide[1, rows] = jnp.where(upper, pltpu.roll(field(m, c, 1), RIM, 0), field(m, c + 1, 1))
        for c in range(noises, fields):
            row = pl.ds(rests + m * (fields - noises) + c - noises, 1)
            wide[0, row] = rest(field(m, c, 0)[:1])
            wide[1, row] = rest(field(m, c, 1)[GROUP - 1 :])
    rows = pl.ds(members * fields * RIM, GROUP)
    ends = [sea[pl.ds(side * (lons - GROUP), GROUP)].astype(f32) for side in range(2)]
    wide[0, rows] = jnp.where(upper, ends[0], 0.0)
    wide[1, rows] = jnp.where(upper, pltpu.roll(ends[1], RIM, 0), 0.0)
    is_odd = lax.axis_index("lon") % 2 == 1
    even[...] = jnp.where(is_odd, wide[0], wide[1]).astype(bf16)
    odd[...] = jnp.where(is_odd, wide[1], wide[0]).astype(bf16)
    for copy in copies[5:]:
        copy.wait()


def lon_rims(even, odd, lanes=slice(None)):
    is_odd = lax.axis_index("lon") % 2 == 1
    a, b = even[:, lanes].astype(f32), odd[:, lanes].astype(f32)
    return jnp.where(is_odd, a, b), jnp.where(is_odd, b, a)


def rim_tile(sizes, m, c, side, rim):
    members, noises, levels = sizes
    fields = noises + 3 * levels
    row = (m * fields + c) * RIM if c < fields else members * fields * RIM
    tile = rim[pl.ds(row // GROUP * GROUP, GROUP)]
    if (row // RIM) % 2 == side:
        return tile
    return pltpu.roll(tile, RIM, 0)


def window(tiles, following, mask, next_mask):
    pair = iota(mask.shape, 0) // 2
    zero = jnp.zeros_like(mask)
    more = []
    for start in range(0, len(tiles), 4):
        total = zero
        for n in range(min(4, len(tiles) - start)):
            moved = pltpu.roll(following[start + n], 2 * n, 0) if n else following[start]
            total = jnp.where(pair == n, moved, total)
        more.append(total)
    return jnp.concatenate(
        tiles + more + [mask - 1.0, next_mask - 1.0, jnp.ones_like(mask)], axis=0
    )


def store_lats(block, t, dst, tile, m, lats, chunks, buffer):
    blocks = (lats + GAP) // chunks
    buffer[...] = jnp.transpose(block)
    for q in range(chunks):
        lo = max(q * blocks, t * LANES)
        hi = min((q + 1) * blocks, (t + 1) * LANES, lats)
        if lo < hi:
            start = (lo - q * blocks) * SUB + m * chunks + q
            dst[tile, pl.ds(start, hi - lo, stride=SUB), :] = buffer[pl.ds(lo - t * LANES, hi - lo), :]


def shifted_tiles(sizes, refs, m, c, t):
    noise, u, v, h, sea = refs
    members, noises, levels = sizes
    fields = noises + 3 * levels
    lons = sea.shape[0]
    lanes = slice(t * LANES, (t + 1) * LANES)
    if c == fields:
        full = sea[:, lanes].astype(f32)
    elif c < noises:
        full = noise[m, c, :, lanes].astype(f32)
    else:
        full = (u, v, h)[(c - noises) // levels][m, (c - noises) % levels, :, lanes]
    full = pltpu.roll(full, lons - RIM, 0)
    tiles = [full[g * GROUP : (g + 1) * GROUP] for g in range(lons // GROUP)]
    return tiles[-1:] + tiles


def prepare_kernel(sizes, noise, u, v, h, sea, *refs):
    w1, w2, w3, bias1, bias2, bias3, t1, t2, t3, head, tail, middle, pre, cells, turned = refs
    held = (noise, u, v, h, sea)
    members, noises, levels = sizes
    fields = noises + 3 * levels
    lons, lats = sea.shape
    groups = lons // GROUP + 1
    first_weights(w1, bias1, t1)
    hidden_weights(w2, w3, bias2, bias3, t2, t3)
    lane = iota((GROUP, LANES), 1)
    for out, t, first in ((head, 0, 0), (tail, lats // LANES - 1, LANES - RIM)):
        for c in range(fields + 1):
            total = jnp.zeros((GROUP, LANES), f32)
            for m in range(members):
                for g, tile in enumerate(shifted_tiles(sizes, held, m, c, t)):
                    place = (g * members + m) * RIM
                    moved = pltpu.roll(tile, (place - first) % LANES, 1)
                    total = jnp.where((lane >= place) & (lane < place + RIM), moved, total)
                    if noises <= c < fields:
                        place = groups * members * RIM + g * members + m
                        edge = 0 if out is head else LANES - 1
                        moved = pltpu.roll(rest(tile), (place - edge) % LANES, 1)
                        total = jnp.where(lane == place, moved, total)
            out[pl.ds(c * GROUP, GROUP)] = total
        for c in range(fields + 1, out.shape[0] // GROUP):
            out[pl.ds(c * GROUP, GROUP)] = jnp.zeros((GROUP, LANES), f32)
    chunks = SUB // members
    rows = cells.shape[1]
    gap_k = lats - (chunks - 1) * ((lats + GAP) // chunks)
    inner = groups - 2
    for m in range(members):
        for g in range(inner):
            empty = pl.ds(gap_k * SUB + (m + 1) * chunks - 1, GAP, stride=SUB)
            cells[g, empty, :] = jnp.zeros((GAP, LANES), f32)
    for t in range(lats // LANES):
        for m in range(members):
            tiles = [shifted_tiles(sizes, held, m, c, t) for c in range(fields + 1)]
            for g in range(1, inner + 1):
                following = [x[g + 1] for x in tiles]
                block = window([x[g] for x in tiles[:fields]], following[:fields], tiles[fields][g], following[fields])
                buffer = turned.at[(t * members + m) * inner + g - 1]
                store_lats(block, t, cells, g - 1, m, lats, chunks, buffer)
    for g in range(inner):
        middle[g, pl.ds(SUB, rows), :] = cells[g].astype(bf16)
        wrap(middle.at[g], rows)
    for g in range(inner):
        for r, step in row_pieces(rows):
            parts = [middle[g, pl.ds(r + SUB * d, step), :] for d in range(3)]
            put(pre, g + 1, r, activate(dot(jnp.concatenate(parts, axis=1), t1[...])))


def row_pieces(rows, count=2):
    cuts = [rows // SUB * n // count * SUB for n in range(count + 1)]
    return [(a, b - a) for a, b in zip(cuts, cuts[1:])]


def activate(pre):
    return (pre * jnp.tanh(pre) + pre).astype(bf16)


def put(y, b, r, out):
    for e in range(out.shape[1] // LANES):
        y[2 * b + e, pl.ds(SUB + r, out.shape[0]), :] = out[:, e * LANES : (e + 1) * LANES]


def wrap(x, rows):
    end = x[pl.ds(rows, SUB), :].astype(f32)
    x[pl.ds(0, SUB), :] = pltpu.roll(end, 1, 0).astype(bf16)
    begin = x[pl.ds(SUB, SUB), :].astype(f32)
    x[pl.ds(SUB + rows, SUB), :] = pltpu.roll(begin, SUB - 1, 0).astype(bf16)


def cells_kernel(sizes, noise, u, v, h, sea, lon_even, lon_odd, after, *refs):
    w4, t1, _, out, base, pre, t4, rims, cells, turned = refs
    members, noises, levels = sizes
    fields = noises + 3 * levels
    lons, lats = sea.shape
    groups = lons // GROUP + 1
    chunks = SUB // members
    rows = cells.shape[1]
    gap_k = lats - (chunks - 1) * ((lats + GAP) // chunks)
    rims[0], rims[1] = lon_rims(lon_even, lon_odd)
    for m in range(members):
        for side in range(2):
            empty = pl.ds(gap_k * SUB + (m + 1) * chunks - 1, GAP, stride=SUB)
            cells[side, empty, :] = jnp.zeros((GAP, LANES), f32)
    blank = jnp.zeros((GROUP, LANES), f32)
    upper = iota((GROUP, LANES), 0) < RIM
    for t in range(lats // LANES):
        lanes = slice(t * LANES, (t + 1) * LANES)
        for m in range(members):
            tiles = []
            for c in range(fields + 1):
                groups_of = shifted_tiles(sizes, (noise, u, v, h, sea), m, c, t)
                ends = [rim_tile(sizes, m, c, side, rims.at[side, :, lanes]) for side in range(2)]
                groups_of[0] = jnp.where(upper, ends[0], groups_of[0])
                groups_of[-1] = jnp.where(upper, groups_of[-1], ends[1])
                tiles.append(groups_of)
            for side, g in enumerate((0, groups - 1)):
                following = [x[g + 1] if g + 1 < groups else blank for x in tiles]
                block = window([x[g] for x in tiles[:fields]], following[:fields], tiles[fields][g], following[fields])
                store_lats(block, t, cells, side, m, lats, chunks, turned.at[(t * members + m) * 2 + side])
    for side in range(2):
        out[side, pl.ds(SUB, rows), :] = cells[side].astype(bf16)
        wrap(out.at[side], rows)
    for side in range(2):
        for r, step in row_pieces(rows):
            parts = [out[side, pl.ds(r + SUB * d, step), :] for d in range(3)]
            put(pre, side * (groups - 1), r, activate(dot(jnp.concatenate(parts, axis=1), t1[...])))
    last_weights(w4, t4)
    step_kernel(sizes, u, v, h, sea, rims, base)


def step_kernel(sizes, u, v, h, sea, rims, base):
    members, noises, levels = sizes
    fields = noises + 3 * levels
    lons, lats = sea.shape
    ocean = sea[...].astype(f32)
    lat_count = lax.axis_size("lat")
    lat_rows = (lax.axis_index("lat") * lats).astype(f32) + iota((lons, lats), 1).astype(f32)
    turn = CORIOLIS * (2.0 * (lat_rows + 0.5) / (lats * lat_count) - 1.0)
    at_first = iota((lons, lats), 0) == 0
    at_last = iota((lons, lats), 0) == lons - 1
    at_south = iota((lons, lats), 1) == 0
    at_north = iota((lons, lats), 1) == lats - 1
    lon_rests = members * fields * RIM + GROUP

    def around(x, m, c):
        row = (m * fields + c) * RIM
        more = lon_rests + m * (fields - noises) + c - noises
        west = rims[0, pl.ds(row + RIM - 1, 1)] + rims[0, pl.ds(more, 1)]
        east = rims[1, pl.ds(row, 1)] + rims[1, pl.ds(more, 1)]
        return (
            jnp.where(at_first, west, pltpu.roll(x, 1, 0)),
            jnp.where(at_last, east, pltpu.roll(x, lons - 1, 0)),
            jnp.where(at_south, 0.0, pltpu.roll(x, 1, 1)),
            jnp.where(at_north, 0.0, pltpu.roll(x, lats - 1, 1)),
        )

    for m in range(members):
        sets = []
        for level in range(levels):
            sets.append(
                [
                    (x[m, level], around(x[m, level], m, noises + n * levels + level))
                    for n, x in enumerate((u, v, h))
                ]
            )
        for level in range(levels):
            (cu, au), (cv, av), (ch, ah) = sets[level]
            upper, lower = sets[0][2][1], sets[1][2][1]
            pressure = [upper[i] + lower[i] for i in range(4)]
            if level == 1:
                pressure = [pressure[i] + REDUCED * lower[i] for i in range(4)]
            lap_u = au[1] + au[0] + au[3] + au[2] - 4.0 * cu
            lap_v = av[1] + av[0] + av[3] + av[2] - 4.0 * cv
            dx = 0.5 * (pressure[1] - pressure[0])
            dy = 0.5 * (pressure[3] - pressure[2])
            base[0, m, level] = ocean * (cu + TIME_STEP * (turn * cv - dx + VISCOSITY * lap_u))
            base[1, m, level] = ocean * (cv + TIME_STEP * (-turn * cu - dy + VISCOSITY * lap_v))
            flow = 0.5 * (ah[1] * au[1] - ah[0] * au[0]) + 0.5 * (ah[3] * av[3] - ah[2] * av[2])
            base[2, m, level] = ch - TIME_STEP * flow


def join_kernel(sizes, lons, lon_even, lon_odd, head, tail, even, odd, rims, wide):
    members, noises, levels = sizes
    fields = noises + 3 * levels
    groups = lons // GROUP + 1
    lats = lon_even.shape[1]
    for n, lanes in enumerate((slice(0, LANES), slice(lats - LANES, lats))):
        rims[0, n], rims[1, n] = lon_rims(lon_even, lon_odd, lanes)
    lane = iota((GROUP, LANES), 1)
    upper = iota((GROUP, LANES), 0) < RIM
    to_south = lax.axis_index("lat") % 2 == 1
    for c in range(fields + 1):
        rows = pl.ds(c * GROUP, GROUP)
        ends = []
        for n, (part, first) in enumerate(((head, 0), (tail, LANES - RIM))):
            total = part[rows]
            for side in range(2):
                held = upper if side == 0 else ~upper
                for m in range(members):
                    place = ((groups - 1) * side * members + m) * RIM
                    tile = rim_tile(sizes, m, c, side, rims.at[side, n])
                    moved = pltpu.roll(tile, (place - first) % LANES, 1)
                    total = jnp.where(held & (lane >= place) & (lane < place + RIM), moved, total)
            ends.append(total)
        wide[0, rows] = jnp.where(to_south, ends[0], ends[1])
        wide[1, rows] = jnp.where(to_south, ends[1], ends[0])
    rows = pl.ds((fields + 1) * GROUP, wide.shape[1] - (fields + 1) * GROUP)
    wide[:, rows] = jnp.zeros((2, wide.shape[1] - (fields + 1) * GROUP, LANES), f32)
    even[...] = wide[0].astype(bf16)
    odd[...] = wide[1].astype(bf16)


def extra_rows(hidden):
    per = LANES // hidden
    bias_row = iota((GROUP, LANES), 0)

    def bias_rows(bias):
        part = 0.5 * jnp.concatenate([bias[...]] * per, axis=1)
        b1 = part.astype(bf16).astype(f32)
        b2 = (part - b1).astype(bf16).astype(f32)
        b3 = part - b1 - b2
        zero = jnp.zeros((GROUP, LANES), f32)
        return jnp.where(
            bias_row == 0,
            b1,
            jnp.where(bias_row == 1, b2, jnp.where(bias_row == 2, b3, zero)),
        )

    def sea_rows(shift, tile):
        lon = iota((2 * GROUP, LANES), 0)
        out = iota((2 * GROUP, LANES), 1) // hidden + per * tile
        return jnp.where(lon == out + shift, LAND, 0.0)

    return sea_rows, bias_rows


def first_weights(w1, bias1, t1):
    hidden = w1.shape[3]
    per = LANES // hidden
    sea_rows, bias_rows = extra_rows(hidden)
    fields = w1.shape[0]
    out_lon = iota((GROUP, LANES), 1) // hidden
    in_row = iota((GROUP, LANES), 0)
    for dj in range(3):
        taps = []
        for di in range(3):
            cells = [w1[c, di].astype(f32)[dj : dj + 1] for c in range(fields)]
            taps.append(
                [jnp.broadcast_to(0.5 * jnp.concatenate([x] * per, axis=1), (GROUP, LANES)) for x in cells]
            )
        for tile in range(2):
            parts = []
            for c in range(fields):
                total = jnp.zeros((GROUP, LANES), f32)
                for di in range(3):
                    hit = in_row == out_lon + per * tile + di
                    total = jnp.where(hit, taps[di][c], total)
                parts.append(total)
            for start in range(0, fields, 4):
                total = jnp.zeros((GROUP, LANES), f32)
                for n in range(min(4, fields - start)):
                    for di in range(3):
                        hit = in_row % 2 + GROUP == out_lon + per * tile + di
                        total = jnp.where(hit & (in_row // 2 == n), taps[di][start + n], total)
                parts.append(total)
            if dj == 1:
                parts += [sea_rows(1, tile), bias_rows(bias1)]
            else:
                parts.append(jnp.zeros((3 * GROUP, LANES), f32))
            block = jnp.concatenate(parts, axis=0)
            t1[pl.ds(dj * LANES, LANES), pl.ds(tile * LANES, LANES)] = block.astype(bf16)


def hidden_weights(w2, w3, bias2, bias3, t2, t3):
    hidden = w2.shape[2]
    per = LANES // hidden
    lane = iota((hidden, LANES), 1)
    sea_rows, bias_rows = extra_rows(hidden)
    for layer, (w, bias, t) in enumerate(((w2, bias2, t2), (w3, bias3, t3))):
        for dj in range(3):
            taps = []
            for di in range(3):
                cell = 0.5 * w[di, dj].astype(f32)
                wide = jnp.concatenate([cell, jnp.zeros((hidden, LANES - hidden), f32)], axis=1)
                square = jnp.concatenate([wide] * per, axis=0)
                taps.append(jnp.transpose(square)[:hidden])
            for lon in range(GROUP + 2):
                for tile in range(2):
                    total = jnp.zeros((hidden, LANES), f32)
                    for di in range(3):
                        total = jnp.where(lane // hidden + per * tile == lon - di, taps[di], total)
                    if lon < GROUP:
                        row = dj * GROUP * hidden + lon * hidden
                    else:
                        row = 3 * GROUP * hidden + dj * 2 * hidden + (lon - GROUP) * hidden
                    t[pl.ds(row, hidden), pl.ds(tile * LANES, LANES)] = total.astype(bf16)
        for tile in range(2):
            block = jnp.concatenate(
                [
                    jnp.zeros((5 * GROUP, LANES), f32),
                    sea_rows(2 + layer, tile),
                    bias_rows(bias),
                ],
                axis=0,
            )
            row = 3 * GROUP * hidden + 6 * hidden
            t[pl.ds(row, 2 * hidden), pl.ds(tile * LANES, LANES)] = block.astype(bf16)


def last_weights(w4, t4):
    hidden = w4.shape[3]
    outs = w4.shape[2]
    half = LANES // 2
    lons = half // outs
    slot = iota((hidden, LANES), 1) // half
    out_lon = iota((hidden, LANES), 1) % lons
    taps = {}
    for dj in range(3):
        for di in range(3):
            cell = w4[di, dj].astype(f32)
            wide = jnp.concatenate([cell, jnp.zeros((outs, LANES - hidden), f32)], axis=1)
            square = jnp.concatenate(
                [jnp.broadcast_to(wide[c : c + 1], (lons, LANES)) for c in range(outs)] * 2, axis=0
            )
            taps[dj, di] = jnp.transpose(square)[:hidden]
    order = ((0, 1, 2, None), (1, 0, None, 2))
    for side in range(2):
        for lon in range(t4.shape[1] // hidden):
            for tile in range(2):
                total = jnp.zeros((hidden, LANES), f32)
                for place in range(2):
                    dj = order[side][2 * tile + place]
                    if dj is None:
                        continue
                    for di in range(3):
                        total = jnp.where((slot == place) & (out_lon == lon - di), taps[dj, di], total)
                t4[side, pl.ds(lon * hidden, hidden), pl.ds(tile * LANES, LANES)] = total.astype(bf16)


def main_kernel(
    sizes,
    bias_last,
    middle_in,
    ends_in,
    pre_in,
    base,
    sea,
    even_rim,
    odd_rim,
    own_tail,
    t1,
    t2,
    t3,
    t4,
    new_u,
    new_v,
    new_h,
    middle,
    ends,
    odd,
    even,
    force,
    gathered,
    turned,
    gaps,
    results,
    done,
):
    members, noises, levels = sizes
    fields = noises + 3 * levels
    lons, lats = sea.shape
    groups = lons // GROUP + 1
    chunks = SUB // members
    blocks = (lats + GAP) // chunks
    rows = blocks * SUB
    gap_k = lats - (chunks - 1) * blocks
    lat_index, lat_count = lax.axis_index("lat"), lax.axis_size("lat")
    top = lat_index == lat_count - 1
    is_odd = lat_index % 2 == 1
    bottom = lat_index == 0
    strip = odd_rim[...].astype(f32)
    paired = even_rim[...].astype(f32)
    south = jnp.where(is_odd, paired, jnp.where(bottom, 0.0, strip))

    wide = strip.shape[0]
    span = members * RIM
    lane = iota((wide, LANES), 1)
    rests = groups * span
    border = ((lane % RIM == 0) & (lane < rests)) | (lane >= rests)
    row_to = iota((wide, wide), 0)
    row_from = iota((wide, wide), 1)
    channel = row_to // GROUP
    mirrored = (channel == row_from // GROUP) & (row_from % GROUP == GROUP - 1 - row_to % GROUP)
    odd_parity = (channel >= noises) & (channel < noises + 2 * levels)
    flip_rows = jnp.where(mirrored, jnp.where(odd_parity, -1.0, 1.0), 0.0).astype(bf16)
    lane_from = iota((LANES, LANES), 0)
    lane_to = iota((LANES, LANES), 1)
    source = (groups - 1 - lane_to // span) * span + lane_to % span + RIM - 1
    moves = (lane_to % RIM == 0) & (lane_to < rests) & (lane_from == source)
    other = lane_to - rests
    source = rests + (groups - 1 - other // members) * members + other % members
    moves = moves | ((other >= 0) & (other < groups * members) & (lane_from == source))
    flip_lanes = jnp.where(moves, 1.0, 0.0).astype(bf16)
    pair = dot(flip_rows, jnp.concatenate([odd_rim[...], own_tail[...]], axis=1)).astype(bf16)
    folded = dot(pair[:, :LANES], flip_lanes)
    ghost = dot(pair[:, LANES:], flip_lanes)
    north = jnp.where(is_odd, strip, paired)
    north_rim = jnp.where(border & top, folded, north)

    for n, message in enumerate((north_rim, strip, ghost, south)):
        after = pltpu.roll(message, LANES - span, 1)
        cut = [message[c * GROUP : (c + 1) * GROUP] for c in range(fields + 1)]
        after = [after[c * GROUP : (c + 1) * GROUP] for c in range(fields + 1)]
        turned[n] = jnp.transpose(window(cut[:fields], after[:fields], cut[fields], after[fields]))
        for g in range(groups):
            for m in range(members):
                gap = (m - 1) % members if n == 3 else m
                start = n * RIM * SUB + gap * chunks + chunks - 1
                gaps[g, pl.ds(start, RIM, stride=SUB), :] = turned[n, pl.ds((g * members + m) * RIM, RIM), :]

    first = [ends.at[0]] + [middle.at[g] for g in range(groups - 2)] + [ends.at[1]]
    in_gap = iota((GAP * SUB, LANES), 0) % chunks == chunks - 1
    for g in range(groups):
        spot = pl.ds((1 + gap_k) * SUB, GAP * SUB)
        kept = first[g][spot, :].astype(f32)
        first[g][spot, :] = jnp.where(in_gap, gaps[g], kept).astype(bf16)
        wrap(first[g], rows)

    hidden = LANES // 4
    per = LANES // hidden
    tiles = odd.shape[0]
    pieces = row_pieces(rows, 4)

    def finish(x, valid):
        used = (valid + per - 1) // per

        @pl.when(top)
        def _():
            strip_top = SUB * (1 + gap_k + STRIP + RIM - 1)
            own_top = SUB * gap_k
            strip_ghost = SUB * (1 + gap_k + GHOST)
            own_ghost = SUB * (1 + gap_k + NORTH)
            last_chunk = iota((SUB, LANES), 0) % chunks == chunks - 1
            spot = iota((SUB, LANES), 1) // hidden
            for src, dst in ((strip_top, own_ghost), (own_top, strip_ghost)):
                found = [x[t, pl.ds(src, SUB), :].astype(f32) for t in range(used)]
                for t in range(used):
                    total = x[t, pl.ds(dst, SUB), :].astype(f32)
                    for i in range(per):
                        lon = valid - 1 - (per * t + i)
                        if lon < 0:
                            continue
                        moved = pltpu.roll(found[lon // per], (hidden * (i - lon % per)) % LANES, 1)
                        total = jnp.where(last_chunk & (spot == i), moved, total)
                    x[t, pl.ds(dst, SUB), :] = total.astype(bf16)

        for t in range(used):
            wrap(x.at[t], rows)

    for x in (odd, even):
        x[tiles - 1] = jnp.zeros(x.shape[1:], bf16)
    even[tiles - 2] = jnp.zeros(even.shape[1:], bf16)

    near = (gap_k - 1) * SUB
    for b in range(groups):
        parts = []
        for d in range(3):
            some = [first[b][pl.ds(near + SUB * d, rows - near), :], first[b][pl.ds(SUB * d, SUB), :]]
            parts.append(jnp.concatenate(some, axis=0))
        out = activate(dot(jnp.concatenate(parts, axis=1), t1[...]))
        put(odd, b, near, out[: rows - near])
        put(odd, b, 0, out[rows - near :])
    finish(odd, lons + 6)

    ocean = sea[...].astype(f32)
    narrow = iota((lons, LANES), 1)
    at_south = narrow == 0
    at_north = narrow == LANES - 1

    def beyond(message, m, offset, to):
        tall = message[noises * GROUP : fields * GROUP]
        columns = []
        for g in range(groups):
            spot = (g * members + m) * RIM + offset
            more = rests + g * members + m
            column = pltpu.roll(tall, (to - spot) % LANES, 1)
            columns.append(column + pltpu.roll(tall, (to - more) % LANES, 1))
        cells = []
        for c in range(fields - noises):
            whole = jnp.concatenate([x[c * GROUP : (c + 1) * GROUP] for x in columns], axis=0)
            cells.append(pltpu.roll(whole, lons + GROUP - RIM, 0)[:lons])
        return cells

    def step_rims(m):
        rims = [beyond(south, m, RIM - 1, 0), beyond(north_rim, m, 0, LANES - 1)]
        for level in range(levels):
            gains = []
            for (sign, spot), rim in zip(((1.0, at_south), (-1.0, at_north)), rims):
                ru, rv, rh = rim[level], rim[levels + level], rim[2 * levels + level]
                pressure = rim[2 * levels] + rim[2 * levels + 1]
                if level == 1:
                    pressure = pressure + REDUCED * rh
                gains.append(
                    [
                        jnp.where(spot, TIME_STEP * VISCOSITY * ru, 0.0),
                        jnp.where(spot, TIME_STEP * (VISCOSITY * rv + sign * 0.5 * pressure), 0.0),
                        jnp.where(spot, TIME_STEP * sign * 0.5 * (rh * rv), 0.0),
                    ]
                )
            middle = [jnp.zeros((lons, lats - 2 * LANES), f32)] if lats > 2 * LANES else []
            gains = [jnp.concatenate([gains[0][n]] + middle + [gains[1][n]], axis=1) for n in range(3)]
            results[0, m, level] = base[0, m, level] + ocean * gains[0]
            results[1, m, level] = base[1, m, level] + ocean * gains[1]
            results[2, m, level] = base[2, m, level] + gains[2]
        pltpu.make_async_copy(results.at[2, m], new_h.at[m], done.at[2, m]).start()

    width = GROUP * hidden

    def layer(x, y, t, left_over, beside):
        for b in range(groups):
            for r, step in pieces:
                lower = iota((step, LANES), 1) < 2 * hidden

                def cells_of(tile, d):
                    return x[tile, pl.ds(r + SUB * d, step), :]

                def packed(tile):
                    more = [cells_of(tile, d) for d in range(3)]
                    return [
                        jnp.where(lower, more[0], pltpu.roll(more[1], 2 * hidden, 1)),
                        jnp.where(lower, more[2], first[b][pl.ds(r + SUB, step), :]),
                    ]

                if b < groups - 1:
                    parts = [cells_of(2 * b + e, d) for d in range(3) for e in range(2)] + packed(2 * b + 2)
                    matrix = t[...]
                elif left_over == per:
                    parts = [cells_of(2 * b, d) for d in range(3)] + packed(2 * b + 1)
                    lanes = pl.ds(0, LANES)
                    matrix = jnp.concatenate(
                        [t[pl.ds(d * width, LANES), lanes] for d in range(3)]
                        + [t[pl.ds(d * width + LANES, 2 * hidden), lanes] for d in range(3)]
                        + [t[pl.ds(3 * width + 6 * hidden, 2 * hidden), lanes]],
                        axis=0,
                    )
                else:
                    parts = [cells_of(2 * b, d) for d in range(3)] + [first[b][pl.ds(r + SUB, step), :]]
                    lanes = pl.ds(0, LANES)
                    matrix = jnp.concatenate(
                        [t[pl.ds(d * width, LANES), lanes] for d in range(3)]
                        + [jnp.zeros((2 * hidden, LANES), bf16)]
                        + [t[pl.ds(3 * width + 6 * hidden, 2 * hidden), lanes]],
                        axis=0,
                    )
                put(y, b, r, activate(dot(jnp.concatenate(parts, axis=1), matrix)))
            for m in beside.get(b, ()):
                step_rims(m)

    beside = {}
    for m in range(members):
        beside.setdefault(min(m, groups - 1), []).append(m)
    layer(odd, even, t2, per, beside)
    finish(even, lons + 4)
    layer(even, odd, t3, per // 2, {})
    finish(odd, lons + 2)

    depth = t4.shape[1] // LANES
    padded = rows + 2 * SUB
    for r, long in row_pieces(padded, 4):
        before = iota((long, LANES), 1) < LANES // 2
        span_rows = pl.ds(r, long)
        sides = []
        for side in range(2):
            parts = [odd[side * (depth - 1) + t, span_rows, :] for t in range(depth)]
            sides.append(dot(jnp.concatenate(parts, axis=1), t4[side]))
        force[0, span_rows, :] = jnp.where(before, sides[0][:, :LANES], sides[1][:, :LANES])
        swapped = jnp.where(before, sides[1][:, :LANES], sides[0][:, :LANES])
        force[1, span_rows, :] = pltpu.roll(swapped, LANES // 2, 1)
        force[2, span_rows, :] = jnp.where(before, sides[0][:, LANES:], sides[1][:, LANES:])

    halves = lons // 2
    for r, step in pieces:
        total = force[0, pl.ds(r, step), :] + force[1, pl.ds(r + SUB, step), :]
        force[0, pl.ds(r, step), :] = total + force[2, pl.ds(r + 2 * SUB, step), :]
    for m in range(members):
        for q in range(chunks):
            size = min(blocks, lats - q * blocks)
            gathered[m, pl.ds(q * blocks, size), :] = force[0, pl.ds(m * chunks + q, size, stride=SUB), :]
        turned_force = jnp.transpose(gathered[m])
        for n, out in enumerate((new_u, new_v)):
            for level in range(levels):
                c = n * levels + level
                parts = [
                    turned_force[side * LANES // 2 + c * halves : side * LANES // 2 + (c + 1) * halves]
                    for side in range(2)
                ]
                push = TIME_STEP * (jnp.concatenate(parts, axis=0) + bias_last[c])
                results[n, m, level] = results[n, m, level] + ocean * push
            pltpu.make_async_copy(results.at[n, m], out.at[m], done.at[n, m]).start()
    for m in range(members):
        for n, out in enumerate((new_u, new_v, new_h)):
            pltpu.make_async_copy(results.at[n, m], out.at[m], done.at[n, m]).wait()


def body(
    noise,
    velocity_u,
    velocity_v,
    thickness,
    land_sea,
    conv_first,
    bias_first,
    conv_second,
    bias_second,
    conv_third,
    bias_third,
    conv_last,
    bias_last,
):
    members, noises, lons, lats = noise.shape
    levels = velocity_u.shape[1]
    fields = noises + 3 * levels
    sizes = (members, noises, levels)
    hidden = conv_first.shape[0]
    outs = conv_last.shape[0]
    groups = lons // GROUP + 1
    rows = members * (lats + GAP)
    assert hidden * 4 == LANES and outs * lons == LANES and members * (RIM + 1) * groups <= LANES
    assert fields % 2 == 0 and 4 * -(-fields // 4) == 12 and GROUP * (fields + 6) == LANES and lons % 16 == 0
    assert lats % LANES == 0 and SUB % members == 0 and (lats + GAP) % (SUB // members) == 0
    lon_count, lat_count = lax.axis_size("lon"), lax.axis_size("lat")
    assert lon_count % 2 == 0 and lat_count % 2 == 0
    state = (noise, velocity_u, velocity_v, thickness, land_sea)
    whole = pl.BlockSpec(memory_space=pltpu.VMEM)

    tall = members * fields * RIM + GROUP + members * 3 * levels
    assert tall % SUB == 0
    args = state + (
        conv_first.transpose(1, 2, 3, 0),
        conv_second.transpose(2, 3, 0, 1),
        conv_third.transpose(2, 3, 0, 1),
        conv_last.transpose(2, 3, 0, 1),
        bias_first[None],
        bias_second[None],
        bias_third[None],
    )
    count = len(args)
    *held, to_even, to_odd = pl.pallas_call(
        functools.partial(pack_lon_kernel, sizes, count),
        out_shape=[pltpu.VMEM(x.shape, x.dtype) for x in args] + [pltpu.VMEM((tall, lats), bf16)] * 2,
        in_specs=[pl.BlockSpec(memory_space=pltpu.HBM)] * count,
        out_specs=[whole] * (count + 2),
        scratch_shapes=[pltpu.VMEM((2, tall, lats), f32), pltpu.SemaphoreType.DMA((count,))],
        compiler_params=pltpu.CompilerParams(vmem_limit_bytes=62 * 2**20),
        name="pack_lon",
    )(*args)
    state = tuple(held[:5])
    lon_even = lax.ppermute(to_even, "lon", [(i, i ^ 1) for i in range(lon_count)])
    lon_odd = lax.ppermute(to_odd, "lon", [(i, (i - 1 + 2 * (i % 2)) % lon_count) for i in range(lon_count)])

    wide = -(-(fields + 1) * GROUP // SUB) * SUB
    part = pltpu.VMEM((wide, LANES), f32)
    message = pltpu.VMEM((wide, LANES), bf16)
    deep = -(-(lons // 2 + 2) * hidden // LANES) * LANES
    padded = rows + 2 * SUB
    tiles = 2 * groups + 1
    t1, t2, t3, own_head, own_tail, middle, pre = pl.pallas_call(
        functools.partial(prepare_kernel, sizes),
        out_shape=[
            pltpu.VMEM((3 * LANES, 2 * LANES), bf16),
            pltpu.VMEM((8 * LANES, 2 * LANES), bf16),
            pltpu.VMEM((8 * LANES, 2 * LANES), bf16),
            part,
            part,
            pltpu.VMEM((groups - 2, padded, LANES), bf16),
            pltpu.VMEM((tiles, padded, LANES), bf16),
        ],
        in_specs=[whole] * 11,
        out_specs=[whole] * 7,
        scratch_shapes=[
            pltpu.VMEM((groups - 2, rows, LANES), f32),
            pltpu.VMEM((members * (groups - 2) * lats // LANES, LANES, LANES), f32),
        ],
        compiler_params=pltpu.CompilerParams(vmem_limit_bytes=12 * 2**20),
        cost_estimate=pl.CostEstimate(flops=10**7, bytes_accessed=10**7, transcendentals=0),
        name="prepare",
    )(*held[:8], *held[9:])
    last = lat_count - 1
    smem = pl.BlockSpec(memory_space=pltpu.SMEM)
    to_even, to_odd = pl.pallas_call(
        functools.partial(join_kernel, sizes, lons),
        out_shape=[message] * 2,
        in_specs=[whole] * 4,
        out_specs=[whole] * 2,
        scratch_shapes=[
            pltpu.VMEM((2, 2, tall, LANES), f32),
            pltpu.VMEM((2, wide, LANES), f32),
        ],
        compiler_params=pltpu.CompilerParams(vmem_limit_bytes=4 * 2**20),
        name="join_rims",
    )(lon_even, lon_odd, own_head, own_tail)
    even_rim = lax.ppermute(to_even, "lat", [(i, i ^ 1) for i in range(lat_count)])
    pairs = []
    for t in range(lon_count):
        at = t * lat_count
        pairs += [(at + k, at + k - 1 + 2 * (k % 2)) for k in range(1, last)]
        pairs += [(at, (t ^ 1) * lat_count), (at + last, (lon_count - 1 - t) * lat_count + last)]
    odd_rim = lax.ppermute(to_odd, ("lon", "lat"), pairs)

    ends, base, pre, t4 = pl.pallas_call(
        functools.partial(cells_kernel, sizes),
        out_shape=[
            pltpu.VMEM((2, padded, LANES), bf16),
            pltpu.VMEM((3, *velocity_u.shape), f32),
            pltpu.VMEM(pre.shape, bf16),
            pltpu.VMEM((2, deep, 2 * LANES), bf16),
        ],
        in_specs=[whole] * 11,
        out_specs=[whole] * 4,
        input_output_aliases={10: 2},
        scratch_shapes=[
            pltpu.VMEM((2, tall, lats), f32),
            pltpu.VMEM((2, rows, LANES), f32),
            pltpu.VMEM((2 * members * lats // LANES, LANES, LANES), f32),
        ],
        compiler_params=pltpu.CompilerParams(vmem_limit_bytes=12 * 2**20),
        cost_estimate=pl.CostEstimate(flops=10**7, bytes_accessed=10**7, transcendentals=0),
        name="cells",
    )(*state, lon_even, lon_odd, to_even, held[8], t1, pre)

    out = jax.ShapeDtypeStruct(velocity_u.shape, f32)
    return pl.pallas_call(
        functools.partial(main_kernel, sizes),
        out_shape=[out] * 3 + [pltpu.VMEM(x.shape, x.dtype) for x in (middle, ends, pre)],
        in_specs=[smem] + [whole] * 12,
        out_specs=[pl.BlockSpec(memory_space=pltpu.HBM)] * 3 + [whole] * 3,
        input_output_aliases={1: 3, 2: 4, 3: 5},
        scratch_shapes=[
            pltpu.VMEM((tiles, padded, LANES), bf16),
            pltpu.VMEM((3, padded, LANES), f32),
            pltpu.VMEM((members, lats, LANES), f32),
            pltpu.VMEM((4, LANES, LANES), f32),
            pltpu.VMEM((groups, GAP * SUB, LANES), f32),
            pltpu.VMEM((3, *velocity_u.shape), f32),
            pltpu.SemaphoreType.DMA((3, members)),
        ],
        compiler_params=pltpu.CompilerParams(vmem_limit_bytes=32 * 2**20),
        cost_estimate=pl.CostEstimate(flops=2 * 10**10, bytes_accessed=10**7, transcendentals=4 * 10**6),
        name="network_and_step",
    )(
        bias_last,
        middle,
        ends,
        pre,
        base,
        state[4],
        even_rim,
        odd_rim,
        to_odd,
        t1,
        t2,
        t3,
        t4,
    )[:3]


def solution(mesh):
    tiles = P(None, None, "lon", "lat")
    return jax.shard_map(
        body,
        mesh=mesh,
        in_specs=(tiles,) * 4 + (P("lon", "lat"),) + (P(),) * 8,
        out_specs=(tiles,) * 3,
        check_vma=False,
    )
```

```python
import functools

import jax
import jax.numpy as jnp
from jax import lax
from jax.experimental import pallas as pl
from jax.experimental.pallas import tpu as pltpu
from jax.sharding import PartitionSpec as P

REDUCED = 0.5
TIME_STEP = 0.2
VISCOSITY = 0.05
CORIOLIS = 0.4

RIM = 4
GAP = 16
NORTH, STRIP, GHOST, SOUTH = 0, 4, 8, 12
SUB = 16
LANES = 128
GROUP = 8
LAND = 2.0**100

f32 = jnp.float32
bf16 = jnp.bfloat16


def iota(shape, dim):
    return lax.broadcasted_iota(jnp.int32, shape, dim)


def dot(a, b):
    return jnp.dot(a, b, preferred_element_type=f32)


def rest(x):
    return x - x.astype(bf16).astype(f32)


def pack_lon_kernel(sizes, count, *refs):
    sources, held, (even, odd, wide, done) = refs[:count], refs[count : 2 * count], refs[2 * count :]
    members, noises, levels = sizes
    fields = noises + 3 * levels
    noise, u, v, h, sea = held[:5]
    lons, lats = sea.shape
    copies = [pltpu.make_async_copy(x, y, done.at[n]) for n, (x, y) in enumerate(zip(sources, held))]
    for copy in copies:
        copy.start()
    for copy in copies[:5]:
        copy.wait()
    upper = iota((GROUP, lats), 0) < RIM

    def field(m, c, side):
        if c < noises:
            full = noise[m, c].astype(f32)
            return full[-GROUP:] if side else full[:GROUP]
        c -= noises
        return (u, v, h)[c // levels][m, c % levels, pl.ds(side * (lons - GROUP), GROUP)]

    rests = members * fields * RIM + GROUP
    for m in range(members):
        for c in range(0, fields, 2):
            rows = pl.ds((m * fields + c) * RIM, GROUP)
            wide[0, rows] = jnp.where(upper, field(m, c, 0), pltpu.roll(field(m, c + 1, 0), RIM, 0))
            wide[1, rows] = jnp.where(upper, pltpu.roll(field(m, c, 1), RIM, 0), field(m, c + 1, 1))
        for c in range(noises, fields):
            row = pl.ds(rests + m * (fields - noises) + c - noises, 1)
            wide[0, row] = rest(field(m, c, 0)[:1])
            wide[1, row] = rest(field(m, c, 1)[GROUP - 1 :])
    rows = pl.ds(members * fields * RIM, GROUP)
    ends = [sea[pl.ds(side * (lons - GROUP), GROUP)].astype(f32) for side in range(2)]
    wide[0, rows] = jnp.where(upper, ends[0], 0.0)
    wide[1, rows] = jnp.where(upper, pltpu.roll(ends[1], RIM, 0), 0.0)
    is_odd = lax.axis_index("lon") % 2 == 1
    even[...] = jnp.where(is_odd, wide[0], wide[1]).astype(bf16)
    odd[...] = jnp.where(is_odd, wide[1], wide[0]).astype(bf16)
    for copy in copies[5:]:
        copy.wait()


def lon_rims(even, odd, lanes=slice(None)):
    is_odd = lax.axis_index("lon") % 2 == 1
    a, b = even[:, lanes].astype(f32), odd[:, lanes].astype(f32)
    return jnp.where(is_odd, a, b), jnp.where(is_odd, b, a)


def rim_tile(sizes, m, c, side, rim):
    members, noises, levels = sizes
    fields = noises + 3 * levels
    row = (m * fields + c) * RIM if c < fields else members * fields * RIM
    tile = rim[pl.ds(row // GROUP * GROUP, GROUP)]
    if (row // RIM) % 2 == side:
        return tile
    return pltpu.roll(tile, RIM, 0)


def window(tiles, following, mask, next_mask):
    pair = iota(mask.shape, 0) // 2
    zero = jnp.zeros_like(mask)
    more = []
    for start in range(0, len(tiles), 4):
        total = zero
        for n in range(min(4, len(tiles) - start)):
            moved = pltpu.roll(following[start + n], 2 * n, 0) if n else following[start]
            total = jnp.where(pair == n, moved, total)
        more.append(total)
    return jnp.concatenate(
        tiles + more + [mask - 1.0, next_mask - 1.0, jnp.ones_like(mask)], axis=0
    )


def store_lats(block, t, dst, tile, m, lats, chunks, buffer):
    blocks = (lats + GAP) // chunks
    buffer[...] = jnp.transpose(block)
    for q in range(chunks):
        lo = max(q * blocks, t * LANES)
        hi = min((q + 1) * blocks, (t + 1) * LANES, lats)
        if lo < hi:
            start = (lo - q * blocks) * SUB + m * chunks + q
            dst[tile, pl.ds(start, hi - lo, stride=SUB), :] = buffer[pl.ds(lo - t * LANES, hi - lo), :]


def shifted_tiles(sizes, refs, m, c, t):
    noise, u, v, h, sea = refs
    members, noises, levels = sizes
    fields = noises + 3 * levels
    lons = sea.shape[0]
    lanes = slice(t * LANES, (t + 1) * LANES)
    if c == fields:
        full = sea[:, lanes].astype(f32)
    elif c < noises:
        full = noise[m, c, :, lanes].astype(f32)
    else:
        full = (u, v, h)[(c - noises) // levels][m, (c - noises) % levels, :, lanes]
    full = pltpu.roll(full, lons - RIM, 0)
    tiles = [full[g * GROUP : (g + 1) * GROUP] for g in range(lons // GROUP)]
    return tiles[-1:] + tiles


def prepare_kernel(sizes, noise, u, v, h, sea, *refs):
    w1, w2, w3, bias1, bias2, bias3, t1, t2, t3, head, tail, middle, pre, cells, turned = refs
    held = (noise, u, v, h, sea)
    members, noises, levels = sizes
    fields = noises + 3 * levels
    lons, lats = sea.shape
    groups = lons // GROUP + 1
    first_weights(w1, bias1, t1)
    hidden_weights(w2, w3, bias2, bias3, t2, t3)
    lane = iota((GROUP, LANES), 1)
    for out, t, first in ((head, 0, 0), (tail, lats // LANES - 1, LANES - RIM)):
        for c in range(fields + 1):
            total = jnp.zeros((GROUP, LANES), f32)
            for m in range(members):
                for g, tile in enumerate(shifted_tiles(sizes, held, m, c, t)):
                    place = (g * members + m) * RIM
                    moved = pltpu.roll(tile, (place - first) % LANES, 1)
                    total = jnp.where((lane >= place) & (lane < place + RIM), moved, total)
                    if noises <= c < fields:
                        place = groups * members * RIM + g * members + m
                        edge = 0 if out is head else LANES - 1
                        moved = pltpu.roll(rest(tile), (place - edge) % LANES, 1)
                        total = jnp.where(lane == place, moved, total)
            out[pl.ds(c * GROUP, GROUP)] = total
        for c in range(fields + 1, out.shape[0] // GROUP):
            out[pl.ds(c * GROUP, GROUP)] = jnp.zeros((GROUP, LANES), f32)
    chunks = SUB // members
    rows = cells.shape[1]
    gap_k = lats - (chunks - 1) * ((lats + GAP) // chunks)
    inner = groups - 2
    for m in range(members):
        for g in range(inner):
            empty = pl.ds(gap_k * SUB + (m + 1) * chunks - 1, GAP, stride=SUB)
            cells[g, empty, :] = jnp.zeros((GAP, LANES), f32)
    for t in range(lats // LANES):
        for m in range(members):
            tiles = [shifted_tiles(sizes, held, m, c, t) for c in range(fields + 1)]
            for g in range(1, inner + 1):
                following = [x[g + 1] for x in tiles]
                block = window([x[g] for x in tiles[:fields]], following[:fields], tiles[fields][g], following[fields])
                buffer = turned.at[(t * members + m) * inner + g - 1]
                store_lats(block, t, cells, g - 1, m, lats, chunks, buffer)
    for g in range(inner):
        middle[g, pl.ds(SUB, rows), :] = cells[g].astype(bf16)
        wrap(middle.at[g], rows)
    for g in range(inner):
        for r, step in row_pieces(rows):
            parts = [middle[g, pl.ds(r + SUB * d, step), :] for d in range(3)]
            put(pre, g + 1, r, activate(dot(jnp.concatenate(parts, axis=1), t1[...])))


def row_pieces(rows, count=2):
    cuts = [rows // SUB * n // count * SUB for n in range(count + 1)]
    return [(a, b - a) for a, b in zip(cuts, cuts[1:])]


def activate(pre):
    return (pre * jnp.tanh(pre) + pre).astype(bf16)


def put(y, b, r, out):
    for e in range(out.shape[1] // LANES):
        y[2 * b + e, pl.ds(SUB + r, out.shape[0]), :] = out[:, e * LANES : (e + 1) * LANES]


def wrap(x, rows):
    end = x[pl.ds(rows, SUB), :].astype(f32)
    x[pl.ds(0, SUB), :] = pltpu.roll(end, 1, 0).astype(bf16)
    begin = x[pl.ds(SUB, SUB), :].astype(f32)
    x[pl.ds(SUB + rows, SUB), :] = pltpu.roll(begin, SUB - 1, 0).astype(bf16)


def cells_kernel(sizes, noise, u, v, h, sea, lon_even, lon_odd, after, *refs):
    w4, t1, _, out, base, pre, t4, rims, cells, turned = refs
    members, noises, levels = sizes
    fields = noises + 3 * levels
    lons, lats = sea.shape
    groups = lons // GROUP + 1
    chunks = SUB // members
    rows = cells.shape[1]
    gap_k = lats - (chunks - 1) * ((lats + GAP) // chunks)
    rims[0], rims[1] = lon_rims(lon_even, lon_odd)
    for m in range(members):
        for side in range(2):
            empty = pl.ds(gap_k * SUB + (m + 1) * chunks - 1, GAP, stride=SUB)
            cells[side, empty, :] = jnp.zeros((GAP, LANES), f32)
    blank = jnp.zeros((GROUP, LANES), f32)
    upper = iota((GROUP, LANES), 0) < RIM
    for t in range(lats // LANES):
        lanes = slice(t * LANES, (t + 1) * LANES)
        for m in range(members):
            tiles = []
            for c in range(fields + 1):
                groups_of = shifted_tiles(sizes, (noise, u, v, h, sea), m, c, t)
                ends = [rim_tile(sizes, m, c, side, rims.at[side, :, lanes]) for side in range(2)]
                groups_of[0] = jnp.where(upper, ends[0], groups_of[0])
                groups_of[-1] = jnp.where(upper, groups_of[-1], ends[1])
                tiles.append(groups_of)
            for side, g in enumerate((0, groups - 1)):
                following = [x[g + 1] if g + 1 < groups else blank for x in tiles]
                block = window([x[g] for x in tiles[:fields]], following[:fields], tiles[fields][g], following[fields])
                store_lats(block, t, cells, side, m, lats, chunks, turned.at[(t * members + m) * 2 + side])
    for side in range(2):
        out[side, pl.ds(SUB, rows), :] = cells[side].astype(bf16)
        wrap(out.at[side], rows)
    for side in range(2):
        for r, step in row_pieces(rows):
            parts = [out[side, pl.ds(r + SUB * d, step), :] for d in range(3)]
            put(pre, side * (groups - 1), r, activate(dot(jnp.concatenate(parts, axis=1), t1[...])))
    last_weights(w4, t4)
    step_kernel(sizes, u, v, h, sea, rims, base)


def step_kernel(sizes, u, v, h, sea, rims, base):
    members, noises, levels = sizes
    fields = noises + 3 * levels
    lons, lats = sea.shape
    ocean = sea[...].astype(f32)
    lat_count = lax.axis_size("lat")
    lat_rows = (lax.axis_index("lat") * lats).astype(f32) + iota((lons, lats), 1).astype(f32)
    turn = CORIOLIS * (2.0 * (lat_rows + 0.5) / (lats * lat_count) - 1.0)
    at_first = iota((lons, lats), 0) == 0
    at_last = iota((lons, lats), 0) == lons - 1
    at_south = iota((lons, lats), 1) == 0
    at_north = iota((lons, lats), 1) == lats - 1
    lon_rests = members * fields * RIM + GROUP

    def around(x, m, c):
        row = (m * fields + c) * RIM
        more = lon_rests + m * (fields - noises) + c - noises
        west = rims[0, pl.ds(row + RIM - 1, 1)] + rims[0, pl.ds(more, 1)]
        east = rims[1, pl.ds(row, 1)] + rims[1, pl.ds(more, 1)]
        return (
            jnp.where(at_first, west, pltpu.roll(x, 1, 0)),
            jnp.where(at_last, east, pltpu.roll(x, lons - 1, 0)),
            jnp.where(at_south, 0.0, pltpu.roll(x, 1, 1)),
            jnp.where(at_north, 0.0, pltpu.roll(x, lats - 1, 1)),
        )

    for m in range(members):
        sets = []
        for level in range(levels):
            sets.append(
                [
                    (x[m, level], around(x[m, level], m, noises + n * levels + level))
                    for n, x in enumerate((u, v, h))
                ]
            )
        for level in range(levels):
            (cu, au), (cv, av), (ch, ah) = sets[level]
            upper, lower = sets[0][2][1], sets[1][2][1]
            pressure = [upper[i] + lower[i] for i in range(4)]
            if level == 1:
                pressure = [pressure[i] + REDUCED * lower[i] for i in range(4)]
            lap_u = au[1] + au[0] + au[3] + au[2] - 4.0 * cu
            lap_v = av[1] + av[0] + av[3] + av[2] - 4.0 * cv
            dx = 0.5 * (pressure[1] - pressure[0])
            dy = 0.5 * (pressure[3] - pressure[2])
            base[0, m, level] = ocean * (cu + TIME_STEP * (turn * cv - dx + VISCOSITY * lap_u))
            base[1, m, level] = ocean * (cv + TIME_STEP * (-turn * cu - dy + VISCOSITY * lap_v))
            flow = 0.5 * (ah[1] * au[1] - ah[0] * au[0]) + 0.5 * (ah[3] * av[3] - ah[2] * av[2])
            base[2, m, level] = ch - TIME_STEP * flow


def join_kernel(sizes, lons, lon_even, lon_odd, head, tail, even, odd, rims, wide):
    members, noises, levels = sizes
    fields = noises + 3 * levels
    groups = lons // GROUP + 1
    lats = lon_even.shape[1]
    for n, lanes in enumerate((slice(0, LANES), slice(lats - LANES, lats))):
        rims[0, n], rims[1, n] = lon_rims(lon_even, lon_odd, lanes)
    lane = iota((GROUP, LANES), 1)
    upper = iota((GROUP, LANES), 0) < RIM
    to_south = lax.axis_index("lat") % 2 == 1
    for c in range(fields + 1):
        rows = pl.ds(c * GROUP, GROUP)
        ends = []
        for n, (part, first) in enumerate(((head, 0), (tail, LANES - RIM))):
            total = part[rows]
            for side in range(2):
                held = upper if side == 0 else ~upper
                for m in range(members):
                    place = ((groups - 1) * side * members + m) * RIM
                    tile = rim_tile(sizes, m, c, side, rims.at[side, n])
                    moved = pltpu.roll(tile, (place - first) % LANES, 1)
                    total = jnp.where(held & (lane >= place) & (lane < place + RIM), moved, total)
            ends.append(total)
        wide[0, rows] = jnp.where(to_south, ends[0], ends[1])
        wide[1, rows] = jnp.where(to_south, ends[1], ends[0])
    rows = pl.ds((fields + 1) * GROUP, wide.shape[1] - (fields + 1) * GROUP)
    wide[:, rows] = jnp.zeros((2, wide.shape[1] - (fields + 1) * GROUP, LANES), f32)
    even[...] = wide[0].astype(bf16)
    odd[...] = wide[1].astype(bf16)


def extra_rows(hidden):
    per = LANES // hidden
    bias_row = iota((GROUP, LANES), 0)

    def bias_rows(bias):
        part = 0.5 * jnp.concatenate([bias[...]] * per, axis=1)
        b1 = part.astype(bf16).astype(f32)
        b2 = (part - b1).astype(bf16).astype(f32)
        b3 = part - b1 - b2
        zero = jnp.zeros((GROUP, LANES), f32)
        return jnp.where(
            bias_row == 0,
            b1,
            jnp.where(bias_row == 1, b2, jnp.where(bias_row == 2, b3, zero)),
        )

    def sea_rows(shift, tile):
        lon = iota((2 * GROUP, LANES), 0)
        out = iota((2 * GROUP, LANES), 1) // hidden + per * tile
        return jnp.where(lon == out + shift, LAND, 0.0)

    return sea_rows, bias_rows


def first_weights(w1, bias1, t1):
    hidden = w1.shape[3]
    per = LANES // hidden
    sea_rows, bias_rows = extra_rows(hidden)
    fields = w1.shape[0]
    out_lon = iota((GROUP, LANES), 1) // hidden
    in_row = iota((GROUP, LANES), 0)
    for dj in range(3):
        taps = []
        for di in range(3):
            cells = [w1[c, di].astype(f32)[dj : dj + 1] for c in range(fields)]
            taps.append(
                [jnp.broadcast_to(0.5 * jnp.concatenate([x] * per, axis=1), (GROUP, LANES)) for x in cells]
            )
        for tile in range(2):
            parts = []
            for c in range(fields):
                total = jnp.zeros((GROUP, LANES), f32)
                for di in range(3):
                    hit = in_row == out_lon + per * tile + di
                    total = jnp.where(hit, taps[di][c], total)
                parts.append(total)
            for start in range(0, fields, 4):
                total = jnp.zeros((GROUP, LANES), f32)
                for n in range(min(4, fields - start)):
                    for di in range(3):
                        hit = in_row % 2 + GROUP == out_lon + per * tile + di
                        total = jnp.where(hit & (in_row // 2 == n), taps[di][start + n], total)
                parts.append(total)
            if dj == 1:
                parts += [sea_rows(1, tile), bias_rows(bias1)]
            else:
                parts.append(jnp.zeros((3 * GROUP, LANES), f32))
            block = jnp.concatenate(parts, axis=0)
            t1[pl.ds(dj * LANES, LANES), pl.ds(tile * LANES, LANES)] = block.astype(bf16)


def hidden_weights(w2, w3, bias2, bias3, t2, t3):
    hidden = w2.shape[2]
    per = LANES // hidden
    lane = iota((hidden, LANES), 1)
    sea_rows, bias_rows = extra_rows(hidden)
    for layer, (w, bias, t) in enumerate(((w2, bias2, t2), (w3, bias3, t3))):
        for dj in range(3):
            taps = []
            for di in range(3):
                cell = 0.5 * w[di, dj].astype(f32)
                wide = jnp.concatenate([cell, jnp.zeros((hidden, LANES - hidden), f32)], axis=1)
                square = jnp.concatenate([wide] * per, axis=0)
                taps.append(jnp.transpose(square)[:hidden])
            for lon in range(GROUP + 2):
                for tile in range(2):
                    total = jnp.zeros((hidden, LANES), f32)
                    for di in range(3):
                        total = jnp.where(lane // hidden + per * tile == lon - di, taps[di], total)
                    if lon < GROUP:
                        row = dj * GROUP * hidden + lon * hidden
                    else:
                        row = 3 * GROUP * hidden + dj * 2 * hidden + (lon - GROUP) * hidden
                    t[pl.ds(row, hidden), pl.ds(tile * LANES, LANES)] = total.astype(bf16)
        for tile in range(2):
            block = jnp.concatenate(
                [
                    jnp.zeros((5 * GROUP, LANES), f32),
                    sea_rows(2 + layer, tile),
                    bias_rows(bias),
                ],
                axis=0,
            )
            row = 3 * GROUP * hidden + 6 * hidden
            t[pl.ds(row, 2 * hidden), pl.ds(tile * LANES, LANES)] = block.astype(bf16)


def last_weights(w4, t4):
    hidden = w4.shape[3]
    outs = w4.shape[2]
    half = LANES // 2
    lons = half // outs
    slot = iota((hidden, LANES), 1) // half
    out_lon = iota((hidden, LANES), 1) % lons
    taps = {}
    for dj in range(3):
        for di in range(3):
            cell = w4[di, dj].astype(f32)
            wide = jnp.concatenate([cell, jnp.zeros((outs, LANES - hidden), f32)], axis=1)
            square = jnp.concatenate(
                [jnp.broadcast_to(wide[c : c + 1], (lons, LANES)) for c in range(outs)] * 2, axis=0
            )
            taps[dj, di] = jnp.transpose(square)[:hidden]
    order = ((0, 1, 2, None), (1, 0, None, 2))
    for side in range(2):
        for lon in range(t4.shape[1] // hidden):
            for tile in range(2):
                total = jnp.zeros((hidden, LANES), f32)
                for place in range(2):
                    dj = order[side][2 * tile + place]
                    if dj is None:
                        continue
                    for di in range(3):
                        total = jnp.where((slot == place) & (out_lon == lon - di), taps[dj, di], total)
                t4[side, pl.ds(lon * hidden, hidden), pl.ds(tile * LANES, LANES)] = total.astype(bf16)


def main_kernel(
    sizes,
    bias_last,
    middle_in,
    ends_in,
    pre_in,
    base,
    sea,
    even_rim,
    odd_rim,
    own_tail,
    t1,
    t2,
    t3,
    t4,
    new_u,
    new_v,
    new_h,
    middle,
    ends,
    odd,
    even,
    force,
    gathered,
    turned,
    gaps,
    results,
    done,
):
    members, noises, levels = sizes
    fields = noises + 3 * levels
    lons, lats = sea.shape
    groups = lons // GROUP + 1
    chunks = SUB // members
    blocks = (lats + GAP) // chunks
    rows = blocks * SUB
    gap_k = lats - (chunks - 1) * blocks
    lat_index, lat_count = lax.axis_index("lat"), lax.axis_size("lat")
    top = lat_index == lat_count - 1
    is_odd = lat_index % 2 == 1
    bottom = lat_index == 0
    strip = odd_rim[...].astype(f32)
    paired = even_rim[...].astype(f32)
    south = jnp.where(is_odd, paired, jnp.where(bottom, 0.0, strip))

    wide = strip.shape[0]
    span = members * RIM
    lane = iota((wide, LANES), 1)
    rests = groups * span
    border = ((lane % RIM == 0) & (lane < rests)) | (lane >= rests)
    row_to = iota((wide, wide), 0)
    row_from = iota((wide, wide), 1)
    channel = row_to // GROUP
    mirrored = (channel == row_from // GROUP) & (row_from % GROUP == GROUP - 1 - row_to % GROUP)
    odd_parity = (channel >= noises) & (channel < noises + 2 * levels)
    flip_rows = jnp.where(mirrored, jnp.where(odd_parity, -1.0, 1.0), 0.0).astype(bf16)
    lane_from = iota((LANES, LANES), 0)
    lane_to = iota((LANES, LANES), 1)
    source = (groups - 1 - lane_to // span) * span + lane_to % span + RIM - 1
    moves = (lane_to % RIM == 0) & (lane_to < rests) & (lane_from == source)
    other = lane_to - rests
    source = rests + (groups - 1 - other // members) * members + other % members
    moves = moves | ((other >= 0) & (other < groups * members) & (lane_from == source))
    flip_lanes = jnp.where(moves, 1.0, 0.0).astype(bf16)
    pair = dot(flip_rows, jnp.concatenate([odd_rim[...], own_tail[...]], axis=1)).astype(bf16)
    folded = dot(pair[:, :LANES], flip_lanes)
    ghost = dot(pair[:, LANES:], flip_lanes)
    north = jnp.where(is_odd, strip, paired)
    north_rim = jnp.where(border & top, folded, north)

    for n, message in enumerate((north_rim, strip, ghost, south)):
        after = pltpu.roll(message, LANES - span, 1)
        cut = [message[c * GROUP : (c + 1) * GROUP] for c in range(fields + 1)]
        after = [after[c * GROUP : (c + 1) * GROUP] for c in range(fields + 1)]
        turned[n] = jnp.transpose(window(cut[:fields], after[:fields], cut[fields], after[fields]))
        for g in range(groups):
            for m in range(members):
                gap = (m - 1) % members if n == 3 else m
                start = n * RIM * SUB + gap * chunks + chunks - 1
                gaps[g, pl.ds(start, RIM, stride=SUB), :] = turned[n, pl.ds((g * members + m) * RIM, RIM), :]

    first = [ends.at[0]] + [middle.at[g] for g in range(groups - 2)] + [ends.at[1]]
    in_gap = iota((GAP * SUB, LANES), 0) % chunks == chunks - 1
    for g in range(groups):
        spot = pl.ds((1 + gap_k) * SUB, GAP * SUB)
        kept = first[g][spot, :].astype(f32)
        first[g][spot, :] = jnp.where(in_gap, gaps[g], kept).astype(bf16)
        wrap(first[g], rows)

    hidden = LANES // 4
    per = LANES // hidden
    tiles = odd.shape[0]
    pieces = row_pieces(rows, 4)

    def finish(x, valid):
        used = (valid + per - 1) // per

        @pl.when(top)
        def _():
            strip_top = SUB * (1 + gap_k + STRIP + RIM - 1)
            own_top = SUB * gap_k
            strip_ghost = SUB * (1 + gap_k + GHOST)
            own_ghost = SUB * (1 + gap_k + NORTH)
            last_chunk = iota((SUB, LANES), 0) % chunks == chunks - 1
            spot = iota((SUB, LANES), 1) // hidden
            for src, dst in ((strip_top, own_ghost), (own_top, strip_ghost)):
                found = [x[t, pl.ds(src, SUB), :].astype(f32) for t in range(used)]
                for t in range(used):
                    total = x[t, pl.ds(dst, SUB), :].astype(f32)
                    for i in range(per):
                        lon = valid - 1 - (per * t + i)
                        if lon < 0:
                            continue
                        moved = pltpu.roll(found[lon // per], (hidden * (i - lon % per)) % LANES, 1)
                        total = jnp.where(last_chunk & (spot == i), moved, total)
                    x[t, pl.ds(dst, SUB), :] = total.astype(bf16)

        for t in range(used):
            wrap(x.at[t], rows)

    for x in (odd, even):
        x[tiles - 1] = jnp.zeros(x.shape[1:], bf16)
    even[tiles - 2] = jnp.zeros(even.shape[1:], bf16)

    near = (gap_k - 1) * SUB
    for b in range(groups):
        parts = []
        for d in range(3):
            some = [first[b][pl.ds(near + SUB * d, rows - near), :], first[b][pl.ds(SUB * d, SUB), :]]
            parts.append(jnp.concatenate(some, axis=0))
        out = activate(dot(jnp.concatenate(parts, axis=1), t1[...]))
        put(odd, b, near, out[: rows - near])
        put(odd, b, 0, out[rows - near :])
    finish(odd, lons + 6)

    ocean = sea[...].astype(f32)
    narrow = iota((lons, LANES), 1)
    at_south = narrow == 0
    at_north = narrow == LANES - 1

    def beyond(message, m, offset, to):
        tall = message[noises * GROUP : fields * GROUP]
        columns = []
        for g in range(groups):
            spot = (g * members + m) * RIM + offset
            more = rests + g * members + m
            column = pltpu.roll(tall, (to - spot) % LANES, 1)
            columns.append(column + pltpu.roll(tall, (to - more) % LANES, 1))
        cells = []
        for c in range(fields - noises):
            whole = jnp.concatenate([x[c * GROUP : (c + 1) * GROUP] for x in columns], axis=0)
            cells.append(pltpu.roll(whole, lons + GROUP - RIM, 0)[:lons])
        return cells

    def step_rims(m):
        rims = [beyond(south, m, RIM - 1, 0), beyond(north_rim, m, 0, LANES - 1)]
        for level in range(levels):
            gains = []
            for (sign, spot), rim in zip(((1.0, at_south), (-1.0, at_north)), rims):
                ru, rv, rh = rim[level], rim[levels + level], rim[2 * levels + level]
                pressure = rim[2 * levels] + rim[2 * levels + 1]
                if level == 1:
                    pressure = pressure + REDUCED * rh
                gains.append(
                    [
                        jnp.where(spot, TIME_STEP * VISCOSITY * ru, 0.0),
                        jnp.where(spot, TIME_STEP * (VISCOSITY * rv + sign * 0.5 * pressure), 0.0),
                        jnp.where(spot, TIME_STEP * sign * 0.5 * (rh * rv), 0.0),
                    ]
                )
            middle = [jnp.zeros((lons, lats - 2 * LANES), f32)] if lats > 2 * LANES else []
            gains = [jnp.concatenate([gains[0][n]] + middle + [gains[1][n]], axis=1) for n in range(3)]
            results[0, m, level] = base[0, m, level] + ocean * gains[0]
            results[1, m, level] = base[1, m, level] + ocean * gains[1]
            results[2, m, level] = base[2, m, level] + gains[2]
        pltpu.make_async_copy(results.at[2, m], new_h.at[m], done.at[2, m]).start()

    width = GROUP * hidden

    def layer(x, y, t, left_over, beside):
        for b in range(groups):
            for r, step in pieces:
                lower = iota((step, LANES), 1) < 2 * hidden

                def cells_of(tile, d):
                    return x[tile, pl.ds(r + SUB * d, step), :]

                def packed(tile):
                    more = [cells_of(tile, d) for d in range(3)]
                    return [
                        jnp.where(lower, more[0], pltpu.roll(more[1], 2 * hidden, 1)),
                        jnp.where(lower, more[2], first[b][pl.ds(r + SUB, step), :]),
                    ]

                if b < groups - 1:
                    parts = [cells_of(2 * b + e, d) for d in range(3) for e in range(2)] + packed(2 * b + 2)
                    matrix = t[...]
                elif left_over == per:
                    parts = [cells_of(2 * b, d) for d in range(3)] + packed(2 * b + 1)
                    lanes = pl.ds(0, LANES)
                    matrix = jnp.concatenate(
                        [t[pl.ds(d * width, LANES), lanes] for d in range(3)]
                        + [t[pl.ds(d * width + LANES, 2 * hidden), lanes] for d in range(3)]
                        + [t[pl.ds(3 * width + 6 * hidden, 2 * hidden), lanes]],
                        axis=0,
                    )
                else:
                    parts = [cells_of(2 * b, d) for d in range(3)] + [first[b][pl.ds(r + SUB, step), :]]
                    lanes = pl.ds(0, LANES)
                    matrix = jnp.concatenate(
                        [t[pl.ds(d * width, LANES), lanes] for d in range(3)]
                        + [jnp.zeros((2 * hidden, LANES), bf16)]
                        + [t[pl.ds(3 * width + 6 * hidden, 2 * hidden), lanes]],
                        axis=0,
                    )
                put(y, b, r, activate(dot(jnp.concatenate(parts, axis=1), matrix)))
            for m in beside.get(b, ()):
                step_rims(m)

    beside = {}
    for m in range(members):
        beside.setdefault(min(m, groups - 1), []).append(m)
    layer(odd, even, t2, per, beside)
    finish(even, lons + 4)
    layer(even, odd, t3, per // 2, {})
    finish(odd, lons + 2)

    depth = t4.shape[1] // LANES
    padded = rows + 2 * SUB
    for r, long in row_pieces(padded, 4):
        before = iota((long, LANES), 1) < LANES // 2
        span_rows = pl.ds(r, long)
        sides = []
        for side in range(2):
            parts = [odd[side * (depth - 1) + t, span_rows, :] for t in range(depth)]
            sides.append(dot(jnp.concatenate(parts, axis=1), t4[side]))
        force[0, span_rows, :] = jnp.where(before, sides[0][:, :LANES], sides[1][:, :LANES])
        swapped = jnp.where(before, sides[1][:, :LANES], sides[0][:, :LANES])
        force[1, span_rows, :] = pltpu.roll(swapped, LANES // 2, 1)
        force[2, span_rows, :] = jnp.where(before, sides[0][:, LANES:], sides[1][:, LANES:])

    halves = lons // 2
    for r, step in pieces:
        total = force[0, pl.ds(r, step), :] + force[1, pl.ds(r + SUB, step), :]
        force[0, pl.ds(r, step), :] = total + force[2, pl.ds(r + 2 * SUB, step), :]
    for m in range(members):
        for q in range(chunks):
            size = min(blocks, lats - q * blocks)
            gathered[m, pl.ds(q * blocks, size), :] = force[0, pl.ds(m * chunks + q, size, stride=SUB), :]
        turned_force = jnp.transpose(gathered[m])
        for n, out in enumerate((new_u, new_v)):
            for level in range(levels):
                c = n * levels + level
                parts = [
                    turned_force[side * LANES // 2 + c * halves : side * LANES // 2 + (c + 1) * halves]
                    for side in range(2)
                ]
                push = TIME_STEP * (jnp.concatenate(parts, axis=0) + bias_last[c])
                results[n, m, level] = results[n, m, level] + ocean * push
            pltpu.make_async_copy(results.at[n, m], out.at[m], done.at[n, m]).start()
    for m in range(members):
        for n, out in enumerate((new_u, new_v, new_h)):
            pltpu.make_async_copy(results.at[n, m], out.at[m], done.at[n, m]).wait()


def body(
    noise,
    velocity_u,
    velocity_v,
    thickness,
    land_sea,
    conv_first,
    bias_first,
    conv_second,
    bias_second,
    conv_third,
    bias_third,
    conv_last,
    bias_last,
):
    members, noises, lons, lats = noise.shape
    levels = velocity_u.shape[1]
    fields = noises + 3 * levels
    sizes = (members, noises, levels)
    hidden = conv_first.shape[0]
    outs = conv_last.shape[0]
    groups = lons // GROUP + 1
    rows = members * (lats + GAP)
    assert hidden * 4 == LANES and outs * lons == LANES and members * (RIM + 1) * groups <= LANES
    assert fields % 2 == 0 and 4 * -(-fields // 4) == 12 and GROUP * (fields + 6) == LANES and lons % 16 == 0
    assert lats % LANES == 0 and SUB % members == 0 and (lats + GAP) % (SUB // members) == 0
    lon_count, lat_count = lax.axis_size("lon"), lax.axis_size("lat")
    assert lon_count % 2 == 0 and lat_count % 2 == 0
    state = (noise, velocity_u, velocity_v, thickness, land_sea)
    whole = pl.BlockSpec(memory_space=pltpu.VMEM)

    tall = members * fields * RIM + GROUP + members * 3 * levels
    assert tall % SUB == 0
    args = state + (
        conv_first.transpose(1, 2, 3, 0),
        conv_second.transpose(2, 3, 0, 1),
        conv_third.transpose(2, 3, 0, 1),
        conv_last.transpose(2, 3, 0, 1),
        bias_first[None],
        bias_second[None],
        bias_third[None],
    )
    count = len(args)
    *held, to_even, to_odd = pl.pallas_call(
        functools.partial(pack_lon_kernel, sizes, count),
        out_shape=[pltpu.VMEM(x.shape, x.dtype) for x in args] + [pltpu.VMEM((tall, lats), bf16)] * 2,
        in_specs=[pl.BlockSpec(memory_space=pltpu.HBM)] * count,
        out_specs=[whole] * (count + 2),
        scratch_shapes=[pltpu.VMEM((2, tall, lats), f32), pltpu.SemaphoreType.DMA((count,))],
        compiler_params=pltpu.CompilerParams(vmem_limit_bytes=62 * 2**20),
        name="pack_lon",
    )(*args)
    state = tuple(held[:5])
    lon_even = lax.ppermute(to_even, "lon", [(i, i ^ 1) for i in range(lon_count)])
    lon_odd = lax.ppermute(to_odd, "lon", [(i, (i - 1 + 2 * (i % 2)) % lon_count) for i in range(lon_count)])

    wide = -(-(fields + 1) * GROUP // SUB) * SUB
    part = pltpu.VMEM((wide, LANES), f32)
    message = pltpu.VMEM((wide, LANES), bf16)
    deep = -(-(lons // 2 + 2) * hidden // LANES) * LANES
    padded = rows + 2 * SUB
    tiles = 2 * groups + 1
    t1, t2, t3, own_head, own_tail, middle, pre = pl.pallas_call(
        functools.partial(prepare_kernel, sizes),
        out_shape=[
            pltpu.VMEM((3 * LANES, 2 * LANES), bf16),
            pltpu.VMEM((8 * LANES, 2 * LANES), bf16),
            pltpu.VMEM((8 * LANES, 2 * LANES), bf16),
            part,
            part,
            pltpu.VMEM((groups - 2, padded, LANES), bf16),
            pltpu.VMEM((tiles, padded, LANES), bf16),
        ],
        in_specs=[whole] * 11,
        out_specs=[whole] * 7,
        scratch_shapes=[
            pltpu.VMEM((groups - 1, rows, LANES), f32),
            pltpu.VMEM((members * (groups - 2) * lats // LANES + 1, LANES, LANES), f32),
        ],
        compiler_params=pltpu.CompilerParams(vmem_limit_bytes=12 * 2**20),
        cost_estimate=pl.CostEstimate(flops=10**7, bytes_accessed=10**7, transcendentals=0),
        name="prepare",
    )(*held[:8], *held[9:])
    last = lat_count - 1
    smem = pl.BlockSpec(memory_space=pltpu.SMEM)
    to_even, to_odd = pl.pallas_call(
        functools.partial(join_kernel, sizes, lons),
        out_shape=[message] * 2,
        in_specs=[whole] * 4,
        out_specs=[whole] * 2,
        scratch_shapes=[
            pltpu.VMEM((2, 2, tall, LANES), f32),
            pltpu.VMEM((2, wide, LANES), f32),
        ],
        compiler_params=pltpu.CompilerParams(vmem_limit_bytes=4 * 2**20),
        name="join_rims",
    )(lon_even, lon_odd, own_head, own_tail)
    even_rim = lax.ppermute(to_even, "lat", [(i, i ^ 1) for i in range(lat_count)])
    pairs = []
    for t in range(lon_count):
        at = t * lat_count
        pairs += [(at + k, at + k - 1 + 2 * (k % 2)) for k in range(1, last)]
        pairs += [(at, (t ^ 1) * lat_count), (at + last, (lon_count - 1 - t) * lat_count + last)]
    odd_rim = lax.ppermute(to_odd, ("lon", "lat"), pairs)

    ends, base, pre, t4 = pl.pallas_call(
        functools.partial(cells_kernel, sizes),
        out_shape=[
            pltpu.VMEM((2, padded, LANES), bf16),
            pltpu.VMEM((3, *velocity_u.shape), f32),
            pltpu.VMEM(pre.shape, bf16),
            pltpu.VMEM((2, deep, 2 * LANES), bf16),
        ],
        in_specs=[whole] * 11,
        out_specs=[whole] * 4,
        input_output_aliases={10: 2},
        scratch_shapes=[
            pltpu.VMEM((2, tall, lats), f32),
            pltpu.VMEM((3, rows, LANES), f32),
            pltpu.VMEM((2 * members * lats // LANES + 1, LANES, LANES), f32),
        ],
        compiler_params=pltpu.CompilerParams(vmem_limit_bytes=12 * 2**20),
        cost_estimate=pl.CostEstimate(flops=10**7, bytes_accessed=10**7, transcendentals=0),
        name="cells",
    )(*state, lon_even, lon_odd, to_even, held[8], t1, pre)

    out = jax.ShapeDtypeStruct(velocity_u.shape, f32)
    return pl.pallas_call(
        functools.partial(main_kernel, sizes),
        out_shape=[out] * 3 + [pltpu.VMEM(x.shape, x.dtype) for x in (middle, ends, pre)],
        in_specs=[smem] + [whole] * 12,
        out_specs=[pl.BlockSpec(memory_space=pltpu.HBM)] * 3 + [whole] * 3,
        input_output_aliases={1: 3, 2: 4, 3: 5},
        scratch_shapes=[
            pltpu.VMEM((tiles, padded, LANES), bf16),
            pltpu.VMEM((3, padded, LANES), f32),
            pltpu.VMEM((members + 1, lats, LANES), f32),
            pltpu.VMEM((5, LANES, LANES), f32),
            pltpu.VMEM((groups + 1, GAP * SUB, LANES), f32),
            pltpu.VMEM((3, *velocity_u.shape), f32),
            pltpu.SemaphoreType.DMA((3, members)),
        ],
        compiler_params=pltpu.CompilerParams(vmem_limit_bytes=32 * 2**20),
        cost_estimate=pl.CostEstimate(flops=2 * 10**10, bytes_accessed=10**7, transcendentals=4 * 10**6),
        name="network_and_step",
    )(
        bias_last,
        middle,
        ends,
        pre,
        base,
        state[4],
        even_rim,
        odd_rim,
        to_odd,
        t1,
        t2,
        t3,
        t4,
    )[:3]


def solution(mesh):
    tiles = P(None, None, "lon", "lat")
    return jax.shard_map(
        body,
        mesh=mesh,
        in_specs=(tiles,) * 4 + (P("lon", "lat"),) + (P(),) * 8,
        out_specs=(tiles,) * 3,
        check_vma=False,
    )
```
